32 devices in a mesh: dp: 4 (over y, x), expert: 8 (over z, core).
Axes of the slice: x: 2, y: 2, z: 4, core: 2. Of those that a mesh axis runs over, the one named last changes fastest.
Arguments:
- tokens: bfloat16 [4096, 1024], P(('dp', 'expert')), may hold values from -6 to 6
- cotangent: bfloat16 [4096, 1024], P(('dp', 'expert')), may hold values from -6 to 6
- seq_lengths: int32 [32, 2], P(('dp', 'expert')), may hold values from 0 to 128, as said below
- routes: int32 [4096, 16], P(('dp', 'expert')), may hold values from 0 to 47, all different within a row; in each aligned block of 128 rows (0 to 127, 128 to 255, ...) at most 64 rows name the same one
- head_experts: int32 [4096, 4, 2], P(('dp', 'expert')), may hold values from 0 to 4, all different within a row
- norm_gain: float32 [1024], replicated, may hold values from 0.25 to 1.75
- w_query: bfloat16 [1024, 512], replicated, may hold values from -0.1875 to 0.1875
- w_key: bfloat16 [1024, 512], replicated, may hold values from -0.1875 to 0.1875
- w_value: bfloat16 [1024, 2560], replicated, may hold values from -0.1875 to 0.1875
- w_output: bfloat16 [1024, 2560], replicated, may hold values from -2 to 2
- w_value_gate: bfloat16 [1024, 20], replicated, may hold values from -0.125 to 0.125
- w_output_gate: bfloat16 [1024, 20], replicated, may hold values from -0.125 to 0.125
- w_router: bfloat16 [1024, 48], replicated, may hold values from -0.0625 to 0.0625
- w_up: bfloat16 [48, 1024, 128], P('expert'), may hold values from -0.1875 to 0.1875
- w_down: bfloat16 [48, 1024, 128], P('expert'), may hold values from -0.5 to 0.5
Outputs:
- mixed: bfloat16 [4096, 1024], P(('dp', 'expert'))
- grad_tokens: float32 [4096, 1024], P(('dp', 'expert'))
- grad_gain: float32 [1024], P(('dp', 'expert'))
- grad_query: float32 [1024, 512], P(('dp', 'expert'))
- grad_key: float32 [1024, 512], P(('dp', 'expert'))
- grad_value: float32 [1024, 2560], P(('dp', 'expert'))
- grad_output: float32 [1024, 2560], P(('dp', 'expert'))
- grad_value_gate: float32 [1024, 20], P(('dp', 'expert'))
- grad_output_gate: float32 [1024, 20], P(('dp', 'expert'))
- grad_router: float32 [1024, 48], P(('dp', 'expert'))
- grad_up: float32 [48, 1024, 128], P('expert', 'dp')
- grad_down: float32 [48, 1024, 128], P('expert', 'dp')
The draws below stay inside these ranges and needn't reach their ends.
Inputs may be any that keep to these rules, and one draw needn't show every extreme that they name: `seq_lengths`: row r lists the lengths of the one or two sequences packed from the start of device block r; each row sums to at most 128, rows past the sum are padding, and in every draw some block holds one sequence of exactly 128 rows. The 16 experts of a token differ. Within the rows of one device block no expert is named by more than 64 routes, and in every draw some expert is named by exactly 64 routes of some block. `head_experts`: the two experts of a token and head differ.
All inputs are finite; a program needn't handle non-finite values.
Results may differ from the reference program's by a relative error of at most 0.013.
Values may be sent and summed in bfloat16 or wider, within the bound.
A program may use at most 192 MiB of HBM per device.

```python
import math
import jax
import jax.numpy as jnp
import numpy as np
from jax import lax

D = 1024
H = 4
DH = 128
EA = 5
FFE = 128
TOPK = 16
TOK_DEV = 128
SHARDS = 32
TOKENS = 4096
EXPERTS = 48
MOST = 64


def draw_seq_lengths(key, part):
    key = jax.random.fold_in(key, 7)
    cut_key, end_key, pair_key, full_key = jax.random.split(key, 4)
    quarter = TOK_DEV // 4
    ends = TOK_DEV - jax.random.randint(end_key, (SHARDS,), 0, quarter + 1).astype(jnp.int32)
    raw_cut = jax.random.randint(cut_key, (SHARDS,), 0, TOK_DEV + 1).astype(jnp.int32)
    cuts = quarter + raw_cut % (ends - 2 * quarter + 1)
    paired = jax.random.randint(pair_key, (SHARDS,), 0, 2) == 1
    first = jnp.where(paired, cuts, ends)
    second = jnp.where(paired, ends - cuts, 0)
    full_block = jax.random.randint(full_key, (), 0, SHARDS)
    is_full = jnp.arange(SHARDS) == full_block
    first = jnp.where(is_full, TOK_DEV, first)
    second = jnp.where(is_full, 0, second)
    return jnp.stack([first, second], axis=1).astype(jnp.int32)


def strengthened(values, own_key, source, target, shards_of, factor):
    def block_of(axis_at):
        return (jnp.arange(values.shape[axis_at]) // (values.shape[axis_at] // shards_of)).reshape((-1,) + (1,) * (values.ndim - 1 - axis_at))

    one_side = jax.random.permutation(own_key, shards_of)[block_of(target)]
    other_side = (block_of(target) + shards_of // 2) % shards_of
    return jnp.where((block_of(source) == one_side) | (block_of(source) == other_side), factor * values, values)


def level_of(stream_key, extent, shards, smallest, top_value):
    factor_of = 1.0
    for position, parts in shards:
        heights = jax.random.uniform(jax.random.fold_in(jax.random.fold_in(stream_key, 6), position), (parts,), jnp.float32, smallest / len(shards), top_value / len(shards))
        factor_of = factor_of * jnp.repeat(jnp.exp(heights), extent[position] // parts).reshape((-1,) + (1,) * (len(extent) - 1 - position))
    return factor_of


def picks_of(own_key, rows, count, top, lift):
    sequence = jax.random.permutation(jax.random.fold_in(own_key, 1), count)
    boost = sequence
    for power in range(3):
        boost = boost * boost // count
    boost = boost * lift // count
    tickets = jax.random.randint(jax.random.fold_in(own_key, 2), (rows, count), 0, 4096) + boost
    sure = jax.random.permutation(jax.random.fold_in(own_key, 3), rows)[jnp.arange(count) % rows]
    tickets = jnp.where(jnp.arange(rows)[:, None] == sure[None, :], 1 << 14, tickets)
    merit = tickets * count + jnp.arange(count)
    return lax.top_k(merit.astype(jnp.int32), top)[1].astype(jnp.int32)


def deal_out(key, own, number, rows, count, top, bound, lean):
    order = jax.random.permutation(key, count)
    heavy_load, common = portions_of(count, rows * top, bound, lean, True), portions_of(count, rows * top, bound, lean, False)
    places = jnp.arange(count)

    def named(sizes, offset_by):
        used = int((sizes > 0).sum())
        fixed = max(1, used // 4)
        moved = fixed + (places - fixed + offset_by * (used - fixed)) % max(1, count - fixed)
        return jnp.zeros((count,), jnp.int32).at[order[jnp.where(places < fixed, places, moved)]].set(jnp.asarray(sizes, jnp.int32))

    sizes = jnp.where(number % 4 == 0, named(heavy_load, number // 4), named(common, number - number // 4 - 1))
    mixed = jax.random.permutation(jax.random.fold_in(own, 3), count)
    giver, taker = mixed[0:count // 2 * 2:2], mixed[1:count // 2 * 2:2]
    room = jnp.minimum(sizes[giver] - 1, bound - sizes[taker]) // 2
    room = jnp.where((giver == order[0]) | (taker == order[0]) | (sizes[taker] == 0), 0, jnp.maximum(room, 0))
    moved = jax.random.randint(jax.random.fold_in(own, 4), (count // 2,), 0, 1 << 20) % (room + 1)
    sizes = sizes.at[giver].add(-moved).at[taker].add(moved)
    items = jnp.searchsorted(jnp.cumsum(sizes), jnp.arange(rows * top), side="right").astype(jnp.int32)
    listing = items.reshape(top, rows).T
    listing = listing[jax.random.permutation(jax.random.fold_in(own, 1), rows)]
    offset_by = jax.random.randint(jax.random.fold_in(own, 2), (rows, 1), 0, top)
    return jnp.take_along_axis(listing, (jnp.arange(top)[None, :] + offset_by) % top, axis=1)


def portions_of(count, total, most, slope, full):
    weights = [(1 << 20) // math.isqrt(standing ** slope) + 1 for standing in range(1, count + 1)]
    largest = most if full else min(most, max(-(-total // count), total * weights[0] // sum(weights)))
    least = 1 if total - largest >= count - 1 else 0
    counts, surplus = [largest] + [least] * (count - 1), total - largest - least * (count - 1)
    while surplus > 0:
        free = [i for i in range(1, count) if counts[i] < largest] or [i for i in range(1, count) if counts[i] < most]
        pool, left = sum([weights[i] for i in free]), surplus
        for i in free:
            addition = min(most - counts[i], max(1, left * weights[i] // pool), surplus)
            counts[i] = counts[i] + addition
            surplus = surplus - addition
    return np.array(counts)


def bell_draw(rng, shape, scale, limit, cuts=(), kind=jnp.bfloat16):
    gain = level_of(rng, shape, cuts, -0.22, 0.18) if cuts else 1.0
    result = jax.random.normal(rng, shape, jnp.float32) * scale * gain
    return jnp.minimum(jnp.maximum(result, -limit), limit).astype(kind)


def heavy_noise(key, extent, scale, bound, cuts, heavy, held_as=jnp.bfloat16):
    values = scale * jax.random.normal(key, extent, jnp.float32)
    if cuts:
        values = values * level_of(key, extent, cuts, -0.22, 0.18)
    return jnp.clip(strengthened(values, jax.random.fold_in(key, 3), *heavy), -bound, bound).astype(held_as)


def setup_inputs(seed: int = 0) -> dict:
    splits = jax.random.split(jax.random.key(seed), 16)
    tokens = bell_draw(splits[0], (TOKENS, D), 1.0, 6.0, ((0, 32),))
    cotangent = heavy_noise(splits[1], (TOKENS, D), 1.0, 6.0, ((0, 32),), (0, 1, 32, 2.75))
    seq_lengths = draw_seq_lengths(jax.random.fold_in(splits[15], 71), 0)
    routes_keys = jax.random.split(jax.random.fold_in(splits[3], 1), TOKENS // TOK_DEV)
    routes_turns = jax.random.permutation(jax.random.fold_in(splits[3], 3), TOKENS // TOK_DEV)
    routes = jax.vmap(lambda own, number: deal_out(jax.random.fold_in(splits[3], 2), own, number, TOK_DEV, EXPERTS, TOPK, MOST, 2))(routes_keys, routes_turns).reshape((TOKENS, TOPK))
    head_experts = picks_of(splits[4], TOKENS * H, EA, 2, 0).reshape((TOKENS, H, 2))
    norm_gain = jnp.clip(1.0 + 0.15 * jax.random.normal(splits[5], (D,), jnp.float32), 0.25, 1.75)
    w_query = bell_draw(splits[6], (D, H * DH), D ** -0.5, 0.1875)
    w_key = bell_draw(splits[7], (D, H * DH), D ** -0.5, 0.1875)
    w_value = bell_draw(splits[8], (D, EA * H * DH), D ** -0.5, 0.1875)
    w_output = bell_draw(splits[9], (D, EA * H * DH), (DH // 16) ** -0.5, 2.0)
    w_value_gate = bell_draw(splits[10], (D, EA * H), (2 * D) ** -0.5, 0.125)
    w_output_gate = bell_draw(splits[11], (D, EA * H), (2 * D) ** -0.5, 0.125)
    w_router = bell_draw(splits[12], (D, EXPERTS), (8 * D) ** -0.5, 0.0625)
    w_up = bell_draw(splits[13], (EXPERTS, D, FFE), D ** -0.5, 0.1875, ((0, 8),))
    w_down = bell_draw(splits[14], (EXPERTS, D, FFE), FFE ** -0.5, 0.5, ((0, 8),))
    return dict(tokens=tokens, cotangent=cotangent, seq_lengths=seq_lengths, routes=routes, head_experts=head_experts, norm_gain=norm_gain, w_query=w_query, w_key=w_key, w_value=w_value, w_output=w_output, w_value_gate=w_value_gate, w_output_gate=w_output_gate, w_router=w_router, w_up=w_up, w_down=w_down)


norm_eps = 1e-05
rope_base = 10000.0
masked_score = -1e+30

@jax.custom_vjp
def low(v):
    return lax.optimization_barrier(v.astype(jnp.bfloat16)).astype(jnp.float32)

@jax.custom_vjp
def low_back(v):
    return v

def low_keep(v):
    return (low(v), None)

def low_pass(kept, grad):
    return (grad,)

def back_keep(v):
    return (v, None)

def back_low(kept, grad):
    return (low(grad),)
low.defvjp(low_keep, low_pass)
low_back.defvjp(back_keep, back_low)

def product(left, right):
    return jnp.dot(left, right, precision=lax.Precision.HIGHEST)

def sequence_layout(lengths, count):
    bounds = jnp.cumsum(lengths).astype(jnp.int32)
    starts = (bounds - lengths).astype(jnp.int32)
    places = jnp.arange(count, dtype=jnp.int32)
    seq_ids = lax.optimization_barrier(jnp.sum((places[:, None] >= bounds[None, :]).astype(jnp.int32), axis=1)).astype(jnp.int32)
    live = places < bounds[-1]
    slot_ids = jnp.arange(lengths.shape[0], dtype=jnp.int32)
    first = lax.optimization_barrier(jnp.sum(jnp.where(seq_ids[:, None] == slot_ids[None, :], starts[None, :], 0), axis=1)).astype(jnp.int32)
    positions = jnp.where(live, places - first, 0).astype(jnp.int32)
    return (seq_ids, live, positions)

def rope_tables(positions, width):
    half = width // 2
    freq = rope_base ** (-(jnp.arange(half, dtype=jnp.float32) * 2.0 / width))
    angles = positions.astype(jnp.float32)[:, None] * freq[None, :]
    return (jnp.cos(angles), jnp.sin(angles))

def rotate(field, cosine, sine):
    half = field.shape[-1] // 2
    first, second = (field[..., :half], field[..., half:])
    cos_h, sin_h = (cosine[:, None, :], sine[:, None, :])
    return jnp.concatenate([first * cos_h - second * sin_h, second * cos_h + first * sin_h], axis=-1)

def slot_tables(routes, experts, most):
    count = routes.shape[0] * routes.shape[1]
    flat = routes.reshape(count).astype(jnp.int32)
    order = jnp.argsort(flat, stable=True).astype(jnp.int32)
    ordered = flat[order]
    firsts = jnp.searchsorted(ordered, jnp.arange(experts, dtype=jnp.int32)).astype(jnp.int32)
    ranks = jnp.arange(count, dtype=jnp.int32) - firsts[ordered]
    sorted_slots = (ordered * most + ranks).astype(jnp.int32)
    slot_of_row = jnp.zeros((count,), jnp.int32).at[order].set(sorted_slots)
    row_of_slot = jnp.full((experts * most,), count, jnp.int32).at[sorted_slots].set(order)
    return (slot_of_row, row_of_slot)

def layer_block(block_in, lengths, routes, head_experts, norm_gain, w_query, w_key, w_value, w_output, w_value_gate, w_output_gate, w_router, w_up, w_down):
    count = TOK_DEV
    seq_ids, live, positions = sequence_layout(lengths, count)
    cosine, sine = rope_tables(positions, DH)
    centred = block_in - lax.optimization_barrier(jnp.mean(block_in, axis=-1, keepdims=True))
    inverse = lax.rsqrt(lax.optimization_barrier(jnp.mean(centred * centred, axis=-1, keepdims=True)) + norm_eps)
    normed = low(centred * inverse * norm_gain)
    query_proj = low_back(product(normed, w_query)).reshape(count, H, DH)
    key_proj = low_back(product(normed, w_key)).reshape(count, H, DH)
    query_rot = low(rotate(query_proj, cosine, sine) * DH ** (-0.5))
    key_rot = low(rotate(key_proj, cosine, sine))
    chosen = jnp.any(head_experts[:, None, :, :] == jnp.arange(EA, dtype=jnp.int32)[None, :, None, None], axis=-1)
    value_gates = jnp.where(chosen, jax.nn.sigmoid(low_back(product(block_in, w_value_gate)).reshape(count, EA, H)), 0.0)
    output_gates = jnp.where(chosen, jax.nn.sigmoid(low_back(product(block_in, w_output_gate)).reshape(count, EA, H)), 0.0)
    value_all = low_back(product(block_in, w_value)).reshape(count, EA, H, DH)
    values = low(lax.optimization_barrier(jnp.sum(value_gates[..., None] * value_all, axis=1)))
    places = jnp.arange(count, dtype=jnp.int32)
    allowed = (seq_ids[:, None] == seq_ids[None, :]) & (places[None, :] <= places[:, None]) & live[None, :] | (places[None, :] == places[:, None])
    scores = low_back(jnp.einsum('qhd,khd->hqk', query_rot, key_rot, precision=lax.Precision.HIGHEST))
    scores = jnp.where(allowed[None], scores, masked_score)
    highest = lax.optimization_barrier(jnp.max(scores, axis=-1, keepdims=True))
    shifted = jnp.exp(scores - highest)
    shares = low(shifted / lax.optimization_barrier(jnp.sum(shifted, axis=-1, keepdims=True)))
    attended = low_back(jnp.einsum('hqk,khd->qhd', shares, values, precision=lax.Precision.HIGHEST))
    heads_mixed = low(output_gates[..., None] * attended[:, None]).reshape(count, EA * H * DH)
    hidden = block_in + low_back(product(heads_mixed, w_output.T))
    hidden_low = low(hidden)
    logits = low_back(product(hidden_low, w_router))
    gates = jax.nn.sigmoid(jnp.take_along_axis(logits, routes, axis=1))
    slot_of_row, row_of_slot = slot_tables(routes, EXPERTS, MOST)
    routed = count * TOPK
    valid = row_of_slot < routed
    source = jnp.minimum(row_of_slot, routed - 1) // TOPK
    outgoing = low_back(jnp.where(valid[:, None], hidden_low[source], 0.0)).reshape(EXPERTS, MOST, D)
    raised = low_back(jnp.einsum('emd,edf->emf', outgoing, w_up, precision=lax.Precision.HIGHEST))
    active = low(jax.nn.silu(raised))
    lowered = low_back(low(jnp.einsum('emf,edf->emd', active, w_down, precision=lax.Precision.HIGHEST)))
    expert_rows = lowered.reshape(EXPERTS * MOST, D)[slot_of_row].reshape(count, TOPK, D)
    return hidden + lax.optimization_barrier(jnp.sum(gates[..., None] * expert_rows, axis=1))

def live_rows(lengths):
    return sequence_layout(lengths, TOK_DEV)[1]

def reference(tokens, cotangent, seq_lengths, routes, head_experts, norm_gain, w_query, w_key, w_value, w_output, w_value_gate, w_output_gate, w_router, w_up, w_down):
    inputs = tokens.astype(jnp.float32)
    weights = tuple((item.astype(jnp.float32) for item in (norm_gain, w_query, w_key, w_value, w_output, w_value_gate, w_output_gate, w_router, w_up, w_down)))

    def forward(block_inputs, *params):

        def step(carry, block):
            block_in, lengths, block_routes, block_heads = block
            return (carry, layer_block(block_in, lengths, block_routes, block_heads, *params))
        blocks = (block_inputs.reshape(SHARDS, TOK_DEV, D), seq_lengths, routes.reshape(SHARDS, TOK_DEV, TOPK), head_experts.reshape(SHARDS, TOK_DEV, H, 2))
        _, outputs = lax.scan(jax.checkpoint(step), jnp.zeros((), jnp.float32), blocks)
        return outputs.reshape(TOKENS, D)
    output, pullback = jax.vjp(forward, inputs, *weights)
    live = jax.vmap(live_rows)(seq_lengths).reshape(TOKENS)
    grads = pullback(cotangent.astype(jnp.float32) * live[:, None].astype(jnp.float32))
    return (output.astype(jnp.bfloat16), grads[0], grads[1], grads[2], grads[3], grads[4], grads[5], grads[6], grads[7], grads[8], grads[9], grads[10])
```

```python
import functools
import math

import jax
import jax.numpy as jnp
from jax import lax
from jax.experimental import pallas as pl
from jax.experimental.pallas import tpu as pltpu
from jax.sharding import PartitionSpec as P

D = 1024
H = 4
DH = 128
EA = 5
TOPK = 16


norm_eps = 1e-05
rope_base = 10000.0
masked_score = -1e30


def sequence_layout(lengths, count):
    bounds = jnp.cumsum(lengths)
    starts = bounds - lengths
    places = jnp.arange(count, dtype=jnp.int32)
    seq_ids = jnp.sum((places[:, None] >= bounds[None, :]).astype(jnp.int32), axis=1)
    live = places < bounds[-1]
    slot_ids = jnp.arange(lengths.shape[0], dtype=jnp.int32)
    first = jnp.sum(jnp.where(seq_ids[:, None] == slot_ids[None, :], starts[None, :], 0), axis=1)
    positions = jnp.where(live, places - first, 0)
    return (seq_ids, live, positions)


def rope_tables(positions, width):
    half = width // 2
    freq = rope_base ** (-(jnp.arange(half, dtype=jnp.float32) * 2.0 / width))
    angles = positions.astype(jnp.float32)[:, None] * freq[None, :]
    return (jnp.cos(angles), jnp.sin(angles))


def rotate(field, cosine, sine):
    half = field.shape[-1] // 2
    first, second = (field[..., :half], field[..., half:])
    cos_h, sin_h = (cosine[:, None, :], sine[:, None, :])
    return jnp.concatenate(
        [first * cos_h - second * sin_h, second * cos_h + first * sin_h], axis=-1
    )


def rotate_back(field, cosine, sine):
    half = field.shape[-1] // 2
    first, second = (field[..., :half], field[..., half:])
    cos_h, sin_h = (cosine[:, None, :], sine[:, None, :])
    return jnp.concatenate(
        [first * cos_h + second * sin_h, second * cos_h - first * sin_h], axis=-1
    )


def slot_tables(routes, experts, most):
    count = routes.shape[0] * routes.shape[1]
    flat = routes.reshape(count)
    order = jnp.argsort(flat, stable=True)
    ordered = flat[order]
    firsts = jnp.searchsorted(ordered, jnp.arange(experts, dtype=jnp.int32))
    ranks = jnp.arange(count, dtype=jnp.int32) - firsts[ordered]
    sorted_slots = ordered * most + ranks
    slot_of_row = jnp.zeros((count,), jnp.int32).at[order].set(sorted_slots)
    row_of_slot = jnp.full((experts * most,), count, jnp.int32).at[sorted_slots].set(order)
    return (slot_of_row, row_of_slot)


def routed_layer(
    tokens,
    cotangent,
    seq_lengths,
    routes,
    head_experts,
    norm_gain,
    w_query,
    w_key,
    w_value,
    w_output,
    w_value_gate,
    w_output_gate,
    w_router,
    w_up,
    w_down,
):
    f32 = jnp.float32
    bf16 = jnp.bfloat16
    count = tokens.shape[0]
    experts = w_router.shape[1]
    local_experts = w_up.shape[0]
    owners = lax.axis_size("expert")
    most = 3 * count * TOPK // (2 * experts)
    routed = count * TOPK
    block = min(512, count)
    block_starts = jnp.arange(count // block, dtype=jnp.int32) * block
    scale = DH ** (-0.5)
    contract_last = (((1,), (1,)), ((), ()))
    contract_first = (((0,), (0,)), ((), ()))
    seq_ids, live, positions = sequence_layout(seq_lengths[0], count)
    cosine, sine = rope_tables(positions, DH)
    inputs = tokens.astype(f32)
    centred = inputs - jnp.mean(inputs, axis=-1, keepdims=True)
    inverse = lax.rsqrt(jnp.mean(centred * centred, axis=-1, keepdims=True) + norm_eps)
    standard = centred * inverse
    normed = (standard * norm_gain).astype(bf16)
    query_proj = jnp.dot(normed, w_query, preferred_element_type=f32).reshape(count, H, DH)
    key_proj = jnp.dot(normed, w_key, preferred_element_type=f32).reshape(count, H, DH)
    query_rot = (rotate(query_proj, cosine, sine) * scale).astype(bf16)
    key_rot = rotate(key_proj, cosine, sine).astype(bf16)
    chosen = jnp.any(
        head_experts[:, None, :, :] == jnp.arange(EA, dtype=jnp.int32)[None, :, None, None], axis=-1
    )
    value_gates = jnp.where(
        chosen,
        jax.nn.sigmoid(
            jnp.dot(tokens, w_value_gate, preferred_element_type=f32).reshape(count, EA, H)
        ),
        0.0,
    )
    output_gates = jnp.where(
        chosen,
        jax.nn.sigmoid(
            jnp.dot(tokens, w_output_gate, preferred_element_type=f32).reshape(count, EA, H)
        ),
        0.0,
    )
    value_all = jnp.dot(tokens, w_value, preferred_element_type=f32).reshape(count, EA, H, DH)
    values = jnp.sum(value_gates[..., None] * value_all, axis=1).astype(bf16)

    def allowed_at(start):
        queries = start + jnp.arange(block, dtype=jnp.int32)
        keys = jnp.arange(count, dtype=jnp.int32)
        same = (
            (seq_ids[:, None] == seq_ids[None, :])
            & (keys[None, :] <= queries[:, None])
            & live[None, :]
        )
        return same | (keys[None, :] == queries[:, None])

    def scores_at(start):
        scores = jnp.einsum("qhd,khd->hqk", query_rot, key_rot, preferred_element_type=f32)
        return (query_rot, jnp.where(allowed_at(start)[None], scores, masked_score))

    def attend(start):
        query_block, scores = scores_at(start)
        highest = jnp.max(scores, axis=-1, keepdims=True)
        shifted = jnp.exp(scores - highest)
        totals = jnp.sum(shifted, axis=-1, keepdims=True)
        shares = (shifted / totals).astype(bf16)
        result = jnp.einsum("hqk,khd->qhd", shares, values, preferred_element_type=f32)
        return (result, (highest + jnp.log(totals))[..., 0])

    attended, log_totals = lax.map(attend, block_starts)
    attended = attended.reshape(count, H, DH)
    log_totals = jnp.transpose(log_totals, (1, 0, 2)).reshape(H, count)
    heads_mixed = (
        (output_gates[..., None] * attended[:, None]).astype(bf16).reshape(count, EA * H * DH)
    )
    hidden = inputs + lax.dot_general(
        heads_mixed, w_output, contract_last, preferred_element_type=f32
    )
    hidden_low = hidden.astype(bf16)
    logits = jnp.dot(hidden_low, w_router, preferred_element_type=f32)
    gates = jax.nn.sigmoid(jnp.take_along_axis(logits, routes, axis=1))
    slot_of_row, row_of_slot = slot_tables(routes, experts, most)
    valid = row_of_slot < routed
    safe_row = jnp.minimum(row_of_slot, routed - 1)
    source = safe_row // TOPK
    outgoing = jnp.where(valid[:, None], hidden_low[source], jnp.zeros((), bf16)).reshape(
        owners, local_experts, most, D
    )

    def expert_apply(items):
        raised = jnp.einsum("nemd,edf->nemf", items, w_up, preferred_element_type=f32)
        active = jax.nn.silu(raised).astype(bf16)
        lowered = jnp.einsum("nemf,edf->nemd", active, w_down, preferred_element_type=f32).astype(
            bf16
        )
        return (lowered, raised)

    lowered, raised = expert_apply(
        lax.all_to_all(outgoing, "expert", split_axis=0, concat_axis=0, tiled=True)
    )
    returned = lax.all_to_all(lowered, "expert", split_axis=0, concat_axis=0, tiled=True).reshape(
        experts * most, D
    )
    expert_rows = returned[slot_of_row].reshape(count, TOPK, D)
    output = hidden + jnp.sum(gates[..., None] * expert_rows, axis=1)
    mixed = output.astype(bf16)
    grad_out = cotangent.astype(f32) * live[:, None].astype(f32)
    grad_gates = jnp.sum(grad_out[:, None, :] * expert_rows, axis=2)
    gate_flat = gates.reshape(routed)
    grad_outgoing = (
        jnp.where(valid[:, None], gate_flat[safe_row][:, None] * grad_out[source], 0.0)
        .astype(bf16)
        .reshape(owners, local_experts, most, D)
    )
    grad_lowered = lax.all_to_all(grad_outgoing, "expert", split_axis=0, concat_axis=0, tiled=True)
    items = lax.all_to_all(outgoing, "expert", split_axis=0, concat_axis=0, tiled=True)
    raised = expert_apply(items)[1]
    grad_active = jnp.einsum("nemd,edf->nemf", grad_lowered, w_down, preferred_element_type=f32)
    sigmoid_raised = jax.nn.sigmoid(raised)
    grad_raised = (grad_active * sigmoid_raised * (1.0 + raised * (1.0 - sigmoid_raised))).astype(
        bf16
    )
    grad_items = jnp.einsum("nemf,edf->nemd", grad_raised, w_up, preferred_element_type=f32).astype(
        bf16
    )
    active = jax.nn.silu(raised).astype(bf16)
    grad_items, grad_raised, active = (grad_items, grad_raised, active)
    grad_items, grad_raised, active, grad_arrived, arrived = (
        grad_items,
        grad_raised,
        active,
        grad_lowered,
        items,
    )
    grad_up_local = jnp.einsum("nemd,nemf->edf", arrived, grad_raised, preferred_element_type=f32)
    grad_down_local = jnp.einsum("nemd,nemf->edf", grad_arrived, active, preferred_element_type=f32)
    grad_up, grad_down = (
        lax.psum_scatter(
            grad_up_local.astype(jnp.bfloat16), "dp", scatter_dimension=1, tiled=True
        ).astype(jnp.float32),
        lax.psum_scatter(
            grad_down_local.astype(jnp.bfloat16), "dp", scatter_dimension=1, tiled=True
        ).astype(jnp.float32),
    )
    grad_back = lax.all_to_all(
        grad_items, "expert", split_axis=0, concat_axis=0, tiled=True
    ).reshape(experts * most, D)
    grad_hidden = grad_out + jnp.sum(
        grad_back[slot_of_row].reshape(count, TOPK, D), axis=1, dtype=f32
    )
    grad_picked = grad_gates * gates * (1.0 - gates)
    expert_ids = jnp.arange(experts, dtype=jnp.int32)
    grad_logits = jnp.sum(
        jnp.where(routes[:, :, None] == expert_ids[None, None, :], grad_picked[..., None], 0.0),
        axis=1,
    ).astype(bf16)
    grad_router = lax.dot_general(
        hidden_low, grad_logits, contract_first, preferred_element_type=f32
    )
    grad_hidden = grad_hidden + lax.dot_general(
        grad_logits, w_router, contract_last, preferred_element_type=f32
    )
    grad_hidden_low = grad_hidden.astype(bf16)
    grad_output = lax.dot_general(
        grad_hidden_low, heads_mixed, contract_first, preferred_element_type=f32
    )
    grad_mixed = jnp.dot(grad_hidden_low, w_output, preferred_element_type=f32).reshape(
        count, EA, H, DH
    )
    grad_attended = jnp.sum(output_gates[..., None] * grad_mixed, axis=1).astype(bf16)
    grad_out_gates = jnp.sum(grad_mixed * attended[:, None], axis=-1)
    grad_out_logits = (
        jnp.where(chosen, grad_out_gates * output_gates * (1.0 - output_gates), 0.0)
        .astype(bf16)
        .reshape(count, EA * H)
    )

    def attend_back(carry, start):
        grad_keys, grad_vals = carry
        query_block, scores = scores_at(start)
        shares = jnp.exp(scores - log_totals[..., None])
        grad_shares = jnp.einsum("qhd,khd->hqk", grad_attended, values, preferred_element_type=f32)
        centre = jnp.sum(shares * grad_shares, axis=-1, keepdims=True)
        grad_scores = (shares * (grad_shares - centre)).astype(bf16)
        grad_query_block = jnp.einsum(
            "hqk,khd->qhd", grad_scores, key_rot, preferred_element_type=f32
        )
        grad_keys = grad_keys + jnp.einsum(
            "hqk,qhd->khd", grad_scores, query_block, preferred_element_type=f32
        )
        grad_vals = grad_vals + jnp.einsum(
            "hqk,qhd->khd", shares.astype(bf16), grad_attended, preferred_element_type=f32
        )
        return ((grad_keys, grad_vals), grad_query_block)

    zero_heads = jnp.zeros((count, H, DH), f32)
    (grad_keys, grad_vals), grad_queries = lax.scan(
        attend_back, (zero_heads, zero_heads), block_starts
    )
    grad_queries = grad_queries.reshape(count, H, DH)
    grad_query_proj = (
        rotate_back(grad_queries * scale, cosine, sine).astype(bf16).reshape(count, H * DH)
    )
    grad_key_proj = rotate_back(grad_keys, cosine, sine).astype(bf16).reshape(count, H * DH)
    grad_value_all = (
        (value_gates[..., None] * grad_vals[:, None]).astype(bf16).reshape(count, EA * H * DH)
    )
    grad_value_gates = jnp.sum(grad_vals[:, None] * value_all, axis=-1)
    grad_value_logits = (
        jnp.where(chosen, grad_value_gates * value_gates * (1.0 - value_gates), 0.0)
        .astype(bf16)
        .reshape(count, EA * H)
    )
    grad_query = lax.dot_general(
        normed, grad_query_proj, contract_first, preferred_element_type=f32
    )
    grad_key = lax.dot_general(normed, grad_key_proj, contract_first, preferred_element_type=f32)
    grad_value = lax.dot_general(tokens, grad_value_all, contract_first, preferred_element_type=f32)
    grad_value_gate = lax.dot_general(
        tokens, grad_value_logits, contract_first, preferred_element_type=f32
    )
    grad_output_gate = lax.dot_general(
        tokens, grad_out_logits, contract_first, preferred_element_type=f32
    )
    grad_normed = lax.dot_general(
        grad_query_proj, w_query, contract_last, preferred_element_type=f32
    ) + lax.dot_general(grad_key_proj, w_key, contract_last, preferred_element_type=f32)
    grad_gain = jnp.sum(grad_normed * standard, axis=0)
    grad_standard = grad_normed * norm_gain
    grad_tokens = grad_hidden + inverse * (
        grad_standard
        - jnp.mean(grad_standard, axis=-1, keepdims=True)
        - standard * jnp.mean(grad_standard * standard, axis=-1, keepdims=True)
    )
    grad_tokens = (
        grad_tokens
        + lax.dot_general(grad_value_all, w_value, contract_last, preferred_element_type=f32)
        + lax.dot_general(
            grad_value_logits, w_value_gate, contract_last, preferred_element_type=f32
        )
        + lax.dot_general(grad_out_logits, w_output_gate, contract_last, preferred_element_type=f32)
    )
    summed = (
        lax.psum_scatter(grad_gain, ("dp", "expert"), scatter_dimension=0, tiled=True),
        lax.psum_scatter(grad_query, ("dp", "expert"), scatter_dimension=0, tiled=True),
        lax.psum_scatter(grad_key, ("dp", "expert"), scatter_dimension=0, tiled=True),
        lax.psum_scatter(grad_value, ("dp", "expert"), scatter_dimension=0, tiled=True),
        lax.psum_scatter(grad_output, ("dp", "expert"), scatter_dimension=0, tiled=True),
        lax.psum_scatter(grad_value_gate, ("dp", "expert"), scatter_dimension=0, tiled=True),
        lax.psum_scatter(grad_output_gate, ("dp", "expert"), scatter_dimension=0, tiled=True),
        lax.psum_scatter(grad_router, ("dp", "expert"), scatter_dimension=0, tiled=True),
    )
    return (
        mixed,
        grad_tokens,
        summed[0],
        summed[1],
        summed[2],
        summed[3],
        summed[4],
        summed[5],
        summed[6],
        summed[7],
        grad_up,
        grad_down,
    )


F32 = jnp.float32
BF16 = jnp.bfloat16
MESH = pl.DeviceIdType.MESH
LANES = 128


def mm(a, b):
    return lax.dot_general(a, b, (((1,), (0,)), ((), ())), preferred_element_type=F32)


def mm_t(a, b):
    return lax.dot_general(a, b, (((1,), (1,)), ((), ())), preferred_element_type=F32)


def tmm(a, b):
    return lax.dot_general(a, b, (((0,), (0,)), ((), ())), preferred_element_type=F32)


def iota(shape, axis):
    return lax.broadcasted_iota(jnp.int32, shape, axis)


def column(x, j, width=LANES):
    return jnp.broadcast_to(x[:, j : j + 1], (x.shape[0], width))


def sigmoid(x):
    return 1.0 / (1.0 + jnp.exp(-x))


class Scratch:
    def __init__(self):
        self.names, self.shapes = [], []

    def add(self, name, shape):
        self.names.append(name)
        self.shapes.append(shape)

    def vmem(self, name, shape, dtype):
        self.add(name, pltpu.VMEM(shape, dtype))

    def sems(self, name, *shape):
        self.add(name, pltpu.SemaphoreType.DMA(shape))


INPUTS = ("tokens", "cot", "lens", "rt", "het", "gain", "wvg", "wog", "wr", "wq", "wk", "wv", "wo", "wu", "wd")
OUTPUTS = ("mixed", "gtok", "ggain", "gq", "gk", "gv", "go", "gvg", "gog", "gr", "gup", "gdn")


def layer_kernel(names, nd, nz, local, *refs):
    r = dict(zip(names, refs))
    R = type("R", (), r)
    C = R.tokens.shape[0]
    own_e = 2 * local
    pad_e = R.maskb.shape[1]
    EF = own_e * DH
    HF = local * DH
    HD = H * DH
    EV = EA * HD
    S = D // (nd * nz * 2)
    SL = S * nz
    GATE = EA * H
    p = lax.axis_index("dp")
    e = lax.axis_index("expert")
    z = e // 2
    c = e % 2
    sib = 1 - c

    def dev(p_, z_, c_):
        return (p_, z_ * 2 + c_)

    def times(i, n):
        return pl.multiple_of(i * n, n)

    def remote(src, dst, ss, rs, to):
        return pltpu.make_async_remote_copy(
            src_ref=src, dst_ref=dst, send_sem=ss, recv_sem=rs, device_id=to, device_id_type=MESH
        )

    def arrived(dst, rs):
        remote(dst, dst, rs, rs, dev(p, z, sib)).wait_recv()

    def sent(src, ss):
        remote(src, src, ss, ss, dev(p, z, sib)).wait_send()

    def plane(k):
        return lax.rem(p + k, nd)

    def line(k):
        return lax.rem(z + k, nz)

    loads = {}

    def load(name, src, dst, sem):
        cp = pltpu.make_async_copy(src, dst, sem)
        cp.start()
        loads.setdefault(name, []).append(cp)

    def loaded(name):
        for cp in loads.pop(name):
            cp.wait()

    load("qk", R.wq, R.wqk_b.at[:, 0:HD], R.ld.at[0])
    load("qk", R.wk, R.wqk_b.at[:, HD : 2 * HD], R.ld.at[1])
    load("v", R.wv, R.wv_b, R.ld.at[2])
    for i in range(local):
        col = times(c * local + i, DH)
        load("up", R.wu.at[i], R.wup_b.at[:, pl.ds(col, DH)], R.ld.at[4 + i])
        load("dn", R.wd.at[i], R.wdn_b.at[:, pl.ds(col, DH)], R.ld.at[4 + local + i])
    load("o", R.wo, R.wo_b, R.ld.at[3])

    barrier = pltpu.get_barrier_semaphore()
    partners = [dev(p, z, sib)]
    partners += [dev(p, line(k), c) for k in range(1, nz)]
    for k in range(1, nd):
        partners += [dev(plane(k), z, c), dev(plane(k), z, sib)]
    for to in partners:
        pl.semaphore_signal(barrier, inc=1, device_id=to, device_id_type=MESH)

    l0 = R.lens[0, 0]
    b1 = l0 + R.lens[0, 1]
    row = iota((C, LANES), 0)
    lane = iota((C, LANES), 1)
    seq_r = (row >= l0).astype(jnp.int32) + (row >= b1).astype(jnp.int32)
    seq_c = (lane >= l0).astype(jnp.int32) + (lane >= b1).astype(jnp.int32)
    live = row < b1
    allowed = ((seq_r == seq_c) & (lane <= row) & (lane < b1)) | (row == lane)
    live_f = jnp.where(live, 1.0, 0.0).astype(F32)
    start = jnp.where(seq_r == 0, 0, l0)
    position = jnp.where(live, row - start, 0).astype(F32)

    for b in range(D // LANES):
        cols = slice(b * LANES, (b + 1) * LANES)
        R.cotb[pl.ds(times(z, C), C), cols] = (R.cot[:, cols].astype(F32) * live_f).astype(BF16)
    ids = iota((pad_e, C), 0)
    for zz in range(nz):
        named = jnp.zeros((pad_e, C), F32)
        for k in range(TOPK):
            hit = jnp.broadcast_to(R.rt[k : k + 1, :], (pad_e, C)) == ids + zz * own_e
            named = jnp.where(hit & (ids < own_e), 1.0, named)
        R.mask_s[zz] = named.astype(BF16)
    R.maskb[z] = R.mask_s[z]

    pl.semaphore_wait(barrier, len(partners))

    def block(buf, o):
        return buf.at[pl.ds(times(o, C), C), :]

    def pass_on(buf, ss, rs, o, right, left):
        @pl.when(right)
        def _():
            remote(block(buf, o), block(buf, o), ss.at[0, o], rs.at[o], dev(p, z + 1, c)).start()

        @pl.when(left)
        def _():
            remote(block(buf, o), block(buf, o), ss.at[1, o], rs.at[o], dev(p, z - 1, c)).start()

    def passed(buf, ss, o, right, left):
        @pl.when(right)
        def _():
            sent(block(buf, o), ss.at[0, o])

        @pl.when(left)
        def _():
            sent(block(buf, o), ss.at[1, o])

    def gather_own(buf, ss, rs):
        pass_on(buf, ss, rs, z, z < nz - 1, z > 0)

    def gather_on(buf, ss, rs, o):
        arrived(block(buf, o), rs.at[o])
        pass_on(buf, ss, rs, o, (o < z) & (z < nz - 1), (o > z) & (z > 0))

    def gather_step(buf, ss, rs, k):
        @pl.when(z >= k)
        def _():
            gather_on(buf, ss, rs, z - k)

        @pl.when(z + k < nz)
        def _():
            gather_on(buf, ss, rs, z + k)

    def gather_end(buf, ss):
        passed(buf, ss, z, z < nz - 1, z > 0)
        for k in range(1, nz):

            @pl.when(z >= k)
            def _():
                passed(buf, ss, z - k, z < nz - 1, False)

            @pl.when(z + k < nz)
            def _():
                passed(buf, ss, z + k, False, z > 0)

    gather_own(R.cotb, R.cot_ss, R.cot_rs)
    masks = []
    for k in range(1, nz):
        o = line(k)
        cp = remote(R.mask_s.at[o], R.maskb.at[z], R.mask_ss.at[k], R.mask_rs.at[z], dev(p, o, c))
        cp.start()
        masks.append(cp)

    s_row, s_col = iota((GATE, LANES), 0), iota((GATE, LANES), 1)
    to_v = jnp.where(s_row == s_col, 1.0, 0.0).astype(BF16)
    to_o = jnp.where(s_row + GATE == s_col, 1.0, 0.0).astype(BF16)
    R.wg_b[...] = (mm(R.wvg[...], to_v) + mm(R.wog[...], to_o)).astype(BF16)
    experts = R.wr.shape[1]
    r_row, r_col = iota((experts, LANES), 0), iota((experts, LANES), 1)
    to_r = jnp.where((r_row == r_col + z * own_e) & (r_col < own_e), 1.0, 0.0).astype(BF16)
    R.wrl_b[...] = mm(R.wr[...], to_r).astype(BF16)

    half = lax.rem(lane, DH // 2).astype(F32)
    angle = position * jnp.exp(half * (-2.0 / DH * math.log(rope_base)))
    cosine = jnp.cos(angle)
    sine = jnp.where(lane < DH // 2, -jnp.sin(angle), jnp.sin(angle))

    def rot(v):
        return v * cosine + pltpu.roll(v, DH // 2, 1) * sine

    def rot_back(v):
        return v * cosine - pltpu.roll(v, DH // 2, 1) * sine

    inputs = R.tokens[...].astype(F32)
    centred = inputs - jnp.mean(inputs, axis=-1, keepdims=True)
    inverse = lax.rsqrt(jnp.mean(centred * centred, axis=-1, keepdims=True) + norm_eps)
    standard = centred * inverse
    R.std_b[...] = standard
    R.normed_b[...] = (standard * R.gain[...]).astype(BF16)

    loaded("qk")
    scale = DH ** (-0.5)
    qk = mm(R.normed_b[...], R.wqk_b[:, 0:HD])
    for h in range(H):
        hs = slice(h * DH, (h + 1) * DH)
        R.q_b[:, hs] = (rot(qk[:, hs]) * scale).astype(BF16)
    qk = mm(R.normed_b[...], R.wqk_b[:, HD : 2 * HD])
    for h in range(H):
        hs = slice(h * DH, (h + 1) * DH)
        R.k_b[:, hs] = rot(qk[:, hs]).astype(BF16)

    hit = []
    for j in range(GATE):
        x, h = divmod(j, H)
        one = (R.het[2 * h : 2 * h + 1, :] == x) | (R.het[2 * h + 1 : 2 * h + 2, :] == x)
        hit.append(jnp.where(one, 1.0, 0.0).astype(F32))
    hit = jnp.concatenate(hit + hit + [jnp.zeros((LANES - 2 * GATE, C), F32)], axis=0)
    R.gate_b[...] = sigmoid(mm(R.tokens[...], R.wg_b[...])) * hit.T

    loaded("up")
    loaded("dn")
    wx = []
    for i, buf in enumerate((R.wup_b, R.wdn_b)):
        part = buf.at[:, pl.ds(times(c, HF), HF)]
        cp = remote(part, part, R.w_ss.at[i], R.w_rs.at[i], dev(p, z, sib))
        cp.start()
        wx.append(cp)

    loaded("v")
    gates = R.gate_b[...]
    total = [None] * H
    for x in range(EA):
        R.val_b[:, x * HD : (x + 1) * HD] = mm(R.tokens[...], R.wv_b[:, x * HD : (x + 1) * HD])
        for h in range(H):
            lo = x * HD + h * DH
            term = column(gates, x * H + h) * R.val_b[:, lo : lo + DH]
            total[h] = term if x == 0 else total[h] + term
    for h in range(H):
        R.v_b[:, h * DH : (h + 1) * DH] = total[h].astype(BF16)

    for h in range(H):
        hs = slice(h * DH, (h + 1) * DH)
        scores = jnp.where(allowed, mm_t(R.q_b[:, hs], R.k_b[:, hs]), masked_score)
        shifted = jnp.exp(scores - jnp.max(scores, axis=-1, keepdims=True))
        shares = shifted / jnp.sum(shifted, axis=-1, keepdims=True)
        R.prob_b[h] = shares
        R.att_b[:, hs] = mm(shares.astype(BF16), R.v_b[:, hs])

    for k in range(1, 2):
        gather_step(R.cotb, R.cot_ss, R.cot_rs, k)

    for x in range(EA):
        for h in range(H):
            lo = x * HD + h * DH
            R.mix_b[:, lo : lo + DH] = (
                column(gates, GATE + x * H + h) * R.att_b[:, h * DH : (h + 1) * DH]
            ).astype(BF16)
    loaded("o")
    half_d = D // 2
    for b in range(2):
        cols = slice(b * half_d, (b + 1) * half_d)
        hidden = R.tokens[:, cols].astype(F32) + mm_t(R.mix_b[...], R.wo_b[cols, :])
        R.hid_f[:, cols] = hidden
        R.hidb[pl.ds(times(z, C), C), cols] = hidden.astype(BF16)
    gather_own(R.hidb, R.hid_ss, R.hid_rs)

    def put_turned(x, w):
        for b in range(D // LANES):
            t = x[:, b * LANES : (b + 1) * LANES].astype(F32).T.astype(BF16)
            for q in range(LANES // S):
                i = (b * LANES) // S + q
                pp, zz, cc = i // (2 * nz), (i % (2 * nz)) // 2, i % 2
                at = (pp * 2 + cc) * SL + zz * S
                R.lt[at : at + S, w * LANES : (w + 1) * LANES] = t[q * S : (q + 1) * S, :]

    plane_all = [(k, dc) for k in range(nd) for dc in range(2) if k or dc]

    def side(dc):
        return sib if dc else c

    def send_turned(w0, w1, ss, rs):
        out = []
        lanes = slice(w0 * LANES, w1 * LANES)
        for k, dc in plane_all:
            to = plane(k)
            slot = 2 * k + dc
            at = times(to * 2 + side(dc), SL)
            cp = remote(
                R.lt.at[pl.ds(at, SL), lanes],
                R.ltr.at[slot, :, lanes],
                ss.at[slot],
                rs.at[slot],
                dev(to, z, side(dc)),
            )
            cp.start()
            out.append(cp)
        R.ltr[0, :, lanes] = R.lt[pl.ds(times(p * 2 + c, SL), SL), lanes]
        return out

    def send_rows(buf, lanes, ss, rs):
        out = []
        for k in range(1, nd):
            cp = remote(
                buf.at[0:C, lanes],
                buf.at[2 * k * C : (2 * k + 1) * C, lanes],
                ss.at[k],
                rs.at[2 * k],
                dev(plane(k), z, c),
            )
            cp.start()
            out.append(cp)
        return out + [hand_over(buf, lanes, ss, rs, 0)]

    def hand_over(buf, lanes, ss, rs, k):
        cp = remote(
            buf.at[2 * k * C : (2 * k + 1) * C, lanes],
            buf.at[(2 * k + 1) * C : (2 * k + 2) * C, lanes],
            ss.at[nd + k],
            rs.at[2 * k + 1],
            dev(p, z, sib),
        )
        cp.start()
        return cp

    def hand_all(buf, lanes, ss, rs, out):
        for k in range(1, nd):
            out[k - 1].wait_recv()
            out.append(hand_over(buf, lanes, ss, rs, k))

    def rows_here(buf, lanes, rs):
        for k in range(nd):
            arrived(buf.at[(2 * k + 1) * C : (2 * k + 2) * C, lanes], rs.at[2 * k + 1])

    put_turned(R.tokens[...], 0)
    put_turned(R.normed_b[...], 1)
    put_turned(R.hid_f[...], 2)
    turned = send_turned(0, 3, R.lt_ss, R.lt_rs)
    R.ra[0:C, 0:HD] = R.att_b[...].astype(BF16)
    R.ra[0:C, HD : HD + LANES] = gates.astype(BF16)
    RA = slice(0, HD + LANES)
    ra_out = send_rows(R.ra, RA, R.ra_ss, R.ra_rs)

    for k in range(2, nz - 1):
        gather_step(R.cotb, R.cot_ss, R.cot_rs, k)

    for cp in wx:
        cp.wait()

    least = jnp.minimum(z, nz - 1 - z)

    def origin(k):
        paired = k <= 2 * least
        dist = jnp.where(paired, (k + 1) // 2, k - least)
        left = jnp.where(paired, lax.rem(k, 2) == 1, z > nz - 1 - z)
        return jnp.where(k == 0, z, jnp.where(left, z - dist, z + dist))

    def expert_block(k, carry):
        o = origin(k)
        rows = pl.ds(times(o, C), C)

        @pl.when(k > 0)
        def _():
            gather_on(R.hidb, R.hid_ss, R.hid_rs, o)

            @pl.when((o == z - nz + 1) | (o == z + nz - 1))
            def _():
                arrived(block(R.cotb, o), R.cot_rs.at[o])

            arrived(R.maskb.at[o], R.mask_rs.at[o])

        hb = R.hidb[rows, :]
        cb = R.cotb[rows, :]
        named = R.maskb[o].astype(F32)
        named = jnp.concatenate([named, jnp.zeros((LANES - pad_e, C), F32)], axis=0).T
        g = sigmoid(mm(hb, R.wrl_b[...])) * named
        glog = jnp.zeros((C, LANES), F32)
        for q in range(own_e // 4):
            cols = slice(q * 4 * DH, (q + 1) * 4 * DH)
            raised = mm(hb, R.wup_b[:, cols])
            back = mm(cb, R.wdn_b[:, cols])
            for i in range(4):
                j = q * 4 + i
                u = raised[:, i * DH : (i + 1) * DH]
                a = back[:, i * DH : (i + 1) * DH]
                gj = column(g, j)
                s = sigmoid(u)
                act = u * s
                lo = j * DH
                R.gact[rows, lo : lo + DH] = (gj * act).astype(BF16)
                R.gra[rows, lo : lo + DH] = (gj * a * (s * (1.0 + u * (1.0 - s)))).astype(BF16)
                gg = jnp.sum(a * act, axis=1, keepdims=True)
                glog = jnp.where(lane == j, jnp.broadcast_to(gg, (C, LANES)), glog)
        glog = glog * g * (1.0 - g)
        low = glog.astype(BF16)
        R.glog_s[o] = glog.T[0:pad_e, :].astype(BF16)
        for b in range(2):
            cols = slice(b * half_d, (b + 1) * half_d)
            gh = mm_t(R.gra[rows, :], R.wup_b[cols, :]) + mm_t(low, R.wrl_b[cols, :])
            R.gh_s[o, :, cols] = gh.astype(BF16)

        @pl.when(k > 0)
        def _():
            remote(R.gh_s.at[o], R.gh_r.at[z], R.gh_ss.at[o], R.gh_rs.at[z], dev(p, o, c)).start()
            remote(
                R.glog_s.at[o], R.glog_r.at[z], R.gl_ss.at[o], R.gl_rs.at[z], dev(p, o, c)
            ).start()

        return carry

    lax.fori_loop(0, nz, expert_block, 0)

    def out_tile(t, carry):
        rows = pl.ds(times(t, 256), 256)
        got = mm_t(R.gact[...], R.wdn_b[rows, :]).astype(BF16)
        for o in range(nz):
            R.out_s[o, :, rows] = got[o * C : (o + 1) * C, :]
        return carry

    lax.fori_loop(0, D // 256, out_tile, 0)
    for k in range(1, nz):
        o = line(k)
        remote(R.out_s.at[o], R.out_r.at[z], R.out_ss.at[o], R.out_rs.at[z], dev(p, o, c)).start()

    pairs = []
    for i, (left_of, right_of, buf) in enumerate(
        ((R.cotb, R.gact, R.wdn_b), (R.hidb, R.gra, R.wup_b))
    ):

        def grad_tile(t, carry, base):
            cols = pl.ds(pl.multiple_of(base + t * 256, 256), 256)
            buf[:, cols] = tmm(left_of[...], right_of[:, cols]).astype(BF16)
            return carry

        lax.fori_loop(0, HF // 256, functools.partial(grad_tile, base=sib * HF), 0)
        cp = remote(
            buf.at[:, pl.ds(times(sib, HF), HF)],
            R.pair_r.at[i],
            R.pair_ss.at[i],
            R.pair_rs.at[i],
            dev(p, z, sib),
        )
        cp.start()
        pairs.append(cp)
        lax.fori_loop(0, HF // 256, functools.partial(grad_tile, base=c * HF), 0)

    hand_all(R.ra, RA, R.ra_ss, R.ra_rs, ra_out)

    ghid = R.cotb[pl.ds(times(z, C), C), :].astype(F32) + R.gh_s[z].astype(F32)
    for k in range(1, nz):
        o = line(k)
        arrived(R.gh_r.at[o], R.gh_rs.at[o])
        arrived(R.glog_r.at[o], R.gl_rs.at[o])
        ghid = ghid + R.gh_r[o].astype(F32)
    R.glog_r[z] = R.glog_s[z]
    R.ghid_f[...] = ghid
    R.ghid_b[...] = ghid.astype(BF16)
    put_turned(R.ghid_f[...], 3)
    turned_late = send_turned(3, 4, R.ltl_ss, R.ltl_rs)

    gates = R.gate_b[...]
    small = jnp.zeros((C, LANES), F32)
    gatt = [None] * H
    for x in range(EA):
        gmix = mm(R.ghid_b[...], R.wo_b[:, x * HD : (x + 1) * HD])
        for h in range(H):
            hs = slice(h * DH, (h + 1) * DH)
            j = GATE + x * H + h
            term = column(gates, j) * gmix[:, hs]
            gatt[h] = term if x == 0 else gatt[h] + term
            gg = jnp.sum(gmix[:, hs] * R.att_b[:, hs], axis=1, keepdims=True)
            small = jnp.where(lane == j, jnp.broadcast_to(gg, (C, LANES)), small)
    for h in range(H):
        hs = slice(h * DH, (h + 1) * DH)
        low = gatt[h].astype(BF16)
        R.gatt_b[:, hs] = low
        gval = tmm(R.prob_b[h].astype(BF16), low)
        R.gval_f[:, hs] = gval
        R.rb[0:C, hs] = gval.astype(BF16)
        for x in range(EA):
            lo = x * HD + h * DH
            j = x * H + h
            gg = jnp.sum(gval * R.val_b[:, lo : lo + DH], axis=1, keepdims=True)
            small = jnp.where(lane == j, jnp.broadcast_to(gg, (C, LANES)), small)
    small = small * gates * (1.0 - gates)
    glog = jnp.concatenate(
        [jnp.zeros((2 * GATE, C), F32)]
        + [R.glog_r[o].astype(F32) for o in range(nz)]
        + [jnp.zeros((LANES - 2 * GATE - nz * pad_e, C), F32)],
        axis=0,
    )
    R.small_b[...] = small.astype(BF16)
    R.rb[0:C, HD : HD + LANES] = (small + glog.T).astype(BF16)
    RV = slice(0, HD + LANES)
    rv_out = send_rows(R.rb, RV, R.rv_ss, R.rv_rs)

    q0 = HD + LANES
    for h in range(H):
        hs = slice(h * DH, (h + 1) * DH)
        low = R.gatt_b[:, hs]
        gsh = mm_t(low, R.v_b[:, hs])
        prob = R.prob_b[h]
        centre = jnp.sum(prob * gsh, axis=-1, keepdims=True)
        gs = (prob * (gsh - centre)).astype(BF16)
        R.rb[0:C, q0 + h * DH : q0 + (h + 1) * DH] = rot_back(
            mm(gs, R.k_b[:, hs]) * scale
        ).astype(BF16)
        R.rb[0:C, q0 + HD + h * DH : q0 + HD + (h + 1) * DH] = rot_back(
            tmm(gs, R.q_b[:, hs])
        ).astype(BF16)
    RQ = slice(q0, q0 + 2 * HD)
    rq_out = send_rows(R.rb, RQ, R.rq_ss, R.rq_rs)

    for cp in turned:
        cp.wait()
    rows_here(R.ra, RA, R.ra_rs)
    for cp in turned_late:
        cp.wait()

    def turned_of(w):
        return jnp.concatenate(
            [R.ltr[s, :, w * LANES : (w + 1) * LANES] for s in range(2 * nd)], axis=1
        )

    def send_part(part, lanes):
        for k in range(1, nz):
            o = line(k)
            remote(
                R.pb.at[pl.ds(times(o, S), S), lanes],
                R.pr.at[z, :, lanes],
                R.p_ss.at[part, o],
                R.p_rs.at[part, z],
                dev(p, o, c),
            ).start()

    def gated_grad(w, rows_of, g0, at):
        left = turned_of(w)
        for x in range(EA):
            right = []
            for h in range(H):
                gx = column(R.ra[:, HD : HD + LANES], g0 + x * H + h).astype(F32)
                right.append((gx * rows_of[:, h * DH : (h + 1) * DH].astype(F32)).astype(BF16))
            right = jnp.concatenate(right, axis=1)
            R.pb[:, at + x * HD : at + (x + 1) * HD] = mm(left, right).astype(BF16)

    PO, PV, PQ, PS = (
        slice(0, EV),
        slice(EV, 2 * EV),
        slice(2 * EV, 2 * EV + 2 * HD),
        slice(2 * EV + 2 * HD, 2 * EV + 2 * HD + LANES),
    )
    gated_grad(3, R.ra, GATE, 0)
    send_part(0, PO)

    gproj = mm_t(R.rb[0:C, RQ], R.wqk_b[...])
    standard = R.std_b[...]
    column_sum = jnp.sum(gproj * standard, axis=0, keepdims=True)
    for b in range(D // LANES):
        R.gp[0, b : b + 1, :] = column_sum[:, b * LANES : (b + 1) * LANES]
    gain_out = []
    for k, dc in plane_all:
        slot = 2 * k + dc
        cp = remote(
            R.gp.at[0], R.gp.at[slot], R.gp_ss.at[slot], R.gp_rs.at[slot], dev(plane(k), z, side(dc))
        )
        cp.start()
        gain_out.append(cp)

    hand_all(R.rb, RV, R.rv_ss, R.rv_rs, rv_out)

    inputs = R.tokens[...].astype(F32)
    centred = inputs - jnp.mean(inputs, axis=-1, keepdims=True)
    inverse = lax.rsqrt(jnp.mean(centred * centred, axis=-1, keepdims=True) + norm_eps)
    gs = gproj * R.gain[...]
    gtok = R.ghid_f[...] + inverse * (
        gs
        - jnp.mean(gs, axis=-1, keepdims=True)
        - standard * jnp.mean(gs * standard, axis=-1, keepdims=True)
    )
    R.gtok[...] = gtok
    for x in range(EA):
        for h in range(H):
            lo = x * HD + h * DH
            R.mix_b[:, lo : lo + DH] = (
                column(gates, x * H + h) * R.gval_f[:, h * DH : (h + 1) * DH]
            ).astype(BF16)
    for b in range(2):
        cols = slice(b * half_d, (b + 1) * half_d)
        R.gtok[:, cols] += mm_t(R.mix_b[...], R.wv_b[cols, :]) + mm_t(
            R.small_b[...], R.wg_b[cols, :]
        )

    rows_here(R.rb, RV, R.rv_rs)
    gated_grad(0, R.rb, 0, EV)
    send_part(1, PV)
    hand_all(R.rb, RQ, R.rq_ss, R.rq_rs, rq_out)
    lane_s = iota((SL, LANES), 1)
    small_t = mm(turned_of(0), R.rb[:, HD : HD + LANES])
    small_h = mm(turned_of(2), R.rb[:, HD : HD + LANES])
    R.pb[:, PS] = jnp.where(lane_s < 2 * GATE, small_t, small_h).astype(BF16)
    send_part(3, PS)
    rows_here(R.rb, RQ, R.rq_rs)
    left = turned_of(1)
    for b in range(2):
        lo = q0 + b * HD
        R.pb[:, 2 * EV + b * HD : 2 * EV + (b + 1) * HD] = mm(left, R.rb[:, lo : lo + HD]).astype(
            BF16
        )
    send_part(2, PQ)

    own_cols = pl.ds(times(c, HF), HF)
    rows_d = D // nd
    plane_out = []
    for i, buf in enumerate((R.wdn_b, R.wup_b)):
        pairs[i].wait()

        def pair_tile(t, carry):
            rows = pl.ds(times(t, 128), 128)
            buf[rows, own_cols] = (
                buf[rows, own_cols].astype(F32) + R.pair_r[i, rows, :].astype(F32)
            ).astype(BF16)
            return carry

        lax.fori_loop(0, D // 128, pair_tile, 0)
        for k in range(1, nd):
            to = plane(k)
            cp = remote(
                buf.at[pl.ds(times(to, rows_d), rows_d), own_cols],
                R.eg_r.at[k - 1, i],
                R.eg_ss.at[k - 1, i],
                R.eg_rs.at[k - 1, i],
                dev(to, z, c),
            )
            cp.start()
            plane_out.append(cp)

    total = R.gp[0]
    for cp, (k, dc) in zip(gain_out, plane_all):
        cp.wait()
        total = total + R.gp[2 * k + dc]
    R.gz_s[...] = total
    for k in range(1, nz):
        o = line(k)
        remote(R.gz_s, R.gz.at[z], R.gz_ss.at[o], R.gz_rs.at[z], dev(p, o, c)).start()

    out = R.hid_f[...] + R.out_s[z].astype(F32)
    for k in range(1, nz):
        o = line(k)
        arrived(R.out_r.at[o], R.out_rs.at[o])
        out = out + R.out_r[o].astype(F32)
    R.mixed[...] = out.astype(BF16)

    for k in range(1, nz):
        o = line(k)
        arrived(R.gz.at[o], R.gz_rs.at[o])
        total = total + R.gz[o]
    first = (p * 2 * nz + z * 2 + c) * S
    pick_row = iota((D // LANES, LANES), 0) == first // LANES
    line_sum = jnp.sum(jnp.where(pick_row, total, 0.0), axis=0, keepdims=True)
    shift = lax.rem(LANES - lax.rem(first, LANES), LANES)
    line_sum = pltpu.roll(jnp.broadcast_to(line_sum, (8, LANES)), shift, 1)
    R.ggain[...] = line_sum[0:1, 0:S]

    own_rows = pl.ds(times(z, S), S)

    def line_total(part, lanes):
        got = R.pb[own_rows, lanes].astype(F32)
        for k in range(1, nz):
            o = line(k)
            arrived(R.pr.at[o, :, lanes], R.p_rs.at[part, o])
            got = got + R.pr[o, :, lanes].astype(F32)
        return got

    R.go[...] = line_total(0, PO)
    R.gv[...] = line_total(1, PV)
    got = line_total(3, PS)

    def pick(width, source):
        a, b = iota((LANES, width), 0), iota((LANES, width), 1)
        sel = jnp.where(a == source(b), 1.0, 0.0).astype(F32)
        return lax.dot_general(
            got,
            sel,
            (((1,), (0,)), ((), ())),
            preferred_element_type=F32,
            precision=lax.Precision.HIGHEST,
        )

    def router_lane(b):
        at = jnp.zeros_like(b)
        for o in range(nz):
            at = jnp.where(b >= o * own_e, 2 * GATE + o * pad_e + b - o * own_e, at)
        return at

    R.gvg[...] = pick(GATE, lambda b: b)
    R.gog[...] = pick(GATE, lambda b: b + GATE)
    R.gr[...] = pick(experts, router_lane)
    got = line_total(2, PQ)
    R.gq[...] = got[:, 0:HD]
    R.gk[...] = got[:, HD : 2 * HD]

    for i, (buf, dst) in enumerate(((R.wdn_b, R.gdn), (R.wup_b, R.gup))):
        for k in range(1, nd):
            plane_out[i * (nd - 1) + k - 1].wait_recv()
        rows = pl.ds(times(p, rows_d), rows_d)
        for x in range(local):
            got = buf[rows, pl.ds(times(c * local + x, DH), DH)].astype(F32)
            for k in range(1, nd):
                got = got + R.eg_r[k - 1, i, :, x * DH : (x + 1) * DH].astype(F32)
            dst[x] = got

    gather_end(R.cotb, R.cot_ss)
    gather_end(R.hidb, R.hid_ss)
    for cp in masks + ra_out + rv_out + rq_out + plane_out:
        cp.wait_send()
    for k in range(1, nz):
        o = line(k)
        sent(R.gh_s.at[o], R.gh_ss.at[o])
        sent(R.glog_s.at[o], R.gl_ss.at[o])
        sent(R.out_s.at[o], R.out_ss.at[o])
        sent(R.gz_s, R.gz_ss.at[o])
        for part, lanes in enumerate((PO, PV, PQ, PS)):
            sent(R.pb.at[pl.ds(times(o, S), S), lanes], R.p_ss.at[part, o])


def fused_layer(nd, nz, *args):
    (tokens, cotangent, seq_lengths, routes, head_experts, norm_gain) = args[:6]
    (w_query, w_key, w_value, w_output, w_value_gate, w_output_gate, w_router) = args[6:13]
    w_up, w_down = args[13:]
    C = tokens.shape[0]
    local = w_up.shape[0]
    experts = w_router.shape[1]
    own_e = 2 * local
    pad_e = -(-own_e // 16) * 16
    EF, HF, HD = own_e * DH, local * DH, H * DH
    EV = EA * HD
    S = D // (nd * nz * 2)
    SL = S * nz
    PW = 2 * EV + 2 * HD + LANES
    s = Scratch()
    s.vmem("wqk_b", (D, 2 * HD), BF16)
    s.vmem("wv_b", (D, EV), BF16)
    s.vmem("wo_b", (D, EV), BF16)
    s.vmem("wup_b", (D, EF), BF16)
    s.vmem("wdn_b", (D, EF), BF16)
    s.vmem("wg_b", (D, LANES), BF16)
    s.vmem("wrl_b", (D, LANES), BF16)
    s.vmem("cotb", (nz * C, D), BF16)
    s.vmem("hidb", (nz * C, D), BF16)
    s.vmem("mask_s", (nz, pad_e, C), BF16)
    s.vmem("maskb", (nz, pad_e, C), BF16)
    s.vmem("std_b", (C, D), F32)
    s.vmem("normed_b", (C, D), BF16)
    s.vmem("q_b", (C, HD), BF16)
    s.vmem("k_b", (C, HD), BF16)
    s.vmem("v_b", (C, HD), BF16)
    s.vmem("gate_b", (C, LANES), F32)
    s.vmem("val_b", (C, EV), F32)
    s.vmem("prob_b", (H, C, C), F32)
    s.vmem("att_b", (C, HD), F32)
    s.vmem("mix_b", (C, EV), BF16)
    s.vmem("hid_f", (C, D), F32)
    s.vmem("lt", (D, 4 * LANES), BF16)
    s.vmem("ltr", (2 * nd, SL, 4 * LANES), BF16)
    s.vmem("ra", (2 * nd * C, HD + LANES), BF16)
    s.vmem("rb", (2 * nd * C, 3 * HD + LANES), BF16)
    s.vmem("gact", (nz * C, EF), BF16)
    s.vmem("gra", (nz * C, EF), BF16)
    for name in ("gh_s", "gh_r", "out_s", "out_r"):
        s.vmem(name, (nz, C, D), BF16)
    for name in ("glog_s", "glog_r"):
        s.vmem(name, (nz, pad_e, C), BF16)
    s.vmem("pair_r", (2, D, HF), BF16)
    s.vmem("eg_r", (nd - 1, 2, D // nd, HF), BF16)
    s.vmem("ghid_f", (C, D), F32)
    s.vmem("ghid_b", (C, D), BF16)
    s.vmem("gatt_b", (C, HD), BF16)
    s.vmem("gval_f", (C, HD), F32)
    s.vmem("small_b", (C, LANES), BF16)
    s.vmem("pb", (SL, PW), BF16)
    s.vmem("pr", (nz, S, PW), BF16)
    s.vmem("gp", (2 * nd, D // LANES, LANES), F32)
    s.vmem("gz_s", (D // LANES, LANES), F32)
    s.vmem("gz", (nz, D // LANES, LANES), F32)
    s.sems("ld", 4 + 2 * local)
    for name in ("cot_ss", "hid_ss"):
        s.sems(name, 2, nz)
    for name in ("cot_rs", "hid_rs", "mask_ss", "mask_rs", "gh_ss", "gh_rs", "gl_ss", "gl_rs", "out_ss", "out_rs", "gz_ss", "gz_rs"):
        s.sems(name, nz)
    for name in "w_ss w_rs pair_ss pair_rs".split():
        s.sems(name, 2)
    for name in ("lt_ss", "lt_rs", "ltl_ss", "ltl_rs", "gp_ss", "gp_rs", "ra_ss", "ra_rs", "rv_ss", "rv_rs", "rq_ss", "rq_rs"):
        s.sems(name, 2 * nd)
    for name in ("eg_ss", "eg_rs"):
        s.sems(name, nd - 1, 2)
    for name in ("p_ss", "p_rs"):
        s.sems(name, 4, nz)

    def out(*shape, dtype=F32):
        return jax.ShapeDtypeStruct(shape, dtype)

    vmem = pl.BlockSpec(memory_space=pltpu.VMEM)
    smem = pl.BlockSpec(memory_space=pltpu.SMEM)
    hbm = pl.BlockSpec(memory_space=pl.ANY)
    outs = pl.pallas_call(
        functools.partial(layer_kernel, INPUTS + OUTPUTS + tuple(s.names), nd, nz, local),
        out_shape=(
            out(C, D, dtype=BF16),
            out(C, D),
            out(1, S),
            out(S, HD),
            out(S, HD),
            out(S, EV),
            out(S, EV),
            out(S, EA * H),
            out(S, EA * H),
            out(S, experts),
            out(local, D // nd, DH),
            out(local, D // nd, DH),
        ),
        in_specs=[vmem, vmem, smem] + [vmem] * 6 + [hbm] * 6,
        out_specs=[vmem] * 12,
        scratch_shapes=s.shapes,
        compiler_params=pltpu.CompilerParams(
            collective_id=0, has_side_effects=True, vmem_limit_bytes=VMEM_LIMIT
        ),
    )(
        tokens,
        cotangent,
        seq_lengths,
        routes.T,
        head_experts.reshape(C, 2 * H).T,
        norm_gain.reshape(1, D),
        w_value_gate,
        w_output_gate,
        w_router,
        w_query,
        w_key,
        w_value,
        w_output,
        w_up,
        w_down,
    )
    outs = list(outs)
    outs[2] = outs[2].reshape(S)
    return tuple(outs)


VMEM_LIMIT = 62 * 1024 * 1024


def fits(nd, nz, count, experts):
    own_e = experts // nz
    pad_e = -(-own_e // 16) * 16
    return (
        count == LANES
        and nz * count <= 512
        and own_e % 4 == 0
        and D % (nd * nz * 2 * 16) == 0
        and LANES % (D // (nd * nz * 2)) == 0
        and 2 * EA * H + nz * pad_e <= LANES
    )


def per_device(nd, ne, *args):
    count, experts = args[0].shape[0], args[12].shape[1]
    if ne % 2 == 0 and fits(nd, ne // 2, count, experts):
        return fused_layer(nd, ne // 2, *args)
    return routed_layer(*args)


def solution(mesh):
    return jax.shard_map(
        functools.partial(per_device, mesh.shape["dp"], mesh.shape["expert"]),
        mesh=mesh,
        in_specs=(
            P(("dp", "expert"), None),
            P(("dp", "expert"), None),
            P(("dp", "expert"), None),
            P(("dp", "expert"), None),
            P(("dp", "expert"), None, None),
            P(),
            P(),
            P(),
            P(),
            P(),
            P(),
            P(),
            P(),
            P("expert", None, None),
            P("expert", None, None),
        ),
        out_specs=(
            P(("dp", "expert"), None),
            P(("dp", "expert"), None),
            P(("dp", "expert")),
            P(("dp", "expert"), None),
            P(("dp", "expert"), None),
            P(("dp", "expert"), None),
            P(("dp", "expert"), None),
            P(("dp", "expert"), None),
            P(("dp", "expert"), None),
            P(("dp", "expert"), None),
            P("expert", "dp", None),
            P("expert", "dp", None),
        ),
        check_vma=False,
    )
```

```python
import functools
import math

import jax
import jax.numpy as jnp
from jax import lax
from jax.experimental import pallas as pl
from jax.experimental.pallas import tpu as pltpu
from jax.sharding import PartitionSpec as P

D = 1024
H = 4
DH = 128
EA = 5
TOPK = 16


norm_eps = 1e-05
rope_base = 10000.0
masked_score = -1e30


def sequence_layout(lengths, count):
    bounds = jnp.cumsum(lengths)
    starts = bounds - lengths
    places = jnp.arange(count, dtype=jnp.int32)
    seq_ids = jnp.sum((places[:, None] >= bounds[None, :]).astype(jnp.int32), axis=1)
    live = places < bounds[-1]
    slot_ids = jnp.arange(lengths.shape[0], dtype=jnp.int32)
    first = jnp.sum(jnp.where(seq_ids[:, None] == slot_ids[None, :], starts[None, :], 0), axis=1)
    positions = jnp.where(live, places - first, 0)
    return (seq_ids, live, positions)


def rope_tables(positions, width):
    half = width // 2
    freq = rope_base ** (-(jnp.arange(half, dtype=jnp.float32) * 2.0 / width))
    angles = positions.astype(jnp.float32)[:, None] * freq[None, :]
    return (jnp.cos(angles), jnp.sin(angles))


def rotate(field, cosine, sine):
    half = field.shape[-1] // 2
    first, second = (field[..., :half], field[..., half:])
    cos_h, sin_h = (cosine[:, None, :], sine[:, None, :])
    return jnp.concatenate(
        [first * cos_h - second * sin_h, second * cos_h + first * sin_h], axis=-1
    )


def rotate_back(field, cosine, sine):
    half = field.shape[-1] // 2
    first, second = (field[..., :half], field[..., half:])
    cos_h, sin_h = (cosine[:, None, :], sine[:, None, :])
    return jnp.concatenate(
        [first * cos_h + second * sin_h, second * cos_h - first * sin_h], axis=-1
    )


def slot_tables(routes, experts, most):
    count = routes.shape[0] * routes.shape[1]
    flat = routes.reshape(count)
    order = jnp.argsort(flat, stable=True)
    ordered = flat[order]
    firsts = jnp.searchsorted(ordered, jnp.arange(experts, dtype=jnp.int32))
    ranks = jnp.arange(count, dtype=jnp.int32) - firsts[ordered]
    sorted_slots = ordered * most + ranks
    slot_of_row = jnp.zeros((count,), jnp.int32).at[order].set(sorted_slots)
    row_of_slot = jnp.full((experts * most,), count, jnp.int32).at[sorted_slots].set(order)
    return (slot_of_row, row_of_slot)


def routed_layer(
    tokens,
    cotangent,
    seq_lengths,
    routes,
    head_experts,
    norm_gain,
    w_query,
    w_key,
    w_value,
    w_output,
    w_value_gate,
    w_output_gate,
    w_router,
    w_up,
    w_down,
):
    f32 = jnp.float32
    bf16 = jnp.bfloat16
    count = tokens.shape[0]
    experts = w_router.shape[1]
    local_experts = w_up.shape[0]
    owners = lax.axis_size("expert")
    most = 3 * count * TOPK // (2 * experts)
    routed = count * TOPK
    block = min(512, count)
    block_starts = jnp.arange(count // block, dtype=jnp.int32) * block
    scale = DH ** (-0.5)
    contract_last = (((1,), (1,)), ((), ()))
    contract_first = (((0,), (0,)), ((), ()))
    seq_ids, live, positions = sequence_layout(seq_lengths[0], count)
    cosine, sine = rope_tables(positions, DH)
    inputs = tokens.astype(f32)
    centred = inputs - jnp.mean(inputs, axis=-1, keepdims=True)
    inverse = lax.rsqrt(jnp.mean(centred * centred, axis=-1, keepdims=True) + norm_eps)
    standard = centred * inverse
    normed = (standard * norm_gain).astype(bf16)
    query_proj = jnp.dot(normed, w_query, preferred_element_type=f32).reshape(count, H, DH)
    key_proj = jnp.dot(normed, w_key, preferred_element_type=f32).reshape(count, H, DH)
    query_rot = (rotate(query_proj, cosine, sine) * scale).astype(bf16)
    key_rot = rotate(key_proj, cosine, sine).astype(bf16)
    chosen = jnp.any(
        head_experts[:, None, :, :] == jnp.arange(EA, dtype=jnp.int32)[None, :, None, None], axis=-1
    )
    value_gates = jnp.where(
        chosen,
        jax.nn.sigmoid(
            jnp.dot(tokens, w_value_gate, preferred_element_type=f32).reshape(count, EA, H)
        ),
        0.0,
    )
    output_gates = jnp.where(
        chosen,
        jax.nn.sigmoid(
            jnp.dot(tokens, w_output_gate, preferred_element_type=f32).reshape(count, EA, H)
        ),
        0.0,
    )
    value_all = jnp.dot(tokens, w_value, preferred_element_type=f32).reshape(count, EA, H, DH)
    values = jnp.sum(value_gates[..., None] * value_all, axis=1).astype(bf16)

    def allowed_at(start):
        queries = start + jnp.arange(block, dtype=jnp.int32)
        keys = jnp.arange(count, dtype=jnp.int32)
        same = (
            (seq_ids[:, None] == seq_ids[None, :])
            & (keys[None, :] <= queries[:, None])
            & live[None, :]
        )
        return same | (keys[None, :] == queries[:, None])

    def scores_at(start):
        scores = jnp.einsum("qhd,khd->hqk", query_rot, key_rot, preferred_element_type=f32)
        return (query_rot, jnp.where(allowed_at(start)[None], scores, masked_score))

    def attend(start):
        query_block, scores = scores_at(start)
        highest = jnp.max(scores, axis=-1, keepdims=True)
        shifted = jnp.exp(scores - highest)
        totals = jnp.sum(shifted, axis=-1, keepdims=True)
        shares = (shifted / totals).astype(bf16)
        result = jnp.einsum("hqk,khd->qhd", shares, values, preferred_element_type=f32)
        return (result, (highest + jnp.log(totals))[..., 0])

    attended, log_totals = lax.map(attend, block_starts)
    attended = attended.reshape(count, H, DH)
    log_totals = jnp.transpose(log_totals, (1, 0, 2)).reshape(H, count)
    heads_mixed = (
        (output_gates[..., None] * attended[:, None]).astype(bf16).reshape(count, EA * H * DH)
    )
    hidden = inputs + lax.dot_general(
        heads_mixed, w_output, contract_last, preferred_element_type=f32
    )
    hidden_low = hidden.astype(bf16)
    logits = jnp.dot(hidden_low, w_router, preferred_element_type=f32)
    gates = jax.nn.sigmoid(jnp.take_along_axis(logits, routes, axis=1))
    slot_of_row, row_of_slot = slot_tables(routes, experts, most)
    valid = row_of_slot < routed
    safe_row = jnp.minimum(row_of_slot, routed - 1)
    source = safe_row // TOPK
    outgoing = jnp.where(valid[:, None], hidden_low[source], jnp.zeros((), bf16)).reshape(
        owners, local_experts, most, D
    )

    def expert_apply(items):
        raised = jnp.einsum("nemd,edf->nemf", items, w_up, preferred_element_type=f32)
        active = jax.nn.silu(raised).astype(bf16)
        lowered = jnp.einsum("nemf,edf->nemd", active, w_down, preferred_element_type=f32).astype(
            bf16
        )
        return (lowered, raised)

    lowered, raised = expert_apply(
        lax.all_to_all(outgoing, "expert", split_axis=0, concat_axis=0, tiled=True)
    )
    returned = lax.all_to_all(lowered, "expert", split_axis=0, concat_axis=0, tiled=True).reshape(
        experts * most, D
    )
    expert_rows = returned[slot_of_row].reshape(count, TOPK, D)
    output = hidden + jnp.sum(gates[..., None] * expert_rows, axis=1)
    mixed = output.astype(bf16)
    grad_out = cotangent.astype(f32) * live[:, None].astype(f32)
    grad_gates = jnp.sum(grad_out[:, None, :] * expert_rows, axis=2)
    gate_flat = gates.reshape(routed)
    grad_outgoing = (
        jnp.where(valid[:, None], gate_flat[safe_row][:, None] * grad_out[source], 0.0)
        .astype(bf16)
        .reshape(owners, local_experts, most, D)
    )
    grad_lowered = lax.all_to_all(grad_outgoing, "expert", split_axis=0, concat_axis=0, tiled=True)
    items = lax.all_to_all(outgoing, "expert", split_axis=0, concat_axis=0, tiled=True)
    raised = expert_apply(items)[1]
    grad_active = jnp.einsum("nemd,edf->nemf", grad_lowered, w_down, preferred_element_type=f32)
    sigmoid_raised = jax.nn.sigmoid(raised)
    grad_raised = (grad_active * sigmoid_raised * (1.0 + raised * (1.0 - sigmoid_raised))).astype(
        bf16
    )
    grad_items = jnp.einsum("nemf,edf->nemd", grad_raised, w_up, preferred_element_type=f32).astype(
        bf16
    )
    active = jax.nn.silu(raised).astype(bf16)
    grad_items, grad_raised, active = (grad_items, grad_raised, active)
    grad_items, grad_raised, active, grad_arrived, arrived = (
        grad_items,
        grad_raised,
        active,
        grad_lowered,
        items,
    )
    grad_up_local = jnp.einsum("nemd,nemf->edf", arrived, grad_raised, preferred_element_type=f32)
    grad_down_local = jnp.einsum("nemd,nemf->edf", grad_arrived, active, preferred_element_type=f32)
    grad_up, grad_down = (
        lax.psum_scatter(
            grad_up_local.astype(jnp.bfloat16), "dp", scatter_dimension=1, tiled=True
        ).astype(jnp.float32),
        lax.psum_scatter(
            grad_down_local.astype(jnp.bfloat16), "dp", scatter_dimension=1, tiled=True
        ).astype(jnp.float32),
    )
    grad_back = lax.all_to_all(
        grad_items, "expert", split_axis=0, concat_axis=0, tiled=True
    ).reshape(experts * most, D)
    grad_hidden = grad_out + jnp.sum(
        grad_back[slot_of_row].reshape(count, TOPK, D), axis=1, dtype=f32
    )
    grad_picked = grad_gates * gates * (1.0 - gates)
    expert_ids = jnp.arange(experts, dtype=jnp.int32)
    grad_logits = jnp.sum(
        jnp.where(routes[:, :, None] == expert_ids[None, None, :], grad_picked[..., None], 0.0),
        axis=1,
    ).astype(bf16)
    grad_router = lax.dot_general(
        hidden_low, grad_logits, contract_first, preferred_element_type=f32
    )
    grad_hidden = grad_hidden + lax.dot_general(
        grad_logits, w_router, contract_last, preferred_element_type=f32
    )
    grad_hidden_low = grad_hidden.astype(bf16)
    grad_output = lax.dot_general(
        grad_hidden_low, heads_mixed, contract_first, preferred_element_type=f32
    )
    grad_mixed = jnp.dot(grad_hidden_low, w_output, preferred_element_type=f32).reshape(
        count, EA, H, DH
    )
    grad_attended = jnp.sum(output_gates[..., None] * grad_mixed, axis=1).astype(bf16)
    grad_out_gates = jnp.sum(grad_mixed * attended[:, None], axis=-1)
    grad_out_logits = (
        jnp.where(chosen, grad_out_gates * output_gates * (1.0 - output_gates), 0.0)
        .astype(bf16)
        .reshape(count, EA * H)
    )

    def attend_back(carry, start):
        grad_keys, grad_vals = carry
        query_block, scores = scores_at(start)
        shares = jnp.exp(scores - log_totals[..., None])
        grad_shares = jnp.einsum("qhd,khd->hqk", grad_attended, values, preferred_element_type=f32)
        centre = jnp.sum(shares * grad_shares, axis=-1, keepdims=True)
        grad_scores = (shares * (grad_shares - centre)).astype(bf16)
        grad_query_block = jnp.einsum(
            "hqk,khd->qhd", grad_scores, key_rot, preferred_element_type=f32
        )
        grad_keys = grad_keys + jnp.einsum(
            "hqk,qhd->khd", grad_scores, query_block, preferred_element_type=f32
        )
        grad_vals = grad_vals + jnp.einsum(
            "hqk,qhd->khd", shares.astype(bf16), grad_attended, preferred_element_type=f32
        )
        return ((grad_keys, grad_vals), grad_query_block)

    zero_heads = jnp.zeros((count, H, DH), f32)
    (grad_keys, grad_vals), grad_queries = lax.scan(
        attend_back, (zero_heads, zero_heads), block_starts
    )
    grad_queries = grad_queries.reshape(count, H, DH)
    grad_query_proj = (
        rotate_back(grad_queries * scale, cosine, sine).astype(bf16).reshape(count, H * DH)
    )
    grad_key_proj = rotate_back(grad_keys, cosine, sine).astype(bf16).reshape(count, H * DH)
    grad_value_all = (
        (value_gates[..., None] * grad_vals[:, None]).astype(bf16).reshape(count, EA * H * DH)
    )
    grad_value_gates = jnp.sum(grad_vals[:, None] * value_all, axis=-1)
    grad_value_logits = (
        jnp.where(chosen, grad_value_gates * value_gates * (1.0 - value_gates), 0.0)
        .astype(bf16)
        .reshape(count, EA * H)
    )
    grad_query = lax.dot_general(
        normed, grad_query_proj, contract_first, preferred_element_type=f32
    )
    grad_key = lax.dot_general(normed, grad_key_proj, contract_first, preferred_element_type=f32)
    grad_value = lax.dot_general(tokens, grad_value_all, contract_first, preferred_element_type=f32)
    grad_value_gate = lax.dot_general(
        tokens, grad_value_logits, contract_first, preferred_element_type=f32
    )
    grad_output_gate = lax.dot_general(
        tokens, grad_out_logits, contract_first, preferred_element_type=f32
    )
    grad_normed = lax.dot_general(
        grad_query_proj, w_query, contract_last, preferred_element_type=f32
    ) + lax.dot_general(grad_key_proj, w_key, contract_last, preferred_element_type=f32)
    grad_gain = jnp.sum(grad_normed * standard, axis=0)
    grad_standard = grad_normed * norm_gain
    grad_tokens = grad_hidden + inverse * (
        grad_standard
        - jnp.mean(grad_standard, axis=-1, keepdims=True)
        - standard * jnp.mean(grad_standard * standard, axis=-1, keepdims=True)
    )
    grad_tokens = (
        grad_tokens
        + lax.dot_general(grad_value_all, w_value, contract_last, preferred_element_type=f32)
        + lax.dot_general(
            grad_value_logits, w_value_gate, contract_last, preferred_element_type=f32
        )
        + lax.dot_general(grad_out_logits, w_output_gate, contract_last, preferred_element_type=f32)
    )
    summed = (
        lax.psum_scatter(grad_gain, ("dp", "expert"), scatter_dimension=0, tiled=True),
        lax.psum_scatter(grad_query, ("dp", "expert"), scatter_dimension=0, tiled=True),
        lax.psum_scatter(grad_key, ("dp", "expert"), scatter_dimension=0, tiled=True),
        lax.psum_scatter(grad_value, ("dp", "expert"), scatter_dimension=0, tiled=True),
        lax.psum_scatter(grad_output, ("dp", "expert"), scatter_dimension=0, tiled=True),
        lax.psum_scatter(grad_value_gate, ("dp", "expert"), scatter_dimension=0, tiled=True),
        lax.psum_scatter(grad_output_gate, ("dp", "expert"), scatter_dimension=0, tiled=True),
        lax.psum_scatter(grad_router, ("dp", "expert"), scatter_dimension=0, tiled=True),
    )
    return (
        mixed,
        grad_tokens,
        summed[0],
        summed[1],
        summed[2],
        summed[3],
        summed[4],
        summed[5],
        summed[6],
        summed[7],
        grad_up,
        grad_down,
    )


F32 = jnp.float32
BF16 = jnp.bfloat16
MESH = pl.DeviceIdType.MESH
LANES = 128


def mm(a, b):
    return lax.dot_general(a, b, (((1,), (0,)), ((), ())), preferred_element_type=F32)


def mm_t(a, b):
    return lax.dot_general(a, b, (((1,), (1,)), ((), ())), preferred_element_type=F32)


def tmm(a, b):
    return lax.dot_general(a, b, (((0,), (0,)), ((), ())), preferred_element_type=F32)


def iota(shape, axis):
    return lax.broadcasted_iota(jnp.int32, shape, axis)


def column(x, j, width=LANES):
    return jnp.broadcast_to(x[:, j : j + 1], (x.shape[0], width))


def sigmoid(x):
    return 1.0 / (1.0 + jnp.exp(-x))


class Scratch:
    def __init__(self):
        self.names, self.shapes = [], []

    def add(self, name, shape):
        self.names.append(name)
        self.shapes.append(shape)

    def vmem(self, name, shape, dtype):
        self.add(name, pltpu.VMEM(shape, dtype))

    def sems(self, name, *shape):
        self.add(name, pltpu.SemaphoreType.DMA(shape))


INPUTS = ("tokens", "cot", "lens", "rt", "het", "gain", "wvg", "wog", "wr", "wq", "wk", "wv", "wo", "wu", "wd")
OUTPUTS = ("mixed", "gtok", "ggain", "gq", "gk", "gv", "go", "gvg", "gog", "gr", "gup", "gdn")


def layer_kernel(names, nd, nz, local, *refs):
    r = dict(zip(names, refs))
    R = type("R", (), r)
    C = R.tokens.shape[0]
    own_e = 2 * local
    pad_e = R.maskb.shape[1]
    EF = own_e * DH
    HF = local * DH
    HD = H * DH
    EV = EA * HD
    S = D // (nd * nz * 2)
    SL = S * nz
    GATE = EA * H
    p = lax.axis_index("dp")
    e = lax.axis_index("expert")
    z = e // 2
    c = e % 2
    sib = 1 - c

    def dev(p_, z_, c_):
        return (p_, z_ * 2 + c_)

    def times(i, n):
        return pl.multiple_of(i * n, n)

    def remote(src, dst, ss, rs, to):
        return pltpu.make_async_remote_copy(
            src_ref=src, dst_ref=dst, send_sem=ss, recv_sem=rs, device_id=to, device_id_type=MESH
        )

    def arrived(dst, rs):
        remote(dst, dst, rs, rs, dev(p, z, sib)).wait_recv()

    def sent(src, ss):
        remote(src, src, ss, ss, dev(p, z, sib)).wait_send()

    def plane(k):
        return lax.rem(p + k, nd)

    def line(k):
        return lax.rem(z + k, nz)

    loads = {}

    def load(name, src, dst, sem):
        cp = pltpu.make_async_copy(src, dst, sem)
        cp.start()
        loads.setdefault(name, []).append(cp)

    def loaded(name):
        for cp in loads.pop(name):
            cp.wait()

    load("qk", R.wq, R.wqk_b.at[:, 0:HD], R.ld.at[0])
    load("qk", R.wk, R.wqk_b.at[:, HD : 2 * HD], R.ld.at[1])
    load("v", R.wv, R.wv_b, R.ld.at[2])
    for i in range(local):
        col = times(c * local + i, DH)
        load("up", R.wu.at[i], R.wup_b.at[:, pl.ds(col, DH)], R.ld.at[4 + i])
        load("dn", R.wd.at[i], R.wdn_b.at[:, pl.ds(col, DH)], R.ld.at[4 + local + i])
    load("o", R.wo, R.wo_b, R.ld.at[3])

    barrier = pltpu.get_barrier_semaphore()
    partners = [dev(p, z, sib)]
    partners += [dev(p, line(k), c) for k in range(1, nz)]
    for k in range(1, nd):
        partners += [dev(plane(k), z, c), dev(plane(k), z, sib)]
    for to in partners:
        pl.semaphore_signal(barrier, inc=1, device_id=to, device_id_type=MESH)

    l0 = R.lens[0, 0]
    b1 = l0 + R.lens[0, 1]
    row = iota((C, LANES), 0)
    lane = iota((C, LANES), 1)
    seq_r = (row >= l0).astype(jnp.int32) + (row >= b1).astype(jnp.int32)
    seq_c = (lane >= l0).astype(jnp.int32) + (lane >= b1).astype(jnp.int32)
    live = row < b1
    allowed = ((seq_r == seq_c) & (lane <= row) & (lane < b1)) | (row == lane)
    live_f = jnp.where(live, 1.0, 0.0).astype(F32)
    start = jnp.where(seq_r == 0, 0, l0)
    position = jnp.where(live, row - start, 0).astype(F32)

    for b in range(D // LANES):
        cols = slice(b * LANES, (b + 1) * LANES)
        R.cotb[pl.ds(times(z, C), C), cols] = (R.cot[:, cols].astype(F32) * live_f).astype(BF16)
    ids = iota((pad_e, C), 0)
    for zz in range(nz):
        named = jnp.zeros((pad_e, C), F32)
        for k in range(TOPK):
            hit = jnp.broadcast_to(R.rt[k : k + 1, :], (pad_e, C)) == ids + zz * own_e
            named = jnp.where(hit & (ids < own_e), 1.0, named)
        R.mask_s[zz] = named.astype(BF16)
    R.maskb[z] = R.mask_s[z]

    pl.semaphore_wait(barrier, len(partners))

    def block(buf, o):
        return buf.at[pl.ds(times(o, C), C), :]

    def pass_on(buf, ss, rs, o, right, left):
        @pl.when(right)
        def _():
            remote(block(buf, o), block(buf, o), ss.at[0, o], rs.at[o], dev(p, z + 1, c)).start()

        @pl.when(left)
        def _():
            remote(block(buf, o), block(buf, o), ss.at[1, o], rs.at[o], dev(p, z - 1, c)).start()

    def passed(buf, ss, o, right, left):
        @pl.when(right)
        def _():
            sent(block(buf, o), ss.at[0, o])

        @pl.when(left)
        def _():
            sent(block(buf, o), ss.at[1, o])

    def gather_own(buf, ss, rs):
        pass_on(buf, ss, rs, z, z < nz - 1, z > 0)

    def gather_on(buf, ss, rs, o):
        arrived(block(buf, o), rs.at[o])
        pass_on(buf, ss, rs, o, (o < z) & (z < nz - 1), (o > z) & (z > 0))

    def gather_step(buf, ss, rs, k):
        @pl.when(z >= k)
        def _():
            gather_on(buf, ss, rs, z - k)

        @pl.when(z + k < nz)
        def _():
            gather_on(buf, ss, rs, z + k)

    def gather_end(buf, ss):
        passed(buf, ss, z, z < nz - 1, z > 0)
        for k in range(1, nz):

            @pl.when(z >= k)
            def _():
                passed(buf, ss, z - k, z < nz - 1, False)

            @pl.when(z + k < nz)
            def _():
                passed(buf, ss, z + k, False, z > 0)

    gather_own(R.cotb, R.cot_ss, R.cot_rs)
    masks = []
    for k in range(1, nz):
        o = line(k)
        cp = remote(R.mask_s.at[o], R.maskb.at[z], R.mask_ss.at[k], R.mask_rs.at[z], dev(p, o, c))
        cp.start()
        masks.append(cp)

    s_row, s_col = iota((GATE, LANES), 0), iota((GATE, LANES), 1)
    to_v = jnp.where(s_row == s_col, 1.0, 0.0).astype(BF16)
    to_o = jnp.where(s_row + GATE == s_col, 1.0, 0.0).astype(BF16)
    R.wg_b[...] = (tmm(R.wvg[...], to_v) + tmm(R.wog[...], to_o)).astype(BF16)
    experts = R.wr.shape[0]
    r_row, r_col = iota((experts, LANES), 0), iota((experts, LANES), 1)
    to_r = jnp.where((r_row == r_col + z * own_e) & (r_col < own_e), 1.0, 0.0).astype(BF16)
    R.wrl_b[...] = tmm(R.wr[...], to_r).astype(BF16)

    half = lax.rem(lane, DH // 2).astype(F32)
    angle = position * jnp.exp(half * (-2.0 / DH * math.log(rope_base)))
    cosine = jnp.cos(angle)
    sine = jnp.where(lane < DH // 2, -jnp.sin(angle), jnp.sin(angle))

    def rot(v):
        return v * cosine + pltpu.roll(v, DH // 2, 1) * sine

    def rot_back(v):
        return v * cosine - pltpu.roll(v, DH // 2, 1) * sine

    inputs = R.tokens[...].astype(F32)
    centred = inputs - jnp.mean(inputs, axis=-1, keepdims=True)
    inverse = lax.rsqrt(jnp.mean(centred * centred, axis=-1, keepdims=True) + norm_eps)
    standard = centred * inverse
    R.std_b[...] = standard
    R.normed_b[...] = (standard * R.gain[...]).astype(BF16)

    loaded("qk")
    scale = DH ** (-0.5)
    qk = mm(R.normed_b[...], R.wqk_b[:, 0:HD])
    for h in range(H):
        hs = slice(h * DH, (h + 1) * DH)
        R.q_b[:, hs] = (rot(qk[:, hs]) * scale).astype(BF16)
    qk = mm(R.normed_b[...], R.wqk_b[:, HD : 2 * HD])
    for h in range(H):
        hs = slice(h * DH, (h + 1) * DH)
        R.k_b[:, hs] = rot(qk[:, hs]).astype(BF16)

    hit = []
    for j in range(GATE):
        x, h = divmod(j, H)
        one = (R.het[2 * h : 2 * h + 1, :] == x) | (R.het[2 * h + 1 : 2 * h + 2, :] == x)
        hit.append(jnp.where(one, 1.0, 0.0).astype(F32))
    hit = jnp.concatenate(hit + hit + [jnp.zeros((LANES - 2 * GATE, C), F32)], axis=0)
    R.gate_b[...] = sigmoid(mm(R.tokens[...], R.wg_b[...])) * hit.T

    loaded("up")
    loaded("dn")
    wx = []
    for i, buf in enumerate((R.wup_b, R.wdn_b)):
        part = buf.at[:, pl.ds(times(c, HF), HF)]
        cp = remote(part, part, R.w_ss.at[i], R.w_rs.at[i], dev(p, z, sib))
        cp.start()
        wx.append(cp)

    loaded("v")
    gates = R.gate_b[...]
    total = [None] * H
    for x in range(EA):
        R.val_b[:, x * HD : (x + 1) * HD] = mm(R.tokens[...], R.wv_b[:, x * HD : (x + 1) * HD])
        for h in range(H):
            lo = x * HD + h * DH
            term = column(gates, x * H + h) * R.val_b[:, lo : lo + DH]
            total[h] = term if x == 0 else total[h] + term
    for h in range(H):
        R.v_b[:, h * DH : (h + 1) * DH] = total[h].astype(BF16)

    for h in range(H):
        hs = slice(h * DH, (h + 1) * DH)
        scores = jnp.where(allowed, mm_t(R.q_b[:, hs], R.k_b[:, hs]), masked_score)
        shifted = jnp.exp(scores - jnp.max(scores, axis=-1, keepdims=True))
        shares = shifted / jnp.sum(shifted, axis=-1, keepdims=True)
        R.prob_b[h] = shares
        R.att_b[:, hs] = mm(shares.astype(BF16), R.v_b[:, hs])

    for k in range(1, 2):
        gather_step(R.cotb, R.cot_ss, R.cot_rs, k)

    for x in range(EA):
        for h in range(H):
            lo = x * HD + h * DH
            R.mix_b[:, lo : lo + DH] = (
                column(gates, GATE + x * H + h) * R.att_b[:, h * DH : (h + 1) * DH]
            ).astype(BF16)
    loaded("o")
    half_d = D // 2
    for b in range(2):
        cols = slice(b * half_d, (b + 1) * half_d)
        hidden = R.tokens[:, cols].astype(F32) + mm_t(R.mix_b[...], R.wo_b[cols, :])
        R.hid_f[:, cols] = hidden
        R.hidb[pl.ds(times(z, C), C), cols] = hidden.astype(BF16)
    gather_own(R.hidb, R.hid_ss, R.hid_rs)

    def put_turned(x, w):
        for b in range(D // LANES):
            t = x[:, b * LANES : (b + 1) * LANES].astype(F32).T.astype(BF16)
            for q in range(LANES // S):
                i = (b * LANES) // S + q
                pp, zz, cc = i // (2 * nz), (i % (2 * nz)) // 2, i % 2
                at = (pp * 2 + cc) * SL + zz * S
                R.lt[at : at + S, w * LANES : (w + 1) * LANES] = t[q * S : (q + 1) * S, :]

    plane_all = [(k, dc) for k in range(nd) for dc in range(2) if k or dc]

    def side(dc):
        return sib if dc else c

    def send_turned(w0, w1, ss, rs):
        out = []
        lanes = slice(w0 * LANES, w1 * LANES)
        for k, dc in plane_all:
            to = plane(k)
            slot = 2 * k + dc
            at = times(to * 2 + side(dc), SL)
            cp = remote(
                R.lt.at[pl.ds(at, SL), lanes],
                R.ltr.at[slot, :, lanes],
                ss.at[slot],
                rs.at[slot],
                dev(to, z, side(dc)),
            )
            cp.start()
            out.append(cp)
        R.ltr[0, :, lanes] = R.lt[pl.ds(times(p * 2 + c, SL), SL), lanes]
        return out

    def send_rows(buf, lanes, ss, rs):
        out = []
        for k in range(1, nd):
            cp = remote(
                buf.at[0:C, lanes],
                buf.at[2 * k * C : (2 * k + 1) * C, lanes],
                ss.at[k],
                rs.at[2 * k],
                dev(plane(k), z, c),
            )
            cp.start()
            out.append(cp)
        return out + [hand_over(buf, lanes, ss, rs, 0)]

    def hand_over(buf, lanes, ss, rs, k):
        cp = remote(
            buf.at[2 * k * C : (2 * k + 1) * C, lanes],
            buf.at[(2 * k + 1) * C : (2 * k + 2) * C, lanes],
            ss.at[nd + k],
            rs.at[2 * k + 1],
            dev(p, z, sib),
        )
        cp.start()
        return cp

    def hand_all(buf, lanes, ss, rs, out):
        for k in range(1, nd):
            out[k - 1].wait_recv()
            out.append(hand_over(buf, lanes, ss, rs, k))

    def rows_here(buf, lanes, rs):
        for k in range(nd):
            arrived(buf.at[(2 * k + 1) * C : (2 * k + 2) * C, lanes], rs.at[2 * k + 1])

    put_turned(R.tokens[...], 0)
    put_turned(R.normed_b[...], 1)
    put_turned(R.hid_f[...], 2)
    turned = send_turned(0, 3, R.lt_ss, R.lt_rs)
    R.ra[0:C, 0:HD] = R.att_b[...].astype(BF16)
    R.ra[0:C, HD : HD + LANES] = gates.astype(BF16)
    RA = slice(0, HD + LANES)
    ra_out = send_rows(R.ra, RA, R.ra_ss, R.ra_rs)

    for k in range(2, nz - 1):
        gather_step(R.cotb, R.cot_ss, R.cot_rs, k)

    for cp in wx:
        cp.wait()

    least = jnp.minimum(z, nz - 1 - z)

    def origin(k):
        paired = k <= 2 * least
        dist = jnp.where(paired, (k + 1) // 2, k - least)
        left = jnp.where(paired, lax.rem(k, 2) == 1, z > nz - 1 - z)
        return jnp.where(k == 0, z, jnp.where(left, z - dist, z + dist))

    def expert_block(k, carry):
        o = origin(k)
        rows = pl.ds(times(o, C), C)

        @pl.when(k > 0)
        def _():
            gather_on(R.hidb, R.hid_ss, R.hid_rs, o)

            @pl.when((o == z - nz + 1) | (o == z + nz - 1))
            def _():
                arrived(block(R.cotb, o), R.cot_rs.at[o])

            arrived(R.maskb.at[o], R.mask_rs.at[o])

        hb = R.hidb[rows, :]
        cb = R.cotb[rows, :]
        named = R.maskb[o].astype(F32)
        named = jnp.concatenate([named, jnp.zeros((LANES - pad_e, C), F32)], axis=0).T
        g = sigmoid(mm(hb, R.wrl_b[...])) * named
        glog = jnp.zeros((C, LANES), F32)
        for q in range(own_e // 4):
            cols = slice(q * 4 * DH, (q + 1) * 4 * DH)
            raised = mm(hb, R.wup_b[:, cols])
            back = mm(cb, R.wdn_b[:, cols])
            for i in range(4):
                j = q * 4 + i
                u = raised[:, i * DH : (i + 1) * DH]
                a = back[:, i * DH : (i + 1) * DH]
                gj = column(g, j)
                s = sigmoid(u)
                act = u * s
                lo = j * DH
                R.gact[rows, lo : lo + DH] = (gj * act).astype(BF16)
                R.gra[rows, lo : lo + DH] = (gj * a * (s * (1.0 + u * (1.0 - s)))).astype(BF16)
                gg = jnp.sum(a * act, axis=1, keepdims=True)
                glog = jnp.where(lane == j, jnp.broadcast_to(gg, (C, LANES)), glog)
        glog = glog * g * (1.0 - g)
        low = glog.astype(BF16)
        R.glog_s[o] = glog.T[0:pad_e, :].astype(BF16)
        for b in range(2):
            cols = slice(b * half_d, (b + 1) * half_d)
            gh = mm_t(R.gra[rows, :], R.wup_b[cols, :]) + mm_t(low, R.wrl_b[cols, :])
            R.gh_s[o, :, cols] = gh.astype(BF16)

        @pl.when(k > 0)
        def _():
            remote(R.gh_s.at[o], R.gh_r.at[z], R.gh_ss.at[o], R.gh_rs.at[z], dev(p, o, c)).start()
            remote(
                R.glog_s.at[o], R.glog_r.at[z], R.gl_ss.at[o], R.gl_rs.at[z], dev(p, o, c)
            ).start()

        return carry

    lax.fori_loop(0, nz, expert_block, 0)

    def out_tile(t, carry):
        rows = pl.ds(times(t, 256), 256)
        got = mm_t(R.gact[...], R.wdn_b[rows, :]).astype(BF16)
        for o in range(nz):
            R.out_s[o, :, rows] = got[o * C : (o + 1) * C, :]
        return carry

    lax.fori_loop(0, D // 256, out_tile, 0)
    for k in range(1, nz):
        o = line(k)
        remote(R.out_s.at[o], R.out_r.at[z], R.out_ss.at[o], R.out_rs.at[z], dev(p, o, c)).start()

    pairs = []
    for i, (left_of, right_of, buf) in enumerate(
        ((R.cotb, R.gact, R.wdn_b), (R.hidb, R.gra, R.wup_b))
    ):

        def grad_tile(t, carry, base):
            cols = pl.ds(pl.multiple_of(base + t * 256, 256), 256)
            buf[:, cols] = tmm(left_of[...], right_of[:, cols]).astype(BF16)
            return carry

        lax.fori_loop(0, HF // 256, functools.partial(grad_tile, base=sib * HF), 0)
        cp = remote(
            buf.at[:, pl.ds(times(sib, HF), HF)],
            R.pair_r.at[i],
            R.pair_ss.at[i],
            R.pair_rs.at[i],
            dev(p, z, sib),
        )
        cp.start()
        pairs.append(cp)
        lax.fori_loop(0, HF // 256, functools.partial(grad_tile, base=c * HF), 0)

    hand_all(R.ra, RA, R.ra_ss, R.ra_rs, ra_out)

    ghid = R.cotb[pl.ds(times(z, C), C), :].astype(F32) + R.gh_s[z].astype(F32)
    for k in range(1, nz):
        o = line(k)
        arrived(R.gh_r.at[o], R.gh_rs.at[o])
        arrived(R.glog_r.at[o], R.gl_rs.at[o])
        ghid = ghid + R.gh_r[o].astype(F32)
    R.glog_r[z] = R.glog_s[z]
    R.ghid_f[...] = ghid
    R.ghid_b[...] = ghid.astype(BF16)
    put_turned(R.ghid_f[...], 3)
    turned_late = send_turned(3, 4, R.ltl_ss, R.ltl_rs)

    gates = R.gate_b[...]
    small = jnp.zeros((C, LANES), F32)
    gatt = [None] * H
    for x in range(EA):
        gmix = mm(R.ghid_b[...], R.wo_b[:, x * HD : (x + 1) * HD])
        for h in range(H):
            hs = slice(h * DH, (h + 1) * DH)
            j = GATE + x * H + h
            term = column(gates, j) * gmix[:, hs]
            gatt[h] = term if x == 0 else gatt[h] + term
            gg = jnp.sum(gmix[:, hs] * R.att_b[:, hs], axis=1, keepdims=True)
            small = jnp.where(lane == j, jnp.broadcast_to(gg, (C, LANES)), small)
    for h in range(H):
        hs = slice(h * DH, (h + 1) * DH)
        low = gatt[h].astype(BF16)
        R.gatt_b[:, hs] = low
        gval = tmm(R.prob_b[h].astype(BF16), low)
        R.gval_f[:, hs] = gval
        R.rb[0:C, hs] = gval.astype(BF16)
        for x in range(EA):
            lo = x * HD + h * DH
            j = x * H + h
            gg = jnp.sum(gval * R.val_b[:, lo : lo + DH], axis=1, keepdims=True)
            small = jnp.where(lane == j, jnp.broadcast_to(gg, (C, LANES)), small)
    small = small * gates * (1.0 - gates)
    glog = jnp.concatenate(
        [jnp.zeros((2 * GATE, C), F32)]
        + [R.glog_r[o].astype(F32) for o in range(nz)]
        + [jnp.zeros((LANES - 2 * GATE - nz * pad_e, C), F32)],
        axis=0,
    )
    R.small_b[...] = small.astype(BF16)
    R.rb[0:C, HD : HD + LANES] = (small + glog.T).astype(BF16)
    RV = slice(0, HD + LANES)
    rv_out = send_rows(R.rb, RV, R.rv_ss, R.rv_rs)

    q0 = HD + LANES
    for h in range(H):
        hs = slice(h * DH, (h + 1) * DH)
        low = R.gatt_b[:, hs]
        gsh = mm_t(low, R.v_b[:, hs])
        prob = R.prob_b[h]
        centre = jnp.sum(prob * gsh, axis=-1, keepdims=True)
        gs = (prob * (gsh - centre)).astype(BF16)
        R.rb[0:C, q0 + h * DH : q0 + (h + 1) * DH] = rot_back(
            mm(gs, R.k_b[:, hs]) * scale
        ).astype(BF16)
        R.rb[0:C, q0 + HD + h * DH : q0 + HD + (h + 1) * DH] = rot_back(
            tmm(gs, R.q_b[:, hs])
        ).astype(BF16)
    RQ = slice(q0, q0 + 2 * HD)
    rq_out = send_rows(R.rb, RQ, R.rq_ss, R.rq_rs)

    for cp in turned:
        cp.wait()
    rows_here(R.ra, RA, R.ra_rs)
    for cp in turned_late:
        cp.wait()

    def turned_of(w):
        return jnp.concatenate(
            [R.ltr[s, :, w * LANES : (w + 1) * LANES] for s in range(2 * nd)], axis=1
        )

    def send_part(part, lanes):
        for k in range(1, nz):
            o = line(k)
            remote(
                R.pb.at[pl.ds(times(o, S), S), lanes],
                R.pr.at[z, :, lanes],
                R.p_ss.at[part, o],
                R.p_rs.at[part, z],
                dev(p, o, c),
            ).start()

    def gated_grad(w, rows_of, g0, at):
        left = turned_of(w)
        for x in range(EA):
            right = []
            for h in range(H):
                gx = column(R.ra[:, HD : HD + LANES], g0 + x * H + h).astype(F32)
                right.append((gx * rows_of[:, h * DH : (h + 1) * DH].astype(F32)).astype(BF16))
            right = jnp.concatenate(right, axis=1)
            R.pb[:, at + x * HD : at + (x + 1) * HD] = mm(left, right).astype(BF16)

    PO, PV, PQ, PS = (
        slice(0, EV),
        slice(EV, 2 * EV),
        slice(2 * EV, 2 * EV + 2 * HD),
        slice(2 * EV + 2 * HD, 2 * EV + 2 * HD + LANES),
    )
    gated_grad(3, R.ra, GATE, 0)
    send_part(0, PO)

    gproj = mm_t(R.rb[0:C, RQ], R.wqk_b[...])
    standard = R.std_b[...]
    column_sum = jnp.sum(gproj * standard, axis=0, keepdims=True)
    for b in range(D // LANES):
        R.gp[0, b : b + 1, :] = column_sum[:, b * LANES : (b + 1) * LANES]
    gain_out = []
    for k, dc in plane_all:
        slot = 2 * k + dc
        cp = remote(
            R.gp.at[0], R.gp.at[slot], R.gp_ss.at[slot], R.gp_rs.at[slot], dev(plane(k), z, side(dc))
        )
        cp.start()
        gain_out.append(cp)

    hand_all(R.rb, RV, R.rv_ss, R.rv_rs, rv_out)

    inputs = R.tokens[...].astype(F32)
    centred = inputs - jnp.mean(inputs, axis=-1, keepdims=True)
    inverse = lax.rsqrt(jnp.mean(centred * centred, axis=-1, keepdims=True) + norm_eps)
    gs = gproj * R.gain[...]
    gtok = R.ghid_f[...] + inverse * (
        gs
        - jnp.mean(gs, axis=-1, keepdims=True)
        - standard * jnp.mean(gs * standard, axis=-1, keepdims=True)
    )
    R.gtok[...] = gtok
    for x in range(EA):
        for h in range(H):
            lo = x * HD + h * DH
            R.mix_b[:, lo : lo + DH] = (
                column(gates, x * H + h) * R.gval_f[:, h * DH : (h + 1) * DH]
            ).astype(BF16)
    for b in range(2):
        cols = slice(b * half_d, (b + 1) * half_d)
        R.gtok[:, cols] += mm_t(R.mix_b[...], R.wv_b[cols, :]) + mm_t(
            R.small_b[...], R.wg_b[cols, :]
        )

    rows_here(R.rb, RV, R.rv_rs)
    gated_grad(0, R.rb, 0, EV)
    send_part(1, PV)
    hand_all(R.rb, RQ, R.rq_ss, R.rq_rs, rq_out)
    lane_s = iota((SL, LANES), 1)
    small_t = mm(turned_of(0), R.rb[:, HD : HD + LANES])
    small_h = mm(turned_of(2), R.rb[:, HD : HD + LANES])
    R.pb[:, PS] = jnp.where(lane_s < 2 * GATE, small_t, small_h).astype(BF16)
    send_part(3, PS)
    rows_here(R.rb, RQ, R.rq_rs)
    left = turned_of(1)
    for b in range(2):
        lo = q0 + b * HD
        R.pb[:, 2 * EV + b * HD : 2 * EV + (b + 1) * HD] = mm(left, R.rb[:, lo : lo + HD]).astype(
            BF16
        )
    send_part(2, PQ)

    own_cols = pl.ds(times(c, HF), HF)
    rows_d = D // nd
    plane_out = []
    for i, buf in enumerate((R.wdn_b, R.wup_b)):
        pairs[i].wait()

        def pair_tile(t, carry):
            rows = pl.ds(times(t, 128), 128)
            buf[rows, own_cols] = (
                buf[rows, own_cols].astype(F32) + R.pair_r[i, rows, :].astype(F32)
            ).astype(BF16)
            return carry

        lax.fori_loop(0, D // 128, pair_tile, 0)
        for k in range(1, nd):
            to = plane(k)
            cp = remote(
                buf.at[pl.ds(times(to, rows_d), rows_d), own_cols],
                R.eg_r.at[k - 1, i],
                R.eg_ss.at[k - 1, i],
                R.eg_rs.at[k - 1, i],
                dev(to, z, c),
            )
            cp.start()
            plane_out.append(cp)

    total = R.gp[0]
    for cp, (k, dc) in zip(gain_out, plane_all):
        cp.wait()
        total = total + R.gp[2 * k + dc]
    R.gz_s[...] = total
    for k in range(1, nz):
        o = line(k)
        remote(R.gz_s, R.gz.at[z], R.gz_ss.at[o], R.gz_rs.at[z], dev(p, o, c)).start()

    out = R.hid_f[...] + R.out_s[z].astype(F32)
    for k in range(1, nz):
        o = line(k)
        arrived(R.out_r.at[o], R.out_rs.at[o])
        out = out + R.out_r[o].astype(F32)
    R.mixed[...] = out.astype(BF16)

    for k in range(1, nz):
        o = line(k)
        arrived(R.gz.at[o], R.gz_rs.at[o])
        total = total + R.gz[o]
    first = (p * 2 * nz + z * 2 + c) * S
    pick_row = iota((D // LANES, LANES), 0) == first // LANES
    line_sum = jnp.sum(jnp.where(pick_row, total, 0.0), axis=0, keepdims=True)
    shift = lax.rem(LANES - lax.rem(first, LANES), LANES)
    line_sum = pltpu.roll(jnp.broadcast_to(line_sum, (8, LANES)), shift, 1)
    R.ggain[...] = line_sum[0:1, 0:S]

    own_rows = pl.ds(times(z, S), S)

    def line_total(part, lanes):
        got = R.pb[own_rows, lanes].astype(F32)
        for k in range(1, nz):
            o = line(k)
            arrived(R.pr.at[o, :, lanes], R.p_rs.at[part, o])
            got = got + R.pr[o, :, lanes].astype(F32)
        return got

    R.go[...] = line_total(0, PO)
    R.gv[...] = line_total(1, PV)
    got = line_total(3, PS)

    def pick(width, source):
        a, b = iota((width, LANES), 1), iota((width, LANES), 0)
        sel = jnp.where(a == source(b), 1.0, 0.0).astype(F32)
        return lax.dot_general(
            sel,
            got,
            (((1,), (1,)), ((), ())),
            preferred_element_type=F32,
            precision=lax.Precision.HIGHEST,
        )

    def router_lane(b):
        at = jnp.zeros_like(b)
        for o in range(nz):
            at = jnp.where(b >= o * own_e, 2 * GATE + o * pad_e + b - o * own_e, at)
        return at

    R.gvg[...] = pick(GATE, lambda b: b)
    R.gog[...] = pick(GATE, lambda b: b + GATE)
    R.gr[...] = pick(experts, router_lane)
    got = line_total(2, PQ)
    R.gq[...] = got[:, 0:HD]
    R.gk[...] = got[:, HD : 2 * HD]

    for i, (buf, dst) in enumerate(((R.wdn_b, R.gdn), (R.wup_b, R.gup))):
        for k in range(1, nd):
            plane_out[i * (nd - 1) + k - 1].wait_recv()
        rows = pl.ds(times(p, rows_d), rows_d)
        for x in range(local):
            got = buf[rows, pl.ds(times(c * local + x, DH), DH)].astype(F32)
            for k in range(1, nd):
                got = got + R.eg_r[k - 1, i, :, x * DH : (x + 1) * DH].astype(F32)
            dst[x] = got

    gather_end(R.cotb, R.cot_ss)
    gather_end(R.hidb, R.hid_ss)
    for cp in masks + ra_out + rv_out + rq_out + plane_out:
        cp.wait_send()
    for k in range(1, nz):
        o = line(k)
        sent(R.gh_s.at[o], R.gh_ss.at[o])
        sent(R.glog_s.at[o], R.gl_ss.at[o])
        sent(R.out_s.at[o], R.out_ss.at[o])
        sent(R.gz_s, R.gz_ss.at[o])
        for part, lanes in enumerate((PO, PV, PQ, PS)):
            sent(R.pb.at[pl.ds(times(o, S), S), lanes], R.p_ss.at[part, o])


def settle_kernel(*refs):
    n = len(refs) // 2
    for src, dst in zip(refs[:n], refs[n:]):
        dst[...] = src[...]


def fused_layer(nd, nz, *args):
    (tokens, cotangent, seq_lengths, routes, head_experts, norm_gain) = args[:6]
    (w_query, w_key, w_value, w_output, w_value_gate, w_output_gate, w_router) = args[6:13]
    w_up, w_down = args[13:]
    C = tokens.shape[0]
    local = w_up.shape[0]
    experts = w_router.shape[1]
    own_e = 2 * local
    pad_e = -(-own_e // 16) * 16
    EF, HF, HD = own_e * DH, local * DH, H * DH
    EV = EA * HD
    S = D // (nd * nz * 2)
    SL = S * nz
    PW = 2 * EV + 2 * HD + LANES
    s = Scratch()
    s.vmem("wqk_b", (D, 2 * HD), BF16)
    s.vmem("wv_b", (D, EV), BF16)
    s.vmem("wo_b", (D, EV), BF16)
    s.vmem("wup_b", (D, EF), BF16)
    s.vmem("wdn_b", (D, EF), BF16)
    s.vmem("wg_b", (D, LANES), BF16)
    s.vmem("wrl_b", (D, LANES), BF16)
    s.vmem("cotb", (nz * C, D), BF16)
    s.vmem("hidb", (nz * C, D), BF16)
    s.vmem("mask_s", (nz, pad_e, C), BF16)
    s.vmem("maskb", (nz, pad_e, C), BF16)
    s.vmem("std_b", (C, D), F32)
    s.vmem("normed_b", (C, D), BF16)
    s.vmem("q_b", (C, HD), BF16)
    s.vmem("k_b", (C, HD), BF16)
    s.vmem("v_b", (C, HD), BF16)
    s.vmem("gate_b", (C, LANES), F32)
    s.vmem("val_b", (C, EV), F32)
    s.vmem("prob_b", (H, C, C), F32)
    s.vmem("att_b", (C, HD), F32)
    s.vmem("mix_b", (C, EV), BF16)
    s.vmem("hid_f", (C, D), F32)
    s.vmem("lt", (D, 4 * LANES), BF16)
    s.vmem("ltr", (2 * nd, SL, 4 * LANES), BF16)
    s.vmem("ra", (2 * nd * C, HD + LANES), BF16)
    s.vmem("rb", (2 * nd * C, 3 * HD + LANES), BF16)
    s.vmem("gact", (nz * C, EF), BF16)
    s.vmem("gra", (nz * C, EF), BF16)
    for name in ("gh_s", "gh_r", "out_s", "out_r"):
        s.vmem(name, (nz, C, D), BF16)
    for name in ("glog_s", "glog_r"):
        s.vmem(name, (nz, pad_e, C), BF16)
    s.vmem("pair_r", (2, D, HF), BF16)
    s.vmem("eg_r", (nd - 1, 2, D // nd, HF), BF16)
    s.vmem("ghid_f", (C, D), F32)
    s.vmem("ghid_b", (C, D), BF16)
    s.vmem("gatt_b", (C, HD), BF16)
    s.vmem("gval_f", (C, HD), F32)
    s.vmem("small_b", (C, LANES), BF16)
    s.vmem("pb", (SL, PW), BF16)
    s.vmem("pr", (nz, S, PW), BF16)
    s.vmem("gp", (2 * nd, D // LANES, LANES), F32)
    s.vmem("gz_s", (D // LANES, LANES), F32)
    s.vmem("gz", (nz, D // LANES, LANES), F32)
    s.sems("ld", 4 + 2 * local)
    for name in ("cot_ss", "hid_ss"):
        s.sems(name, 2, nz)
    for name in ("cot_rs", "hid_rs", "mask_ss", "mask_rs", "gh_ss", "gh_rs", "gl_ss", "gl_rs", "out_ss", "out_rs", "gz_ss", "gz_rs"):
        s.sems(name, nz)
    for name in "w_ss w_rs pair_ss pair_rs".split():
        s.sems(name, 2)
    for name in ("lt_ss", "lt_rs", "ltl_ss", "ltl_rs", "gp_ss", "gp_rs", "ra_ss", "ra_rs", "rv_ss", "rv_rs", "rq_ss", "rq_rs"):
        s.sems(name, 2 * nd)
    for name in ("eg_ss", "eg_rs"):
        s.sems(name, nd - 1, 2)
    for name in ("p_ss", "p_rs"):
        s.sems(name, 4, nz)

    def out(*shape, dtype=F32):
        return jax.ShapeDtypeStruct(shape, dtype)

    vmem = pl.BlockSpec(memory_space=pltpu.VMEM)
    smem = pl.BlockSpec(memory_space=pltpu.SMEM)
    hbm = pl.BlockSpec(memory_space=pl.ANY)
    outs = pl.pallas_call(
        functools.partial(layer_kernel, INPUTS + OUTPUTS + tuple(s.names), nd, nz, local),
        out_shape=(
            out(C, D, dtype=BF16),
            out(C, D),
            out(1, S),
            out(S, HD),
            out(S, HD),
            out(S, EV),
            out(S, EV),
            out(EA * H, S),
            out(EA * H, S),
            out(experts, S),
            out(local, D // nd, DH),
            out(local, D // nd, DH),
        ),
        in_specs=[vmem, vmem, smem] + [vmem] * 6 + [hbm] * 6,
        out_specs=[vmem] * 12,
        scratch_shapes=s.shapes,
        compiler_params=pltpu.CompilerParams(
            collective_id=0, has_side_effects=True, vmem_limit_bytes=VMEM_LIMIT
        ),
    )(
        tokens,
        cotangent,
        seq_lengths,
        routes.T,
        head_experts.reshape(C, 2 * H).T,
        norm_gain.reshape(1, D),
        w_value_gate.T,
        w_output_gate.T,
        w_router.T,
        w_query,
        w_key,
        w_value,
        w_output,
        w_up,
        w_down,
    )
    outs = list(
        pl.pallas_call(
            settle_kernel,
            out_shape=[out(*x.shape, dtype=x.dtype) for x in outs],
            in_specs=[vmem] * 12,
            out_specs=[vmem] * 12,
            compiler_params=pltpu.CompilerParams(vmem_limit_bytes=VMEM_LIMIT),
        )(*outs)
    )
    outs[2] = outs[2].reshape(S)
    for i in (7, 8, 9):
        outs[i] = outs[i].T
    return tuple(outs)


VMEM_LIMIT = 62 * 1024 * 1024


def fits(nd, nz, count, experts):
    own_e = experts // nz
    pad_e = -(-own_e // 16) * 16
    return (
        count == LANES
        and nz * count <= 512
        and own_e % 4 == 0
        and D % (nd * nz * 2 * 16) == 0
        and LANES % (D // (nd * nz * 2)) == 0
        and 2 * EA * H + nz * pad_e <= LANES
    )


def per_device(nd, ne, *args):
    count, experts = args[0].shape[0], args[12].shape[1]
    if ne % 2 == 0 and fits(nd, ne // 2, count, experts):
        return fused_layer(nd, ne // 2, *args)
    return routed_layer(*args)


def solution(mesh):
    return jax.shard_map(
        functools.partial(per_device, mesh.shape["dp"], mesh.shape["expert"]),
        mesh=mesh,
        in_specs=(
            P(("dp", "expert"), None),
            P(("dp", "expert"), None),
            P(("dp", "expert"), None),
            P(("dp", "expert"), None),
            P(("dp", "expert"), None, None),
            P(),
            P(),
            P(),
            P(),
            P(),
            P(),
            P(),
            P(),
            P("expert", None, None),
            P("expert", None, None),
        ),
        out_specs=(
            P(("dp", "expert"), None),
            P(("dp", "expert"), None),
            P(("dp", "expert")),
            P(("dp", "expert"), None),
            P(("dp", "expert"), None),
            P(("dp", "expert"), None),
            P(("dp", "expert"), None),
            P(("dp", "expert"), None),
            P(("dp", "expert"), None),
            P(("dp", "expert"), None),
            P("expert", "dp", None),
            P("expert", "dp", None),
        ),
        check_vma=False,
    )
```

```python
import functools
import math

import jax
import jax.numpy as jnp
from jax import lax
from jax.experimental import pallas as pl
from jax.experimental.pallas import tpu as pltpu
from jax.sharding import PartitionSpec as P

D = 1024
H = 4
DH = 128
EA = 5
TOPK = 16


norm_eps = 1e-05
rope_base = 10000.0
masked_score = -1e30


def sequence_layout(lengths, count):
    bounds = jnp.cumsum(lengths)
    starts = bounds - lengths
    places = jnp.arange(count, dtype=jnp.int32)
    seq_ids = jnp.sum((places[:, None] >= bounds[None, :]).astype(jnp.int32), axis=1)
    live = places < bounds[-1]
    slot_ids = jnp.arange(lengths.shape[0], dtype=jnp.int32)
    first = jnp.sum(jnp.where(seq_ids[:, None] == slot_ids[None, :], starts[None, :], 0), axis=1)
    positions = jnp.where(live, places - first, 0)
    return (seq_ids, live, positions)


def rope_tables(positions, width):
    half = width // 2
    freq = rope_base ** (-(jnp.arange(half, dtype=jnp.float32) * 2.0 / width))
    angles = positions.astype(jnp.float32)[:, None] * freq[None, :]
    return (jnp.cos(angles), jnp.sin(angles))


def rotate(field, cosine, sine):
    half = field.shape[-1] // 2
    first, second = (field[..., :half], field[..., half:])
    cos_h, sin_h = (cosine[:, None, :], sine[:, None, :])
    return jnp.concatenate(
        [first * cos_h - second * sin_h, second * cos_h + first * sin_h], axis=-1
    )


def rotate_back(field, cosine, sine):
    half = field.shape[-1] // 2
    first, second = (field[..., :half], field[..., half:])
    cos_h, sin_h = (cosine[:, None, :], sine[:, None, :])
    return jnp.concatenate(
        [first * cos_h + second * sin_h, second * cos_h - first * sin_h], axis=-1
    )


def slot_tables(routes, experts, most):
    count = routes.shape[0] * routes.shape[1]
    flat = routes.reshape(count)
    order = jnp.argsort(flat, stable=True)
    ordered = flat[order]
    firsts = jnp.searchsorted(ordered, jnp.arange(experts, dtype=jnp.int32))
    ranks = jnp.arange(count, dtype=jnp.int32) - firsts[ordered]
    sorted_slots = ordered * most + ranks
    slot_of_row = jnp.zeros((count,), jnp.int32).at[order].set(sorted_slots)
    row_of_slot = jnp.full((experts * most,), count, jnp.int32).at[sorted_slots].set(order)
    return (slot_of_row, row_of_slot)


def routed_layer(
    tokens,
    cotangent,
    seq_lengths,
    routes,
    head_experts,
    norm_gain,
    w_query,
    w_key,
    w_value,
    w_output,
    w_value_gate,
    w_output_gate,
    w_router,
    w_up,
    w_down,
):
    f32 = jnp.float32
    bf16 = jnp.bfloat16
    count = tokens.shape[0]
    experts = w_router.shape[1]
    local_experts = w_up.shape[0]
    owners = lax.axis_size("expert")
    most = 3 * count * TOPK // (2 * experts)
    routed = count * TOPK
    block = min(512, count)
    block_starts = jnp.arange(count // block, dtype=jnp.int32) * block
    scale = DH ** (-0.5)
    contract_last = (((1,), (1,)), ((), ()))
    contract_first = (((0,), (0,)), ((), ()))
    seq_ids, live, positions = sequence_layout(seq_lengths[0], count)
    cosine, sine = rope_tables(positions, DH)
    inputs = tokens.astype(f32)
    centred = inputs - jnp.mean(inputs, axis=-1, keepdims=True)
    inverse = lax.rsqrt(jnp.mean(centred * centred, axis=-1, keepdims=True) + norm_eps)
    standard = centred * inverse
    normed = (standard * norm_gain).astype(bf16)
    query_proj = jnp.dot(normed, w_query, preferred_element_type=f32).reshape(count, H, DH)
    key_proj = jnp.dot(normed, w_key, preferred_element_type=f32).reshape(count, H, DH)
    query_rot = (rotate(query_proj, cosine, sine) * scale).astype(bf16)
    key_rot = rotate(key_proj, cosine, sine).astype(bf16)
    chosen = jnp.any(
        head_experts[:, None, :, :] == jnp.arange(EA, dtype=jnp.int32)[None, :, None, None], axis=-1
    )
    value_gates = jnp.where(
        chosen,
        jax.nn.sigmoid(
            jnp.dot(tokens, w_value_gate, preferred_element_type=f32).reshape(count, EA, H)
        ),
        0.0,
    )
    output_gates = jnp.where(
        chosen,
        jax.nn.sigmoid(
            jnp.dot(tokens, w_output_gate, preferred_element_type=f32).reshape(count, EA, H)
        ),
        0.0,
    )
    value_all = jnp.dot(tokens, w_value, preferred_element_type=f32).reshape(count, EA, H, DH)
    values = jnp.sum(value_gates[..., None] * value_all, axis=1).astype(bf16)

    def allowed_at(start):
        queries = start + jnp.arange(block, dtype=jnp.int32)
        keys = jnp.arange(count, dtype=jnp.int32)
        same = (
            (seq_ids[:, None] == seq_ids[None, :])
            & (keys[None, :] <= queries[:, None])
            & live[None, :]
        )
        return same | (keys[None, :] == queries[:, None])

    def scores_at(start):
        scores = jnp.einsum("qhd,khd->hqk", query_rot, key_rot, preferred_element_type=f32)
        return (query_rot, jnp.where(allowed_at(start)[None], scores, masked_score))

    def attend(start):
        query_block, scores = scores_at(start)
        highest = jnp.max(scores, axis=-1, keepdims=True)
        shifted = jnp.exp(scores - highest)
        totals = jnp.sum(shifted, axis=-1, keepdims=True)
        shares = (shifted / totals).astype(bf16)
        result = jnp.einsum("hqk,khd->qhd", shares, values, preferred_element_type=f32)
        return (result, (highest + jnp.log(totals))[..., 0])

    attended, log_totals = lax.map(attend, block_starts)
    attended = attended.reshape(count, H, DH)
    log_totals = jnp.transpose(log_totals, (1, 0, 2)).reshape(H, count)
    heads_mixed = (
        (output_gates[..., None] * attended[:, None]).astype(bf16).reshape(count, EA * H * DH)
    )
    hidden = inputs + lax.dot_general(
        heads_mixed, w_output, contract_last, preferred_element_type=f32
    )
    hidden_low = hidden.astype(bf16)
    logits = jnp.dot(hidden_low, w_router, preferred_element_type=f32)
    gates = jax.nn.sigmoid(jnp.take_along_axis(logits, routes, axis=1))
    slot_of_row, row_of_slot = slot_tables(routes, experts, most)
    valid = row_of_slot < routed
    safe_row = jnp.minimum(row_of_slot, routed - 1)
    source = safe_row // TOPK
    outgoing = jnp.where(valid[:, None], hidden_low[source], jnp.zeros((), bf16)).reshape(
        owners, local_experts, most, D
    )

    def expert_apply(items):
        raised = jnp.einsum("nemd,edf->nemf", items, w_up, preferred_element_type=f32)
        active = jax.nn.silu(raised).astype(bf16)
        lowered = jnp.einsum("nemf,edf->nemd", active, w_down, preferred_element_type=f32).astype(
            bf16
        )
        return (lowered, raised)

    lowered, raised = expert_apply(
        lax.all_to_all(outgoing, "expert", split_axis=0, concat_axis=0, tiled=True)
    )
    returned = lax.all_to_all(lowered, "expert", split_axis=0, concat_axis=0, tiled=True).reshape(
        experts * most, D
    )
    expert_rows = returned[slot_of_row].reshape(count, TOPK, D)
    output = hidden + jnp.sum(gates[..., None] * expert_rows, axis=1)
    mixed = output.astype(bf16)
    grad_out = cotangent.astype(f32) * live[:, None].astype(f32)
    grad_gates = jnp.sum(grad_out[:, None, :] * expert_rows, axis=2)
    gate_flat = gates.reshape(routed)
    grad_outgoing = (
        jnp.where(valid[:, None], gate_flat[safe_row][:, None] * grad_out[source], 0.0)
        .astype(bf16)
        .reshape(owners, local_experts, most, D)
    )
    grad_lowered = lax.all_to_all(grad_outgoing, "expert", split_axis=0, concat_axis=0, tiled=True)
    items = lax.all_to_all(outgoing, "expert", split_axis=0, concat_axis=0, tiled=True)
    raised = expert_apply(items)[1]
    grad_active = jnp.einsum("nemd,edf->nemf", grad_lowered, w_down, preferred_element_type=f32)
    sigmoid_raised = jax.nn.sigmoid(raised)
    grad_raised = (grad_active * sigmoid_raised * (1.0 + raised * (1.0 - sigmoid_raised))).astype(
        bf16
    )
    grad_items = jnp.einsum("nemf,edf->nemd", grad_raised, w_up, preferred_element_type=f32).astype(
        bf16
    )
    active = jax.nn.silu(raised).astype(bf16)
    grad_items, grad_raised, active = (grad_items, grad_raised, active)
    grad_items, grad_raised, active, grad_arrived, arrived = (
        grad_items,
        grad_raised,
        active,
        grad_lowered,
        items,
    )
    grad_up_local = jnp.einsum("nemd,nemf->edf", arrived, grad_raised, preferred_element_type=f32)
    grad_down_local = jnp.einsum("nemd,nemf->edf", grad_arrived, active, preferred_element_type=f32)
    grad_up, grad_down = (
        lax.psum_scatter(
            grad_up_local.astype(jnp.bfloat16), "dp", scatter_dimension=1, tiled=True
        ).astype(jnp.float32),
        lax.psum_scatter(
            grad_down_local.astype(jnp.bfloat16), "dp", scatter_dimension=1, tiled=True
        ).astype(jnp.float32),
    )
    grad_back = lax.all_to_all(
        grad_items, "expert", split_axis=0, concat_axis=0, tiled=True
    ).reshape(experts * most, D)
    grad_hidden = grad_out + jnp.sum(
        grad_back[slot_of_row].reshape(count, TOPK, D), axis=1, dtype=f32
    )
    grad_picked = grad_gates * gates * (1.0 - gates)
    expert_ids = jnp.arange(experts, dtype=jnp.int32)
    grad_logits = jnp.sum(
        jnp.where(routes[:, :, None] == expert_ids[None, None, :], grad_picked[..., None], 0.0),
        axis=1,
    ).astype(bf16)
    grad_router = lax.dot_general(
        hidden_low, grad_logits, contract_first, preferred_element_type=f32
    )
    grad_hidden = grad_hidden + lax.dot_general(
        grad_logits, w_router, contract_last, preferred_element_type=f32
    )
    grad_hidden_low = grad_hidden.astype(bf16)
    grad_output = lax.dot_general(
        grad_hidden_low, heads_mixed, contract_first, preferred_element_type=f32
    )
    grad_mixed = jnp.dot(grad_hidden_low, w_output, preferred_element_type=f32).reshape(
        count, EA, H, DH
    )
    grad_attended = jnp.sum(output_gates[..., None] * grad_mixed, axis=1).astype(bf16)
    grad_out_gates = jnp.sum(grad_mixed * attended[:, None], axis=-1)
    grad_out_logits = (
        jnp.where(chosen, grad_out_gates * output_gates * (1.0 - output_gates), 0.0)
        .astype(bf16)
        .reshape(count, EA * H)
    )

    def attend_back(carry, start):
        grad_keys, grad_vals = carry
        query_block, scores = scores_at(start)
        shares = jnp.exp(scores - log_totals[..., None])
        grad_shares = jnp.einsum("qhd,khd->hqk", grad_attended, values, preferred_element_type=f32)
        centre = jnp.sum(shares * grad_shares, axis=-1, keepdims=True)
        grad_scores = (shares * (grad_shares - centre)).astype(bf16)
        grad_query_block = jnp.einsum(
            "hqk,khd->qhd", grad_scores, key_rot, preferred_element_type=f32
        )
        grad_keys = grad_keys + jnp.einsum(
            "hqk,qhd->khd", grad_scores, query_block, preferred_element_type=f32
        )
        grad_vals = grad_vals + jnp.einsum(
            "hqk,qhd->khd", shares.astype(bf16), grad_attended, preferred_element_type=f32
        )
        return ((grad_keys, grad_vals), grad_query_block)

    zero_heads = jnp.zeros((count, H, DH), f32)
    (grad_keys, grad_vals), grad_queries = lax.scan(
        attend_back, (zero_heads, zero_heads), block_starts
    )
    grad_queries = grad_queries.reshape(count, H, DH)
    grad_query_proj = (
        rotate_back(grad_queries * scale, cosine, sine).astype(bf16).reshape(count, H * DH)
    )
    grad_key_proj = rotate_back(grad_keys, cosine, sine).astype(bf16).reshape(count, H * DH)
    grad_value_all = (
        (value_gates[..., None] * grad_vals[:, None]).astype(bf16).reshape(count, EA * H * DH)
    )
    grad_value_gates = jnp.sum(grad_vals[:, None] * value_all, axis=-1)
    grad_value_logits = (
        jnp.where(chosen, grad_value_gates * value_gates * (1.0 - value_gates), 0.0)
        .astype(bf16)
        .reshape(count, EA * H)
    )
    grad_query = lax.dot_general(
        normed, grad_query_proj, contract_first, preferred_element_type=f32
    )
    grad_key = lax.dot_general(normed, grad_key_proj, contract_first, preferred_element_type=f32)
    grad_value = lax.dot_general(tokens, grad_value_all, contract_first, preferred_element_type=f32)
    grad_value_gate = lax.dot_general(
        tokens, grad_value_logits, contract_first, preferred_element_type=f32
    )
    grad_output_gate = lax.dot_general(
        tokens, grad_out_logits, contract_first, preferred_element_type=f32
    )
    grad_normed = lax.dot_general(
        grad_query_proj, w_query, contract_last, preferred_element_type=f32
    ) + lax.dot_general(grad_key_proj, w_key, contract_last, preferred_element_type=f32)
    grad_gain = jnp.sum(grad_normed * standard, axis=0)
    grad_standard = grad_normed * norm_gain
    grad_tokens = grad_hidden + inverse * (
        grad_standard
        - jnp.mean(grad_standard, axis=-1, keepdims=True)
        - standard * jnp.mean(grad_standard * standard, axis=-1, keepdims=True)
    )
    grad_tokens = (
        grad_tokens
        + lax.dot_general(grad_value_all, w_value, contract_last, preferred_element_type=f32)
        + lax.dot_general(
            grad_value_logits, w_value_gate, contract_last, preferred_element_type=f32
        )
        + lax.dot_general(grad_out_logits, w_output_gate, contract_last, preferred_element_type=f32)
    )
    summed = (
        lax.psum_scatter(grad_gain, ("dp", "expert"), scatter_dimension=0, tiled=True),
        lax.psum_scatter(grad_query, ("dp", "expert"), scatter_dimension=0, tiled=True),
        lax.psum_scatter(grad_key, ("dp", "expert"), scatter_dimension=0, tiled=True),
        lax.psum_scatter(grad_value, ("dp", "expert"), scatter_dimension=0, tiled=True),
        lax.psum_scatter(grad_output, ("dp", "expert"), scatter_dimension=0, tiled=True),
        lax.psum_scatter(grad_value_gate, ("dp", "expert"), scatter_dimension=0, tiled=True),
        lax.psum_scatter(grad_output_gate, ("dp", "expert"), scatter_dimension=0, tiled=True),
        lax.psum_scatter(grad_router, ("dp", "expert"), scatter_dimension=0, tiled=True),
    )
    return (
        mixed,
        grad_tokens,
        summed[0],
        summed[1],
        summed[2],
        summed[3],
        summed[4],
        summed[5],
        summed[6],
        summed[7],
        grad_up,
        grad_down,
    )


F32 = jnp.float32
BF16 = jnp.bfloat16
MESH = pl.DeviceIdType.MESH
LANES = 128


def mm(a, b):
    return lax.dot_general(a, b, (((1,), (0,)), ((), ())), preferred_element_type=F32)


def mm_t(a, b):
    return lax.dot_general(a, b, (((1,), (1,)), ((), ())), preferred_element_type=F32)


def tmm(a, b):
    return lax.dot_general(a, b, (((0,), (0,)), ((), ())), preferred_element_type=F32)


def iota(shape, axis):
    return lax.broadcasted_iota(jnp.int32, shape, axis)


def column(x, j, width=LANES):
    return jnp.broadcast_to(x[:, j : j + 1], (x.shape[0], width))


def sigmoid(x):
    return 1.0 / (1.0 + jnp.exp(-x))


class Scratch:
    def __init__(self):
        self.names, self.shapes = [], []

    def add(self, name, shape):
        self.names.append(name)
        self.shapes.append(shape)

    def vmem(self, name, shape, dtype):
        self.add(name, pltpu.VMEM(shape, dtype))

    def sems(self, name, *shape):
        self.add(name, pltpu.SemaphoreType.DMA(shape))


INPUTS = ("tokens", "cot", "lens", "rt", "het", "gain", "wvg", "wog", "wr", "wq", "wk", "wv", "wo", "wu", "wd")
OUTPUTS = ("mixed", "gtok", "ggain", "gq", "gk", "gv", "go", "gvg", "gog", "gr", "gup", "gdn")


def layer_kernel(names, nd, nz, local, *refs):
    r = dict(zip(names, refs))
    R = type("R", (), r)
    C = R.tokens.shape[0]
    own_e = 2 * local
    pad_e = R.maskb.shape[1]
    EF = own_e * DH
    HF = local * DH
    HD = H * DH
    EV = EA * HD
    S = D // (nd * nz * 2)
    SL = S * nz
    GATE = EA * H
    p = lax.axis_index("dp")
    e = lax.axis_index("expert")
    z = e // 2
    c = e % 2
    sib = 1 - c

    def dev(p_, z_, c_):
        return (p_, z_ * 2 + c_)

    def times(i, n):
        return pl.multiple_of(i * n, n)

    def remote(src, dst, ss, rs, to):
        return pltpu.make_async_remote_copy(
            src_ref=src, dst_ref=dst, send_sem=ss, recv_sem=rs, device_id=to, device_id_type=MESH
        )

    def arrived(dst, rs):
        remote(dst, dst, rs, rs, dev(p, z, sib)).wait_recv()

    def sent(src, ss):
        remote(src, src, ss, ss, dev(p, z, sib)).wait_send()

    beside = p + 1 - 2 * lax.rem(p, 2)
    across = lax.rem(p + 2, nd)
    diagonal = lax.rem(beside + 2, nd)

    def plane(k):
        return (p, beside, across, diagonal)[k]

    def line(k):
        return lax.rem(z + k, nz)

    loads = {}

    def load(name, src, dst, sem):
        cp = pltpu.make_async_copy(src, dst, sem)
        cp.start()
        loads.setdefault(name, []).append(cp)

    def loaded(name):
        for cp in loads.pop(name):
            cp.wait()

    load("qk", R.wq, R.wqk_b.at[:, 0:HD], R.ld.at[0])
    load("qk", R.wk, R.wqk_b.at[:, HD : 2 * HD], R.ld.at[1])
    load("v", R.wv, R.wv_b, R.ld.at[2])
    for i in range(local):
        col = times(c * local + i, DH)
        load("up", R.wu.at[i], R.wup_b.at[:, pl.ds(col, DH)], R.ld.at[4 + i])
        load("dn", R.wd.at[i], R.wdn_b.at[:, pl.ds(col, DH)], R.ld.at[4 + local + i])
    load("o", R.wo, R.wo_b, R.ld.at[3])

    barrier = pltpu.get_barrier_semaphore()
    partners = [dev(p, z, sib)]
    partners += [dev(p, line(k), c) for k in range(1, nz)]
    for k in range(1, nd):
        partners += [dev(plane(k), z, c), dev(plane(k), z, sib)]
    for to in partners:
        pl.semaphore_signal(barrier, inc=1, device_id=to, device_id_type=MESH)

    l0 = R.lens[0, 0]
    b1 = l0 + R.lens[0, 1]
    row = iota((C, LANES), 0)
    lane = iota((C, LANES), 1)
    seq_r = (row >= l0).astype(jnp.int32) + (row >= b1).astype(jnp.int32)
    seq_c = (lane >= l0).astype(jnp.int32) + (lane >= b1).astype(jnp.int32)
    live = row < b1
    allowed = ((seq_r == seq_c) & (lane <= row) & (lane < b1)) | (row == lane)
    live_f = jnp.where(live, 1.0, 0.0).astype(F32)
    start = jnp.where(seq_r == 0, 0, l0)
    position = jnp.where(live, row - start, 0).astype(F32)

    for b in range(D // LANES):
        cols = slice(b * LANES, (b + 1) * LANES)
        R.cotb[pl.ds(times(z, C), C), cols] = (R.cot[:, cols].astype(F32) * live_f).astype(BF16)
    ids = iota((pad_e, C), 0)
    for zz in range(nz):
        named = jnp.zeros((pad_e, C), F32)
        for k in range(TOPK):
            hit = jnp.broadcast_to(R.rt[k : k + 1, :], (pad_e, C)) == ids + zz * own_e
            named = jnp.where(hit & (ids < own_e), 1.0, named)
        R.mask_s[zz] = named.astype(BF16)
    R.maskb[z] = R.mask_s[z]

    pl.semaphore_wait(barrier, len(partners))

    def block(buf, o):
        return buf.at[pl.ds(times(o, C), C), :]

    def pass_on(buf, ss, rs, o, right, left):
        @pl.when(right)
        def _():
            remote(block(buf, o), block(buf, o), ss.at[0, o], rs.at[o], dev(p, z + 1, c)).start()

        @pl.when(left)
        def _():
            remote(block(buf, o), block(buf, o), ss.at[1, o], rs.at[o], dev(p, z - 1, c)).start()

    def passed(buf, ss, o, right, left):
        @pl.when(right)
        def _():
            sent(block(buf, o), ss.at[0, o])

        @pl.when(left)
        def _():
            sent(block(buf, o), ss.at[1, o])

    def gather_own(buf, ss, rs):
        pass_on(buf, ss, rs, z, z < nz - 1, z > 0)

    def gather_on(buf, ss, rs, o):
        arrived(block(buf, o), rs.at[o])
        pass_on(buf, ss, rs, o, (o < z) & (z < nz - 1), (o > z) & (z > 0))

    def gather_step(buf, ss, rs, k):
        @pl.when(z >= k)
        def _():
            gather_on(buf, ss, rs, z - k)

        @pl.when(z + k < nz)
        def _():
            gather_on(buf, ss, rs, z + k)

    def gather_end(buf, ss):
        passed(buf, ss, z, z < nz - 1, z > 0)
        for k in range(1, nz):

            @pl.when(z >= k)
            def _():
                passed(buf, ss, z - k, z < nz - 1, False)

            @pl.when(z + k < nz)
            def _():
                passed(buf, ss, z + k, False, z > 0)

    gather_own(R.cotb, R.cot_ss, R.cot_rs)
    masks = []
    for k in range(1, nz):
        o = line(k)
        cp = remote(R.mask_s.at[o], R.maskb.at[z], R.mask_ss.at[k], R.mask_rs.at[z], dev(p, o, c))
        cp.start()
        masks.append(cp)

    s_row, s_col = iota((GATE, LANES), 0), iota((GATE, LANES), 1)
    to_v = jnp.where(s_row == s_col, 1.0, 0.0).astype(BF16)
    to_o = jnp.where(s_row + GATE == s_col, 1.0, 0.0).astype(BF16)
    R.wg_b[...] = (tmm(R.wvg[...], to_v) + tmm(R.wog[...], to_o)).astype(BF16)
    experts = R.wr.shape[0]
    r_row, r_col = iota((experts, LANES), 0), iota((experts, LANES), 1)
    to_r = jnp.where((r_row == r_col + z * own_e) & (r_col < own_e), 1.0, 0.0).astype(BF16)
    R.wrl_b[...] = tmm(R.wr[...], to_r).astype(BF16)

    half = lax.rem(lane, DH // 2).astype(F32)
    angle = position * jnp.exp(half * (-2.0 / DH * math.log(rope_base)))
    cosine = jnp.cos(angle)
    sine = jnp.where(lane < DH // 2, -jnp.sin(angle), jnp.sin(angle))

    def rot(v):
        return v * cosine + pltpu.roll(v, DH // 2, 1) * sine

    def rot_back(v):
        return v * cosine - pltpu.roll(v, DH // 2, 1) * sine

    inputs = R.tokens[...].astype(F32)
    centred = inputs - jnp.mean(inputs, axis=-1, keepdims=True)
    inverse = lax.rsqrt(jnp.mean(centred * centred, axis=-1, keepdims=True) + norm_eps)
    standard = centred * inverse
    R.std_b[...] = standard
    R.normed_b[...] = (standard * R.gain[...]).astype(BF16)

    loaded("qk")
    scale = DH ** (-0.5)
    qk = mm(R.normed_b[...], R.wqk_b[:, 0:HD])
    for h in range(H):
        hs = slice(h * DH, (h + 1) * DH)
        R.q_b[:, hs] = (rot(qk[:, hs]) * scale).astype(BF16)
    qk = mm(R.normed_b[...], R.wqk_b[:, HD : 2 * HD])
    for h in range(H):
        hs = slice(h * DH, (h + 1) * DH)
        R.k_b[:, hs] = rot(qk[:, hs]).astype(BF16)

    hit = []
    for j in range(GATE):
        x, h = divmod(j, H)
        one = (R.het[2 * h : 2 * h + 1, :] == x) | (R.het[2 * h + 1 : 2 * h + 2, :] == x)
        hit.append(jnp.where(one, 1.0, 0.0).astype(F32))
    hit = jnp.concatenate(hit + hit + [jnp.zeros((LANES - 2 * GATE, C), F32)], axis=0)
    R.gate_b[...] = sigmoid(mm(R.tokens[...], R.wg_b[...])) * hit.T

    loaded("up")
    loaded("dn")
    wx = []
    for i, buf in enumerate((R.wup_b, R.wdn_b)):
        part = buf.at[:, pl.ds(times(c, HF), HF)]
        cp = remote(part, part, R.w_ss.at[i], R.w_rs.at[i], dev(p, z, sib))
        cp.start()
        wx.append(cp)

    loaded("v")
    gates = R.gate_b[...]
    total = [None] * H
    for x in range(EA):
        R.val_b[:, x * HD : (x + 1) * HD] = mm(R.tokens[...], R.wv_b[:, x * HD : (x + 1) * HD])
        for h in range(H):
            lo = x * HD + h * DH
            term = column(gates, x * H + h) * R.val_b[:, lo : lo + DH]
            total[h] = term if x == 0 else total[h] + term
    for h in range(H):
        R.v_b[:, h * DH : (h + 1) * DH] = total[h].astype(BF16)

    for h in range(H):
        hs = slice(h * DH, (h + 1) * DH)
        scores = jnp.where(allowed, mm_t(R.q_b[:, hs], R.k_b[:, hs]), masked_score)
        shifted = jnp.exp(scores - jnp.max(scores, axis=-1, keepdims=True))
        shares = shifted / jnp.sum(shifted, axis=-1, keepdims=True)
        R.prob_b[h] = shares
        R.att_b[:, hs] = mm(shares.astype(BF16), R.v_b[:, hs])

    for x in range(EA):
        for h in range(H):
            lo = x * HD + h * DH
            R.mix_b[:, lo : lo + DH] = (
                column(gates, GATE + x * H + h) * R.att_b[:, h * DH : (h + 1) * DH]
            ).astype(BF16)
    loaded("o")
    half_d = D // 2
    for b in range(2):
        cols = slice(b * half_d, (b + 1) * half_d)
        hidden = R.tokens[:, cols].astype(F32) + mm_t(R.mix_b[...], R.wo_b[cols, :])
        R.hid_f[:, cols] = hidden
        R.hidb[pl.ds(times(z, C), C), cols] = hidden.astype(BF16)
    gather_own(R.hidb, R.hid_ss, R.hid_rs)
    gather_step(R.cotb, R.cot_ss, R.cot_rs, 1)

    def put_turned(x, w):
        for b in range(D // LANES):
            t = x[:, b * LANES : (b + 1) * LANES].astype(F32).T.astype(BF16)
            for q in range(LANES // S):
                i = (b * LANES) // S + q
                pp, zz, cc = i // (2 * nz), (i % (2 * nz)) // 2, i % 2
                at = (pp * 2 + cc) * SL + zz * S
                R.lt[at : at + S, w * LANES : (w + 1) * LANES] = t[q * S : (q + 1) * S, :]

    plane_all = [(k, dc) for k in range(nd) for dc in range(2) if k or dc]

    def side(dc):
        return sib if dc else c

    def send_turned(w0, w1, ss, rs):
        out = []
        lanes = slice(w0 * LANES, w1 * LANES)
        for k, dc in plane_all:
            to = plane(k)
            slot = 2 * k + dc
            at = times(to * 2 + side(dc), SL)
            cp = remote(
                R.lt.at[pl.ds(at, SL), lanes],
                R.ltr.at[slot, :, lanes],
                ss.at[slot],
                rs.at[slot],
                dev(to, z, side(dc)),
            )
            cp.start()
            out.append(cp)
        R.ltr[0, :, lanes] = R.lt[pl.ds(times(p * 2 + c, SL), SL), lanes]
        return out

    def rows_at(buf, lanes, slot):
        return buf.at[slot * C : (slot + 1) * C, lanes]

    def send_rows(buf, lanes, ss, rs):
        out = []
        for k in (1, 2):
            cp = remote(
                rows_at(buf, lanes, 0),
                rows_at(buf, lanes, 2 * k),
                ss.at[k],
                rs.at[2 * k],
                dev(plane(k), z, c),
            )
            cp.start()
            out.append(cp)
        return out + [hand_over(buf, lanes, ss, rs, 0)]

    def hand_over(buf, lanes, ss, rs, k):
        cp = remote(
            rows_at(buf, lanes, 2 * k),
            rows_at(buf, lanes, 2 * k + 1),
            ss.at[nd + k],
            rs.at[2 * k + 1],
            dev(p, z, sib),
        )
        cp.start()
        return cp

    def hand_near(buf, lanes, ss, rs, out, via):
        for k in (via, 3 - via):
            arrived(rows_at(buf, lanes, 2 * k), rs.at[2 * k])
            if k == via:
                cp = remote(
                    rows_at(buf, lanes, 2 * k),
                    rows_at(buf, lanes, 6),
                    ss.at[3],
                    rs.at[6],
                    dev(plane(3 - via), z, c),
                )
                cp.start()
                out.append(cp)
            out.append(hand_over(buf, lanes, ss, rs, k))

    def hand_far(buf, lanes, ss, rs, out):
        arrived(rows_at(buf, lanes, 6), rs.at[6])
        out.append(hand_over(buf, lanes, ss, rs, 3))

    def rows_here(buf, lanes, rs):
        for k in range(nd):
            arrived(rows_at(buf, lanes, 2 * k + 1), rs.at[2 * k + 1])

    put_turned(R.tokens[...], 0)
    put_turned(R.normed_b[...], 1)
    put_turned(R.hid_f[...], 2)
    turned = send_turned(0, 3, R.lt_ss, R.lt_rs)
    R.ra[0:C, 0:HD] = R.att_b[...].astype(BF16)
    R.ra[0:C, HD : HD + LANES] = gates.astype(BF16)
    RA = slice(0, HD + LANES)
    ra_out = send_rows(R.ra, RA, R.ra_ss, R.ra_rs)

    for k in range(2, nz - 1):
        gather_step(R.cotb, R.cot_ss, R.cot_rs, k)

    for cp in wx:
        cp.wait()

    least = jnp.minimum(z, nz - 1 - z)
    inner = least > 0
    left_half = z < nz // 2
    near = jnp.where(inner, jnp.where(left_half, 0, nz - 1), jnp.where(left_half, 1, nz - 2))
    fellow = jnp.where(left_half, nz // 2, nz // 2 - 1)
    far = jnp.where(left_half, nz - 1, 0)

    def origin(k):
        paired = k <= 2 * least
        dist = jnp.where(paired, (k + 1) // 2, k - least)
        left = jnp.where(paired, lax.rem(k, 2) == 1, z > nz - 1 - z)
        return jnp.where(k == 0, z, jnp.where(left, z - dist, z + dist))

    def expert_block(k, carry):
        o = origin(k)
        rows = pl.ds(times(o, C), C)

        @pl.when((k == 1) & inner)
        def _():
            gather_on(R.hidb, R.hid_ss, R.hid_rs, origin(1))

        @pl.when((k > 0) & (k + inner.astype(jnp.int32) < nz))
        def _():
            gather_on(R.hidb, R.hid_ss, R.hid_rs, origin(k + inner.astype(jnp.int32)))

        @pl.when(k > 0)
        def _():
            @pl.when((o == z - nz + 1) | (o == z + nz - 1))
            def _():
                arrived(block(R.cotb, o), R.cot_rs.at[o])

            arrived(R.maskb.at[o], R.mask_rs.at[o])

        hb = R.hidb[rows, :]
        cb = R.cotb[rows, :]
        named = R.maskb[o].astype(F32)
        named = jnp.concatenate([named, jnp.zeros((LANES - pad_e, C), F32)], axis=0).T
        g = sigmoid(mm(hb, R.wrl_b[...])) * named
        glog = jnp.zeros((C, LANES), F32)
        for q in range(2):
            cols = slice(q * HF, (q + 1) * HF)
            raised = mm(hb, R.wup_b[:, cols])
            back = mm(cb, R.wdn_b[:, cols])
            for i in range(local):
                j = q * local + i
                u = raised[:, i * DH : (i + 1) * DH]
                a = back[:, i * DH : (i + 1) * DH]
                gj = column(g, j)
                s = sigmoid(u)
                act = u * s
                lo = j * DH
                R.gact[rows, lo : lo + DH] = (gj * act).astype(BF16)
                R.gra[rows, lo : lo + DH] = (gj * a * (s * (1.0 + u * (1.0 - s)))).astype(BF16)
                gg = jnp.sum(a * act, axis=1, keepdims=True)
                glog = jnp.where(lane == j, jnp.broadcast_to(gg, (C, LANES)), glog)
        glog = glog * g * (1.0 - g)
        low = glog.astype(BF16)
        R.glog_s[o] = glog.T[0:pad_e, :].astype(BF16)
        for b in range(2):
            cols = slice(b * half_d, (b + 1) * half_d)
            gh = mm_t(R.gra[rows, :], R.wup_b[cols, :]) + mm_t(low, R.wrl_b[cols, :])
            R.gh_s[o, :, cols] = gh.astype(BF16)

        @pl.when(k > 0)
        def _():
            remote(
                R.glog_s.at[o], R.glog_r.at[z], R.gl_ss.at[o], R.gl_rs.at[z], dev(p, o, c)
            ).start()

        @pl.when((k > 0) & (least == 0) & (o != fellow))
        def _():
            send_back(o)

        @pl.when((k > 0) & (least == 0) & (o == fellow))
        def _():
            send_by(o, near, 0)

        @pl.when((k > 0) & inner & (o == far))
        def _():
            send_by(o, fellow, 1)

        return carry

    def send_back(o):
        remote(R.gh_s.at[o], R.gh_r.at[z], R.gh_ss.at[o], R.gh_rs.at[z], dev(p, o, c)).start()

    def send_by(o, by, slot):
        remote(
            R.gh_s.at[o], R.gh_x.at[slot], R.gh_ss.at[o], R.gx_rs.at[slot], dev(p, by, c)
        ).start()

    def relay_back(o, slot):
        arrived(R.gh_x.at[slot], R.gx_rs.at[slot])
        R.gh_s[o] = (R.gh_s[o].astype(F32) + R.gh_x[slot].astype(F32)).astype(BF16)
        send_back(o)

    lax.fori_loop(0, nz, expert_block, 0)

    pairs = {}

    def expert_grad(buf, left_of, right_of, whose):
        cols = pl.ds(times(whose, HF), HF)
        buf[:, cols] = tmm(left_of[...], right_of[:, cols]).astype(BF16)

    def to_fellow_core(i, buf):
        cp = remote(
            buf.at[:, pl.ds(times(sib, HF), HF)],
            R.pair_r.at[i],
            R.pair_ss.at[i],
            R.pair_rs.at[i],
            dev(p, z, sib),
        )
        cp.start()
        pairs[i] = cp

    own_cols = pl.ds(times(c, HF), HF)
    rows_d = D // nd
    plane_out = []

    def expert_grad_on(i, buf):
        pairs[i].wait()

        def pair_tile(t, carry):
            rows = pl.ds(times(t, 128), 128)
            buf[rows, own_cols] = (
                buf[rows, own_cols].astype(F32) + R.pair_r[i, rows, :].astype(F32)
            ).astype(BF16)
            return carry

        lax.fori_loop(0, D // 128, pair_tile, 0)
        part_on(i, buf, diagonal, beside if i == 0 else across, 1)

    def rows_of(at):
        return pl.ds(times(at, rows_d), rows_d)

    def part_on(i, buf, whose, to, slot):
        cp = remote(
            buf.at[rows_of(whose), own_cols],
            R.eg_r.at[slot, i],
            R.eg_ss.at[slot, i],
            R.eg_rs.at[slot, i],
            dev(to, z, c),
        )
        cp.start()
        plane_out.append(cp)

    def expert_grad_relay(i, buf):
        first, to = (beside, across) if i == 0 else (across, beside)
        part_on(i, buf, first, first, 0)
        arrived(R.eg_r.at[1, i], R.eg_rs.at[1, i])
        rows = rows_of(to)
        buf[rows, own_cols] = (
            buf[rows, own_cols].astype(F32) + R.eg_r[1, i].astype(F32)
        ).astype(BF16)
        part_on(i, buf, to, to, 2)

    def to_place(own, got, ss, rs, o):
        remote(own(o), got(z), ss.at[o], rs.at[z], dev(p, o, c)).start()

    def sum_out(own, got, ss, rs, via, via_sem):
        @pl.when(inner)
        def _():
            to_place(own, got, ss, rs, far)
            to_place(own, got, ss, rs, near)

        @pl.when(least == 0)
        def _():
            remote(own(fellow), via, ss.at[fellow], via_sem, dev(p, near, c)).start()
            to_place(own, got, ss, rs, far)
            to_place(own, got, ss, rs, near)

    def sum_on(own, got, ss, rs, via, via_sem):
        @pl.when(inner)
        def _():
            arrived(via, via_sem)
            own(fellow)[...] = (own(fellow)[...].astype(F32) + via[...].astype(F32)).astype(BF16)
            to_place(own, got, ss, rs, fellow)

    def sum_in(total, got, rs):
        def add(o):
            arrived(got(o), rs.at[o])
            total[...] += got(o)[...].astype(F32)

        add(near)
        add(fellow)

        @pl.when(least == 0)
        def _():
            add(far)

    def out_run(k, n):
        def hand(d, slot, to):
            if k > 1:
                arrived(R.out_r.at[d], R.out_rs.at[d])
                R.out_s[d] = (R.out_s[d].astype(F32) + R.out_r[d].astype(F32)).astype(BF16)
            remote(
                R.out_s.at[d], R.out_r.at[slot], R.out_ss.at[d], R.out_rs.at[slot], dev(p, to, c)
            ).start()

        @pl.when(z == k - 1)
        def _():
            hand(nz - 1 - n, nz - 1 - n, k)

        @pl.when(z == nz - k)
        def _():
            hand(n, nz if n == nz - k - 1 else n, nz - k - 1)

    def part_sum(i, lanes):
        return (
            lambda o: R.pb.at[pl.ds(times(o, S), S), lanes],
            lambda o: R.pr.at[o, :, lanes],
            R.p_ss.at[i],
            R.p_rs.at[i],
        )

    hand_near(R.ra, RA, R.ra_ss, R.ra_rs, ra_out, 2)
    expert_grad(R.wup_b, R.hidb, R.gra, sib)
    to_fellow_core(1, R.wup_b)
    expert_grad(R.wup_b, R.hidb, R.gra, c)

    def out_tile(t, carry):
        rows = pl.ds(times(t, 256), 256)
        got = mm_t(R.gact[...], R.wdn_b[rows, :]).astype(BF16)
        for o in range(nz):
            R.out_s[o, :, rows] = got[o * C : (o + 1) * C, :]
        return carry

    lax.fori_loop(0, D // 256, out_tile, 0)
    out_run(1, 0)
    expert_grad(R.wdn_b, R.cotb, R.gact, sib)
    to_fellow_core(0, R.wdn_b)

    @pl.when(inner)
    def _():
        relay_back(near, 1)
        relay_back(fellow, 0)

    expert_grad_on(1, R.wup_b)
    expert_grad(R.wdn_b, R.cotb, R.gact, c)
    expert_grad_on(0, R.wdn_b)
    hand_far(R.ra, RA, R.ra_ss, R.ra_rs, ra_out)

    out_run(1, 1)
    out_run(2, 0)

    R.ghid_f[...] = R.cotb[pl.ds(times(z, C), C), :].astype(F32) + R.gh_s[z].astype(F32)

    def add_back(o):
        arrived(R.gh_r.at[o], R.gh_rs.at[o])
        R.ghid_f[...] += R.gh_r[o].astype(F32)

    add_back(near)
    add_back(jnp.where(inner, fellow, far))

    for k in range(1, nz):
        o = line(k)
        arrived(R.glog_r.at[o], R.gl_rs.at[o])
    R.glog_r[z] = R.glog_s[z]
    R.ghid_b[...] = R.ghid_f[...].astype(BF16)
    put_turned(R.ghid_f[...], 3)
    turned_late = send_turned(3, 4, R.ltl_ss, R.ltl_rs)

    gates = R.gate_b[...]
    small = jnp.zeros((C, LANES), F32)
    gatt = [None] * H
    for x in range(EA):
        gmix = mm(R.ghid_b[...], R.wo_b[:, x * HD : (x + 1) * HD])
        for h in range(H):
            hs = slice(h * DH, (h + 1) * DH)
            j = GATE + x * H + h
            term = column(gates, j) * gmix[:, hs]
            gatt[h] = term if x == 0 else gatt[h] + term
            gg = jnp.sum(gmix[:, hs] * R.att_b[:, hs], axis=1, keepdims=True)
            small = jnp.where(lane == j, jnp.broadcast_to(gg, (C, LANES)), small)
    for h in range(H):
        hs = slice(h * DH, (h + 1) * DH)
        low = gatt[h].astype(BF16)
        R.gatt_b[:, hs] = low
        gval = tmm(R.prob_b[h].astype(BF16), low)
        R.gval_f[:, hs] = gval
        R.rb[0:C, hs] = gval.astype(BF16)
        for x in range(EA):
            lo = x * HD + h * DH
            j = x * H + h
            gg = jnp.sum(gval * R.val_b[:, lo : lo + DH], axis=1, keepdims=True)
            small = jnp.where(lane == j, jnp.broadcast_to(gg, (C, LANES)), small)
    small = small * gates * (1.0 - gates)
    glog = jnp.concatenate(
        [jnp.zeros((2 * GATE, C), F32)]
        + [R.glog_r[o].astype(F32) for o in range(nz)]
        + [jnp.zeros((LANES - 2 * GATE - nz * pad_e, C), F32)],
        axis=0,
    )
    R.small_b[...] = small.astype(BF16)
    R.rb[0:C, HD : HD + LANES] = (small + glog.T).astype(BF16)
    RV = slice(0, HD + LANES)
    rv_out = send_rows(R.rb, RV, R.rv_ss, R.rv_rs)

    q0 = HD + LANES
    for h in range(H):
        hs = slice(h * DH, (h + 1) * DH)
        low = R.gatt_b[:, hs]
        gsh = mm_t(low, R.v_b[:, hs])
        prob = R.prob_b[h]
        centre = jnp.sum(prob * gsh, axis=-1, keepdims=True)
        gs = (prob * (gsh - centre)).astype(BF16)
        R.rb[0:C, q0 + h * DH : q0 + (h + 1) * DH] = rot_back(
            mm(gs, R.k_b[:, hs]) * scale
        ).astype(BF16)
        R.rb[0:C, q0 + HD + h * DH : q0 + HD + (h + 1) * DH] = rot_back(
            tmm(gs, R.q_b[:, hs])
        ).astype(BF16)
    RQ = slice(q0, q0 + 2 * HD)
    rq_out = send_rows(R.rb, RQ, R.rq_ss, R.rq_rs)

    gproj = mm_t(R.rb[0:C, RQ], R.wqk_b[...])
    standard = R.std_b[...]
    column_sum = jnp.sum(gproj * standard, axis=0, keepdims=True)
    for b in range(D // LANES):
        R.gp[0, b : b + 1, :] = column_sum[:, b * LANES : (b + 1) * LANES]
    gain_out = []
    for k, dc in plane_all:
        slot = 2 * k + dc
        cp = remote(
            R.gp.at[0], R.gp.at[slot], R.gp_ss.at[slot], R.gp_rs.at[slot], dev(plane(k), z, side(dc))
        )
        cp.start()
        gain_out.append(cp)

    out_run(1, 2)
    out_run(2, 1)
    out_run(3, 0)
    for cp in turned:
        cp.wait()
    rows_here(R.ra, RA, R.ra_rs)
    for cp in turned_late:
        cp.wait()

    def turned_of(w):
        return jnp.concatenate(
            [R.ltr[s, :, w * LANES : (w + 1) * LANES] for s in range(2 * nd)], axis=1
        )

    def send_part(part, lanes):
        for o in (far, fellow, near):
            to_place(*part_sum(part, lanes), o)

    def gated_grad(w, rows_of, g0, at):
        left = turned_of(w)
        for x in range(EA):
            right = []
            for h in range(H):
                gx = column(R.ra[:, HD : HD + LANES], g0 + x * H + h).astype(F32)
                right.append((gx * rows_of[:, h * DH : (h + 1) * DH].astype(F32)).astype(BF16))
            right = jnp.concatenate(right, axis=1)
            R.pb[:, at + x * HD : at + (x + 1) * HD] = mm(left, right).astype(BF16)

    PO, PV, PQ, PS = (
        slice(0, EV),
        slice(EV, 2 * EV),
        slice(2 * EV, 2 * EV + 2 * HD),
        slice(2 * EV + 2 * HD, 2 * EV + 2 * HD + LANES),
    )
    gated_grad(3, R.ra, GATE, 0)
    sum_out(*part_sum(0, PO), R.px.at[0], R.px_rs.at[0])

    hand_near(R.rb, RV, R.rv_ss, R.rv_rs, rv_out, 2)
    hand_near(R.rb, RQ, R.rq_ss, R.rq_rs, rq_out, 1)
    hand_far(R.rb, RV, R.rv_ss, R.rv_rs, rv_out)
    expert_grad_relay(0, R.wdn_b)
    expert_grad_relay(1, R.wup_b)
    total = R.gp[0]
    for cp, (k, dc) in zip(gain_out, plane_all):
        cp.wait()
        total = total + R.gp[2 * k + dc]
    R.gz_s[...] = total
    for k in range(1, nz):
        o = line(k)
        remote(R.gz_s, R.gz.at[z], R.gz_ss.at[o], R.gz_rs.at[z], dev(p, o, c)).start()

    rows_here(R.rb, RV, R.rv_rs)
    gated_grad(0, R.rb, 0, EV)
    sum_out(*part_sum(1, PV), R.px.at[1], R.px_rs.at[1])
    sum_on(*part_sum(0, PO), R.px.at[0], R.px_rs.at[0])
    hand_far(R.rb, RQ, R.rq_ss, R.rq_rs, rq_out)
    lane_s = iota((SL, LANES), 1)
    small_t = mm(turned_of(0), R.rb[:, HD : HD + LANES])
    small_h = mm(turned_of(2), R.rb[:, HD : HD + LANES])
    R.pb[:, PS] = jnp.where(lane_s < 2 * GATE, small_t, small_h).astype(BF16)
    send_part(3, PS)
    rows_here(R.rb, RQ, R.rq_rs)
    left = turned_of(1)
    for b in range(2):
        lo = q0 + b * HD
        R.pb[:, 2 * EV + b * HD : 2 * EV + (b + 1) * HD] = mm(left, R.rb[:, lo : lo + HD]).astype(
            BF16
        )
    send_part(2, PQ)
    sum_on(*part_sum(1, PV), R.px.at[1], R.px_rs.at[1])


    inputs = R.tokens[...].astype(F32)
    centred = inputs - jnp.mean(inputs, axis=-1, keepdims=True)
    inverse = lax.rsqrt(jnp.mean(centred * centred, axis=-1, keepdims=True) + norm_eps)
    gs = gproj * R.gain[...]
    gtok = R.ghid_f[...] + inverse * (
        gs
        - jnp.mean(gs, axis=-1, keepdims=True)
        - standard * jnp.mean(gs * standard, axis=-1, keepdims=True)
    )
    R.gtok[...] = gtok
    for x in range(EA):
        for h in range(H):
            lo = x * HD + h * DH
            R.mix_b[:, lo : lo + DH] = (
                column(gates, x * H + h) * R.gval_f[:, h * DH : (h + 1) * DH]
            ).astype(BF16)
    for b in range(2):
        cols = slice(b * half_d, (b + 1) * half_d)
        R.gtok[:, cols] += mm_t(R.mix_b[...], R.wv_b[cols, :]) + mm_t(
            R.small_b[...], R.wg_b[cols, :]
        )

    R.hid_f[...] += R.out_s[z].astype(F32)

    @pl.when(z > 0)
    def _():
        arrived(R.out_r.at[z], R.out_rs.at[z])
        R.hid_f[...] += R.out_r[z].astype(F32)

    @pl.when(z < nz - 1)
    def _():
        arrived(R.out_r.at[nz], R.out_rs.at[nz])
        R.hid_f[...] += R.out_r[nz].astype(F32)

    R.mixed[...] = R.hid_f[...].astype(BF16)

    for k in range(1, nz):
        o = line(k)
        arrived(R.gz.at[o], R.gz_rs.at[o])
        total = total + R.gz[o]
    first = (p * 2 * nz + z * 2 + c) * S
    pick_row = iota((D // LANES, LANES), 0) == first // LANES
    line_sum = jnp.sum(jnp.where(pick_row, total, 0.0), axis=0, keepdims=True)
    shift = lax.rem(LANES - lax.rem(first, LANES), LANES)
    line_sum = pltpu.roll(jnp.broadcast_to(line_sum, (8, LANES)), shift, 1)
    R.ggain[...] = line_sum[0:1, 0:S]

    own_rows = pl.ds(times(z, S), S)

    def line_total(part, lanes):
        got = R.pb[own_rows, lanes].astype(F32)
        for k in range(1, nz):
            o = line(k)
            arrived(R.pr.at[o, :, lanes], R.p_rs.at[part, o])
            got = got + R.pr[o, :, lanes].astype(F32)
        return got

    for i, (dst, lanes) in enumerate(((R.go, PO), (R.gv, PV))):
        dst[...] = R.pb[own_rows, lanes].astype(F32)
        sum_in(dst, part_sum(i, lanes)[1], R.p_rs.at[i])
    got = line_total(3, PS)

    def pick(width, source):
        a, b = iota((width, LANES), 1), iota((width, LANES), 0)
        return jnp.where(a == source(b), 1.0, 0.0).astype(F32)

    def picked(left, right):
        return lax.dot_general(
            left,
            right,
            (((1,), (1,)), ((), ())),
            preferred_element_type=F32,
            precision=lax.Precision.HIGHEST,
        )

    def router_lane(b):
        at = jnp.zeros_like(b)
        for o in range(nz):
            at = jnp.where(b >= o * own_e, 2 * GATE + o * pad_e + b - o * own_e, at)
        return at

    R.gvg[...] = picked(pick(GATE, lambda b: b), got)
    R.gog[...] = picked(pick(GATE, lambda b: b + GATE), got)
    R.gr[...] = picked(got, pick(experts, router_lane))
    got = line_total(2, PQ)
    R.gq[...] = got[:, 0:HD]
    R.gk[...] = got[:, HD : 2 * HD]

    for i, (buf, dst) in enumerate(((R.wdn_b, R.gdn), (R.wup_b, R.gup))):
        for slot in (0, 2):
            arrived(R.eg_r.at[slot, i], R.eg_rs.at[slot, i])
        rows = rows_of(p)
        for x in range(local):
            got = buf[rows, pl.ds(times(c * local + x, DH), DH)].astype(F32)
            for slot in (0, 2):
                got = got + R.eg_r[slot, i, :, x * DH : (x + 1) * DH].astype(F32)
            dst[x] = got

    gather_end(R.cotb, R.cot_ss)
    gather_end(R.hidb, R.hid_ss)
    for cp in masks + ra_out + rv_out + rq_out + plane_out:
        cp.wait_send()
    for k in range(1, nz):
        o = line(k)
        sent(R.gh_s.at[o], R.gh_ss.at[o])
        sent(R.glog_s.at[o], R.gl_ss.at[o])
        sent(R.out_s.at[o], R.out_ss.at[o])
        sent(R.gz_s, R.gz_ss.at[o])
        for part, lanes in enumerate((PO, PV, PQ, PS)):
            sent(R.pb.at[pl.ds(times(o, S), S), lanes], R.p_ss.at[part, o])


def settle_kernel(*refs):
    n = len(refs) // 2
    for src, dst in zip(refs[:n], refs[n:]):
        dst[...] = src[...]


def fused_layer(nd, nz, *args):
    (tokens, cotangent, seq_lengths, routes, head_experts, norm_gain) = args[:6]
    (w_query, w_key, w_value, w_output, w_value_gate, w_output_gate, w_router) = args[6:13]
    w_up, w_down = args[13:]
    C = tokens.shape[0]
    local = w_up.shape[0]
    experts = w_router.shape[1]
    own_e = 2 * local
    pad_e = -(-own_e // 16) * 16
    EF, HF, HD = own_e * DH, local * DH, H * DH
    EV = EA * HD
    S = D // (nd * nz * 2)
    SL = S * nz
    PW = 2 * EV + 2 * HD + LANES
    s = Scratch()
    s.vmem("wqk_b", (D, 2 * HD), BF16)
    s.vmem("wv_b", (D, EV), BF16)
    s.vmem("wo_b", (D, EV), BF16)
    s.vmem("wup_b", (D, EF), BF16)
    s.vmem("wdn_b", (D, EF), BF16)
    s.vmem("wg_b", (D, LANES), BF16)
    s.vmem("wrl_b", (D, LANES), BF16)
    s.vmem("cotb", (nz * C, D), BF16)
    s.vmem("hidb", (nz * C, D), BF16)
    s.vmem("mask_s", (nz, pad_e, C), BF16)
    s.vmem("maskb", (nz, pad_e, C), BF16)
    s.vmem("std_b", (C, D), F32)
    s.vmem("normed_b", (C, D), BF16)
    s.vmem("q_b", (C, HD), BF16)
    s.vmem("k_b", (C, HD), BF16)
    s.vmem("v_b", (C, HD), BF16)
    s.vmem("gate_b", (C, LANES), F32)
    s.vmem("val_b", (C, EV), F32)
    s.vmem("prob_b", (H, C, C), F32)
    s.vmem("att_b", (C, HD), F32)
    s.vmem("mix_b", (C, EV), BF16)
    s.vmem("hid_f", (C, D), F32)
    s.vmem("lt", (D, 4 * LANES), BF16)
    s.vmem("ltr", (2 * nd, SL, 4 * LANES), BF16)
    s.vmem("ra", (2 * nd * C, HD + LANES), BF16)
    s.vmem("rb", (2 * nd * C, 3 * HD + LANES), BF16)
    s.vmem("gact", (nz * C, EF), BF16)
    s.vmem("gra", (nz * C, EF), BF16)
    for name in ("gh_s", "gh_r", "out_s"):
        s.vmem(name, (nz, C, D), BF16)
    s.vmem("out_r", (nz + 1, C, D), BF16)
    s.vmem("gh_x", (2, C, D), BF16)
    for name in ("glog_s", "glog_r"):
        s.vmem(name, (nz, pad_e, C), BF16)
    s.vmem("pair_r", (2, D, HF), BF16)
    s.vmem("eg_r", (nd - 1, 2, D // nd, HF), BF16)
    s.vmem("ghid_f", (C, D), F32)
    s.vmem("ghid_b", (C, D), BF16)
    s.vmem("gatt_b", (C, HD), BF16)
    s.vmem("gval_f", (C, HD), F32)
    s.vmem("small_b", (C, LANES), BF16)
    s.vmem("pb", (SL, PW), BF16)
    s.vmem("pr", (nz, S, PW), BF16)
    s.vmem("px", (2, S, EV), BF16)
    s.vmem("gp", (2 * nd, D // LANES, LANES), F32)
    s.vmem("gz_s", (D // LANES, LANES), F32)
    s.vmem("gz", (nz, D // LANES, LANES), F32)
    s.sems("ld", 4 + 2 * local)
    s.sems("gx_rs", 2)
    s.sems("out_rs", nz + 1)
    s.sems("px_rs", 2)
    for name in ("cot_ss", "hid_ss"):
        s.sems(name, 2, nz)
    for name in ("cot_rs", "hid_rs", "mask_ss", "mask_rs", "gh_ss", "gh_rs", "gl_ss", "gl_rs", "out_ss", "gz_ss", "gz_rs"):
        s.sems(name, nz)
    for name in "w_ss w_rs pair_ss pair_rs".split():
        s.sems(name, 2)
    for name in ("lt_ss", "lt_rs", "ltl_ss", "ltl_rs", "gp_ss", "gp_rs", "ra_ss", "ra_rs", "rv_ss", "rv_rs", "rq_ss", "rq_rs"):
        s.sems(name, 2 * nd)
    for name in ("eg_ss", "eg_rs"):
        s.sems(name, nd - 1, 2)
    for name in ("p_ss", "p_rs"):
        s.sems(name, 4, nz)

    def out(*shape, dtype=F32):
        return jax.ShapeDtypeStruct(shape, dtype)

    vmem = pl.BlockSpec(memory_space=pltpu.VMEM)
    smem = pl.BlockSpec(memory_space=pltpu.SMEM)
    hbm = pl.BlockSpec(memory_space=pl.ANY)
    outs = pl.pallas_call(
        functools.partial(layer_kernel, INPUTS + OUTPUTS + tuple(s.names), nd, nz, local),
        out_shape=(
            out(C, D, dtype=BF16),
            out(C, D),
            out(1, S),
            out(S, HD),
            out(S, HD),
            out(S, EV),
            out(S, EV),
            out(EA * H, S),
            out(EA * H, S),
            out(S, experts),
            out(local, D // nd, DH),
            out(local, D // nd, DH),
        ),
        in_specs=[vmem, vmem, smem] + [vmem] * 6 + [hbm] * 6,
        out_specs=[vmem] * 12,
        scratch_shapes=s.shapes,
        compiler_params=pltpu.CompilerParams(
            collective_id=0, has_side_effects=True, vmem_limit_bytes=VMEM_LIMIT
        ),
    )(
        tokens,
        cotangent,
        seq_lengths,
        routes.T,
        head_experts.reshape(C, 2 * H).T,
        norm_gain.reshape(1, D),
        w_value_gate.T,
        w_output_gate.T,
        w_router.T,
        w_query,
        w_key,
        w_value,
        w_output,
        w_up,
        w_down,
    )
    outs = list(
        pl.pallas_call(
            settle_kernel,
            out_shape=[out(*x.shape, dtype=x.dtype) for x in outs],
            in_specs=[vmem] * 12,
            out_specs=[vmem] * 12,
            compiler_params=pltpu.CompilerParams(vmem_limit_bytes=VMEM_LIMIT),
        )(*outs)
    )
    outs[2] = outs[2].reshape(S)
    for i in (7, 8):
        outs[i] = outs[i].T
    return tuple(outs)


VMEM_LIMIT = 62 * 1024 * 1024


def fits(nd, nz, count, experts):
    own_e = experts // nz
    pad_e = -(-own_e // 16) * 16
    return (
        count == LANES
        and nz == 4
        and nd == 4
        and own_e % 4 == 0
        and D % (nd * nz * 2 * 16) == 0
        and LANES % (D // (nd * nz * 2)) == 0
        and 2 * EA * H + nz * pad_e <= LANES
    )


def per_device(nd, ne, *args):
    count, experts = args[0].shape[0], args[12].shape[1]
    if ne % 2 == 0 and fits(nd, ne // 2, count, experts):
        return fused_layer(nd, ne // 2, *args)
    return routed_layer(*args)


def solution(mesh):
    return jax.shard_map(
        functools.partial(per_device, mesh.shape["dp"], mesh.shape["expert"]),
        mesh=mesh,
        in_specs=(
            P(("dp", "expert"), None),
            P(("dp", "expert"), None),
            P(("dp", "expert"), None),
            P(("dp", "expert"), None),
            P(("dp", "expert"), None, None),
            P(),
            P(),
            P(),
            P(),
            P(),
            P(),
            P(),
            P(),
            P("expert", None, None),
            P("expert", None, None),
        ),
        out_specs=(
            P(("dp", "expert"), None),
            P(("dp", "expert"), None),
            P(("dp", "expert")),
            P(("dp", "expert"), None),
            P(("dp", "expert"), None),
            P(("dp", "expert"), None),
            P(("dp", "expert"), None),
            P(("dp", "expert"), None),
            P(("dp", "expert"), None),
            P(("dp", "expert"), None),
            P("expert", "dp", None),
            P("expert", "dp", None),
        ),
        check_vma=False,
    )
```

```python
import functools
import math

import jax
import jax.numpy as jnp
from jax import lax
from jax.experimental import pallas as pl
from jax.experimental.pallas import tpu as pltpu
from jax.sharding import PartitionSpec as P

D = 1024
H = 4
DH = 128
EA = 5
TOPK = 16


norm_eps = 1e-05
rope_base = 10000.0
masked_score = -1e30


def sequence_layout(lengths, count):
    bounds = jnp.cumsum(lengths)
    starts = bounds - lengths
    places = jnp.arange(count, dtype=jnp.int32)
    seq_ids = jnp.sum((places[:, None] >= bounds[None, :]).astype(jnp.int32), axis=1)
    live = places < bounds[-1]
    slot_ids = jnp.arange(lengths.shape[0], dtype=jnp.int32)
    first = jnp.sum(jnp.where(seq_ids[:, None] == slot_ids[None, :], starts[None, :], 0), axis=1)
    positions = jnp.where(live, places - first, 0)
    return (seq_ids, live, positions)


def rope_tables(positions, width):
    half = width // 2
    freq = rope_base ** (-(jnp.arange(half, dtype=jnp.float32) * 2.0 / width))
    angles = positions.astype(jnp.float32)[:, None] * freq[None, :]
    return (jnp.cos(angles), jnp.sin(angles))


def rotate(field, cosine, sine):
    half = field.shape[-1] // 2
    first, second = (field[..., :half], field[..., half:])
    cos_h, sin_h = (cosine[:, None, :], sine[:, None, :])
    return jnp.concatenate(
        [first * cos_h - second * sin_h, second * cos_h + first * sin_h], axis=-1
    )


def rotate_back(field, cosine, sine):
    half = field.shape[-1] // 2
    first, second = (field[..., :half], field[..., half:])
    cos_h, sin_h = (cosine[:, None, :], sine[:, None, :])
    return jnp.concatenate(
        [first * cos_h + second * sin_h, second * cos_h - first * sin_h], axis=-1
    )


def slot_tables(routes, experts, most):
    count = routes.shape[0] * routes.shape[1]
    flat = routes.reshape(count)
    order = jnp.argsort(flat, stable=True)
    ordered = flat[order]
    firsts = jnp.searchsorted(ordered, jnp.arange(experts, dtype=jnp.int32))
    ranks = jnp.arange(count, dtype=jnp.int32) - firsts[ordered]
    sorted_slots = ordered * most + ranks
    slot_of_row = jnp.zeros((count,), jnp.int32).at[order].set(sorted_slots)
    row_of_slot = jnp.full((experts * most,), count, jnp.int32).at[sorted_slots].set(order)
    return (slot_of_row, row_of_slot)


def routed_layer(
    tokens,
    cotangent,
    seq_lengths,
    routes,
    head_experts,
    norm_gain,
    w_query,
    w_key,
    w_value,
    w_output,
    w_value_gate,
    w_output_gate,
    w_router,
    w_up,
    w_down,
):
    f32 = jnp.float32
    bf16 = jnp.bfloat16
    count = tokens.shape[0]
    experts = w_router.shape[1]
    local_experts = w_up.shape[0]
    owners = lax.axis_size("expert")
    most = 3 * count * TOPK // (2 * experts)
    routed = count * TOPK
    block = min(512, count)
    block_starts = jnp.arange(count // block, dtype=jnp.int32) * block
    scale = DH ** (-0.5)
    contract_last = (((1,), (1,)), ((), ()))
    contract_first = (((0,), (0,)), ((), ()))
    seq_ids, live, positions = sequence_layout(seq_lengths[0], count)
    cosine, sine = rope_tables(positions, DH)
    inputs = tokens.astype(f32)
    centred = inputs - jnp.mean(inputs, axis=-1, keepdims=True)
    inverse = lax.rsqrt(jnp.mean(centred * centred, axis=-1, keepdims=True) + norm_eps)
    standard = centred * inverse
    normed = (standard * norm_gain).astype(bf16)
    query_proj = jnp.dot(normed, w_query, preferred_element_type=f32).reshape(count, H, DH)
    key_proj = jnp.dot(normed, w_key, preferred_element_type=f32).reshape(count, H, DH)
    query_rot = (rotate(query_proj, cosine, sine) * scale).astype(bf16)
    key_rot = rotate(key_proj, cosine, sine).astype(bf16)
    chosen = jnp.any(
        head_experts[:, None, :, :] == jnp.arange(EA, dtype=jnp.int32)[None, :, None, None], axis=-1
    )
    value_gates = jnp.where(
        chosen,
        jax.nn.sigmoid(
            jnp.dot(tokens, w_value_gate, preferred_element_type=f32).reshape(count, EA, H)
        ),
        0.0,
    )
    output_gates = jnp.where(
        chosen,
        jax.nn.sigmoid(
            jnp.dot(tokens, w_output_gate, preferred_element_type=f32).reshape(count, EA, H)
        ),
        0.0,
    )
    value_all = jnp.dot(tokens, w_value, preferred_element_type=f32).reshape(count, EA, H, DH)
    values = jnp.sum(value_gates[..., None] * value_all, axis=1).astype(bf16)

    def allowed_at(start):
        queries = start + jnp.arange(block, dtype=jnp.int32)
        keys = jnp.arange(count, dtype=jnp.int32)
        same = (
            (seq_ids[:, None] == seq_ids[None, :])
            & (keys[None, :] <= queries[:, None])
            & live[None, :]
        )
        return same | (keys[None, :] == queries[:, None])

    def scores_at(start):
        scores = jnp.einsum("qhd,khd->hqk", query_rot, key_rot, preferred_element_type=f32)
        return (query_rot, jnp.where(allowed_at(start)[None], scores, masked_score))

    def attend(start):
        query_block, scores = scores_at(start)
        highest = jnp.max(scores, axis=-1, keepdims=True)
        shifted = jnp.exp(scores - highest)
        totals = jnp.sum(shifted, axis=-1, keepdims=True)
        shares = (shifted / totals).astype(bf16)
        result = jnp.einsum("hqk,khd->qhd", shares, values, preferred_element_type=f32)
        return (result, (highest + jnp.log(totals))[..., 0])

    attended, log_totals = lax.map(attend, block_starts)
    attended = attended.reshape(count, H, DH)
    log_totals = jnp.transpose(log_totals, (1, 0, 2)).reshape(H, count)
    heads_mixed = (
        (output_gates[..., None] * attended[:, None]).astype(bf16).reshape(count, EA * H * DH)
    )
    hidden = inputs + lax.dot_general(
        heads_mixed, w_output, contract_last, preferred_element_type=f32
    )
    hidden_low = hidden.astype(bf16)
    logits = jnp.dot(hidden_low, w_router, preferred_element_type=f32)
    gates = jax.nn.sigmoid(jnp.take_along_axis(logits, routes, axis=1))
    slot_of_row, row_of_slot = slot_tables(routes, experts, most)
    valid = row_of_slot < routed
    safe_row = jnp.minimum(row_of_slot, routed - 1)
    source = safe_row // TOPK
    outgoing = jnp.where(valid[:, None], hidden_low[source], jnp.zeros((), bf16)).reshape(
        owners, local_experts, most, D
    )

    def expert_apply(items):
        raised = jnp.einsum("nemd,edf->nemf", items, w_up, preferred_element_type=f32)
        active = jax.nn.silu(raised).astype(bf16)
        lowered = jnp.einsum("nemf,edf->nemd", active, w_down, preferred_element_type=f32).astype(
            bf16
        )
        return (lowered, raised)

    lowered, raised = expert_apply(
        lax.all_to_all(outgoing, "expert", split_axis=0, concat_axis=0, tiled=True)
    )
    returned = lax.all_to_all(lowered, "expert", split_axis=0, concat_axis=0, tiled=True).reshape(
        experts * most, D
    )
    expert_rows = returned[slot_of_row].reshape(count, TOPK, D)
    output = hidden + jnp.sum(gates[..., None] * expert_rows, axis=1)
    mixed = output.astype(bf16)
    grad_out = cotangent.astype(f32) * live[:, None].astype(f32)
    grad_gates = jnp.sum(grad_out[:, None, :] * expert_rows, axis=2)
    gate_flat = gates.reshape(routed)
    grad_outgoing = (
        jnp.where(valid[:, None], gate_flat[safe_row][:, None] * grad_out[source], 0.0)
        .astype(bf16)
        .reshape(owners, local_experts, most, D)
    )
    grad_lowered = lax.all_to_all(grad_outgoing, "expert", split_axis=0, concat_axis=0, tiled=True)
    items = lax.all_to_all(outgoing, "expert", split_axis=0, concat_axis=0, tiled=True)
    raised = expert_apply(items)[1]
    grad_active = jnp.einsum("nemd,edf->nemf", grad_lowered, w_down, preferred_element_type=f32)
    sigmoid_raised = jax.nn.sigmoid(raised)
    grad_raised = (grad_active * sigmoid_raised * (1.0 + raised * (1.0 - sigmoid_raised))).astype(
        bf16
    )
    grad_items = jnp.einsum("nemf,edf->nemd", grad_raised, w_up, preferred_element_type=f32).astype(
        bf16
    )
    active = jax.nn.silu(raised).astype(bf16)
    grad_items, grad_raised, active = (grad_items, grad_raised, active)
    grad_items, grad_raised, active, grad_arrived, arrived = (
        grad_items,
        grad_raised,
        active,
        grad_lowered,
        items,
    )
    grad_up_local = jnp.einsum("nemd,nemf->edf", arrived, grad_raised, preferred_element_type=f32)
    grad_down_local = jnp.einsum("nemd,nemf->edf", grad_arrived, active, preferred_element_type=f32)
    grad_up, grad_down = (
        lax.psum_scatter(
            grad_up_local.astype(jnp.bfloat16), "dp", scatter_dimension=1, tiled=True
        ).astype(jnp.float32),
        lax.psum_scatter(
            grad_down_local.astype(jnp.bfloat16), "dp", scatter_dimension=1, tiled=True
        ).astype(jnp.float32),
    )
    grad_back = lax.all_to_all(
        grad_items, "expert", split_axis=0, concat_axis=0, tiled=True
    ).reshape(experts * most, D)
    grad_hidden = grad_out + jnp.sum(
        grad_back[slot_of_row].reshape(count, TOPK, D), axis=1, dtype=f32
    )
    grad_picked = grad_gates * gates * (1.0 - gates)
    expert_ids = jnp.arange(experts, dtype=jnp.int32)
    grad_logits = jnp.sum(
        jnp.where(routes[:, :, None] == expert_ids[None, None, :], grad_picked[..., None], 0.0),
        axis=1,
    ).astype(bf16)
    grad_router = lax.dot_general(
        hidden_low, grad_logits, contract_first, preferred_element_type=f32
    )
    grad_hidden = grad_hidden + lax.dot_general(
        grad_logits, w_router, contract_last, preferred_element_type=f32
    )
    grad_hidden_low = grad_hidden.astype(bf16)
    grad_output = lax.dot_general(
        grad_hidden_low, heads_mixed, contract_first, preferred_element_type=f32
    )
    grad_mixed = jnp.dot(grad_hidden_low, w_output, preferred_element_type=f32).reshape(
        count, EA, H, DH
    )
    grad_attended = jnp.sum(output_gates[..., None] * grad_mixed, axis=1).astype(bf16)
    grad_out_gates = jnp.sum(grad_mixed * attended[:, None], axis=-1)
    grad_out_logits = (
        jnp.where(chosen, grad_out_gates * output_gates * (1.0 - output_gates), 0.0)
        .astype(bf16)
        .reshape(count, EA * H)
    )

    def attend_back(carry, start):
        grad_keys, grad_vals = carry
        query_block, scores = scores_at(start)
        shares = jnp.exp(scores - log_totals[..., None])
        grad_shares = jnp.einsum("qhd,khd->hqk", grad_attended, values, preferred_element_type=f32)
        centre = jnp.sum(shares * grad_shares, axis=-1, keepdims=True)
        grad_scores = (shares * (grad_shares - centre)).astype(bf16)
        grad_query_block = jnp.einsum(
            "hqk,khd->qhd", grad_scores, key_rot, preferred_element_type=f32
        )
        grad_keys = grad_keys + jnp.einsum(
            "hqk,qhd->khd", grad_scores, query_block, preferred_element_type=f32
        )
        grad_vals = grad_vals + jnp.einsum(
            "hqk,qhd->khd", shares.astype(bf16), grad_attended, preferred_element_type=f32
        )
        return ((grad_keys, grad_vals), grad_query_block)

    zero_heads = jnp.zeros((count, H, DH), f32)
    (grad_keys, grad_vals), grad_queries = lax.scan(
        attend_back, (zero_heads, zero_heads), block_starts
    )
    grad_queries = grad_queries.reshape(count, H, DH)
    grad_query_proj = (
        rotate_back(grad_queries * scale, cosine, sine).astype(bf16).reshape(count, H * DH)
    )
    grad_key_proj = rotate_back(grad_keys, cosine, sine).astype(bf16).reshape(count, H * DH)
    grad_value_all = (
        (value_gates[..., None] * grad_vals[:, None]).astype(bf16).reshape(count, EA * H * DH)
    )
    grad_value_gates = jnp.sum(grad_vals[:, None] * value_all, axis=-1)
    grad_value_logits = (
        jnp.where(chosen, grad_value_gates * value_gates * (1.0 - value_gates), 0.0)
        .astype(bf16)
        .reshape(count, EA * H)
    )
    grad_query = lax.dot_general(
        normed, grad_query_proj, contract_first, preferred_element_type=f32
    )
    grad_key = lax.dot_general(normed, grad_key_proj, contract_first, preferred_element_type=f32)
    grad_value = lax.dot_general(tokens, grad_value_all, contract_first, preferred_element_type=f32)
    grad_value_gate = lax.dot_general(
        tokens, grad_value_logits, contract_first, preferred_element_type=f32
    )
    grad_output_gate = lax.dot_general(
        tokens, grad_out_logits, contract_first, preferred_element_type=f32
    )
    grad_normed = lax.dot_general(
        grad_query_proj, w_query, contract_last, preferred_element_type=f32
    ) + lax.dot_general(grad_key_proj, w_key, contract_last, preferred_element_type=f32)
    grad_gain = jnp.sum(grad_normed * standard, axis=0)
    grad_standard = grad_normed * norm_gain
    grad_tokens = grad_hidden + inverse * (
        grad_standard
        - jnp.mean(grad_standard, axis=-1, keepdims=True)
        - standard * jnp.mean(grad_standard * standard, axis=-1, keepdims=True)
    )
    grad_tokens = (
        grad_tokens
        + lax.dot_general(grad_value_all, w_value, contract_last, preferred_element_type=f32)
        + lax.dot_general(
            grad_value_logits, w_value_gate, contract_last, preferred_element_type=f32
        )
        + lax.dot_general(grad_out_logits, w_output_gate, contract_last, preferred_element_type=f32)
    )
    summed = (
        lax.psum_scatter(grad_gain, ("dp", "expert"), scatter_dimension=0, tiled=True),
        lax.psum_scatter(grad_query, ("dp", "expert"), scatter_dimension=0, tiled=True),
        lax.psum_scatter(grad_key, ("dp", "expert"), scatter_dimension=0, tiled=True),
        lax.psum_scatter(grad_value, ("dp", "expert"), scatter_dimension=0, tiled=True),
        lax.psum_scatter(grad_output, ("dp", "expert"), scatter_dimension=0, tiled=True),
        lax.psum_scatter(grad_value_gate, ("dp", "expert"), scatter_dimension=0, tiled=True),
        lax.psum_scatter(grad_output_gate, ("dp", "expert"), scatter_dimension=0, tiled=True),
        lax.psum_scatter(grad_router, ("dp", "expert"), scatter_dimension=0, tiled=True),
    )
    return (
        mixed,
        grad_tokens,
        summed[0],
        summed[1],
        summed[2],
        summed[3],
        summed[4],
        summed[5],
        summed[6],
        summed[7],
        grad_up,
        grad_down,
    )


F32 = jnp.float32
BF16 = jnp.bfloat16
MESH = pl.DeviceIdType.MESH
LANES = 128


def mm(a, b):
    return lax.dot_general(a, b, (((1,), (0,)), ((), ())), preferred_element_type=F32)


def mm_t(a, b):
    return lax.dot_general(a, b, (((1,), (1,)), ((), ())), preferred_element_type=F32)


def tmm(a, b):
    return lax.dot_general(a, b, (((0,), (0,)), ((), ())), preferred_element_type=F32)


def iota(shape, axis):
    return lax.broadcasted_iota(jnp.int32, shape, axis)


def column(x, j, width=LANES):
    return jnp.broadcast_to(x[:, j : j + 1], (x.shape[0], width))


def sigmoid(x):
    return 1.0 / (1.0 + jnp.exp(-x))


class Scratch:
    def __init__(self):
        self.names, self.shapes = [], []

    def add(self, name, shape):
        self.names.append(name)
        self.shapes.append(shape)

    def vmem(self, name, shape, dtype):
        self.add(name, pltpu.VMEM(shape, dtype))

    def sems(self, name, *shape):
        self.add(name, pltpu.SemaphoreType.DMA(shape))


INPUTS = ("tokens", "cot", "lens", "rt", "het", "gain", "wvg", "wog", "wr", "wq", "wk", "wv", "wo", "wu", "wd")
OUTPUTS = ("mixed", "gtok", "ggain", "gq", "gk", "gv", "go", "gvg", "gog", "gr", "gup", "gdn")


def layer_kernel(names, nd, nz, local, *refs):
    r = dict(zip(names, refs))
    R = type("R", (), r)
    C = R.tokens.shape[0]
    own_e = 2 * local
    pad_e = R.maskb.shape[1]
    EF = own_e * DH
    HF = local * DH
    HD = H * DH
    EV = EA * HD
    S = D // (nd * nz * 2)
    SL = S * nz
    GATE = EA * H
    p = lax.axis_index("dp")
    e = lax.axis_index("expert")
    z = e // 2
    c = e % 2
    sib = 1 - c

    def dev(p_, z_, c_):
        return (p_, z_ * 2 + c_)

    def times(i, n):
        return pl.multiple_of(i * n, n)

    def remote(src, dst, ss, rs, to):
        return pltpu.make_async_remote_copy(
            src_ref=src, dst_ref=dst, send_sem=ss, recv_sem=rs, device_id=to, device_id_type=MESH
        )

    def arrived(dst, rs):
        remote(dst, dst, rs, rs, dev(p, z, sib)).wait_recv()

    def sent(src, ss):
        remote(src, src, ss, ss, dev(p, z, sib)).wait_send()

    beside = p + 1 - 2 * lax.rem(p, 2)
    across = lax.rem(p + 2, nd)
    diagonal = lax.rem(beside + 2, nd)

    def plane(k):
        return (p, beside, across, diagonal)[k]

    def line(k):
        return lax.rem(z + k, nz)

    loads = {}

    def load(name, src, dst, sem):
        cp = pltpu.make_async_copy(src, dst, sem)
        cp.start()
        loads.setdefault(name, []).append(cp)

    def loaded(name):
        for cp in loads.pop(name):
            cp.wait()

    load("qk", R.wq, R.wqk_b.at[:, 0:HD], R.ld.at[0])
    load("qk", R.wk, R.wqk_b.at[:, HD : 2 * HD], R.ld.at[1])
    load("v", R.wv, R.wv_b, R.ld.at[2])
    for i in range(local):
        col = times(c * local + i, DH)
        load("up", R.wu.at[i], R.wup_b.at[:, pl.ds(col, DH)], R.ld.at[4 + i])
        load("dn", R.wd.at[i], R.wdn_b.at[:, pl.ds(col, DH)], R.ld.at[4 + local + i])
    load("o", R.wo, R.wo_b, R.ld.at[3])

    barrier = pltpu.get_barrier_semaphore()
    partners = [dev(p, z, sib)]
    partners += [dev(p, line(k), c) for k in range(1, nz)]
    for k in range(1, nd):
        partners += [dev(plane(k), z, c), dev(plane(k), z, sib)]
    for to in partners:
        pl.semaphore_signal(barrier, inc=1, device_id=to, device_id_type=MESH)

    l0 = R.lens[0, 0]
    b1 = l0 + R.lens[0, 1]
    row = iota((C, LANES), 0)
    lane = iota((C, LANES), 1)
    seq_r = (row >= l0).astype(jnp.int32) + (row >= b1).astype(jnp.int32)
    seq_c = (lane >= l0).astype(jnp.int32) + (lane >= b1).astype(jnp.int32)
    live = row < b1
    allowed = ((seq_r == seq_c) & (lane <= row) & (lane < b1)) | (row == lane)
    live_f = jnp.where(live, 1.0, 0.0).astype(F32)
    start = jnp.where(seq_r == 0, 0, l0)
    position = jnp.where(live, row - start, 0).astype(F32)

    for b in range(D // LANES):
        cols = slice(b * LANES, (b + 1) * LANES)
        R.cotb[pl.ds(times(z, C), C), cols] = (R.cot[:, cols].astype(F32) * live_f).astype(BF16)
    ids = iota((pad_e, C), 0)
    for zz in range(nz):
        named = jnp.zeros((pad_e, C), F32)
        for k in range(TOPK):
            hit = jnp.broadcast_to(R.rt[k : k + 1, :], (pad_e, C)) == ids + zz * own_e
            named = jnp.where(hit & (ids < own_e), 1.0, named)
        R.mask_s[zz] = named.astype(BF16)
    R.maskb[z] = R.mask_s[z]

    pl.semaphore_wait(barrier, len(partners))

    def block(buf, o):
        return buf.at[pl.ds(times(o, C), C), :]

    def pass_on(buf, ss, rs, o, right, left):
        @pl.when(right)
        def _():
            remote(block(buf, o), block(buf, o), ss.at[0, o], rs.at[o], dev(p, z + 1, c)).start()

        @pl.when(left)
        def _():
            remote(block(buf, o), block(buf, o), ss.at[1, o], rs.at[o], dev(p, z - 1, c)).start()

    def passed(buf, ss, o, right, left):
        @pl.when(right)
        def _():
            sent(block(buf, o), ss.at[0, o])

        @pl.when(left)
        def _():
            sent(block(buf, o), ss.at[1, o])

    def gather_own(buf, ss, rs):
        pass_on(buf, ss, rs, z, z < nz - 1, z > 0)

    def gather_on(buf, ss, rs, o):
        arrived(block(buf, o), rs.at[o])
        pass_on(buf, ss, rs, o, (o < z) & (z < nz - 1), (o > z) & (z > 0))

    def gather_step(buf, ss, rs, k):
        @pl.when(z >= k)
        def _():
            gather_on(buf, ss, rs, z - k)

        @pl.when(z + k < nz)
        def _():
            gather_on(buf, ss, rs, z + k)

    def gather_end(buf, ss):
        passed(buf, ss, z, z < nz - 1, z > 0)
        for k in range(1, nz):

            @pl.when(z >= k)
            def _():
                passed(buf, ss, z - k, z < nz - 1, False)

            @pl.when(z + k < nz)
            def _():
                passed(buf, ss, z + k, False, z > 0)

    gather_own(R.cotb, R.cot_ss, R.cot_rs)
    masks = []
    for k in range(1, nz):
        o = line(k)
        cp = remote(R.mask_s.at[o], R.maskb.at[z], R.mask_ss.at[k], R.mask_rs.at[z], dev(p, o, c))
        cp.start()
        masks.append(cp)

    s_row, s_col = iota((GATE, LANES), 0), iota((GATE, LANES), 1)
    to_v = jnp.where(s_row == s_col, 1.0, 0.0).astype(BF16)
    to_o = jnp.where(s_row + GATE == s_col, 1.0, 0.0).astype(BF16)
    R.wg_b[...] = (tmm(R.wvg[...], to_v) + tmm(R.wog[...], to_o)).astype(BF16)
    experts = R.wr.shape[0]
    r_row, r_col = iota((experts, LANES), 0), iota((experts, LANES), 1)
    to_r = jnp.where((r_row == r_col + z * own_e) & (r_col < own_e), 1.0, 0.0).astype(BF16)
    R.wrl_b[...] = tmm(R.wr[...], to_r).astype(BF16)

    half = lax.rem(lane, DH // 2).astype(F32)
    angle = position * jnp.exp(half * (-2.0 / DH * math.log(rope_base)))
    cosine = jnp.cos(angle)
    sine = jnp.where(lane < DH // 2, -jnp.sin(angle), jnp.sin(angle))

    def rot(v):
        return v * cosine + pltpu.roll(v, DH // 2, 1) * sine

    def rot_back(v):
        return v * cosine - pltpu.roll(v, DH // 2, 1) * sine

    inputs = R.tokens[...].astype(F32)
    centred = inputs - jnp.mean(inputs, axis=-1, keepdims=True)
    inverse = lax.rsqrt(jnp.mean(centred * centred, axis=-1, keepdims=True) + norm_eps)
    standard = centred * inverse
    R.std_b[...] = standard
    R.normed_b[...] = (standard * R.gain[...]).astype(BF16)

    loaded("qk")
    scale = DH ** (-0.5)
    qk = mm(R.normed_b[...], R.wqk_b[:, 0:HD])
    for h in range(H):
        hs = slice(h * DH, (h + 1) * DH)
        R.q_b[:, hs] = (rot(qk[:, hs]) * scale).astype(BF16)
    qk = mm(R.normed_b[...], R.wqk_b[:, HD : 2 * HD])
    for h in range(H):
        hs = slice(h * DH, (h + 1) * DH)
        R.k_b[:, hs] = rot(qk[:, hs]).astype(BF16)

    hit = []
    for j in range(GATE):
        x, h = divmod(j, H)
        one = (R.het[2 * h : 2 * h + 1, :] == x) | (R.het[2 * h + 1 : 2 * h + 2, :] == x)
        hit.append(jnp.where(one, 1.0, 0.0).astype(F32))
    hit = jnp.concatenate(hit + hit + [jnp.zeros((LANES - 2 * GATE, C), F32)], axis=0)
    R.gate_b[...] = sigmoid(mm(R.tokens[...], R.wg_b[...])) * hit.T

    loaded("up")
    loaded("dn")
    wx = []
    for i, buf in enumerate((R.wup_b, R.wdn_b)):
        part = buf.at[:, pl.ds(times(c, HF), HF)]
        cp = remote(part, part, R.w_ss.at[i], R.w_rs.at[i], dev(p, z, sib))
        cp.start()
        wx.append(cp)

    loaded("v")
    gates = R.gate_b[...]
    total = [None] * H
    for x in range(EA):
        R.val_b[:, x * HD : (x + 1) * HD] = mm(R.tokens[...], R.wv_b[:, x * HD : (x + 1) * HD])
        for h in range(H):
            lo = x * HD + h * DH
            term = column(gates, x * H + h) * R.val_b[:, lo : lo + DH]
            total[h] = term if x == 0 else total[h] + term
    for h in range(H):
        R.v_b[:, h * DH : (h + 1) * DH] = total[h].astype(BF16)

    for h in range(H):
        hs = slice(h * DH, (h + 1) * DH)
        scores = jnp.where(allowed, mm_t(R.q_b[:, hs], R.k_b[:, hs]), masked_score)
        shifted = jnp.exp(scores - jnp.max(scores, axis=-1, keepdims=True))
        shares = shifted / jnp.sum(shifted, axis=-1, keepdims=True)
        R.prob_b[h] = shares
        R.att_b[:, hs] = mm(shares.astype(BF16), R.v_b[:, hs])

    for x in range(EA):
        for h in range(H):
            lo = x * HD + h * DH
            R.mix_b[:, lo : lo + DH] = (
                column(gates, GATE + x * H + h) * R.att_b[:, h * DH : (h + 1) * DH]
            ).astype(BF16)
    loaded("o")
    half_d = D // 2
    for b in range(2):
        cols = slice(b * half_d, (b + 1) * half_d)
        hidden = R.tokens[:, cols].astype(F32) + mm_t(R.mix_b[...], R.wo_b[cols, :])
        R.hid_f[:, cols] = hidden
        R.hidb[pl.ds(times(z, C), C), cols] = hidden.astype(BF16)
    gather_own(R.hidb, R.hid_ss, R.hid_rs)
    gather_step(R.cotb, R.cot_ss, R.cot_rs, 1)

    def put_turned(x, w):
        for b in range(D // LANES):
            t = x[:, b * LANES : (b + 1) * LANES].astype(F32).T.astype(BF16)
            for q in range(LANES // S):
                i = (b * LANES) // S + q
                pp, zz, cc = i // (2 * nz), (i % (2 * nz)) // 2, i % 2
                at = (pp * 2 + cc) * SL + zz * S
                R.lt[at : at + S, w * LANES : (w + 1) * LANES] = t[q * S : (q + 1) * S, :]

    plane_all = [(k, dc) for k in range(nd) for dc in range(2) if k or dc]

    def side(dc):
        return sib if dc else c

    def send_turned(w0, w1, ss, rs):
        out = []
        lanes = slice(w0 * LANES, w1 * LANES)
        for k, dc in plane_all:
            to = plane(k)
            slot = 2 * k + dc
            at = times(to * 2 + side(dc), SL)
            cp = remote(
                R.lt.at[pl.ds(at, SL), lanes],
                R.ltr.at[slot, :, lanes],
                ss.at[slot],
                rs.at[slot],
                dev(to, z, side(dc)),
            )
            cp.start()
            out.append(cp)
        R.ltr[0, :, lanes] = R.lt[pl.ds(times(p * 2 + c, SL), SL), lanes]
        return out

    def rows_at(buf, lanes, slot):
        return buf.at[slot * C : (slot + 1) * C, lanes]

    def send_rows(buf, lanes, ss, rs, ways=(1, 2)):
        out = []
        for k in ways:
            cp = remote(
                rows_at(buf, lanes, 0),
                rows_at(buf, lanes, 2 * k),
                ss.at[k],
                rs.at[2 * k],
                dev(plane(k), z, c),
            )
            cp.start()
            out.append(cp)
        return out + [hand_over(buf, lanes, ss, rs, 0)]

    def hand_over(buf, lanes, ss, rs, k):
        cp = remote(
            rows_at(buf, lanes, 2 * k),
            rows_at(buf, lanes, 2 * k + 1),
            ss.at[nd + k],
            rs.at[2 * k + 1],
            dev(p, z, sib),
        )
        cp.start()
        return cp

    def hand_near(buf, lanes, ss, rs, out, via):
        for k in (via, 3 - via) if via else (1, 2):
            arrived(rows_at(buf, lanes, 2 * k), rs.at[2 * k])
            if k == via:
                cp = remote(
                    rows_at(buf, lanes, 2 * k),
                    rows_at(buf, lanes, 6),
                    ss.at[3],
                    rs.at[6],
                    dev(plane(3 - via), z, c),
                )
                cp.start()
                out.append(cp)
            out.append(hand_over(buf, lanes, ss, rs, k))

    def hand_far(buf, lanes, ss, rs, out):
        arrived(rows_at(buf, lanes, 6), rs.at[6])
        out.append(hand_over(buf, lanes, ss, rs, 3))

    def rows_here(buf, lanes, rs):
        for k in range(nd):
            arrived(rows_at(buf, lanes, 2 * k + 1), rs.at[2 * k + 1])

    put_turned(R.tokens[...], 0)
    put_turned(R.normed_b[...], 1)
    put_turned(R.hid_f[...], 2)
    turned = send_turned(0, 3, R.lt_ss, R.lt_rs)
    R.ra[0:C, 0:HD] = R.att_b[...].astype(BF16)
    R.ra[0:C, HD : HD + LANES] = gates.astype(BF16)
    RA = slice(0, HD + LANES)
    ra_out = send_rows(R.ra, RA, R.ra_ss, R.ra_rs)

    for cp in wx:
        cp.wait()

    least = jnp.minimum(z, nz - 1 - z)
    inner = least > 0
    left_half = z < nz // 2
    near = jnp.where(inner, jnp.where(left_half, 0, nz - 1), jnp.where(left_half, 1, nz - 2))
    fellow = jnp.where(left_half, nz // 2, nz // 2 - 1)
    far = jnp.where(left_half, nz - 1, 0)

    def origin(k):
        paired = k <= 2 * least
        dist = jnp.where(paired, (k + 1) // 2, k - least)
        left = jnp.where(paired, lax.rem(k, 2) == 1, z > nz - 1 - z)
        return jnp.where(k == 0, z, jnp.where(left, z - dist, z + dist))

    def expert_block(k, carry):
        o = origin(k)
        rows = pl.ds(times(o, C), C)

        @pl.when((k == 1) & inner)
        def _():
            gather_on(R.hidb, R.hid_ss, R.hid_rs, origin(1))

        @pl.when((k > 0) & (k + inner.astype(jnp.int32) < nz))
        def _():
            gather_on(R.hidb, R.hid_ss, R.hid_rs, origin(k + inner.astype(jnp.int32)))

        @pl.when(k == 1)
        def _():
            for far_step in range(2, nz - 1):
                gather_step(R.cotb, R.cot_ss, R.cot_rs, far_step)

        @pl.when(k > 0)
        def _():
            @pl.when((o == z - nz + 1) | (o == z + nz - 1))
            def _():
                arrived(block(R.cotb, o), R.cot_rs.at[o])

            arrived(R.maskb.at[o], R.mask_rs.at[o])

        hb = R.hidb[rows, :]
        cb = R.cotb[rows, :]
        named = R.maskb[o].astype(F32)
        named = jnp.concatenate([named, jnp.zeros((LANES - pad_e, C), F32)], axis=0).T
        g = sigmoid(mm(hb, R.wrl_b[...])) * named
        glog = jnp.zeros((C, LANES), F32)
        for q in range(2):
            cols = slice(q * HF, (q + 1) * HF)
            raised = mm(hb, R.wup_b[:, cols])
            back = mm(cb, R.wdn_b[:, cols])
            for i in range(local):
                j = q * local + i
                u = raised[:, i * DH : (i + 1) * DH]
                a = back[:, i * DH : (i + 1) * DH]
                gj = column(g, j)
                s = sigmoid(u)
                act = u * s
                lo = j * DH
                R.gact[rows, lo : lo + DH] = (gj * act).astype(BF16)
                R.gra[rows, lo : lo + DH] = (gj * a * (s * (1.0 + u * (1.0 - s)))).astype(BF16)
                gg = jnp.sum(a * act, axis=1, keepdims=True)
                glog = jnp.where(lane == j, jnp.broadcast_to(gg, (C, LANES)), glog)
        glog = glog * g * (1.0 - g)
        low = glog.astype(BF16)
        R.glog_s[o] = glog.T[0:pad_e, :].astype(BF16)
        for b in range(2):
            cols = slice(b * half_d, (b + 1) * half_d)
            gh = mm_t(R.gra[rows, :], R.wup_b[cols, :]) + mm_t(low, R.wrl_b[cols, :])
            R.gh_s[o, :, cols] = gh.astype(BF16)

        @pl.when(k > 0)
        def _():
            remote(
                R.glog_s.at[o], R.glog_r.at[z], R.gl_ss.at[o], R.gl_rs.at[z], dev(p, o, c)
            ).start()

        @pl.when((k > 0) & (least == 0) & (o != fellow))
        def _():
            send_back(o)

        @pl.when((k > 0) & (least == 0) & (o == fellow))
        def _():
            send_by(o, near, 0)

        @pl.when((k > 0) & inner & (o == far))
        def _():
            send_by(o, fellow, 1)

        @pl.when((k == 2) & (least == 0))
        def _():
            there = pl.ds(times(near, C), C)
            for b in range(2):
                cols = slice(b * half_d, (b + 1) * half_d)
                R.out_s[near, :, cols] = mm_t(R.gact[there, :], R.wdn_b[cols, :]).astype(BF16)
            slot = jnp.where(z == 0, near, nz)
            remote(
                R.out_s.at[near],
                R.out_r.at[slot],
                R.out_ss.at[near],
                R.out_rs.at[slot],
                dev(p, near, c),
            ).start()

        return carry

    def send_back(o):
        remote(R.gh_s.at[o], R.gh_r.at[z], R.gh_ss.at[o], R.gh_rs.at[z], dev(p, o, c)).start()

    def send_by(o, by, slot):
        remote(
            R.gh_s.at[o], R.gh_x.at[slot], R.gh_ss.at[o], R.gx_rs.at[slot], dev(p, by, c)
        ).start()

    def relay_back(o, slot):
        arrived(R.gh_x.at[slot], R.gx_rs.at[slot])
        R.gh_s[o] = (R.gh_s[o].astype(F32) + R.gh_x[slot].astype(F32)).astype(BF16)
        send_back(o)

    lax.fori_loop(0, nz, expert_block, 0)

    pairs = {}

    def rows_of(at):
        return pl.ds(times(at, rows_d), rows_d)


    rows_d = D // nd
    plane_out = []

    def half(cc):
        return pl.ds(times(cc, HF), HF)

    def grad_at(i, k, cc):
        if i == 0 and k == 3:
            return R.dg.at[:, half(cc)]
        return (R.wdn_b, R.wup_b)[i].at[rows_of(plane(k)), half(cc)]

    def expert_grad(i, k):
        left, right = ((R.cotb, R.gact), (R.hidb, R.gra))[i]
        for cc in (sib, c):
            grad_at(i, k, cc)[...] = tmm(left[:, rows_of(plane(k))], right[:, half(cc)]).astype(BF16)
            if cc is sib:
                cp = remote(
                    grad_at(i, k, sib),
                    R.pair_r.at[i, k],
                    R.pair_ss.at[i, k],
                    R.pair_rs.at[i, k],
                    dev(p, z, sib),
                )
                cp.start()
                pairs[i, k] = cp

    def pair_sum(i, k):
        pairs[i, k].wait()
        own = grad_at(i, k, c)
        own[...] = (own[...].astype(F32) + R.pair_r[i, k].astype(F32)).astype(BF16)

    def part_on(i, k, to, slot):
        cp = remote(
            grad_at(i, k, c),
            R.eg_r.at[slot, i],
            R.eg_ss.at[slot, i],
            R.eg_rs.at[slot, i],
            dev(plane(to), z, c),
        )
        cp.start()
        plane_out.append(cp)

    def expert_grad_relay(i):
        first, second = (1, 2) if i == 0 else (2, 1)
        part_on(i, first, first, 0)
        arrived(R.eg_r.at[1, i], R.eg_rs.at[1, i])
        own = grad_at(i, second, c)
        own[...] = (own[...].astype(F32) + R.eg_r[1, i].astype(F32)).astype(BF16)
        part_on(i, second, second, 2)

    def to_place(own, got, ss, rs, o):
        remote(own(o), got(z), ss.at[o], rs.at[z], dev(p, o, c)).start()

    def run(own, got, ss, rs, k, n):
        def hand(d, slot, to):
            if k > 1:
                arrived(got(d), rs.at[d])
                own(d)[...] = (own(d)[...].astype(F32) + got(d)[...].astype(F32)).astype(BF16)
            remote(own(d), got(slot), ss.at[d], rs.at[slot], dev(p, to, c)).start()

        @pl.when(z == k - 1)
        def _():
            hand(nz - 1 - n, nz - 1 - n, k)

        @pl.when(z == nz - k)
        def _():
            hand(n, nz if n == nz - k - 1 else n, nz - k - 1)

    def run_end(total, got, rs):
        for there, slot in ((z > 0, z), (z < nz - 1, nz)):

            @pl.when(there)
            def _():
                arrived(got(slot), rs.at[slot])
                total[...] += got(slot)[...].astype(F32)

    out_sum = (lambda d: R.out_s.at[d], lambda d: R.out_r.at[d], R.out_ss, R.out_rs)
    out_run = functools.partial(run, *out_sum)

    def grad_sum(i, lanes):
        return (
            lambda d: R.pb.at[d * S : (d + 1) * S, lanes],
            lambda d: R.pn.at[i, d],
            R.pn_ss.at[i],
            R.pn_rs.at[i],
        )

    def part_sum(i, lanes):
        return (
            lambda o: R.pb.at[pl.ds(times(o, S), S), lanes],
            lambda o: R.pr.at[o, :, slice(lanes.start - 2 * EV, lanes.stop - 2 * EV)],
            R.p_ss.at[i],
            R.p_rs.at[i],
        )

    hand_near(R.ra, RA, R.ra_ss, R.ra_rs, ra_out, 2)
    expert_grad(1, 3)
    expert_grad(0, 3)
    for i, to in ((1, 2), (0, 1)):
        pair_sum(i, 3)
        part_on(i, 3, to, 1)

    def out_tile(t, carry):
        rows = pl.ds(times(t, 256), 256)
        got = mm_t(R.gact[...], R.wdn_b[rows, :]).astype(BF16)
        for o in range(nz):

            @pl.when(inner | (o != near))
            def _():
                R.out_s[o, :, rows] = got[o * C : (o + 1) * C, :]

        return carry

    lax.fori_loop(0, D // 256, out_tile, 0)
    out_run(1, 0)

    @pl.when(inner)
    def _():
        relay_back(near, 1)
        relay_back(fellow, 0)

    for k in (1, 2, 0):
        expert_grad(1, k)
        expert_grad(0, k)
    for k in (1, 2, 0):
        pair_sum(1, k)
        pair_sum(0, k)
    hand_far(R.ra, RA, R.ra_ss, R.ra_rs, ra_out)

    R.ghid_f[...] = R.cotb[pl.ds(times(z, C), C), :].astype(F32) + R.gh_s[z].astype(F32)

    def add_back(o):
        arrived(R.gh_r.at[o], R.gh_rs.at[o])
        R.ghid_f[...] += R.gh_r[o].astype(F32)

    add_back(near)
    add_back(jnp.where(inner, fellow, far))

    for k in range(1, nz):
        o = line(k)
        arrived(R.glog_r.at[o], R.gl_rs.at[o])
    out_run(1, 1)
    R.glog_r[z] = R.glog_s[z]
    R.ghid_b[...] = R.ghid_f[...].astype(BF16)
    put_turned(R.ghid_f[...], 3)
    turned_late = send_turned(3, 4, R.ltl_ss, R.ltl_rs)
    out_run(2, 0)

    gates = R.gate_b[...]
    small = jnp.zeros((C, LANES), F32)
    gatt = [None] * H
    for x in range(EA):
        gmix = mm(R.ghid_b[...], R.wo_b[:, x * HD : (x + 1) * HD])
        for h in range(H):
            hs = slice(h * DH, (h + 1) * DH)
            j = GATE + x * H + h
            term = column(gates, j) * gmix[:, hs]
            gatt[h] = term if x == 0 else gatt[h] + term
            gg = jnp.sum(gmix[:, hs] * R.att_b[:, hs], axis=1, keepdims=True)
            small = jnp.where(lane == j, jnp.broadcast_to(gg, (C, LANES)), small)
    for h in range(H):
        hs = slice(h * DH, (h + 1) * DH)
        low = gatt[h].astype(BF16)
        R.gatt_b[:, hs] = low
        gval = tmm(R.prob_b[h].astype(BF16), low)
        R.gval_f[:, hs] = gval
        R.rb[0:C, hs] = gval.astype(BF16)
        for x in range(EA):
            lo = x * HD + h * DH
            j = x * H + h
            gg = jnp.sum(gval * R.val_b[:, lo : lo + DH], axis=1, keepdims=True)
            small = jnp.where(lane == j, jnp.broadcast_to(gg, (C, LANES)), small)
    small = small * gates * (1.0 - gates)
    glog = jnp.concatenate(
        [jnp.zeros((2 * GATE, C), F32)]
        + [R.glog_r[o].astype(F32) for o in range(nz)]
        + [jnp.zeros((LANES - 2 * GATE - nz * pad_e, C), F32)],
        axis=0,
    )
    R.small_b[...] = small.astype(BF16)
    R.rb[0:C, HD : HD + LANES] = (small + glog.T).astype(BF16)
    RV = slice(0, HD + LANES)
    rv_out = send_rows(R.rb, RV, R.rv_ss, R.rv_rs, (1, 2, 3))

    q0 = HD + LANES
    for h in range(H):
        hs = slice(h * DH, (h + 1) * DH)
        low = R.gatt_b[:, hs]
        gsh = mm_t(low, R.v_b[:, hs])
        prob = R.prob_b[h]
        centre = jnp.sum(prob * gsh, axis=-1, keepdims=True)
        gs = (prob * (gsh - centre)).astype(BF16)
        R.rb[0:C, q0 + h * DH : q0 + (h + 1) * DH] = rot_back(
            mm(gs, R.k_b[:, hs]) * scale
        ).astype(BF16)
        R.rb[0:C, q0 + HD + h * DH : q0 + HD + (h + 1) * DH] = rot_back(
            tmm(gs, R.q_b[:, hs])
        ).astype(BF16)
    RQ, RK = slice(q0, q0 + HD), slice(q0 + HD, q0 + 2 * HD)
    rq_out = send_rows(R.rb, RQ, R.rq_ss, R.rq_rs)
    rk_out = send_rows(R.rb, RK, R.rk_ss, R.rk_rs)

    gproj = mm_t(R.rb[0:C, q0 : q0 + 2 * HD], R.wqk_b[...])
    standard = R.std_b[...]
    column_sum = jnp.sum(gproj * standard, axis=0, keepdims=True)
    for b in range(D // LANES):
        R.gp[0, b : b + 1, :] = column_sum[:, b * LANES : (b + 1) * LANES]
    gain_out = []
    for k, dc in plane_all:
        slot = 2 * k + dc
        cp = remote(
            R.gp.at[0], R.gp.at[slot], R.gp_ss.at[slot], R.gp_rs.at[slot], dev(plane(k), z, side(dc))
        )
        cp.start()
        gain_out.append(cp)

    out_run(2, 1)
    for cp in turned:
        cp.wait()
    rows_here(R.ra, RA, R.ra_rs)
    for cp in turned_late:
        cp.wait()

    def turned_of(w):
        return jnp.concatenate(
            [R.ltr[s, :, w * LANES : (w + 1) * LANES] for s in range(2 * nd)], axis=1
        )

    def send_part(part, lanes):
        for o in (far, fellow, near):
            to_place(*part_sum(part, lanes), o)

    def gated_grad(w, rows_of, g0, at):
        left = turned_of(w)
        for x in range(EA):
            right = []
            for h in range(H):
                gx = column(R.ra[:, HD : HD + LANES], g0 + x * H + h).astype(F32)
                right.append((gx * rows_of[:, h * DH : (h + 1) * DH].astype(F32)).astype(BF16))
            right = jnp.concatenate(right, axis=1)
            R.pb[:, at + x * HD : at + (x + 1) * HD] = mm(left, right).astype(BF16)

    PO, PV, PQ, PS = (
        slice(0, EV),
        slice(EV, 2 * EV),
        slice(2 * EV, 2 * EV + 2 * HD),
        slice(2 * EV + 2 * HD, 2 * EV + 2 * HD + LANES),
    )
    gated_grad(3, R.ra, GATE, 0)
    o_run = functools.partial(run, *grad_sum(0, PO))
    v_run = functools.partial(run, *grad_sum(1, PV))
    for n in range(nz - 1):
        o_run(1, n)

    out_run(3, 0)
    hand_near(R.rb, RV, R.rv_ss, R.rv_rs, rv_out, 0)
    hand_far(R.rb, RV, R.rv_ss, R.rv_rs, rv_out)
    o_run(2, 0)
    rows_here(R.rb, RV, R.rv_rs)
    gated_grad(0, R.rb, 0, EV)
    for n in range(nz - 1):
        v_run(1, n)
    o_run(2, 1)
    hand_near(R.rb, RK, R.rk_ss, R.rk_rs, rk_out, 2)
    hand_near(R.rb, RQ, R.rq_ss, R.rq_rs, rq_out, 1)
    expert_grad_relay(0)
    expert_grad_relay(1)
    o_run(3, 0)
    total = R.gp[0]
    for cp, (k, dc) in zip(gain_out, plane_all):
        cp.wait()
        total = total + R.gp[2 * k + dc]
    R.gz_s[...] = total
    for k in range(1, nz):
        o = line(k)
        remote(R.gz_s, R.gz.at[z], R.gz_ss.at[o], R.gz_rs.at[z], dev(p, o, c)).start()

    lane_s = iota((SL, LANES), 1)
    small_t = mm(turned_of(0), R.rb[:, HD : HD + LANES])
    small_h = mm(turned_of(2), R.rb[:, HD : HD + LANES])
    R.pb[:, PS] = jnp.where(lane_s < 2 * GATE, small_t, small_h).astype(BF16)
    send_part(1, PS)
    hand_far(R.rb, RQ, R.rq_ss, R.rq_rs, rq_out)
    hand_far(R.rb, RK, R.rk_ss, R.rk_rs, rk_out)
    rows_here(R.rb, RQ, R.rq_rs)
    rows_here(R.rb, RK, R.rk_rs)
    left = turned_of(1)
    for b in range(2):
        lo = q0 + b * HD
        R.pb[:, 2 * EV + b * HD : 2 * EV + (b + 1) * HD] = mm(left, R.rb[:, lo : lo + HD]).astype(
            BF16
        )
    v_run(2, 0)
    send_part(0, PQ)
    v_run(2, 1)
    v_run(3, 0)


    inputs = R.tokens[...].astype(F32)
    centred = inputs - jnp.mean(inputs, axis=-1, keepdims=True)
    inverse = lax.rsqrt(jnp.mean(centred * centred, axis=-1, keepdims=True) + norm_eps)
    gs = gproj * R.gain[...]
    gtok = R.ghid_f[...] + inverse * (
        gs
        - jnp.mean(gs, axis=-1, keepdims=True)
        - standard * jnp.mean(gs * standard, axis=-1, keepdims=True)
    )
    R.gtok[...] = gtok
    for x in range(EA):
        for h in range(H):
            lo = x * HD + h * DH
            R.mix_b[:, lo : lo + DH] = (
                column(gates, x * H + h) * R.gval_f[:, h * DH : (h + 1) * DH]
            ).astype(BF16)
    for b in range(2):
        cols = slice(b * half_d, (b + 1) * half_d)
        R.gtok[:, cols] += mm_t(R.mix_b[...], R.wv_b[cols, :]) + mm_t(
            R.small_b[...], R.wg_b[cols, :]
        )

    R.hid_f[...] += R.out_s[z].astype(F32)
    run_end(R.hid_f, out_sum[1], R.out_rs)
    R.mixed[...] = R.hid_f[...].astype(BF16)

    for k in range(1, nz):
        o = line(k)
        arrived(R.gz.at[o], R.gz_rs.at[o])
        total = total + R.gz[o]
    first = (p * 2 * nz + z * 2 + c) * S
    pick_row = iota((D // LANES, LANES), 0) == first // LANES
    line_sum = jnp.sum(jnp.where(pick_row, total, 0.0), axis=0, keepdims=True)
    shift = lax.rem(LANES - lax.rem(first, LANES), LANES)
    line_sum = pltpu.roll(jnp.broadcast_to(line_sum, (8, LANES)), shift, 1)
    R.ggain[...] = line_sum[0:1, 0:S]

    own_rows = pl.ds(times(z, S), S)

    def line_total(part, lanes):
        got = R.pb[own_rows, lanes].astype(F32)
        for k in range(1, nz):
            o = line(k)
            there = part_sum(part, lanes)[1](o)
            arrived(there, R.p_rs.at[part, o])
            got = got + there[...].astype(F32)
        return got

    for i, (dst, lanes) in enumerate(((R.go, PO), (R.gv, PV))):
        dst[...] = R.pb[own_rows, lanes].astype(F32)
        run_end(dst, grad_sum(i, lanes)[1], R.pn_rs.at[i])
    got = line_total(1, PS)

    def pick(width, source):
        a, b = iota((width, LANES), 1), iota((width, LANES), 0)
        return jnp.where(a == source(b), 1.0, 0.0).astype(F32)

    def picked(left, right):
        return lax.dot_general(
            left,
            right,
            (((1,), (1,)), ((), ())),
            preferred_element_type=F32,
            precision=lax.Precision.HIGHEST,
        )

    def router_lane(b):
        at = jnp.zeros_like(b)
        for o in range(nz):
            at = jnp.where(b >= o * own_e, 2 * GATE + o * pad_e + b - o * own_e, at)
        return at

    R.gvg[...] = picked(pick(GATE, lambda b: b), got)
    R.gog[...] = picked(pick(GATE, lambda b: b + GATE), got)
    R.gr[...] = picked(got, pick(experts, router_lane))
    got = line_total(0, PQ)
    R.gq[...] = got[:, 0:HD]
    R.gk[...] = got[:, HD : 2 * HD]

    for i, (buf, dst) in enumerate(((R.wdn_b, R.gdn), (R.wup_b, R.gup))):
        for slot in (0, 2):
            arrived(R.eg_r.at[slot, i], R.eg_rs.at[slot, i])
        rows = rows_of(p)
        for x in range(local):
            got = buf[rows, pl.ds(times(c * local + x, DH), DH)].astype(F32)
            for slot in (0, 2):
                got = got + R.eg_r[slot, i, :, x * DH : (x + 1) * DH].astype(F32)
            dst[x] = got

    gather_end(R.cotb, R.cot_ss)
    gather_end(R.hidb, R.hid_ss)
    for cp in masks + ra_out + rv_out + rq_out + rk_out + plane_out:
        cp.wait_send()
    for k in range(1, nz):
        o = line(k)
        sent(R.gh_s.at[o], R.gh_ss.at[o])
        sent(R.glog_s.at[o], R.gl_ss.at[o])
        sent(R.out_s.at[o], R.out_ss.at[o])
        sent(R.gz_s, R.gz_ss.at[o])
        for lanes, ss in (
            (PO, R.pn_ss.at[0]),
            (PV, R.pn_ss.at[1]),
            (PQ, R.p_ss.at[0]),
            (PS, R.p_ss.at[1]),
        ):
            sent(R.pb.at[pl.ds(times(o, S), S), lanes], ss.at[o])


def settle_kernel(*refs):
    n = len(refs) // 2
    for src, dst in zip(refs[:n], refs[n:]):
        dst[...] = src[...]


def fused_layer(nd, nz, *args):
    (tokens, cotangent, seq_lengths, routes, head_experts, norm_gain) = args[:6]
    (w_query, w_key, w_value, w_output, w_value_gate, w_output_gate, w_router) = args[6:13]
    w_up, w_down = args[13:]
    C = tokens.shape[0]
    local = w_up.shape[0]
    experts = w_router.shape[1]
    own_e = 2 * local
    pad_e = -(-own_e // 16) * 16
    EF, HF, HD = own_e * DH, local * DH, H * DH
    EV = EA * HD
    S = D // (nd * nz * 2)
    SL = S * nz
    PW = 2 * EV + 2 * HD + LANES
    s = Scratch()
    s.vmem("wqk_b", (D, 2 * HD), BF16)
    s.vmem("wv_b", (D, EV), BF16)
    s.vmem("wo_b", (D, EV), BF16)
    s.vmem("wup_b", (D, EF), BF16)
    s.vmem("wdn_b", (D, EF), BF16)
    s.vmem("wg_b", (D, LANES), BF16)
    s.vmem("wrl_b", (D, LANES), BF16)
    s.vmem("cotb", (nz * C, D), BF16)
    s.vmem("hidb", (nz * C, D), BF16)
    s.vmem("mask_s", (nz, pad_e, C), BF16)
    s.vmem("maskb", (nz, pad_e, C), BF16)
    s.vmem("std_b", (C, D), F32)
    s.vmem("normed_b", (C, D), BF16)
    s.vmem("q_b", (C, HD), BF16)
    s.vmem("k_b", (C, HD), BF16)
    s.vmem("v_b", (C, HD), BF16)
    s.vmem("gate_b", (C, LANES), F32)
    s.vmem("val_b", (C, EV), F32)
    s.vmem("prob_b", (H, C, C), F32)
    s.vmem("att_b", (C, HD), F32)
    s.vmem("mix_b", (C, EV), BF16)
    s.vmem("hid_f", (C, D), F32)
    s.vmem("lt", (D, 4 * LANES), BF16)
    s.vmem("ltr", (2 * nd, SL, 4 * LANES), BF16)
    s.vmem("ra", (2 * nd * C, HD + LANES), BF16)
    s.vmem("rb", (2 * nd * C, 3 * HD + LANES), BF16)
    s.vmem("gact", (nz * C, EF), BF16)
    s.vmem("gra", (nz * C, EF), BF16)
    for name in ("gh_s", "gh_r", "out_s"):
        s.vmem(name, (nz, C, D), BF16)
    s.vmem("out_r", (nz + 1, C, D), BF16)
    s.vmem("gh_x", (2, C, D), BF16)
    for name in ("glog_s", "glog_r"):
        s.vmem(name, (nz, pad_e, C), BF16)
    s.vmem("dg", (D // nd, EF), BF16)
    s.vmem("pair_r", (2, nd, D // nd, HF), BF16)
    s.vmem("eg_r", (nd - 1, 2, D // nd, HF), BF16)
    s.vmem("ghid_f", (C, D), F32)
    s.vmem("ghid_b", (C, D), BF16)
    s.vmem("gatt_b", (C, HD), BF16)
    s.vmem("gval_f", (C, HD), F32)
    s.vmem("small_b", (C, LANES), BF16)
    s.vmem("pb", (SL, PW), BF16)
    s.vmem("pr", (nz, S, PW - 2 * EV), BF16)
    s.vmem("pn", (2, nz + 1, S, EV), BF16)
    s.vmem("gp", (2 * nd, D // LANES, LANES), F32)
    s.vmem("gz_s", (D // LANES, LANES), F32)
    s.vmem("gz", (nz, D // LANES, LANES), F32)
    s.sems("ld", 4 + 2 * local)
    s.sems("gx_rs", 2)
    s.sems("out_rs", nz + 1)
    for name in ("cot_ss", "hid_ss"):
        s.sems(name, 2, nz)
    for name in ("cot_rs", "hid_rs", "mask_ss", "mask_rs", "gh_ss", "gh_rs", "gl_ss", "gl_rs", "out_ss", "gz_ss", "gz_rs"):
        s.sems(name, nz)
    for name in ("w_ss", "w_rs"):
        s.sems(name, 2)
    for name in ("pair_ss", "pair_rs"):
        s.sems(name, 2, nd)
    for name in ("lt_ss", "lt_rs", "ltl_ss", "ltl_rs", "gp_ss", "gp_rs", "ra_ss", "ra_rs", "rv_ss", "rv_rs", "rq_ss", "rq_rs", "rk_ss", "rk_rs"):
        s.sems(name, 2 * nd)
    for name in ("eg_ss", "eg_rs"):
        s.sems(name, nd - 1, 2)
    for name in ("p_ss", "p_rs", "pn_ss"):
        s.sems(name, 2, nz)
    s.sems("pn_rs", 2, nz + 1)

    def out(*shape, dtype=F32):
        return jax.ShapeDtypeStruct(shape, dtype)

    vmem = pl.BlockSpec(memory_space=pltpu.VMEM)
    smem = pl.BlockSpec(memory_space=pltpu.SMEM)
    hbm = pl.BlockSpec(memory_space=pl.ANY)
    outs = pl.pallas_call(
        functools.partial(layer_kernel, INPUTS + OUTPUTS + tuple(s.names), nd, nz, local),
        out_shape=(
            out(C, D, dtype=BF16),
            out(C, D),
            out(1, S),
            out(S, HD),
            out(S, HD),
            out(S, EV),
            out(S, EV),
            out(EA * H, S),
            out(EA * H, S),
            out(S, experts),
            out(local, D // nd, DH),
            out(local, D // nd, DH),
        ),
        in_specs=[vmem, vmem, smem] + [vmem] * 6 + [hbm] * 6,
        out_specs=[vmem] * 12,
        scratch_shapes=s.shapes,
        compiler_params=pltpu.CompilerParams(
            collective_id=0, has_side_effects=True, vmem_limit_bytes=VMEM_LIMIT
        ),
    )(
        tokens,
        cotangent,
        seq_lengths,
        routes.T,
        head_experts.reshape(C, 2 * H).T,
        norm_gain.reshape(1, D),
        w_value_gate.T,
        w_output_gate.T,
        w_router.T,
        w_query,
        w_key,
        w_value,
        w_output,
        w_up,
        w_down,
    )
    outs = list(
        pl.pallas_call(
            settle_kernel,
            out_shape=[out(*x.shape, dtype=x.dtype) for x in outs],
            in_specs=[vmem] * 12,
            out_specs=[vmem] * 12,
            compiler_params=pltpu.CompilerParams(vmem_limit_bytes=VMEM_LIMIT),
        )(*outs)
    )
    outs[2] = outs[2].reshape(S)
    for i in (7, 8):
        outs[i] = outs[i].T
    return tuple(outs)


VMEM_LIMIT = 62 * 1024 * 1024


def fits(nd, nz, count, experts):
    own_e = experts // nz
    pad_e = -(-own_e // 16) * 16
    return (
        count == LANES
        and nz == 4
        and nd == 4
        and own_e % 4 == 0
        and D % (nd * nz * 2 * 16) == 0
        and LANES % (D // (nd * nz * 2)) == 0
        and 2 * EA * H + nz * pad_e <= LANES
    )


def per_device(nd, ne, *args):
    count, experts = args[0].shape[0], args[12].shape[1]
    if ne % 2 == 0 and fits(nd, ne // 2, count, experts):
        return fused_layer(nd, ne // 2, *args)
    return routed_layer(*args)


def solution(mesh):
    return jax.shard_map(
        functools.partial(per_device, mesh.shape["dp"], mesh.shape["expert"]),
        mesh=mesh,
        in_specs=(
            P(("dp", "expert"), None),
            P(("dp", "expert"), None),
            P(("dp", "expert"), None),
            P(("dp", "expert"), None),
            P(("dp", "expert"), None, None),
            P(),
            P(),
            P(),
            P(),
            P(),
            P(),
            P(),
            P(),
            P("expert", None, None),
            P("expert", None, None),
        ),
        out_specs=(
            P(("dp", "expert"), None),
            P(("dp", "expert"), None),
            P(("dp", "expert")),
            P(("dp", "expert"), None),
            P(("dp", "expert"), None),
            P(("dp", "expert"), None),
            P(("dp", "expert"), None),
            P(("dp", "expert"), None),
            P(("dp", "expert"), None),
            P(("dp", "expert"), None),
            P("expert", "dp", None),
            P("expert", "dp", None),
        ),
        check_vma=False,
    )
```

```python
import functools
import math

import jax
import jax.numpy as jnp
from jax import lax
from jax.experimental import pallas as pl
from jax.experimental.pallas import tpu as pltpu
from jax.sharding import PartitionSpec as P

D = 1024
H = 4
DH = 128
EA = 5
TOPK = 16


norm_eps = 1e-05
rope_base = 10000.0
masked_score = -1e30


def sequence_layout(lengths, count):
    bounds = jnp.cumsum(lengths)
    starts = bounds - lengths
    places = jnp.arange(count, dtype=jnp.int32)
    seq_ids = jnp.sum((places[:, None] >= bounds[None, :]).astype(jnp.int32), axis=1)
    live = places < bounds[-1]
    slot_ids = jnp.arange(lengths.shape[0], dtype=jnp.int32)
    first = jnp.sum(jnp.where(seq_ids[:, None] == slot_ids[None, :], starts[None, :], 0), axis=1)
    positions = jnp.where(live, places - first, 0)
    return (seq_ids, live, positions)


def rope_tables(positions, width):
    half = width // 2
    freq = rope_base ** (-(jnp.arange(half, dtype=jnp.float32) * 2.0 / width))
    angles = positions.astype(jnp.float32)[:, None] * freq[None, :]
    return (jnp.cos(angles), jnp.sin(angles))


def rotate(field, cosine, sine):
    half = field.shape[-1] // 2
    first, second = (field[..., :half], field[..., half:])
    cos_h, sin_h = (cosine[:, None, :], sine[:, None, :])
    return jnp.concatenate(
        [first * cos_h - second * sin_h, second * cos_h + first * sin_h], axis=-1
    )


def rotate_back(field, cosine, sine):
    half = field.shape[-1] // 2
    first, second = (field[..., :half], field[..., half:])
    cos_h, sin_h = (cosine[:, None, :], sine[:, None, :])
    return jnp.concatenate(
        [first * cos_h + second * sin_h, second * cos_h - first * sin_h], axis=-1
    )


def slot_tables(routes, experts, most):
    count = routes.shape[0] * routes.shape[1]
    flat = routes.reshape(count)
    order = jnp.argsort(flat, stable=True)
    ordered = flat[order]
    firsts = jnp.searchsorted(ordered, jnp.arange(experts, dtype=jnp.int32))
    ranks = jnp.arange(count, dtype=jnp.int32) - firsts[ordered]
    sorted_slots = ordered * most + ranks
    slot_of_row = jnp.zeros((count,), jnp.int32).at[order].set(sorted_slots)
    row_of_slot = jnp.full((experts * most,), count, jnp.int32).at[sorted_slots].set(order)
    return (slot_of_row, row_of_slot)


def routed_layer(
    tokens,
    cotangent,
    seq_lengths,
    routes,
    head_experts,
    norm_gain,
    w_query,
    w_key,
    w_value,
    w_output,
    w_value_gate,
    w_output_gate,
    w_router,
    w_up,
    w_down,
):
    f32 = jnp.float32
    bf16 = jnp.bfloat16
    count = tokens.shape[0]
    experts = w_router.shape[1]
    local_experts = w_up.shape[0]
    owners = lax.axis_size("expert")
    most = 3 * count * TOPK // (2 * experts)
    routed = count * TOPK
    block = min(512, count)
    block_starts = jnp.arange(count // block, dtype=jnp.int32) * block
    scale = DH ** (-0.5)
    contract_last = (((1,), (1,)), ((), ()))
    contract_first = (((0,), (0,)), ((), ()))
    seq_ids, live, positions = sequence_layout(seq_lengths[0], count)
    cosine, sine = rope_tables(positions, DH)
    inputs = tokens.astype(f32)
    centred = inputs - jnp.mean(inputs, axis=-1, keepdims=True)
    inverse = lax.rsqrt(jnp.mean(centred * centred, axis=-1, keepdims=True) + norm_eps)
    standard = centred * inverse
    normed = (standard * norm_gain).astype(bf16)
    query_proj = jnp.dot(normed, w_query, preferred_element_type=f32).reshape(count, H, DH)
    key_proj = jnp.dot(normed, w_key, preferred_element_type=f32).reshape(count, H, DH)
    query_rot = (rotate(query_proj, cosine, sine) * scale).astype(bf16)
    key_rot = rotate(key_proj, cosine, sine).astype(bf16)
    chosen = jnp.any(
        head_experts[:, None, :, :] == jnp.arange(EA, dtype=jnp.int32)[None, :, None, None], axis=-1
    )
    value_gates = jnp.where(
        chosen,
        jax.nn.sigmoid(
            jnp.dot(tokens, w_value_gate, preferred_element_type=f32).reshape(count, EA, H)
        ),
        0.0,
    )
    output_gates = jnp.where(
        chosen,
        jax.nn.sigmoid(
            jnp.dot(tokens, w_output_gate, preferred_element_type=f32).reshape(count, EA, H)
        ),
        0.0,
    )
    value_all = jnp.dot(tokens, w_value, preferred_element_type=f32).reshape(count, EA, H, DH)
    values = jnp.sum(value_gates[..., None] * value_all, axis=1).astype(bf16)

    def allowed_at(start):
        queries = start + jnp.arange(block, dtype=jnp.int32)
        keys = jnp.arange(count, dtype=jnp.int32)
        same = (
            (seq_ids[:, None] == seq_ids[None, :])
            & (keys[None, :] <= queries[:, None])
            & live[None, :]
        )
        return same | (keys[None, :] == queries[:, None])

    def scores_at(start):
        scores = jnp.einsum("qhd,khd->hqk", query_rot, key_rot, preferred_element_type=f32)
        return (query_rot, jnp.where(allowed_at(start)[None], scores, masked_score))

    def attend(start):
        query_block, scores = scores_at(start)
        highest = jnp.max(scores, axis=-1, keepdims=True)
        shifted = jnp.exp(scores - highest)
        totals = jnp.sum(shifted, axis=-1, keepdims=True)
        shares = (shifted / totals).astype(bf16)
        result = jnp.einsum("hqk,khd->qhd", shares, values, preferred_element_type=f32)
        return (result, (highest + jnp.log(totals))[..., 0])

    attended, log_totals = lax.map(attend, block_starts)
    attended = attended.reshape(count, H, DH)
    log_totals = jnp.transpose(log_totals, (1, 0, 2)).reshape(H, count)
    heads_mixed = (
        (output_gates[..., None] * attended[:, None]).astype(bf16).reshape(count, EA * H * DH)
    )
    hidden = inputs + lax.dot_general(
        heads_mixed, w_output, contract_last, preferred_element_type=f32
    )
    hidden_low = hidden.astype(bf16)
    logits = jnp.dot(hidden_low, w_router, preferred_element_type=f32)
    gates = jax.nn.sigmoid(jnp.take_along_axis(logits, routes, axis=1))
    slot_of_row, row_of_slot = slot_tables(routes, experts, most)
    valid = row_of_slot < routed
    safe_row = jnp.minimum(row_of_slot, routed - 1)
    source = safe_row // TOPK
    outgoing = jnp.where(valid[:, None], hidden_low[source], jnp.zeros((), bf16)).reshape(
        owners, local_experts, most, D
    )

    def expert_apply(items):
        raised = jnp.einsum("nemd,edf->nemf", items, w_up, preferred_element_type=f32)
        active = jax.nn.silu(raised).astype(bf16)
        lowered = jnp.einsum("nemf,edf->nemd", active, w_down, preferred_element_type=f32).astype(
            bf16
        )
        return (lowered, raised)

    lowered, raised = expert_apply(
        lax.all_to_all(outgoing, "expert", split_axis=0, concat_axis=0, tiled=True)
    )
    returned = lax.all_to_all(lowered, "expert", split_axis=0, concat_axis=0, tiled=True).reshape(
        experts * most, D
    )
    expert_rows = returned[slot_of_row].reshape(count, TOPK, D)
    output = hidden + jnp.sum(gates[..., None] * expert_rows, axis=1)
    mixed = output.astype(bf16)
    grad_out = cotangent.astype(f32) * live[:, None].astype(f32)
    grad_gates = jnp.sum(grad_out[:, None, :] * expert_rows, axis=2)
    gate_flat = gates.reshape(routed)
    grad_outgoing = (
        jnp.where(valid[:, None], gate_flat[safe_row][:, None] * grad_out[source], 0.0)
        .astype(bf16)
        .reshape(owners, local_experts, most, D)
    )
    grad_lowered = lax.all_to_all(grad_outgoing, "expert", split_axis=0, concat_axis=0, tiled=True)
    items = lax.all_to_all(outgoing, "expert", split_axis=0, concat_axis=0, tiled=True)
    raised = expert_apply(items)[1]
    grad_active = jnp.einsum("nemd,edf->nemf", grad_lowered, w_down, preferred_element_type=f32)
    sigmoid_raised = jax.nn.sigmoid(raised)
    grad_raised = (grad_active * sigmoid_raised * (1.0 + raised * (1.0 - sigmoid_raised))).astype(
        bf16
    )
    grad_items = jnp.einsum("nemf,edf->nemd", grad_raised, w_up, preferred_element_type=f32).astype(
        bf16
    )
    active = jax.nn.silu(raised).astype(bf16)
    grad_items, grad_raised, active = (grad_items, grad_raised, active)
    grad_items, grad_raised, active, grad_arrived, arrived = (
        grad_items,
        grad_raised,
        active,
        grad_lowered,
        items,
    )
    grad_up_local = jnp.einsum("nemd,nemf->edf", arrived, grad_raised, preferred_element_type=f32)
    grad_down_local = jnp.einsum("nemd,nemf->edf", grad_arrived, active, preferred_element_type=f32)
    grad_up, grad_down = (
        lax.psum_scatter(
            grad_up_local.astype(jnp.bfloat16), "dp", scatter_dimension=1, tiled=True
        ).astype(jnp.float32),
        lax.psum_scatter(
            grad_down_local.astype(jnp.bfloat16), "dp", scatter_dimension=1, tiled=True
        ).astype(jnp.float32),
    )
    grad_back = lax.all_to_all(
        grad_items, "expert", split_axis=0, concat_axis=0, tiled=True
    ).reshape(experts * most, D)
    grad_hidden = grad_out + jnp.sum(
        grad_back[slot_of_row].reshape(count, TOPK, D), axis=1, dtype=f32
    )
    grad_picked = grad_gates * gates * (1.0 - gates)
    expert_ids = jnp.arange(experts, dtype=jnp.int32)
    grad_logits = jnp.sum(
        jnp.where(routes[:, :, None] == expert_ids[None, None, :], grad_picked[..., None], 0.0),
        axis=1,
    ).astype(bf16)
    grad_router = lax.dot_general(
        hidden_low, grad_logits, contract_first, preferred_element_type=f32
    )
    grad_hidden = grad_hidden + lax.dot_general(
        grad_logits, w_router, contract_last, preferred_element_type=f32
    )
    grad_hidden_low = grad_hidden.astype(bf16)
    grad_output = lax.dot_general(
        grad_hidden_low, heads_mixed, contract_first, preferred_element_type=f32
    )
    grad_mixed = jnp.dot(grad_hidden_low, w_output, preferred_element_type=f32).reshape(
        count, EA, H, DH
    )
    grad_attended = jnp.sum(output_gates[..., None] * grad_mixed, axis=1).astype(bf16)
    grad_out_gates = jnp.sum(grad_mixed * attended[:, None], axis=-1)
    grad_out_logits = (
        jnp.where(chosen, grad_out_gates * output_gates * (1.0 - output_gates), 0.0)
        .astype(bf16)
        .reshape(count, EA * H)
    )

    def attend_back(carry, start):
        grad_keys, grad_vals = carry
        query_block, scores = scores_at(start)
        shares = jnp.exp(scores - log_totals[..., None])
        grad_shares = jnp.einsum("qhd,khd->hqk", grad_attended, values, preferred_element_type=f32)
        centre = jnp.sum(shares * grad_shares, axis=-1, keepdims=True)
        grad_scores = (shares * (grad_shares - centre)).astype(bf16)
        grad_query_block = jnp.einsum(
            "hqk,khd->qhd", grad_scores, key_rot, preferred_element_type=f32
        )
        grad_keys = grad_keys + jnp.einsum(
            "hqk,qhd->khd", grad_scores, query_block, preferred_element_type=f32
        )
        grad_vals = grad_vals + jnp.einsum(
            "hqk,qhd->khd", shares.astype(bf16), grad_attended, preferred_element_type=f32
        )
        return ((grad_keys, grad_vals), grad_query_block)

    zero_heads = jnp.zeros((count, H, DH), f32)
    (grad_keys, grad_vals), grad_queries = lax.scan(
        attend_back, (zero_heads, zero_heads), block_starts
    )
    grad_queries = grad_queries.reshape(count, H, DH)
    grad_query_proj = (
        rotate_back(grad_queries * scale, cosine, sine).astype(bf16).reshape(count, H * DH)
    )
    grad_key_proj = rotate_back(grad_keys, cosine, sine).astype(bf16).reshape(count, H * DH)
    grad_value_all = (
        (value_gates[..., None] * grad_vals[:, None]).astype(bf16).reshape(count, EA * H * DH)
    )
    grad_value_gates = jnp.sum(grad_vals[:, None] * value_all, axis=-1)
    grad_value_logits = (
        jnp.where(chosen, grad_value_gates * value_gates * (1.0 - value_gates), 0.0)
        .astype(bf16)
        .reshape(count, EA * H)
    )
    grad_query = lax.dot_general(
        normed, grad_query_proj, contract_first, preferred_element_type=f32
    )
    grad_key = lax.dot_general(normed, grad_key_proj, contract_first, preferred_element_type=f32)
    grad_value = lax.dot_general(tokens, grad_value_all, contract_first, preferred_element_type=f32)
    grad_value_gate = lax.dot_general(
        tokens, grad_value_logits, contract_first, preferred_element_type=f32
    )
    grad_output_gate = lax.dot_general(
        tokens, grad_out_logits, contract_first, preferred_element_type=f32
    )
    grad_normed = lax.dot_general(
        grad_query_proj, w_query, contract_last, preferred_element_type=f32
    ) + lax.dot_general(grad_key_proj, w_key, contract_last, preferred_element_type=f32)
    grad_gain = jnp.sum(grad_normed * standard, axis=0)
    grad_standard = grad_normed * norm_gain
    grad_tokens = grad_hidden + inverse * (
        grad_standard
        - jnp.mean(grad_standard, axis=-1, keepdims=True)
        - standard * jnp.mean(grad_standard * standard, axis=-1, keepdims=True)
    )
    grad_tokens = (
        grad_tokens
        + lax.dot_general(grad_value_all, w_value, contract_last, preferred_element_type=f32)
        + lax.dot_general(
            grad_value_logits, w_value_gate, contract_last, preferred_element_type=f32
        )
        + lax.dot_general(grad_out_logits, w_output_gate, contract_last, preferred_element_type=f32)
    )
    summed = (
        lax.psum_scatter(grad_gain, ("dp", "expert"), scatter_dimension=0, tiled=True),
        lax.psum_scatter(grad_query, ("dp", "expert"), scatter_dimension=0, tiled=True),
        lax.psum_scatter(grad_key, ("dp", "expert"), scatter_dimension=0, tiled=True),
        lax.psum_scatter(grad_value, ("dp", "expert"), scatter_dimension=0, tiled=True),
        lax.psum_scatter(grad_output, ("dp", "expert"), scatter_dimension=0, tiled=True),
        lax.psum_scatter(grad_value_gate, ("dp", "expert"), scatter_dimension=0, tiled=True),
        lax.psum_scatter(grad_output_gate, ("dp", "expert"), scatter_dimension=0, tiled=True),
        lax.psum_scatter(grad_router, ("dp", "expert"), scatter_dimension=0, tiled=True),
    )
    return (
        mixed,
        grad_tokens,
        summed[0],
        summed[1],
        summed[2],
        summed[3],
        summed[4],
        summed[5],
        summed[6],
        summed[7],
        grad_up,
        grad_down,
    )


F32 = jnp.float32
BF16 = jnp.bfloat16
MESH = pl.DeviceIdType.MESH
LANES = 128


def mm(a, b):
    return lax.dot_general(a, b, (((1,), (0,)), ((), ())), preferred_element_type=F32)


def mm_t(a, b):
    return lax.dot_general(a, b, (((1,), (1,)), ((), ())), preferred_element_type=F32)


def tmm(a, b):
    return lax.dot_general(a, b, (((0,), (0,)), ((), ())), preferred_element_type=F32)


def iota(shape, axis):
    return lax.broadcasted_iota(jnp.int32, shape, axis)


def column(x, j, width=LANES):
    return jnp.broadcast_to(x[:, j : j + 1], (x.shape[0], width))


def sigmoid(x):
    return 1.0 / (1.0 + jnp.exp(-x))


class Scratch:
    def __init__(self):
        self.names, self.shapes = [], []

    def add(self, name, shape):
        self.names.append(name)
        self.shapes.append(shape)

    def vmem(self, name, shape, dtype):
        self.add(name, pltpu.VMEM(shape, dtype))

    def sems(self, name, *shape):
        self.add(name, pltpu.SemaphoreType.DMA(shape))


SMALL = ("tokens", "cot", "lens", "rt", "het", "gain", "wvg", "wog", "wr")
WEIGHTS = ("wq", "wk", "wv", "wo", "wu", "wd")
OUTPUTS = ("mixed", "gtok", "ggain", "gq", "gk", "gv", "go", "gvg", "gog", "gr", "gup", "gdn")


def in_hbm(names):
    return tuple(name + "_h" for name in names)


def layer_kernel(names, nd, nz, local, *refs):
    r = dict(zip(names, refs))
    R = type("R", (), r)
    C = R.tokens.shape[0]
    own_e = 2 * local
    pad_e = R.maskb.shape[1]
    EF = own_e * DH
    HF = local * DH
    HD = H * DH
    EV = EA * HD
    S = D // (nd * nz * 2)
    SL = S * nz
    GATE = EA * H
    p = lax.axis_index("dp")
    e = lax.axis_index("expert")
    z = e // 2
    c = e % 2
    sib = 1 - c

    def dev(p_, z_, c_):
        return (p_, z_ * 2 + c_)

    def times(i, n):
        return pl.multiple_of(i * n, n)

    def remote(src, dst, ss, rs, to):
        return pltpu.make_async_remote_copy(
            src_ref=src, dst_ref=dst, send_sem=ss, recv_sem=rs, device_id=to, device_id_type=MESH
        )

    def arrived(dst, rs):
        remote(dst, dst, rs, rs, dev(p, z, sib)).wait_recv()

    def sent(src, ss):
        remote(src, src, ss, ss, dev(p, z, sib)).wait_send()

    beside = p + 1 - 2 * lax.rem(p, 2)
    across = lax.rem(p + 2, nd)
    diagonal = lax.rem(beside + 2, nd)

    def plane(k):
        return (p, beside, across, diagonal)[k]

    def line(k):
        return lax.rem(z + k, nz)

    barrier = pltpu.get_barrier_semaphore()
    partners = [dev(p, z, sib)]
    partners += [dev(p, line(k), c) for k in range(1, nz)]
    for k in range(1, nd):
        partners += [dev(plane(k), z, c), dev(plane(k), z, sib)]
    for to in partners:
        pl.semaphore_signal(barrier, inc=1, device_id=to, device_id_type=MESH)

    loads = {}

    def load(name, src, dst, sem):
        cp = pltpu.make_async_copy(src, dst, sem)
        cp.start()
        loads.setdefault(name, []).append(cp)

    def loaded(name):
        for cp in loads.pop(name):
            cp.wait()

    for i, name in enumerate(("cot", "lens", "rt", "tokens", "gain", "het", "wvg", "wog", "wr")):
        load(name, r[name + "_h"], r[name], R.ld_in.at[i])
    stores = []

    def store(*names):
        for name in names:
            cp = pltpu.make_async_copy(r[name], r[name + "_h"], R.st.at[OUTPUTS.index(name)])
            cp.start()
            stores.append(cp)

    loaded("lens")
    l0 = R.lens[0, 0]
    b1 = l0 + R.lens[0, 1]
    row = iota((C, LANES), 0)
    lane = iota((C, LANES), 1)
    seq_r = (row >= l0).astype(jnp.int32) + (row >= b1).astype(jnp.int32)
    seq_c = (lane >= l0).astype(jnp.int32) + (lane >= b1).astype(jnp.int32)
    live = row < b1
    allowed = ((seq_r == seq_c) & (lane <= row) & (lane < b1)) | (row == lane)
    live_f = jnp.where(live, 1.0, 0.0).astype(F32)
    start = jnp.where(seq_r == 0, 0, l0)
    position = jnp.where(live, row - start, 0).astype(F32)

    loaded("cot")
    for b in range(D // LANES):
        cols = slice(b * LANES, (b + 1) * LANES)
        R.cotb[pl.ds(times(z, C), C), cols] = (R.cot[:, cols].astype(F32) * live_f).astype(BF16)
    load("qk", R.wq, R.wqk_b.at[:, 0:HD], R.ld.at[0])
    load("qk", R.wk, R.wqk_b.at[:, HD : 2 * HD], R.ld.at[1])
    load("v", R.wv, R.wv_b, R.ld.at[2])
    for i in range(local):
        col = times(c * local + i, DH)
        load("up", R.wu.at[i], R.wup_b.at[:, pl.ds(col, DH)], R.ld.at[4 + i])
        load("dn", R.wd.at[i], R.wdn_b.at[:, pl.ds(col, DH)], R.ld.at[4 + local + i])
    load("o", R.wo, R.wo_b, R.ld.at[3])
    loaded("rt")
    ids = iota((pad_e, C), 0)
    for zz in range(nz):
        named = jnp.zeros((pad_e, C), F32)
        for k in range(TOPK):
            hit = jnp.broadcast_to(R.rt[k : k + 1, :], (pad_e, C)) == ids + zz * own_e
            named = jnp.where(hit & (ids < own_e), 1.0, named)
        R.mask_s[zz] = named.astype(BF16)
    R.maskb[z] = R.mask_s[z]

    pl.semaphore_wait(barrier, len(partners))

    def block(buf, o):
        return buf.at[pl.ds(times(o, C), C), :]

    def pass_on(buf, ss, rs, o, right, left):
        @pl.when(right)
        def _():
            remote(block(buf, o), block(buf, o), ss.at[0, o], rs.at[o], dev(p, z + 1, c)).start()

        @pl.when(left)
        def _():
            remote(block(buf, o), block(buf, o), ss.at[1, o], rs.at[o], dev(p, z - 1, c)).start()

    def passed(buf, ss, o, right, left):
        @pl.when(right)
        def _():
            sent(block(buf, o), ss.at[0, o])

        @pl.when(left)
        def _():
            sent(block(buf, o), ss.at[1, o])

    def gather_own(buf, ss, rs):
        pass_on(buf, ss, rs, z, z < nz - 1, z > 0)

    def gather_on(buf, ss, rs, o):
        arrived(block(buf, o), rs.at[o])
        pass_on(buf, ss, rs, o, (o < z) & (z < nz - 1), (o > z) & (z > 0))

    def gather_step(buf, ss, rs, k):
        @pl.when(z >= k)
        def _():
            gather_on(buf, ss, rs, z - k)

        @pl.when(z + k < nz)
        def _():
            gather_on(buf, ss, rs, z + k)

    def gather_end(buf, ss):
        passed(buf, ss, z, z < nz - 1, z > 0)
        for k in range(1, nz):

            @pl.when(z >= k)
            def _():
                passed(buf, ss, z - k, z < nz - 1, False)

            @pl.when(z + k < nz)
            def _():
                passed(buf, ss, z + k, False, z > 0)

    gather_own(R.cotb, R.cot_ss, R.cot_rs)
    masks = []
    for k in range(1, nz):
        o = line(k)
        cp = remote(R.mask_s.at[o], R.maskb.at[z], R.mask_ss.at[k], R.mask_rs.at[z], dev(p, o, c))
        cp.start()
        masks.append(cp)

    for name in ("tokens", "gain", "het", "wvg", "wog", "wr"):
        loaded(name)

    s_row, s_col = iota((GATE, LANES), 0), iota((GATE, LANES), 1)
    to_v = jnp.where(s_row == s_col, 1.0, 0.0).astype(BF16)
    to_o = jnp.where(s_row + GATE == s_col, 1.0, 0.0).astype(BF16)
    R.wg_b[...] = (tmm(R.wvg[...], to_v) + tmm(R.wog[...], to_o)).astype(BF16)
    experts = R.wr.shape[0]
    r_row, r_col = iota((experts, LANES), 0), iota((experts, LANES), 1)
    to_r = jnp.where((r_row == r_col + z * own_e) & (r_col < own_e), 1.0, 0.0).astype(BF16)
    R.wrl_b[...] = tmm(R.wr[...], to_r).astype(BF16)

    half = lax.rem(lane, DH // 2).astype(F32)
    angle = position * jnp.exp(half * (-2.0 / DH * math.log(rope_base)))
    cosine = jnp.cos(angle)
    sine = jnp.where(lane < DH // 2, -jnp.sin(angle), jnp.sin(angle))

    def rot(v):
        return v * cosine + pltpu.roll(v, DH // 2, 1) * sine

    def rot_back(v):
        return v * cosine - pltpu.roll(v, DH // 2, 1) * sine

    inputs = R.tokens[...].astype(F32)
    centred = inputs - jnp.mean(inputs, axis=-1, keepdims=True)
    inverse = lax.rsqrt(jnp.mean(centred * centred, axis=-1, keepdims=True) + norm_eps)
    standard = centred * inverse
    R.std_b[...] = standard
    R.normed_b[...] = (standard * R.gain[...]).astype(BF16)

    loaded("qk")
    scale = DH ** (-0.5)
    qk = mm(R.normed_b[...], R.wqk_b[:, 0:HD])
    for h in range(H):
        hs = slice(h * DH, (h + 1) * DH)
        R.q_b[:, hs] = (rot(qk[:, hs]) * scale).astype(BF16)
    qk = mm(R.normed_b[...], R.wqk_b[:, HD : 2 * HD])
    for h in range(H):
        hs = slice(h * DH, (h + 1) * DH)
        R.k_b[:, hs] = rot(qk[:, hs]).astype(BF16)

    hit = []
    for j in range(GATE):
        x, h = divmod(j, H)
        one = (R.het[2 * h : 2 * h + 1, :] == x) | (R.het[2 * h + 1 : 2 * h + 2, :] == x)
        hit.append(jnp.where(one, 1.0, 0.0).astype(F32))
    hit = jnp.concatenate(hit + hit + [jnp.zeros((LANES - 2 * GATE, C), F32)], axis=0)
    R.gate_b[...] = sigmoid(mm(R.tokens[...], R.wg_b[...])) * hit.T

    loaded("up")
    loaded("dn")
    wx = []
    for i, buf in enumerate((R.wup_b, R.wdn_b)):
        part = buf.at[:, pl.ds(times(c, HF), HF)]
        cp = remote(part, part, R.w_ss.at[i], R.w_rs.at[i], dev(p, z, sib))
        cp.start()
        wx.append(cp)

    loaded("v")
    gates = R.gate_b[...]
    total = [None] * H
    for x in range(EA):
        R.val_b[:, x * HD : (x + 1) * HD] = mm(R.tokens[...], R.wv_b[:, x * HD : (x + 1) * HD])
        for h in range(H):
            lo = x * HD + h * DH
            term = column(gates, x * H + h) * R.val_b[:, lo : lo + DH]
            total[h] = term if x == 0 else total[h] + term
    for h in range(H):
        R.v_b[:, h * DH : (h + 1) * DH] = total[h].astype(BF16)

    for h in range(H):
        hs = slice(h * DH, (h + 1) * DH)
        scores = jnp.where(allowed, mm_t(R.q_b[:, hs], R.k_b[:, hs]), masked_score)
        shifted = jnp.exp(scores - jnp.max(scores, axis=-1, keepdims=True))
        shares = shifted / jnp.sum(shifted, axis=-1, keepdims=True)
        R.prob_b[h] = shares
        R.att_b[:, hs] = mm(shares.astype(BF16), R.v_b[:, hs])

    for x in range(EA):
        for h in range(H):
            lo = x * HD + h * DH
            R.mix_b[:, lo : lo + DH] = (
                column(gates, GATE + x * H + h) * R.att_b[:, h * DH : (h + 1) * DH]
            ).astype(BF16)
    loaded("o")
    half_d = D // 2
    for b in range(2):
        cols = slice(b * half_d, (b + 1) * half_d)
        hidden = R.tokens[:, cols].astype(F32) + mm_t(R.mix_b[...], R.wo_b[cols, :])
        R.hid_f[:, cols] = hidden
        R.hidb[pl.ds(times(z, C), C), cols] = hidden.astype(BF16)
    gather_own(R.hidb, R.hid_ss, R.hid_rs)
    gather_step(R.cotb, R.cot_ss, R.cot_rs, 1)

    def put_turned(x, w):
        for b in range(D // LANES):
            t = x[:, b * LANES : (b + 1) * LANES].astype(F32).T.astype(BF16)
            for q in range(LANES // S):
                i = (b * LANES) // S + q
                pp, zz, cc = i // (2 * nz), (i % (2 * nz)) // 2, i % 2
                at = (pp * 2 + cc) * SL + zz * S
                R.lt[at : at + S, w * LANES : (w + 1) * LANES] = t[q * S : (q + 1) * S, :]

    plane_all = [(k, dc) for k in range(nd) for dc in range(2) if k or dc]

    def side(dc):
        return sib if dc else c

    def send_turned(w0, w1, ss, rs):
        out = []
        lanes = slice(w0 * LANES, w1 * LANES)
        for k, dc in plane_all:
            to = plane(k)
            slot = 2 * k + dc
            at = times(to * 2 + side(dc), SL)
            cp = remote(
                R.lt.at[pl.ds(at, SL), lanes],
                R.ltr.at[slot, :, lanes],
                ss.at[slot],
                rs.at[slot],
                dev(to, z, side(dc)),
            )
            cp.start()
            out.append(cp)
        R.ltr[0, :, lanes] = R.lt[pl.ds(times(p * 2 + c, SL), SL), lanes]
        return out

    def rows_at(buf, lanes, slot):
        return buf.at[slot * C : (slot + 1) * C, lanes]

    def send_rows(buf, lanes, ss, rs, ways=(1, 2)):
        out = []
        for k in ways:
            cp = remote(
                rows_at(buf, lanes, 0),
                rows_at(buf, lanes, 2 * k),
                ss.at[k],
                rs.at[2 * k],
                dev(plane(k), z, c),
            )
            cp.start()
            out.append(cp)
        return out + [hand_over(buf, lanes, ss, rs, 0)]

    def hand_over(buf, lanes, ss, rs, k):
        cp = remote(
            rows_at(buf, lanes, 2 * k),
            rows_at(buf, lanes, 2 * k + 1),
            ss.at[nd + k],
            rs.at[2 * k + 1],
            dev(p, z, sib),
        )
        cp.start()
        return cp

    def hand_near(buf, lanes, ss, rs, out, via):
        for k in (via, 3 - via) if via else (1, 2):
            arrived(rows_at(buf, lanes, 2 * k), rs.at[2 * k])
            if k == via:
                cp = remote(
                    rows_at(buf, lanes, 2 * k),
                    rows_at(buf, lanes, 6),
                    ss.at[3],
                    rs.at[6],
                    dev(plane(3 - via), z, c),
                )
                cp.start()
                out.append(cp)
            out.append(hand_over(buf, lanes, ss, rs, k))

    def hand_far(buf, lanes, ss, rs, out):
        arrived(rows_at(buf, lanes, 6), rs.at[6])
        out.append(hand_over(buf, lanes, ss, rs, 3))

    def rows_here(buf, lanes, rs):
        for k in range(nd):
            arrived(rows_at(buf, lanes, 2 * k + 1), rs.at[2 * k + 1])

    put_turned(R.tokens[...], 0)
    put_turned(R.normed_b[...], 1)
    put_turned(R.hid_f[...], 2)
    turned = send_turned(0, 3, R.lt_ss, R.lt_rs)
    R.ra[0:C, 0:HD] = R.att_b[...].astype(BF16)
    R.ra[0:C, HD : HD + LANES] = gates.astype(BF16)
    RA = slice(0, HD + LANES)
    ra_out = send_rows(R.ra, RA, R.ra_ss, R.ra_rs)

    for cp in wx:
        cp.wait()

    least = jnp.minimum(z, nz - 1 - z)
    inner = least > 0
    left_half = z < nz // 2
    near = jnp.where(inner, jnp.where(left_half, 0, nz - 1), jnp.where(left_half, 1, nz - 2))
    fellow = jnp.where(left_half, nz // 2, nz // 2 - 1)
    far = jnp.where(left_half, nz - 1, 0)

    def origin(k):
        paired = k <= 2 * least
        dist = jnp.where(paired, (k + 1) // 2, k - least)
        left = jnp.where(paired, lax.rem(k, 2) == 1, z > nz - 1 - z)
        return jnp.where(k == 0, z, jnp.where(left, z - dist, z + dist))

    def expert_block(k, carry):
        o = origin(k)
        rows = pl.ds(times(o, C), C)

        @pl.when((k == 1) & inner)
        def _():
            gather_on(R.hidb, R.hid_ss, R.hid_rs, origin(1))

        @pl.when((k > 0) & (k + inner.astype(jnp.int32) < nz))
        def _():
            gather_on(R.hidb, R.hid_ss, R.hid_rs, origin(k + inner.astype(jnp.int32)))

        @pl.when(k == jnp.where(inner, 1, 2))
        def _():
            for far_step in range(2, nz - 1):
                gather_step(R.cotb, R.cot_ss, R.cot_rs, far_step)

        @pl.when(k > 0)
        def _():
            @pl.when((o == z - nz + 1) | (o == z + nz - 1))
            def _():
                arrived(block(R.cotb, o), R.cot_rs.at[o])

            arrived(R.maskb.at[o], R.mask_rs.at[o])

        hb = R.hidb[rows, :]
        cb = R.cotb[rows, :]
        named = R.maskb[o].astype(F32)
        named = jnp.concatenate([named, jnp.zeros((LANES - pad_e, C), F32)], axis=0).T
        g = sigmoid(mm(hb, R.wrl_b[...])) * named
        glog = jnp.zeros((C, LANES), F32)
        for q in range(2):
            cols = slice(q * HF, (q + 1) * HF)
            raised = mm(hb, R.wup_b[:, cols])
            back = mm(cb, R.wdn_b[:, cols])
            for i in range(local):
                j = q * local + i
                u = raised[:, i * DH : (i + 1) * DH]
                a = back[:, i * DH : (i + 1) * DH]
                gj = column(g, j)
                s = sigmoid(u)
                act = u * s
                lo = j * DH
                R.gact[rows, lo : lo + DH] = (gj * act).astype(BF16)
                R.gra[rows, lo : lo + DH] = (gj * a * (s * (1.0 + u * (1.0 - s)))).astype(BF16)
                gg = jnp.sum(a * act, axis=1, keepdims=True)
                glog = jnp.where(lane == j, jnp.broadcast_to(gg, (C, LANES)), glog)
        glog = glog * g * (1.0 - g)
        low = glog.astype(BF16)
        R.glog_s[o] = glog.T[0:pad_e, :].astype(BF16)
        for b in range(2):
            cols = slice(b * half_d, (b + 1) * half_d)
            gh = mm_t(R.gra[rows, :], R.wup_b[cols, :]) + mm_t(low, R.wrl_b[cols, :])
            R.gh_s[o, :, cols] = gh.astype(BF16)

        @pl.when(k > 0)
        def _():
            remote(
                R.glog_s.at[o], R.glog_r.at[z], R.gl_ss.at[o], R.gl_rs.at[z], dev(p, o, c)
            ).start()

        @pl.when((k > 0) & (least == 0) & (o != fellow))
        def _():
            send_back(o)

        @pl.when((k > 0) & (least == 0) & (o == fellow))
        def _():
            send_by(o, near, 0)

        @pl.when((k > 0) & inner & (o == far))
        def _():
            send_by(o, fellow, 1)

        @pl.when(k == 2)
        def _():
            hand_near(R.ra, RA, R.ra_ss, R.ra_rs, [], 2)

        @pl.when((k == 2) & (least == 0))
        def _():
            there = pl.ds(times(near, C), C)
            for b in range(2):
                cols = slice(b * half_d, (b + 1) * half_d)
                R.out_s[near, :, cols] = mm_t(R.gact[there, :], R.wdn_b[cols, :]).astype(BF16)
            slot = jnp.where(z == 0, near, nz)
            remote(
                R.out_s.at[near],
                R.out_r.at[slot],
                R.out_ss.at[near],
                R.out_rs.at[slot],
                dev(p, near, c),
            ).start()

        return carry

    def send_back(o):
        remote(R.gh_s.at[o], R.gh_r.at[z], R.gh_ss.at[o], R.gh_rs.at[z], dev(p, o, c)).start()

    def send_by(o, by, slot):
        remote(
            R.gh_s.at[o], R.gh_x.at[slot], R.gh_ss.at[o], R.gx_rs.at[slot], dev(p, by, c)
        ).start()

    def relay_back(o, slot):
        arrived(R.gh_x.at[slot], R.gx_rs.at[slot])
        R.gh_s[o] = (R.gh_s[o].astype(F32) + R.gh_x[slot].astype(F32)).astype(BF16)
        send_back(o)

    lax.fori_loop(0, nz, expert_block, 0)

    pairs = {}

    def rows_of(at):
        return pl.ds(times(at, rows_d), rows_d)


    rows_d = D // nd
    plane_out = []

    def half(cc):
        return pl.ds(times(cc, HF), HF)

    def grad_at(i, k, cc):
        if i == 0 and k == 3:
            return R.dg.at[:, half(cc)]
        return (R.wdn_b, R.wup_b)[i].at[rows_of(plane(k)), half(cc)]

    def expert_grad(i, k):
        left, right = ((R.cotb, R.gact), (R.hidb, R.gra))[i]
        for cc in (sib, c):
            grad_at(i, k, cc)[...] = tmm(left[:, rows_of(plane(k))], right[:, half(cc)]).astype(BF16)
            if cc is sib:
                cp = remote(
                    grad_at(i, k, sib),
                    R.pair_r.at[i, k],
                    R.pair_ss.at[i, k],
                    R.pair_rs.at[i, k],
                    dev(p, z, sib),
                )
                cp.start()
                pairs[i, k] = cp

    def pair_sum(i, k):
        pairs[i, k].wait()
        own = grad_at(i, k, c)
        own[...] = (own[...].astype(F32) + R.pair_r[i, k].astype(F32)).astype(BF16)

    def part_on(i, k, to, slot):
        cp = remote(
            grad_at(i, k, c),
            R.eg_r.at[slot, i],
            R.eg_ss.at[slot, i],
            R.eg_rs.at[slot, i],
            dev(plane(to), z, c),
        )
        cp.start()
        plane_out.append(cp)

    def first_half(i, n):
        first = 1 if i == 0 else 2
        rows = slice(n * rows_d // 2, (n + 1) * rows_d // 2)
        cp = remote(
            grad_at(i, first, c).at[rows],
            R.eg_r.at[0, i, rows],
            R.eg_ss.at[3 * n, i],
            R.eg_rs.at[3 * n, i],
            dev(plane(first), z, c),
        )
        cp.start()
        plane_out.append(cp)

    def expert_grad_relay(i):
        second = 2 if i == 0 else 1
        first_half(i, 1)
        arrived(R.eg_r.at[1, i], R.eg_rs.at[1, i])
        own = grad_at(i, second, c)
        own[...] = (own[...].astype(F32) + R.eg_r[1, i].astype(F32)).astype(BF16)
        part_on(i, second, second, 2)

    def to_place(own, got, ss, rs, o):
        remote(own(o), got(z), ss.at[o], rs.at[z], dev(p, o, c)).start()

    def run(own, got, ss, rs, k, n):
        def hand(d, slot, to):
            if k > 1:
                arrived(got(d), rs.at[d])
                own(d)[...] = (own(d)[...].astype(F32) + got(d)[...].astype(F32)).astype(BF16)
            remote(own(d), got(slot), ss.at[d], rs.at[slot], dev(p, to, c)).start()

        @pl.when(z == k - 1)
        def _():
            hand(nz - 1 - n, nz - 1 - n, k)

        @pl.when(z == nz - k)
        def _():
            hand(n, nz if n == nz - k - 1 else n, nz - k - 1)

    def run_end(total, got, rs):
        for there, slot in ((z > 0, z), (z < nz - 1, nz)):

            @pl.when(there)
            def _():
                arrived(got(slot), rs.at[slot])
                total[...] += got(slot)[...].astype(F32)

    out_sum = (lambda d: R.out_s.at[d], lambda d: R.out_r.at[d], R.out_ss, R.out_rs)
    out_run = functools.partial(run, *out_sum)

    def grad_sum(i, lanes):
        return (
            lambda d: R.pb.at[d * S : (d + 1) * S, lanes],
            lambda d: R.pn.at[i, d],
            R.pn_ss.at[i],
            R.pn_rs.at[i],
        )

    def part_sum(i, lanes):
        return (
            lambda o: R.pb.at[pl.ds(times(o, S), S), lanes],
            lambda o: R.pr.at[o, :, slice(lanes.start - 2 * EV, lanes.stop - 2 * EV)],
            R.p_ss.at[i],
            R.p_rs.at[i],
        )

    expert_grad(1, 3)
    expert_grad(0, 3)
    for i, to in ((1, 2), (0, 1)):
        pair_sum(i, 3)
        part_on(i, 3, to, 1)

    def out_tile(t, carry):
        rows = pl.ds(times(t, 256), 256)
        got = mm_t(R.gact[...], R.wdn_b[rows, :]).astype(BF16)
        for o in range(nz):

            @pl.when(inner | (o != near))
            def _():
                R.out_s[o, :, rows] = got[o * C : (o + 1) * C, :]

        return carry

    lax.fori_loop(0, D // 256, out_tile, 0)
    out_run(1, 0)

    @pl.when(inner)
    def _():
        relay_back(near, 1)
        relay_back(fellow, 0)

    for k in (1, 2, 0):
        expert_grad(1, k)
        expert_grad(0, k)
    R.ghid_f[...] = R.cotb[pl.ds(times(z, C), C), :].astype(F32) + R.gh_s[z].astype(F32)

    def add_back(o):
        arrived(R.gh_r.at[o], R.gh_rs.at[o])
        R.ghid_f[...] += R.gh_r[o].astype(F32)

    add_back(near)
    add_back(jnp.where(inner, fellow, far))

    for k in range(1, nz):
        o = line(k)
        arrived(R.glog_r.at[o], R.gl_rs.at[o])
    out_run(1, 1)
    R.glog_r[z] = R.glog_s[z]
    R.ghid_b[...] = R.ghid_f[...].astype(BF16)
    put_turned(R.ghid_f[...], 3)
    turned_late = send_turned(3, 4, R.ltl_ss, R.ltl_rs)
    out_run(2, 0)

    gates = R.gate_b[...]
    small = jnp.zeros((C, LANES), F32)
    gatt = [None] * H
    for x in range(EA):
        gmix = mm(R.ghid_b[...], R.wo_b[:, x * HD : (x + 1) * HD])
        for h in range(H):
            hs = slice(h * DH, (h + 1) * DH)
            j = GATE + x * H + h
            term = column(gates, j) * gmix[:, hs]
            gatt[h] = term if x == 0 else gatt[h] + term
            gg = jnp.sum(gmix[:, hs] * R.att_b[:, hs], axis=1, keepdims=True)
            small = jnp.where(lane == j, jnp.broadcast_to(gg, (C, LANES)), small)
    for h in range(H):
        hs = slice(h * DH, (h + 1) * DH)
        low = gatt[h].astype(BF16)
        R.gatt_b[:, hs] = low
        gval = tmm(R.prob_b[h].astype(BF16), low)
        R.gval_f[:, hs] = gval
        R.rb[0:C, hs] = gval.astype(BF16)
        for x in range(EA):
            lo = x * HD + h * DH
            j = x * H + h
            gg = jnp.sum(gval * R.val_b[:, lo : lo + DH], axis=1, keepdims=True)
            small = jnp.where(lane == j, jnp.broadcast_to(gg, (C, LANES)), small)
    small = small * gates * (1.0 - gates)
    glog = jnp.concatenate(
        [jnp.zeros((2 * GATE, C), F32)]
        + [R.glog_r[o].astype(F32) for o in range(nz)]
        + [jnp.zeros((LANES - 2 * GATE - nz * pad_e, C), F32)],
        axis=0,
    )
    R.small_b[...] = small.astype(BF16)
    R.rb[0:C, HD : HD + LANES] = (small + glog.T).astype(BF16)
    RV = slice(0, HD + LANES)
    rv_out = send_rows(R.rb, RV, R.rv_ss, R.rv_rs, (1, 2, 3))

    q0 = HD + LANES
    for h in range(H):
        hs = slice(h * DH, (h + 1) * DH)
        low = R.gatt_b[:, hs]
        gsh = mm_t(low, R.v_b[:, hs])
        prob = R.prob_b[h]
        centre = jnp.sum(prob * gsh, axis=-1, keepdims=True)
        gs = (prob * (gsh - centre)).astype(BF16)
        R.rb[0:C, q0 + h * DH : q0 + (h + 1) * DH] = rot_back(
            mm(gs, R.k_b[:, hs]) * scale
        ).astype(BF16)
        R.rb[0:C, q0 + HD + h * DH : q0 + HD + (h + 1) * DH] = rot_back(
            tmm(gs, R.q_b[:, hs])
        ).astype(BF16)
    RQ, RK = slice(q0, q0 + HD), slice(q0 + HD, q0 + 2 * HD)
    rq_out = send_rows(R.rb, RQ, R.rq_ss, R.rq_rs)
    rk_out = send_rows(R.rb, RK, R.rk_ss, R.rk_rs)

    gproj = mm_t(R.rb[0:C, q0 : q0 + 2 * HD], R.wqk_b[...])
    standard = R.std_b[...]
    column_sum = jnp.sum(gproj * standard, axis=0, keepdims=True)
    for b in range(D // LANES):
        R.gp[0, b : b + 1, :] = column_sum[:, b * LANES : (b + 1) * LANES]
    gain_out = []
    for k, dc in plane_all:
        slot = 2 * k + dc
        cp = remote(
            R.gp.at[0], R.gp.at[slot], R.gp_ss.at[slot], R.gp_rs.at[slot], dev(plane(k), z, side(dc))
        )
        cp.start()
        gain_out.append(cp)

    out_run(2, 1)
    for k in (1, 2, 0):
        pair_sum(1, k)
        pair_sum(0, k)
    first_half(0, 0)
    first_half(1, 0)
    hand_far(R.ra, RA, R.ra_ss, R.ra_rs, ra_out)
    for cp in turned:
        cp.wait()
    rows_here(R.ra, RA, R.ra_rs)

    def turned_of(w):
        return jnp.concatenate(
            [R.ltr[s, :, w * LANES : (w + 1) * LANES] for s in range(2 * nd)], axis=1
        )

    def send_part(part, lanes):
        for o in (far, fellow, near):
            to_place(*part_sum(part, lanes), o)

    def gate_rows(dst, rows_of, g0, s0, s1):
        rows = slice(s0 * C, s1 * C)
        for x in range(EA):
            for h in range(H):
                lo = x * HD + h * DH
                gx = column(R.ra[rows, HD : HD + LANES], g0 + x * H + h).astype(F32)
                dst[rows, lo : lo + DH] = (
                    gx * rows_of[rows, h * DH : (h + 1) * DH].astype(F32)
                ).astype(BF16)

    def gated_grad(w, gated, at):
        left = turned_of(w)
        for x in range(EA):
            cols = slice(x * HD, (x + 1) * HD)
            R.pb[:, at + x * HD : at + (x + 1) * HD] = mm(left, gated[:, cols]).astype(BF16)

    PO, PV, PQ, PS = (
        slice(0, EV),
        slice(EV, 2 * EV),
        slice(2 * EV, 2 * EV + 2 * HD),
        slice(2 * EV + 2 * HD, 2 * EV + 2 * HD + LANES),
    )
    gate_rows(R.wo_b, R.ra, GATE, 0, 2 * nd)
    for cp in turned_late:
        cp.wait()
    gated_grad(3, R.wo_b, 0)
    o_run = functools.partial(run, *grad_sum(0, PO))
    v_run = functools.partial(run, *grad_sum(1, PV))
    o_run(1, 0)
    o_run(1, 1)
    out_run(3, 0)
    hand_near(R.rb, RV, R.rv_ss, R.rv_rs, rv_out, 0)

    inputs = R.tokens[...].astype(F32)
    centred = inputs - jnp.mean(inputs, axis=-1, keepdims=True)
    inverse = lax.rsqrt(jnp.mean(centred * centred, axis=-1, keepdims=True) + norm_eps)
    gs = gproj * R.gain[...]
    gtok = R.ghid_f[...] + inverse * (
        gs
        - jnp.mean(gs, axis=-1, keepdims=True)
        - standard * jnp.mean(gs * standard, axis=-1, keepdims=True)
    )
    R.gtok[...] = gtok
    for x in range(EA):
        for h in range(H):
            lo = x * HD + h * DH
            R.mix_b[:, lo : lo + DH] = (
                column(gates, x * H + h) * R.gval_f[:, h * DH : (h + 1) * DH]
            ).astype(BF16)
    for b in range(2):
        cols = slice(b * half_d, (b + 1) * half_d)
        R.gtok[:, cols] += mm_t(R.mix_b[...], R.wv_b[cols, :]) + mm_t(
            R.small_b[...], R.wg_b[cols, :]
        )

    store("gtok")

    o_run(2, 0)
    for k in range(3):
        arrived(rows_at(R.rb, RV, 2 * k + 1), R.rv_rs.at[2 * k + 1])
    gate_rows(R.wv_b, R.rb, 0, 0, 6)
    o_run(2, 1)
    hand_far(R.rb, RV, R.rv_ss, R.rv_rs, rv_out)
    arrived(rows_at(R.rb, RV, 7), R.rv_rs.at[7])
    gate_rows(R.wv_b, R.rb, 0, 6, 8)
    gated_grad(0, R.wv_b, EV)
    v_run(1, 0)
    v_run(1, 1)
    o_run(1, 2)
    hand_near(R.rb, RK, R.rk_ss, R.rk_rs, rk_out, 2)
    hand_near(R.rb, RQ, R.rq_ss, R.rq_rs, rq_out, 1)
    expert_grad_relay(0)
    expert_grad_relay(1)
    o_run(3, 0)
    total = R.gp[0]
    for cp, (k, dc) in zip(gain_out, plane_all):
        cp.wait()
        total = total + R.gp[2 * k + dc]
    R.gz_s[...] = total
    for k in range(1, nz):
        o = line(k)
        remote(R.gz_s, R.gz.at[z], R.gz_ss.at[o], R.gz_rs.at[z], dev(p, o, c)).start()

    lane_s = iota((SL, LANES), 1)
    small_t = mm(turned_of(0), R.rb[:, HD : HD + LANES])
    small_h = mm(turned_of(2), R.rb[:, HD : HD + LANES])
    R.pb[:, PS] = jnp.where(lane_s < 2 * GATE, small_t, small_h).astype(BF16)
    send_part(1, PS)
    v_run(2, 0)
    v_run(2, 1)
    hand_far(R.rb, RQ, R.rq_ss, R.rq_rs, rq_out)
    hand_far(R.rb, RK, R.rk_ss, R.rk_rs, rk_out)
    rows_here(R.rb, RQ, R.rq_rs)
    rows_here(R.rb, RK, R.rk_rs)
    left = turned_of(1)
    for b in range(2):
        lo = q0 + b * HD
        R.pb[:, 2 * EV + b * HD : 2 * EV + (b + 1) * HD] = mm(left, R.rb[:, lo : lo + HD]).astype(
            BF16
        )
    send_part(0, PQ)
    v_run(1, 2)
    v_run(3, 0)

    R.hid_f[...] += R.out_s[z].astype(F32)
    run_end(R.hid_f, out_sum[1], R.out_rs)
    R.mixed[...] = R.hid_f[...].astype(BF16)
    store("mixed")

    for k in range(1, nz):
        o = line(k)
        arrived(R.gz.at[o], R.gz_rs.at[o])
        total = total + R.gz[o]
    first = (p * 2 * nz + z * 2 + c) * S
    pick_row = iota((D // LANES, LANES), 0) == first // LANES
    line_sum = jnp.sum(jnp.where(pick_row, total, 0.0), axis=0, keepdims=True)
    shift = lax.rem(LANES - lax.rem(first, LANES), LANES)
    line_sum = pltpu.roll(jnp.broadcast_to(line_sum, (8, LANES)), shift, 1)
    R.ggain[...] = line_sum[0:1, 0:S]
    store("ggain")

    own_rows = pl.ds(times(z, S), S)

    def line_total(part, lanes):
        got = R.pb[own_rows, lanes].astype(F32)
        for k in range(1, nz):
            o = line(k)
            there = part_sum(part, lanes)[1](o)
            arrived(there, R.p_rs.at[part, o])
            got = got + there[...].astype(F32)
        return got

    for i, (dst, lanes) in enumerate(((R.go, PO), (R.gv, PV))):
        dst[...] = R.pb[own_rows, lanes].astype(F32)
        run_end(dst, grad_sum(i, lanes)[1], R.pn_rs.at[i])
    store("go", "gv")
    got = line_total(1, PS)

    def pick(width, source):
        a, b = iota((width, LANES), 1), iota((width, LANES), 0)
        return jnp.where(a == source(b), 1.0, 0.0).astype(F32)

    def picked(left, right):
        return lax.dot_general(
            left,
            right,
            (((1,), (1,)), ((), ())),
            preferred_element_type=F32,
            precision=lax.Precision.HIGHEST,
        )

    def router_lane(b):
        at = jnp.zeros_like(b)
        for o in range(nz):
            at = jnp.where(b >= o * own_e, 2 * GATE + o * pad_e + b - o * own_e, at)
        return at

    R.gvg[...] = picked(pick(GATE, lambda b: b), got)
    R.gog[...] = picked(pick(GATE, lambda b: b + GATE), got)
    R.gr[...] = picked(got, pick(experts, router_lane))
    store("gvg", "gog", "gr")
    got = line_total(0, PQ)
    R.gq[...] = got[:, 0:HD]
    R.gk[...] = got[:, HD : 2 * HD]
    store("gq", "gk")

    for i, (buf, dst) in enumerate(((R.wdn_b, R.gdn), (R.wup_b, R.gup))):
        for n in range(2):
            rows = slice(n * rows_d // 2, (n + 1) * rows_d // 2)
            arrived(R.eg_r.at[0, i, rows], R.eg_rs.at[3 * n, i])
        arrived(R.eg_r.at[2, i], R.eg_rs.at[2, i])
        rows = rows_of(p)
        for x in range(local):
            got = buf[rows, pl.ds(times(c * local + x, DH), DH)].astype(F32)
            for slot in (0, 2):
                got = got + R.eg_r[slot, i, :, x * DH : (x + 1) * DH].astype(F32)
            dst[x] = got
        store(("gdn", "gup")[i])

    for cp in stores:
        cp.wait()
    gather_end(R.cotb, R.cot_ss)
    gather_end(R.hidb, R.hid_ss)
    for cp in masks + ra_out + rv_out + rq_out + rk_out + plane_out:
        cp.wait_send()
    sent(rows_at(R.ra, RA, 4), R.ra_ss.at[3])
    for k in (1, 2):
        sent(rows_at(R.ra, RA, 2 * k), R.ra_ss.at[nd + k])
    for k in range(1, nz):
        o = line(k)
        sent(R.gh_s.at[o], R.gh_ss.at[o])
        sent(R.glog_s.at[o], R.gl_ss.at[o])
        sent(R.out_s.at[o], R.out_ss.at[o])
        sent(R.gz_s, R.gz_ss.at[o])
        for lanes, ss in (
            (PO, R.pn_ss.at[0]),
            (PV, R.pn_ss.at[1]),
            (PQ, R.p_ss.at[0]),
            (PS, R.p_ss.at[1]),
        ):
            sent(R.pb.at[pl.ds(times(o, S), S), lanes], ss.at[o])


def settle_kernel(n, *refs):
    src, dst, held, sems = refs[:n], refs[n : 2 * n], refs[2 * n : 3 * n], refs[-1]
    ins = [pltpu.make_async_copy(src[i], held[i], sems.at[0, i]) for i in range(n)]
    outs = [pltpu.make_async_copy(held[i], dst[i], sems.at[1, i]) for i in range(n)]
    for cp in ins:
        cp.start()
    for there, back in zip(ins, outs):
        there.wait()
        back.start()
    for cp in outs:
        cp.wait()


def fused_layer(nd, nz, *args):
    (tokens, cotangent, seq_lengths, routes, head_experts, norm_gain) = args[:6]
    (w_query, w_key, w_value, w_output, w_value_gate, w_output_gate, w_router) = args[6:13]
    w_up, w_down = args[13:]
    C = tokens.shape[0]
    local = w_up.shape[0]
    experts = w_router.shape[1]
    own_e = 2 * local
    pad_e = -(-own_e // 16) * 16
    EF, HF, HD = own_e * DH, local * DH, H * DH
    EV = EA * HD
    S = D // (nd * nz * 2)
    SL = S * nz
    PW = 2 * EV + 2 * HD + LANES
    s = Scratch()
    s.vmem("wqk_b", (D, 2 * HD), BF16)
    s.vmem("wv_b", (D, EV), BF16)
    s.vmem("wo_b", (D, EV), BF16)
    s.vmem("wup_b", (D, EF), BF16)
    s.vmem("wdn_b", (D, EF), BF16)
    s.vmem("wg_b", (D, LANES), BF16)
    s.vmem("wrl_b", (D, LANES), BF16)
    s.vmem("cotb", (nz * C, D), BF16)
    s.vmem("hidb", (nz * C, D), BF16)
    s.vmem("mask_s", (nz, pad_e, C), BF16)
    s.vmem("maskb", (nz, pad_e, C), BF16)
    s.vmem("std_b", (C, D), F32)
    s.vmem("normed_b", (C, D), BF16)
    s.vmem("q_b", (C, HD), BF16)
    s.vmem("k_b", (C, HD), BF16)
    s.vmem("v_b", (C, HD), BF16)
    s.vmem("gate_b", (C, LANES), F32)
    s.vmem("val_b", (C, EV), F32)
    s.vmem("prob_b", (H, C, C), F32)
    s.vmem("att_b", (C, HD), F32)
    s.vmem("mix_b", (C, EV), BF16)
    s.vmem("hid_f", (C, D), F32)
    s.vmem("lt", (D, 4 * LANES), BF16)
    s.vmem("ltr", (2 * nd, SL, 4 * LANES), BF16)
    s.vmem("ra", (2 * nd * C, HD + LANES), BF16)
    s.vmem("rb", (2 * nd * C, 3 * HD + LANES), BF16)
    s.vmem("gact", (nz * C, EF), BF16)
    s.vmem("gra", (nz * C, EF), BF16)
    for name in ("gh_s", "gh_r", "out_s"):
        s.vmem(name, (nz, C, D), BF16)
    s.vmem("out_r", (nz + 1, C, D), BF16)
    s.vmem("gh_x", (2, C, D), BF16)
    for name in ("glog_s", "glog_r"):
        s.vmem(name, (nz, pad_e, C), BF16)
    s.vmem("dg", (D // nd, EF), BF16)
    s.vmem("pair_r", (2, nd, D // nd, HF), BF16)
    s.vmem("eg_r", (nd - 1, 2, D // nd, HF), BF16)
    s.vmem("ghid_f", (C, D), F32)
    s.vmem("ghid_b", (C, D), BF16)
    s.vmem("gatt_b", (C, HD), BF16)
    s.vmem("gval_f", (C, HD), F32)
    s.vmem("small_b", (C, LANES), BF16)
    s.vmem("pb", (SL, PW), BF16)
    s.vmem("pr", (nz, S, PW - 2 * EV), BF16)
    s.vmem("pn", (2, nz + 1, S, EV), BF16)
    s.vmem("gp", (2 * nd, D // LANES, LANES), F32)
    s.vmem("gz_s", (D // LANES, LANES), F32)
    s.vmem("gz", (nz, D // LANES, LANES), F32)
    s.sems("ld", 4 + 2 * local)
    s.sems("gx_rs", 2)
    s.sems("out_rs", nz + 1)
    for name in ("cot_ss", "hid_ss"):
        s.sems(name, 2, nz)
    for name in ("cot_rs", "hid_rs", "mask_ss", "mask_rs", "gh_ss", "gh_rs", "gl_ss", "gl_rs", "out_ss", "gz_ss", "gz_rs"):
        s.sems(name, nz)
    for name in ("w_ss", "w_rs"):
        s.sems(name, 2)
    for name in ("pair_ss", "pair_rs"):
        s.sems(name, 2, nd)
    for name in ("lt_ss", "lt_rs", "ltl_ss", "ltl_rs", "gp_ss", "gp_rs", "ra_ss", "ra_rs", "rv_ss", "rv_rs", "rq_ss", "rq_rs", "rk_ss", "rk_rs"):
        s.sems(name, 2 * nd)
    for name in ("eg_ss", "eg_rs"):
        s.sems(name, 4, 2)
    for name in ("p_ss", "p_rs", "pn_ss"):
        s.sems(name, 2, nz)
    s.sems("pn_rs", 2, nz + 1)

    def out(*shape, dtype=F32):
        return jax.ShapeDtypeStruct(shape, dtype)

    hbm = pl.BlockSpec(memory_space=pl.ANY)
    names = in_hbm(SMALL) + WEIGHTS + in_hbm(OUTPUTS)
    results = (
        out(C, D, dtype=BF16),
        out(C, D),
        out(1, S),
        out(S, HD),
        out(S, HD),
        out(S, EV),
        out(S, EV),
        out(EA * H, S),
        out(EA * H, S),
        out(S, experts),
        out(local, D // nd, DH),
        out(local, D // nd, DH),
    )
    for name, x in zip(OUTPUTS, results):
        s.vmem(name, x.shape, x.dtype)
    s.vmem("tokens", (C, D), BF16)
    s.vmem("cot", (C, D), BF16)
    s.add("lens", pltpu.SMEM((1, 2), jnp.int32))
    s.vmem("rt", (TOPK, C), jnp.int32)
    s.vmem("het", (2 * H, C), jnp.int32)
    s.vmem("gain", (1, D), F32)
    s.vmem("wvg", (EA * H, D), BF16)
    s.vmem("wog", (EA * H, D), BF16)
    s.vmem("wr", (experts, D), BF16)
    s.sems("ld_in", len(SMALL))
    s.sems("st", len(OUTPUTS))
    outs = pl.pallas_call(
        functools.partial(layer_kernel, names + tuple(s.names), nd, nz, local),
        out_shape=results,
        in_specs=[hbm] * 15,
        out_specs=[hbm] * len(OUTPUTS),
        scratch_shapes=s.shapes,
        compiler_params=pltpu.CompilerParams(
            collective_id=0, has_side_effects=True, vmem_limit_bytes=VMEM_LIMIT
        ),
    )(
        tokens,
        cotangent,
        seq_lengths,
        routes.T,
        head_experts.reshape(C, 2 * H).T,
        norm_gain.reshape(1, D),
        w_value_gate.T,
        w_output_gate.T,
        w_router.T,
        w_query,
        w_key,
        w_value,
        w_output,
        w_up,
        w_down,
    )
    outs = list(
        pl.pallas_call(
            functools.partial(settle_kernel, len(outs)),
            out_shape=results,
            in_specs=[hbm] * len(outs),
            out_specs=[hbm] * len(outs),
            scratch_shapes=[pltpu.VMEM(x.shape, x.dtype) for x in outs]
            + [pltpu.SemaphoreType.DMA((2, len(outs)))],
            compiler_params=pltpu.CompilerParams(vmem_limit_bytes=VMEM_LIMIT),
        )(*outs)
    )
    outs[2] = outs[2].reshape(S)
    for i in (7, 8):
        outs[i] = outs[i].T
    return tuple(outs)


VMEM_LIMIT = 62 * 1024 * 1024


def fits(nd, nz, count, experts):
    own_e = experts // nz
    pad_e = -(-own_e // 16) * 16
    return (
        count == LANES
        and nz == 4
        and nd == 4
        and own_e % 4 == 0
        and D % (nd * nz * 2 * 16) == 0
        and LANES % (D // (nd * nz * 2)) == 0
        and 2 * EA * H + nz * pad_e <= LANES
    )


def per_device(nd, ne, *args):
    count, experts = args[0].shape[0], args[12].shape[1]
    if ne % 2 == 0 and fits(nd, ne // 2, count, experts):
        return fused_layer(nd, ne // 2, *args)
    return routed_layer(*args)


def solution(mesh):
    return jax.shard_map(
        functools.partial(per_device, mesh.shape["dp"], mesh.shape["expert"]),
        mesh=mesh,
        in_specs=(
            P(("dp", "expert"), None),
            P(("dp", "expert"), None),
            P(("dp", "expert"), None),
            P(("dp", "expert"), None),
            P(("dp", "expert"), None, None),
            P(),
            P(),
            P(),
            P(),
            P(),
            P(),
            P(),
            P(),
            P("expert", None, None),
            P("expert", None, None),
        ),
        out_specs=(
            P(("dp", "expert"), None),
            P(("dp", "expert"), None),
            P(("dp", "expert")),
            P(("dp", "expert"), None),
            P(("dp", "expert"), None),
            P(("dp", "expert"), None),
            P(("dp", "expert"), None),
            P(("dp", "expert"), None),
            P(("dp", "expert"), None),
            P(("dp", "expert"), None),
            P("expert", "dp", None),
            P("expert", "dp", None),
        ),
        check_vma=False,
    )
```

```python
import functools
import math

import jax
import jax.numpy as jnp
from jax import lax
from jax.experimental import pallas as pl
from jax.experimental.pallas import tpu as pltpu
from jax.sharding import PartitionSpec as P

D = 1024
H = 4
DH = 128
EA = 5
TOPK = 16


norm_eps = 1e-05
rope_base = 10000.0
masked_score = -1e30


def sequence_layout(lengths, count):
    bounds = jnp.cumsum(lengths)
    starts = bounds - lengths
    places = jnp.arange(count, dtype=jnp.int32)
    seq_ids = jnp.sum((places[:, None] >= bounds[None, :]).astype(jnp.int32), axis=1)
    live = places < bounds[-1]
    slot_ids = jnp.arange(lengths.shape[0], dtype=jnp.int32)
    first = jnp.sum(jnp.where(seq_ids[:, None] == slot_ids[None, :], starts[None, :], 0), axis=1)
    positions = jnp.where(live, places - first, 0)
    return (seq_ids, live, positions)


def rope_tables(positions, width):
    half = width // 2
    freq = rope_base ** (-(jnp.arange(half, dtype=jnp.float32) * 2.0 / width))
    angles = positions.astype(jnp.float32)[:, None] * freq[None, :]
    return (jnp.cos(angles), jnp.sin(angles))


def rotate(field, cosine, sine):
    half = field.shape[-1] // 2
    first, second = (field[..., :half], field[..., half:])
    cos_h, sin_h = (cosine[:, None, :], sine[:, None, :])
    return jnp.concatenate(
        [first * cos_h - second * sin_h, second * cos_h + first * sin_h], axis=-1
    )


def rotate_back(field, cosine, sine):
    half = field.shape[-1] // 2
    first, second = (field[..., :half], field[..., half:])
    cos_h, sin_h = (cosine[:, None, :], sine[:, None, :])
    return jnp.concatenate(
        [first * cos_h + second * sin_h, second * cos_h - first * sin_h], axis=-1
    )


def slot_tables(routes, experts, most):
    count = routes.shape[0] * routes.shape[1]
    flat = routes.reshape(count)
    order = jnp.argsort(flat, stable=True)
    ordered = flat[order]
    firsts = jnp.searchsorted(ordered, jnp.arange(experts, dtype=jnp.int32))
    ranks = jnp.arange(count, dtype=jnp.int32) - firsts[ordered]
    sorted_slots = ordered * most + ranks
    slot_of_row = jnp.zeros((count,), jnp.int32).at[order].set(sorted_slots)
    row_of_slot = jnp.full((experts * most,), count, jnp.int32).at[sorted_slots].set(order)
    return (slot_of_row, row_of_slot)


def routed_layer(
    tokens,
    cotangent,
    seq_lengths,
    routes,
    head_experts,
    norm_gain,
    w_query,
    w_key,
    w_value,
    w_output,
    w_value_gate,
    w_output_gate,
    w_router,
    w_up,
    w_down,
):
    f32 = jnp.float32
    bf16 = jnp.bfloat16
    count = tokens.shape[0]
    experts = w_router.shape[1]
    local_experts = w_up.shape[0]
    owners = lax.axis_size("expert")
    most = 3 * count * TOPK // (2 * experts)
    routed = count * TOPK
    block = min(512, count)
    block_starts = jnp.arange(count // block, dtype=jnp.int32) * block
    scale = DH ** (-0.5)
    contract_last = (((1,), (1,)), ((), ()))
    contract_first = (((0,), (0,)), ((), ()))
    seq_ids, live, positions = sequence_layout(seq_lengths[0], count)
    cosine, sine = rope_tables(positions, DH)
    inputs = tokens.astype(f32)
    centred = inputs - jnp.mean(inputs, axis=-1, keepdims=True)
    inverse = lax.rsqrt(jnp.mean(centred * centred, axis=-1, keepdims=True) + norm_eps)
    standard = centred * inverse
    normed = (standard * norm_gain).astype(bf16)
    query_proj = jnp.dot(normed, w_query, preferred_element_type=f32).reshape(count, H, DH)
    key_proj = jnp.dot(normed, w_key, preferred_element_type=f32).reshape(count, H, DH)
    query_rot = (rotate(query_proj, cosine, sine) * scale).astype(bf16)
    key_rot = rotate(key_proj, cosine, sine).astype(bf16)
    chosen = jnp.any(
        head_experts[:, None, :, :] == jnp.arange(EA, dtype=jnp.int32)[None, :, None, None], axis=-1
    )
    value_gates = jnp.where(
        chosen,
        jax.nn.sigmoid(
            jnp.dot(tokens, w_value_gate, preferred_element_type=f32).reshape(count, EA, H)
        ),
        0.0,
    )
    output_gates = jnp.where(
        chosen,
        jax.nn.sigmoid(
            jnp.dot(tokens, w_output_gate, preferred_element_type=f32).reshape(count, EA, H)
        ),
        0.0,
    )
    value_all = jnp.dot(tokens, w_value, preferred_element_type=f32).reshape(count, EA, H, DH)
    values = jnp.sum(value_gates[..., None] * value_all, axis=1).astype(bf16)

    def allowed_at(start):
        queries = start + jnp.arange(block, dtype=jnp.int32)
        keys = jnp.arange(count, dtype=jnp.int32)
        same = (
            (seq_ids[:, None] == seq_ids[None, :])
            & (keys[None, :] <= queries[:, None])
            & live[None, :]
        )
        return same | (keys[None, :] == queries[:, None])

    def scores_at(start):
        scores = jnp.einsum("qhd,khd->hqk", query_rot, key_rot, preferred_element_type=f32)
        return (query_rot, jnp.where(allowed_at(start)[None], scores, masked_score))

    def attend(start):
        query_block, scores = scores_at(start)
        highest = jnp.max(scores, axis=-1, keepdims=True)
        shifted = jnp.exp(scores - highest)
        totals = jnp.sum(shifted, axis=-1, keepdims=True)
        shares = (shifted / totals).astype(bf16)
        result = jnp.einsum("hqk,khd->qhd", shares, values, preferred_element_type=f32)
        return (result, (highest + jnp.log(totals))[..., 0])

    attended, log_totals = lax.map(attend, block_starts)
    attended = attended.reshape(count, H, DH)
    log_totals = jnp.transpose(log_totals, (1, 0, 2)).reshape(H, count)
    heads_mixed = (
        (output_gates[..., None] * attended[:, None]).astype(bf16).reshape(count, EA * H * DH)
    )
    hidden = inputs + lax.dot_general(
        heads_mixed, w_output, contract_last, preferred_element_type=f32
    )
    hidden_low = hidden.astype(bf16)
    logits = jnp.dot(hidden_low, w_router, preferred_element_type=f32)
    gates = jax.nn.sigmoid(jnp.take_along_axis(logits, routes, axis=1))
    slot_of_row, row_of_slot = slot_tables(routes, experts, most)
    valid = row_of_slot < routed
    safe_row = jnp.minimum(row_of_slot, routed - 1)
    source = safe_row // TOPK
    outgoing = jnp.where(valid[:, None], hidden_low[source], jnp.zeros((), bf16)).reshape(
        owners, local_experts, most, D
    )

    def expert_apply(items):
        raised = jnp.einsum("nemd,edf->nemf", items, w_up, preferred_element_type=f32)
        active = jax.nn.silu(raised).astype(bf16)
        lowered = jnp.einsum("nemf,edf->nemd", active, w_down, preferred_element_type=f32).astype(
            bf16
        )
        return (lowered, raised)

    lowered, raised = expert_apply(
        lax.all_to_all(outgoing, "expert", split_axis=0, concat_axis=0, tiled=True)
    )
    returned = lax.all_to_all(lowered, "expert", split_axis=0, concat_axis=0, tiled=True).reshape(
        experts * most, D
    )
    expert_rows = returned[slot_of_row].reshape(count, TOPK, D)
    output = hidden + jnp.sum(gates[..., None] * expert_rows, axis=1)
    mixed = output.astype(bf16)
    grad_out = cotangent.astype(f32) * live[:, None].astype(f32)
    grad_gates = jnp.sum(grad_out[:, None, :] * expert_rows, axis=2)
    gate_flat = gates.reshape(routed)
    grad_outgoing = (
        jnp.where(valid[:, None], gate_flat[safe_row][:, None] * grad_out[source], 0.0)
        .astype(bf16)
        .reshape(owners, local_experts, most, D)
    )
    grad_lowered = lax.all_to_all(grad_outgoing, "expert", split_axis=0, concat_axis=0, tiled=True)
    items = lax.all_to_all(outgoing, "expert", split_axis=0, concat_axis=0, tiled=True)
    raised = expert_apply(items)[1]
    grad_active = jnp.einsum("nemd,edf->nemf", grad_lowered, w_down, preferred_element_type=f32)
    sigmoid_raised = jax.nn.sigmoid(raised)
    grad_raised = (grad_active * sigmoid_raised * (1.0 + raised * (1.0 - sigmoid_raised))).astype(
        bf16
    )
    grad_items = jnp.einsum("nemf,edf->nemd", grad_raised, w_up, preferred_element_type=f32).astype(
        bf16
    )
    active = jax.nn.silu(raised).astype(bf16)
    grad_items, grad_raised, active = (grad_items, grad_raised, active)
    grad_items, grad_raised, active, grad_arrived, arrived = (
        grad_items,
        grad_raised,
        active,
        grad_lowered,
        items,
    )
    grad_up_local = jnp.einsum("nemd,nemf->edf", arrived, grad_raised, preferred_element_type=f32)
    grad_down_local = jnp.einsum("nemd,nemf->edf", grad_arrived, active, preferred_element_type=f32)
    grad_up, grad_down = (
        lax.psum_scatter(
            grad_up_local.astype(jnp.bfloat16), "dp", scatter_dimension=1, tiled=True
        ).astype(jnp.float32),
        lax.psum_scatter(
            grad_down_local.astype(jnp.bfloat16), "dp", scatter_dimension=1, tiled=True
        ).astype(jnp.float32),
    )
    grad_back = lax.all_to_all(
        grad_items, "expert", split_axis=0, concat_axis=0, tiled=True
    ).reshape(experts * most, D)
    grad_hidden = grad_out + jnp.sum(
        grad_back[slot_of_row].reshape(count, TOPK, D), axis=1, dtype=f32
    )
    grad_picked = grad_gates * gates * (1.0 - gates)
    expert_ids = jnp.arange(experts, dtype=jnp.int32)
    grad_logits = jnp.sum(
        jnp.where(routes[:, :, None] == expert_ids[None, None, :], grad_picked[..., None], 0.0),
        axis=1,
    ).astype(bf16)
    grad_router = lax.dot_general(
        hidden_low, grad_logits, contract_first, preferred_element_type=f32
    )
    grad_hidden = grad_hidden + lax.dot_general(
        grad_logits, w_router, contract_last, preferred_element_type=f32
    )
    grad_hidden_low = grad_hidden.astype(bf16)
    grad_output = lax.dot_general(
        grad_hidden_low, heads_mixed, contract_first, preferred_element_type=f32
    )
    grad_mixed = jnp.dot(grad_hidden_low, w_output, preferred_element_type=f32).reshape(
        count, EA, H, DH
    )
    grad_attended = jnp.sum(output_gates[..., None] * grad_mixed, axis=1).astype(bf16)
    grad_out_gates = jnp.sum(grad_mixed * attended[:, None], axis=-1)
    grad_out_logits = (
        jnp.where(chosen, grad_out_gates * output_gates * (1.0 - output_gates), 0.0)
        .astype(bf16)
        .reshape(count, EA * H)
    )

    def attend_back(carry, start):
        grad_keys, grad_vals = carry
        query_block, scores = scores_at(start)
        shares = jnp.exp(scores - log_totals[..., None])
        grad_shares = jnp.einsum("qhd,khd->hqk", grad_attended, values, preferred_element_type=f32)
        centre = jnp.sum(shares * grad_shares, axis=-1, keepdims=True)
        grad_scores = (shares * (grad_shares - centre)).astype(bf16)
        grad_query_block = jnp.einsum(
            "hqk,khd->qhd", grad_scores, key_rot, preferred_element_type=f32
        )
        grad_keys = grad_keys + jnp.einsum(
            "hqk,qhd->khd", grad_scores, query_block, preferred_element_type=f32
        )
        grad_vals = grad_vals + jnp.einsum(
            "hqk,qhd->khd", shares.astype(bf16), grad_attended, preferred_element_type=f32
        )
        return ((grad_keys, grad_vals), grad_query_block)

    zero_heads = jnp.zeros((count, H, DH), f32)
    (grad_keys, grad_vals), grad_queries = lax.scan(
        attend_back, (zero_heads, zero_heads), block_starts
    )
    grad_queries = grad_queries.reshape(count, H, DH)
    grad_query_proj = (
        rotate_back(grad_queries * scale, cosine, sine).astype(bf16).reshape(count, H * DH)
    )
    grad_key_proj = rotate_back(grad_keys, cosine, sine).astype(bf16).reshape(count, H * DH)
    grad_value_all = (
        (value_gates[..., None] * grad_vals[:, None]).astype(bf16).reshape(count, EA * H * DH)
    )
    grad_value_gates = jnp.sum(grad_vals[:, None] * value_all, axis=-1)
    grad_value_logits = (
        jnp.where(chosen, grad_value_gates * value_gates * (1.0 - value_gates), 0.0)
        .astype(bf16)
        .reshape(count, EA * H)
    )
    grad_query = lax.dot_general(
        normed, grad_query_proj, contract_first, preferred_element_type=f32
    )
    grad_key = lax.dot_general(normed, grad_key_proj, contract_first, preferred_element_type=f32)
    grad_value = lax.dot_general(tokens, grad_value_all, contract_first, preferred_element_type=f32)
    grad_value_gate = lax.dot_general(
        tokens, grad_value_logits, contract_first, preferred_element_type=f32
    )
    grad_output_gate = lax.dot_general(
        tokens, grad_out_logits, contract_first, preferred_element_type=f32
    )
    grad_normed = lax.dot_general(
        grad_query_proj, w_query, contract_last, preferred_element_type=f32
    ) + lax.dot_general(grad_key_proj, w_key, contract_last, preferred_element_type=f32)
    grad_gain = jnp.sum(grad_normed * standard, axis=0)
    grad_standard = grad_normed * norm_gain
    grad_tokens = grad_hidden + inverse * (
        grad_standard
        - jnp.mean(grad_standard, axis=-1, keepdims=True)
        - standard * jnp.mean(grad_standard * standard, axis=-1, keepdims=True)
    )
    grad_tokens = (
        grad_tokens
        + lax.dot_general(grad_value_all, w_value, contract_last, preferred_element_type=f32)
        + lax.dot_general(
            grad_value_logits, w_value_gate, contract_last, preferred_element_type=f32
        )
        + lax.dot_general(grad_out_logits, w_output_gate, contract_last, preferred_element_type=f32)
    )
    summed = (
        lax.psum_scatter(grad_gain, ("dp", "expert"), scatter_dimension=0, tiled=True),
        lax.psum_scatter(grad_query, ("dp", "expert"), scatter_dimension=0, tiled=True),
        lax.psum_scatter(grad_key, ("dp", "expert"), scatter_dimension=0, tiled=True),
        lax.psum_scatter(grad_value, ("dp", "expert"), scatter_dimension=0, tiled=True),
        lax.psum_scatter(grad_output, ("dp", "expert"), scatter_dimension=0, tiled=True),
        lax.psum_scatter(grad_value_gate, ("dp", "expert"), scatter_dimension=0, tiled=True),
        lax.psum_scatter(grad_output_gate, ("dp", "expert"), scatter_dimension=0, tiled=True),
        lax.psum_scatter(grad_router, ("dp", "expert"), scatter_dimension=0, tiled=True),
    )
    return (
        mixed,
        grad_tokens,
        summed[0],
        summed[1],
        summed[2],
        summed[3],
        summed[4],
        summed[5],
        summed[6],
        summed[7],
        grad_up,
        grad_down,
    )


F32 = jnp.float32
BF16 = jnp.bfloat16
MESH = pl.DeviceIdType.MESH
LANES = 128


def mm(a, b):
    return lax.dot_general(a, b, (((1,), (0,)), ((), ())), preferred_element_type=F32)


def mm_t(a, b):
    return lax.dot_general(a, b, (((1,), (1,)), ((), ())), preferred_element_type=F32)


def tmm(a, b):
    return lax.dot_general(a, b, (((0,), (0,)), ((), ())), preferred_element_type=F32)


def iota(shape, axis):
    return lax.broadcasted_iota(jnp.int32, shape, axis)


def column(x, j, width=LANES):
    return jnp.broadcast_to(x[:, j : j + 1], (x.shape[0], width))


def sigmoid(x):
    return 1.0 / (1.0 + jnp.exp(-x))


class Scratch:
    def __init__(self):
        self.names, self.shapes = [], []

    def add(self, name, shape):
        self.names.append(name)
        self.shapes.append(shape)

    def vmem(self, name, shape, dtype):
        self.add(name, pltpu.VMEM(shape, dtype))

    def sems(self, name, *shape):
        self.add(name, pltpu.SemaphoreType.DMA(shape))


SMALL = ("tokens", "cot", "lens", "rt", "het", "gain", "wvg", "wog", "wr")
WEIGHTS = ("wq", "wk", "wv", "wo", "wu", "wd")
OUTPUTS = ("mixed", "gtok", "ggain", "gq", "gk", "gv", "go", "gvg", "gog", "gr", "gup", "gdn")


def in_hbm(names):
    return tuple(name + "_h" for name in names)


def layer_kernel(names, nd, nz, local, *refs):
    r = dict(zip(names, refs))
    R = type("R", (), r)
    C = R.tokens.shape[0]
    own_e = 2 * local
    pad_e = R.maskb.shape[1]
    EF = own_e * DH
    HF = local * DH
    HD = H * DH
    EV = EA * HD
    S = D // (nd * nz * 2)
    SL = S * nz
    GATE = EA * H
    p = lax.axis_index("dp")
    e = lax.axis_index("expert")
    z = e // 2
    c = e % 2
    sib = 1 - c

    def dev(p_, z_, c_):
        return (p_, z_ * 2 + c_)

    def times(i, n):
        return pl.multiple_of(i * n, n)

    def remote(src, dst, ss, rs, to):
        return pltpu.make_async_remote_copy(
            src_ref=src, dst_ref=dst, send_sem=ss, recv_sem=rs, device_id=to, device_id_type=MESH
        )

    def arrived(dst, rs):
        remote(dst, dst, rs, rs, dev(p, z, sib)).wait_recv()

    def sent(src, ss):
        remote(src, src, ss, ss, dev(p, z, sib)).wait_send()

    beside = p + 1 - 2 * lax.rem(p, 2)
    across = lax.rem(p + 2, nd)
    diagonal = lax.rem(beside + 2, nd)

    def core_cols(cc):
        return pl.ds(times(cc, HF), HF)

    def plane(k):
        return (p, beside, across, diagonal)[k]

    def line(k):
        return lax.rem(z + k, nz)

    barrier = pltpu.get_barrier_semaphore()
    partners = [dev(p, z, sib)]
    partners += [dev(p, line(k), c) for k in range(1, nz)]
    for k in range(1, nd):
        partners += [dev(plane(k), z, c), dev(plane(k), z, sib)]
    for to in partners:
        pl.semaphore_signal(barrier, inc=1, device_id=to, device_id_type=MESH)

    loads = {}

    def load(name, src, dst, sem):
        cp = pltpu.make_async_copy(src, dst, sem)
        cp.start()
        loads[name] = cp

    def loaded(*names):
        for name in names:
            loads.pop(name).wait()

    def landed(dst, sem):
        pltpu.make_async_copy(dst, dst, sem).wait()

    for i, name in enumerate(("cot", "lens", "rt", "tokens", "gain", "het", "wvg", "wog", "wr")):
        load(name, r[name + "_h"], r[name], R.ld_in.at[i])
    stores = []

    def store(*names):
        for name in names:
            cp = pltpu.make_async_copy(r[name], r[name + "_h"], R.ld_in.at[OUTPUTS.index(name)])
            cp.start()
            stores.append(cp)

    loaded("lens")
    l0 = R.lens[0, 0]
    b1 = l0 + R.lens[0, 1]
    row = iota((C, LANES), 0)
    lane = iota((C, LANES), 1)
    seq_r = (row >= l0).astype(jnp.int32) + (row >= b1).astype(jnp.int32)
    seq_c = (lane >= l0).astype(jnp.int32) + (lane >= b1).astype(jnp.int32)
    live = row < b1
    allowed = ((seq_r == seq_c) & (lane <= row) & (lane < b1)) | (row == lane)
    live_f = jnp.where(live, 1.0, 0.0).astype(F32)
    start = jnp.where(seq_r == 0, 0, l0)
    position = jnp.where(live, row - start, 0).astype(F32)

    loaded("cot")
    for b in range(D // LANES):
        cols = slice(b * LANES, (b + 1) * LANES)
        R.cotb[pl.ds(times(z, C), C), cols] = (R.cot[:, cols].astype(F32) * live_f).astype(BF16)
    load("qk", R.wq, R.wqk_b.at[:, 0:HD], R.ld.at[0])
    load("qk", R.wk, R.wqk_b.at[:, HD : 2 * HD], R.ld.at[0])
    load("v", R.wv, R.wv_b, R.ld.at[1])
    for i in range(local):
        col = times(c * local + i, DH)
        load("up", R.wu.at[i], R.wup_b.at[:, pl.ds(col, DH)], R.ld.at[2])
        load("dn", R.wd.at[i], R.wdn_b.at[:, pl.ds(col, DH)], R.ld.at[3])
    load("o", R.wo, R.wo_b, R.ld.at[4])
    loaded("rt")
    ids = iota((pad_e, C), 0)
    for zz in range(nz):
        named = jnp.zeros((pad_e, C), F32)
        for k in range(TOPK):
            hit = jnp.broadcast_to(R.rt[k : k + 1, :], (pad_e, C)) == ids + zz * own_e
            named = jnp.where(hit & (ids < own_e), 1.0, named)
        R.mask_s[zz] = named.astype(BF16)
    R.maskb[z] = R.mask_s[z]

    pl.semaphore_wait(barrier, len(partners))

    def block(buf, o):
        return buf.at[pl.ds(times(o, C), C), :]

    def pass_on(buf, ss, rs, o, right, left):
        @pl.when(right)
        def _():
            remote(block(buf, o), block(buf, o), ss.at[o], rs.at[o], dev(p, z + 1, c)).start()

        @pl.when(left)
        def _():
            way = jnp.where(o == z, nz, o)
            remote(block(buf, o), block(buf, o), ss.at[way], rs.at[o], dev(p, z - 1, c)).start()

    def passed(buf, ss, o, right, left):
        @pl.when(right)
        def _():
            sent(block(buf, o), ss.at[o])

        @pl.when(left)
        def _():
            sent(block(buf, o), ss.at[jnp.where(o == z, nz, o)])

    def gather_own(buf, ss, rs):
        pass_on(buf, ss, rs, z, z < nz - 1, z > 0)

    def gather_on(buf, ss, rs, o):
        arrived(block(buf, o), rs.at[o])
        pass_on(buf, ss, rs, o, (o < z) & (z < nz - 1), (o > z) & (z > 0))

    def gather_step(buf, ss, rs, k):
        @pl.when(z >= k)
        def _():
            gather_on(buf, ss, rs, z - k)

        @pl.when(z + k < nz)
        def _():
            gather_on(buf, ss, rs, z + k)

    def gather_end(buf, ss):
        passed(buf, ss, z, z < nz - 1, z > 0)
        for k in range(1, nz):

            @pl.when(z >= k)
            def _():
                passed(buf, ss, z - k, z < nz - 1, False)

            @pl.when(z + k < nz)
            def _():
                passed(buf, ss, z + k, False, z > 0)

    gather_own(R.cotb, R.cot_ss, R.cot_rs)
    for k in range(1, nz):
        o = line(k)
        remote(R.mask_s.at[o], R.maskb.at[z], R.tiny_s.at[0], R.tiny_r.at[0], dev(p, o, c)).start()

    loaded("tokens", "gain", "het", "wvg", "wog", "wr")

    s_row, s_col = iota((GATE, LANES), 0), iota((GATE, LANES), 1)
    to_v = jnp.where(s_row == s_col, 1.0, 0.0).astype(BF16)
    to_o = jnp.where(s_row + GATE == s_col, 1.0, 0.0).astype(BF16)
    R.wg_b[...] = (tmm(R.wvg[...], to_v) + tmm(R.wog[...], to_o)).astype(BF16)
    experts = R.wr.shape[0]
    r_row, r_col = iota((experts, LANES), 0), iota((experts, LANES), 1)
    to_r = jnp.where((r_row == r_col + z * own_e) & (r_col < own_e), 1.0, 0.0).astype(BF16)
    R.wrl_b[...] = tmm(R.wr[...], to_r).astype(BF16)

    half = lax.rem(lane, DH // 2).astype(F32)
    angle = position * jnp.exp(half * (-2.0 / DH * math.log(rope_base)))
    cosine = jnp.cos(angle)
    sine = jnp.where(lane < DH // 2, -jnp.sin(angle), jnp.sin(angle))

    def rot(v):
        return v * cosine + pltpu.roll(v, DH // 2, 1) * sine

    def rot_back(v):
        return v * cosine - pltpu.roll(v, DH // 2, 1) * sine

    inputs = R.tokens[...].astype(F32)
    centred = inputs - jnp.mean(inputs, axis=-1, keepdims=True)
    inverse = lax.rsqrt(jnp.mean(centred * centred, axis=-1, keepdims=True) + norm_eps)
    standard = centred * inverse
    R.std_b[...] = standard
    R.normed_b[...] = (standard * R.gain[...]).astype(BF16)

    landed(R.wqk_b, R.ld.at[0])
    scale = DH ** (-0.5)
    qk = mm(R.normed_b[...], R.wqk_b[:, 0:HD])
    for h in range(H):
        hs = slice(h * DH, (h + 1) * DH)
        R.q_b[:, hs] = (rot(qk[:, hs]) * scale).astype(BF16)
    qk = mm(R.normed_b[...], R.wqk_b[:, HD : 2 * HD])
    for h in range(H):
        hs = slice(h * DH, (h + 1) * DH)
        R.k_b[:, hs] = rot(qk[:, hs]).astype(BF16)

    hit = []
    for j in range(GATE):
        x, h = divmod(j, H)
        one = (R.het[2 * h : 2 * h + 1, :] == x) | (R.het[2 * h + 1 : 2 * h + 2, :] == x)
        hit.append(jnp.where(one, 1.0, 0.0).astype(F32))
    hit = jnp.concatenate(hit + hit + [jnp.zeros((LANES - 2 * GATE, C), F32)], axis=0)
    R.gate_b[...] = sigmoid(mm(R.tokens[...], R.wg_b[...])) * hit.T

    landed(R.wup_b.at[:, core_cols(c)], R.ld.at[2])
    landed(R.wdn_b.at[:, core_cols(c)], R.ld.at[3])
    for i, buf in enumerate((R.wup_b, R.wdn_b)):
        part = buf.at[:, pl.ds(times(c, HF), HF)]
        cp = remote(part, part, R.w_s.at[0], R.w_s.at[1], dev(p, z, sib))
        cp.start()

    landed(R.wv_b, R.ld.at[1])
    gates = R.gate_b[...]
    total = [None] * H
    for x in range(EA):
        R.val_b[:, x * HD : (x + 1) * HD] = mm(R.tokens[...], R.wv_b[:, x * HD : (x + 1) * HD])
        for h in range(H):
            lo = x * HD + h * DH
            term = column(gates, x * H + h) * R.val_b[:, lo : lo + DH]
            total[h] = term if x == 0 else total[h] + term
    for h in range(H):
        R.v_b[:, h * DH : (h + 1) * DH] = total[h].astype(BF16)

    for h in range(H):
        hs = slice(h * DH, (h + 1) * DH)
        scores = jnp.where(allowed, mm_t(R.q_b[:, hs], R.k_b[:, hs]), masked_score)
        shifted = jnp.exp(scores - jnp.max(scores, axis=-1, keepdims=True))
        shares = shifted / jnp.sum(shifted, axis=-1, keepdims=True)
        R.prob_b[h] = shares
        R.att_b[:, hs] = mm(shares.astype(BF16), R.v_b[:, hs])

    for x in range(EA):
        for h in range(H):
            lo = x * HD + h * DH
            R.mix_b[:, lo : lo + DH] = (
                column(gates, GATE + x * H + h) * R.att_b[:, h * DH : (h + 1) * DH]
            ).astype(BF16)
    landed(R.wo_b, R.ld.at[4])
    half_d = D // 2
    for b in range(2):
        cols = slice(b * half_d, (b + 1) * half_d)
        hidden = R.tokens[:, cols].astype(F32) + mm_t(R.mix_b[...], R.wo_b[cols, :])
        R.hid_f[:, cols] = hidden
        R.hidb[pl.ds(times(z, C), C), cols] = hidden.astype(BF16)
    gather_own(R.hidb, R.hid_ss, R.hid_rs)
    gather_step(R.cotb, R.cot_ss, R.cot_rs, 1)

    def put_turned(x, w):
        for b in range(D // LANES):
            t = x[:, b * LANES : (b + 1) * LANES].astype(F32).T.astype(BF16)
            for q in range(LANES // S):
                i = (b * LANES) // S + q
                pp, zz, cc = i // (2 * nz), (i % (2 * nz)) // 2, i % 2
                at = (pp * 2 + cc) * SL + zz * S
                R.lt[at : at + S, w * LANES : (w + 1) * LANES] = t[q * S : (q + 1) * S, :]

    plane_all = [(k, dc) for k in range(nd) for dc in range(2) if k or dc]

    def side(dc):
        return sib if dc else c

    def send_turned(w0, w1, ss, rs):
        lanes = slice(w0 * LANES, w1 * LANES)
        for k, dc in plane_all:
            to = plane(k)
            slot = 2 * k + dc
            at = times(to * 2 + side(dc), SL)
            cp = remote(
                R.lt.at[pl.ds(at, SL), lanes],
                R.ltr.at[slot, :, lanes],
                ss,
                rs,
                dev(to, z, side(dc)),
            )
            cp.start()
        R.ltr[0, :, lanes] = R.lt[pl.ds(times(p * 2 + c, SL), SL), lanes]

    def turned_here(w0, w1, ss, rs):
        there = R.ltr.at[1 : 2 * nd, :, w0 * LANES : w1 * LANES]
        sent(there, ss)
        arrived(there, rs)

    def rows_at(buf, lanes, slot):
        return buf.at[slot * C : (slot + 1) * C, lanes]

    def send_rows(buf, lanes, sem, ways=(1, 2)):
        for k in ways:
            remote(
                rows_at(buf, lanes, 0),
                rows_at(buf, lanes, 2 * k),
                sem.at[0],
                sem.at[k],
                dev(plane(k), z, c),
            ).start()
        hand_over(buf, lanes, sem, 0)

    def hand_over(buf, lanes, sem, k):
        remote(
            rows_at(buf, lanes, 2 * k),
            rows_at(buf, lanes, 2 * k + 1),
            sem.at[0],
            sem.at[5 if k == 3 else 4],
            dev(p, z, sib),
        ).start()

    def hand_near(buf, lanes, sem, via):
        for k in (via, 3 - via) if via else (1, 2):
            arrived(rows_at(buf, lanes, 2 * k), sem.at[k])
            if k == via:
                remote(
                    rows_at(buf, lanes, 2 * k),
                    rows_at(buf, lanes, 6),
                    sem.at[0],
                    sem.at[3],
                    dev(plane(3 - via), z, c),
                ).start()
            hand_over(buf, lanes, sem, k)

    def hand_far(buf, lanes, sem):
        arrived(rows_at(buf, lanes, 6), sem.at[3])
        hand_over(buf, lanes, sem, 3)

    def near_here(buf, lanes, sem):
        arrived(buf.at[0 : 3 * C, lanes], sem.at[4])

    def far_here(buf, lanes, sem):
        arrived(rows_at(buf, lanes, 7), sem.at[5])

    def rows_sent(buf, lanes, sem):
        sent(buf.at[0 : 7 * C, lanes], sem.at[0])

    put_turned(R.tokens[...], 0)
    put_turned(R.normed_b[...], 1)
    put_turned(R.hid_f[...], 2)
    send_turned(0, 3, R.lt_s.at[0], R.lt_s.at[1])
    R.ra[0:C, 0:HD] = R.att_b[...].astype(BF16)
    R.ra[0:C, HD : HD + LANES] = gates.astype(BF16)
    RA = slice(0, HD + LANES)
    send_rows(R.ra, RA, R.ra_s)

    sent(R.wup_b, R.w_s.at[0])
    arrived(R.wup_b, R.w_s.at[1])

    least = jnp.minimum(z, nz - 1 - z)
    inner = least > 0
    left_half = z < nz // 2
    near = jnp.where(inner, jnp.where(left_half, 0, nz - 1), jnp.where(left_half, 1, nz - 2))
    fellow = jnp.where(left_half, nz // 2, nz // 2 - 1)
    far = jnp.where(left_half, nz - 1, 0)

    def origin(k):
        paired = k <= 2 * least
        dist = jnp.where(paired, (k + 1) // 2, k - least)
        left = jnp.where(paired, lax.rem(k, 2) == 1, z > nz - 1 - z)
        return jnp.where(k == 0, z, jnp.where(left, z - dist, z + dist))

    def expert_block(k, carry):
        o = origin(k)
        rows = pl.ds(times(o, C), C)

        @pl.when((k == 1) & inner)
        def _():
            gather_on(R.hidb, R.hid_ss, R.hid_rs, origin(1))

        @pl.when((k > 0) & (k + inner.astype(jnp.int32) < nz))
        def _():
            gather_on(R.hidb, R.hid_ss, R.hid_rs, origin(k + inner.astype(jnp.int32)))

        @pl.when(k == jnp.where(inner, 1, 2))
        def _():
            for far_step in range(2, nz - 1):
                gather_step(R.cotb, R.cot_ss, R.cot_rs, far_step)

        @pl.when(k > 0)
        def _():
            @pl.when((o == z - nz + 1) | (o == z + nz - 1))
            def _():
                arrived(block(R.cotb, o), R.cot_rs.at[o])

        @pl.when(k == 1)
        def _():
            arrived(R.maskb.at[0 : nz - 1], R.tiny_r.at[0])

        hb = R.hidb[rows, :]
        cb = R.cotb[rows, :]
        named = R.maskb[o].astype(F32)
        named = jnp.concatenate([named, jnp.zeros((LANES - pad_e, C), F32)], axis=0).T
        g = sigmoid(mm(hb, R.wrl_b[...])) * named
        glog = jnp.zeros((C, LANES), F32)
        for q in range(2):
            cols = slice(q * HF, (q + 1) * HF)
            raised = mm(hb, R.wup_b[:, cols])
            back = mm(cb, R.wdn_b[:, cols])
            for i in range(local):
                j = q * local + i
                u = raised[:, i * DH : (i + 1) * DH]
                a = back[:, i * DH : (i + 1) * DH]
                gj = column(g, j)
                s = sigmoid(u)
                act = u * s
                lo = j * DH
                R.gact[rows, lo : lo + DH] = (gj * act).astype(BF16)
                R.gra[rows, lo : lo + DH] = (gj * a * (s * (1.0 + u * (1.0 - s)))).astype(BF16)
                gg = jnp.sum(a * act, axis=1, keepdims=True)
                glog = jnp.where(lane == j, jnp.broadcast_to(gg, (C, LANES)), glog)
        glog = glog * g * (1.0 - g)
        low = glog.astype(BF16)
        R.glog_s[o] = glog.T[0:pad_e, :].astype(BF16)
        for b in range(2):
            cols = slice(b * half_d, (b + 1) * half_d)
            gh = mm_t(R.gra[rows, :], R.wup_b[cols, :]) + mm_t(low, R.wrl_b[cols, :])
            R.gh_s[o, :, cols] = gh.astype(BF16)

        @pl.when(k > 0)
        def _():
            remote(
                R.glog_s.at[o], R.glog_r.at[z], R.tiny_s.at[1], R.tiny_r.at[1], dev(p, o, c)
            ).start()

        @pl.when((k > 0) & (least == 0) & (o != fellow))
        def _():
            send_back(o)

        @pl.when((k > 0) & (least == 0) & (o == fellow))
        def _():
            send_by(o, near, 0)

        @pl.when((k > 0) & inner & (o == far))
        def _():
            send_by(o, fellow, 1)

        @pl.when(k == 2)
        def _():
            hand_near(R.ra, RA, R.ra_s, 2)

        @pl.when((k == 2) & (least == 0))
        def _():
            there = pl.ds(times(near, C), C)
            for b in range(2):
                cols = slice(b * half_d, (b + 1) * half_d)
                R.out_s[near, :, cols] = mm_t(R.gact[there, :], R.wdn_b[cols, :]).astype(BF16)
            slot = jnp.where(z == 0, near, nz)
            remote(
                R.out_s.at[near],
                R.out_r.at[slot],
                R.out_sem.at[nz + 1],
                R.out_sem.at[slot],
                dev(p, near, c),
            ).start()

        return carry

    def send_back(o):
        remote(R.gh_s.at[o], R.gh_r.at[z], R.gh_sem.at[0], R.gh_sem.at[1], dev(p, o, c)).start()

    def send_by(o, by, slot):
        remote(
            R.gh_s.at[o], R.gh_x.at[slot], R.gh_sem.at[0], R.gh_sem.at[2 + slot], dev(p, by, c)
        ).start()

    def relay_back(o, slot):
        arrived(R.gh_x.at[slot], R.gh_sem.at[2 + slot])
        R.gh_s[o] = (R.gh_s[o].astype(F32) + R.gh_x[slot].astype(F32)).astype(BF16)
        send_back(o)

    lax.fori_loop(0, nz, expert_block, 0)

    def rows_of(at):
        return pl.ds(times(at, rows_d), rows_d)


    rows_d = D // nd

    def grad_at(i, k, cc):
        if i == 0 and k == 3:
            return R.dg.at[:, core_cols(cc)]
        return (R.wdn_b, R.wup_b)[i].at[rows_of(plane(k)), core_cols(cc)]

    def expert_grad(i, k):
        left, right = ((R.cotb, R.gact), (R.hidb, R.gra))[i]
        for cc in (sib, c):
            grad_at(i, k, cc)[...] = tmm(left[:, rows_of(plane(k))], right[:, core_cols(cc)]).astype(BF16)
            if cc is sib:
                remote(
                    grad_at(i, k, sib),
                    R.pair_r.at[i, k],
                    R.pair_s.at[0],
                    R.pair_s.at[1 + i if k == 3 else 3],
                    dev(p, z, sib),
                ).start()

    def pair_sum(i, k):
        if k == 3:
            arrived(R.pair_r.at[i, k], R.pair_s.at[1 + i])
        own = grad_at(i, k, c)
        own[...] = (own[...].astype(F32) + R.pair_r[i, k].astype(F32)).astype(BF16)

    def part_on(i, k, to, slot):
        remote(
            grad_at(i, k, c),
            R.eg_r.at[slot, i],
            R.eg_s.at[0],
            R.eg_s.at[1 + i if slot == 1 else 3 + i],
            dev(plane(to), z, c),
        ).start()

    def first_half(i, n):
        first = 1 if i == 0 else 2
        rows = slice(n * rows_d // 2, (n + 1) * rows_d // 2)
        remote(
            grad_at(i, first, c).at[rows],
            R.eg_r.at[0, i, rows],
            R.eg_s.at[0],
            R.eg_s.at[3 + i],
            dev(plane(first), z, c),
        ).start()

    def expert_grad_relay(i):
        second = 2 if i == 0 else 1
        first_half(i, 1)
        arrived(R.eg_r.at[1, i], R.eg_s.at[1 + i])
        own = grad_at(i, second, c)
        own[...] = (own[...].astype(F32) + R.eg_r[1, i].astype(F32)).astype(BF16)
        part_on(i, second, second, 2)

    def to_place(own, got, ss, rs, o):
        remote(own(o), got(z), ss, rs, dev(p, o, c)).start()

    def run(own, got, ss, rs, k, n):
        def hand(d, slot, to):
            if k > 1:
                arrived(got(d), rs.at[d])
                own(d)[...] = (own(d)[...].astype(F32) + got(d)[...].astype(F32)).astype(BF16)
            remote(own(d), got(slot), ss, rs.at[slot], dev(p, to, c)).start()

        @pl.when(z == k - 1)
        def _():
            hand(nz - 1 - n, nz - 1 - n, k)

        @pl.when(z == nz - k)
        def _():
            hand(n, nz if n == nz - k - 1 else n, nz - k - 1)

    def run_end(total, got, rs):
        for there, slot in ((z > 0, z), (z < nz - 1, nz)):

            @pl.when(there)
            def _():
                arrived(got(slot), rs.at[slot])
                total[...] += got(slot)[...].astype(F32)

    out_sum = (lambda d: R.out_s.at[d], lambda d: R.out_r.at[d], R.out_sem.at[nz + 1], R.out_sem)
    out_run = functools.partial(run, *out_sum)

    def grad_sum(i, lanes):
        return (
            lambda d: R.pb.at[d * S : (d + 1) * S, lanes],
            lambda d: R.pn.at[i, d],
            R.pn_sem.at[i, nz + 1],
            R.pn_sem.at[i],
        )

    def part_sum(i, lanes):
        return (
            lambda o: R.pb.at[pl.ds(times(o, S), S), lanes],
            lambda o: R.pr.at[o, :, slice(lanes.start - 2 * EV, lanes.stop - 2 * EV)],
            R.p_sem.at[0],
            R.p_sem.at[1 + i],
        )

    expert_grad(1, 3)
    expert_grad(0, 3)
    for i, to in ((1, 2), (0, 1)):
        pair_sum(i, 3)
        part_on(i, 3, to, 1)

    def out_tile(t, carry):
        rows = pl.ds(times(t, 256), 256)
        got = mm_t(R.gact[...], R.wdn_b[rows, :]).astype(BF16)
        for o in range(nz):

            @pl.when(inner | (o != near))
            def _():
                R.out_s[o, :, rows] = got[o * C : (o + 1) * C, :]

        return carry

    lax.fori_loop(0, D // 256, out_tile, 0)
    out_run(1, 0)

    @pl.when(inner)
    def _():
        relay_back(near, 1)
        relay_back(fellow, 0)

    for k in (1, 2, 0):
        expert_grad(1, k)
        expert_grad(0, k)
    R.ghid_f[...] = R.cotb[pl.ds(times(z, C), C), :].astype(F32) + R.gh_s[z].astype(F32)

    arrived(R.gh_r.at[0:2], R.gh_sem.at[1])

    def add_back(o):
        R.ghid_f[...] += R.gh_r[o].astype(F32)

    add_back(near)
    add_back(jnp.where(inner, fellow, far))

    arrived(R.glog_r.at[0 : nz - 1], R.tiny_r.at[1])
    out_run(1, 1)
    R.glog_r[z] = R.glog_s[z]
    R.ghid_b[...] = R.ghid_f[...].astype(BF16)
    put_turned(R.ghid_f[...], 3)
    send_turned(3, 4, R.lt_s.at[2], R.lt_s.at[3])
    out_run(2, 0)

    gates = R.gate_b[...]
    small = jnp.zeros((C, LANES), F32)
    gatt = [None] * H
    for x in range(EA):
        gmix = mm(R.ghid_b[...], R.wo_b[:, x * HD : (x + 1) * HD])
        for h in range(H):
            hs = slice(h * DH, (h + 1) * DH)
            j = GATE + x * H + h
            term = column(gates, j) * gmix[:, hs]
            gatt[h] = term if x == 0 else gatt[h] + term
            gg = jnp.sum(gmix[:, hs] * R.att_b[:, hs], axis=1, keepdims=True)
            small = jnp.where(lane == j, jnp.broadcast_to(gg, (C, LANES)), small)
    for h in range(H):
        hs = slice(h * DH, (h + 1) * DH)
        low = gatt[h].astype(BF16)
        R.gatt_b[:, hs] = low
        gval = tmm(R.prob_b[h].astype(BF16), low)
        R.gval_f[:, hs] = gval
        R.rb[0:C, hs] = gval.astype(BF16)
        for x in range(EA):
            lo = x * HD + h * DH
            j = x * H + h
            gg = jnp.sum(gval * R.val_b[:, lo : lo + DH], axis=1, keepdims=True)
            small = jnp.where(lane == j, jnp.broadcast_to(gg, (C, LANES)), small)
    small = small * gates * (1.0 - gates)
    glog = jnp.concatenate(
        [jnp.zeros((2 * GATE, C), F32)]
        + [R.glog_r[o].astype(F32) for o in range(nz)]
        + [jnp.zeros((LANES - 2 * GATE - nz * pad_e, C), F32)],
        axis=0,
    )
    R.small_b[...] = small.astype(BF16)
    R.rb[0:C, HD : HD + LANES] = (small + glog.T).astype(BF16)
    RV = slice(0, HD + LANES)
    send_rows(R.rb, RV, R.rv_s, (1, 2, 3))

    q0 = HD + LANES
    for h in range(H):
        hs = slice(h * DH, (h + 1) * DH)
        low = R.gatt_b[:, hs]
        gsh = mm_t(low, R.v_b[:, hs])
        prob = R.prob_b[h]
        centre = jnp.sum(prob * gsh, axis=-1, keepdims=True)
        gs = (prob * (gsh - centre)).astype(BF16)
        R.rb[0:C, q0 + h * DH : q0 + (h + 1) * DH] = rot_back(
            mm(gs, R.k_b[:, hs]) * scale
        ).astype(BF16)
        R.rb[0:C, q0 + HD + h * DH : q0 + HD + (h + 1) * DH] = rot_back(
            tmm(gs, R.q_b[:, hs])
        ).astype(BF16)
    RQ, RK = slice(q0, q0 + HD), slice(q0 + HD, q0 + 2 * HD)
    send_rows(R.rb, RQ, R.rq_s)
    send_rows(R.rb, RK, R.rk_s)

    gproj = mm_t(R.rb[0:C, q0 : q0 + 2 * HD], R.wqk_b[...])
    standard = R.std_b[...]
    column_sum = jnp.sum(gproj * standard, axis=0, keepdims=True)
    for b in range(D // LANES):
        R.gp[0, b : b + 1, :] = column_sum[:, b * LANES : (b + 1) * LANES]
    for k, dc in plane_all:
        slot = 2 * k + dc
        cp = remote(
            R.gp.at[0], R.gp.at[slot], R.tiny_s.at[2], R.tiny_r.at[2], dev(plane(k), z, side(dc))
        )
        cp.start()

    out_run(2, 1)
    arrived(R.pair_r.at[:, 0:3], R.pair_s.at[3])
    for k in (1, 2, 0):
        pair_sum(1, k)
        pair_sum(0, k)
    first_half(0, 0)
    first_half(1, 0)
    hand_far(R.ra, RA, R.ra_s)
    turned_here(0, 3, R.lt_s.at[0], R.lt_s.at[1])
    near_here(R.ra, RA, R.ra_s)
    far_here(R.ra, RA, R.ra_s)

    def turned_of(w):
        return jnp.concatenate(
            [R.ltr[s, :, w * LANES : (w + 1) * LANES] for s in range(2 * nd)], axis=1
        )

    def send_part(part, lanes):
        for o in (far, fellow, near):
            to_place(*part_sum(part, lanes), o)

    def gate_rows(dst, rows_of, g0, s0, s1):
        rows = slice(s0 * C, s1 * C)
        for x in range(EA):
            for h in range(H):
                lo = x * HD + h * DH
                gx = column(R.ra[rows, HD : HD + LANES], g0 + x * H + h).astype(F32)
                dst[rows, lo : lo + DH] = (
                    gx * rows_of[rows, h * DH : (h + 1) * DH].astype(F32)
                ).astype(BF16)

    def gated_grad(w, gated, at):
        left = turned_of(w)
        for x in range(EA):
            cols = slice(x * HD, (x + 1) * HD)
            R.pb[:, at + x * HD : at + (x + 1) * HD] = mm(left, gated[:, cols]).astype(BF16)

    PO, PV, PQ, PS = (
        slice(0, EV),
        slice(EV, 2 * EV),
        slice(2 * EV, 2 * EV + 2 * HD),
        slice(2 * EV + 2 * HD, 2 * EV + 2 * HD + LANES),
    )
    gate_rows(R.wo_b, R.ra, GATE, 0, 2 * nd)
    turned_here(3, 4, R.lt_s.at[2], R.lt_s.at[3])
    gated_grad(3, R.wo_b, 0)
    o_run = functools.partial(run, *grad_sum(0, PO))
    v_run = functools.partial(run, *grad_sum(1, PV))
    o_run(1, 0)
    o_run(1, 1)
    out_run(3, 0)
    hand_near(R.rb, RV, R.rv_s, 0)

    inputs = R.tokens[...].astype(F32)
    centred = inputs - jnp.mean(inputs, axis=-1, keepdims=True)
    inverse = lax.rsqrt(jnp.mean(centred * centred, axis=-1, keepdims=True) + norm_eps)
    gs = gproj * R.gain[...]
    gtok = R.ghid_f[...] + inverse * (
        gs
        - jnp.mean(gs, axis=-1, keepdims=True)
        - standard * jnp.mean(gs * standard, axis=-1, keepdims=True)
    )
    R.gtok[...] = gtok
    for x in range(EA):
        for h in range(H):
            lo = x * HD + h * DH
            R.mix_b[:, lo : lo + DH] = (
                column(gates, x * H + h) * R.gval_f[:, h * DH : (h + 1) * DH]
            ).astype(BF16)
    for b in range(2):
        cols = slice(b * half_d, (b + 1) * half_d)
        R.gtok[:, cols] += mm_t(R.mix_b[...], R.wv_b[cols, :]) + mm_t(
            R.small_b[...], R.wg_b[cols, :]
        )

    store("gtok")

    o_run(2, 0)
    near_here(R.rb, RV, R.rv_s)
    gate_rows(R.wv_b, R.rb, 0, 0, 6)
    o_run(2, 1)
    hand_far(R.rb, RV, R.rv_s)
    far_here(R.rb, RV, R.rv_s)
    gate_rows(R.wv_b, R.rb, 0, 6, 8)
    gated_grad(0, R.wv_b, EV)
    v_run(1, 0)
    v_run(1, 1)
    o_run(1, 2)
    hand_near(R.rb, RK, R.rk_s, 2)
    hand_near(R.rb, RQ, R.rq_s, 1)
    expert_grad_relay(0)
    expert_grad_relay(1)
    o_run(3, 0)
    total = R.gp[0]
    sent(R.gp.at[1:], R.tiny_s.at[2])
    arrived(R.gp.at[1:], R.tiny_r.at[2])
    for k, dc in plane_all:
        total = total + R.gp[2 * k + dc]
    R.gz_s[...] = total
    for k in range(1, nz):
        o = line(k)
        remote(R.gz_s, R.gz.at[z], R.tiny_s.at[3], R.tiny_r.at[3], dev(p, o, c)).start()

    lane_s = iota((SL, LANES), 1)
    small_t = mm(turned_of(0), R.rb[:, HD : HD + LANES])
    small_h = mm(turned_of(2), R.rb[:, HD : HD + LANES])
    R.pb[:, PS] = jnp.where(lane_s < 2 * GATE, small_t, small_h).astype(BF16)
    send_part(1, PS)
    v_run(2, 0)
    v_run(2, 1)
    hand_far(R.rb, RQ, R.rq_s)
    hand_far(R.rb, RK, R.rk_s)
    for lanes, sem in ((RQ, R.rq_s), (RK, R.rk_s)):
        near_here(R.rb, lanes, sem)
        far_here(R.rb, lanes, sem)
    left = turned_of(1)
    for b in range(2):
        lo = q0 + b * HD
        R.pb[:, 2 * EV + b * HD : 2 * EV + (b + 1) * HD] = mm(left, R.rb[:, lo : lo + HD]).astype(
            BF16
        )
    send_part(0, PQ)
    v_run(1, 2)
    v_run(3, 0)

    R.hid_f[...] += R.out_s[z].astype(F32)
    run_end(R.hid_f, out_sum[1], R.out_sem)
    R.mixed[...] = R.hid_f[...].astype(BF16)
    store("mixed")

    arrived(R.gz.at[0 : nz - 1], R.tiny_r.at[3])
    for k in range(1, nz):
        total = total + R.gz[line(k)]
    first = (p * 2 * nz + z * 2 + c) * S
    pick_row = iota((D // LANES, LANES), 0) == first // LANES
    line_sum = jnp.sum(jnp.where(pick_row, total, 0.0), axis=0, keepdims=True)
    shift = lax.rem(LANES - lax.rem(first, LANES), LANES)
    line_sum = pltpu.roll(jnp.broadcast_to(line_sum, (8, LANES)), shift, 1)
    R.ggain[...] = line_sum[0:1, 0:S]
    store("ggain")

    own_rows = pl.ds(times(z, S), S)

    def line_total(part, lanes):
        got = R.pb[own_rows, lanes].astype(F32)
        slots = part_sum(part, lanes)[1]
        arrived(slots(slice(0, nz - 1)), R.p_sem.at[1 + part])
        for k in range(1, nz):
            got = got + slots(line(k))[...].astype(F32)
        return got

    for i, (dst, lanes) in enumerate(((R.go, PO), (R.gv, PV))):
        dst[...] = R.pb[own_rows, lanes].astype(F32)
        run_end(dst, grad_sum(i, lanes)[1], R.pn_sem.at[i])
    store("go", "gv")
    got = line_total(1, PS)

    def pick(width, source):
        a, b = iota((width, LANES), 1), iota((width, LANES), 0)
        return jnp.where(a == source(b), 1.0, 0.0).astype(F32)

    def picked(left, right):
        return lax.dot_general(
            left,
            right,
            (((1,), (1,)), ((), ())),
            preferred_element_type=F32,
            precision=lax.Precision.HIGHEST,
        )

    def router_lane(b):
        at = jnp.zeros_like(b)
        for o in range(nz):
            at = jnp.where(b >= o * own_e, 2 * GATE + o * pad_e + b - o * own_e, at)
        return at

    R.gvg[...] = picked(pick(GATE, lambda b: b), got)
    R.gog[...] = picked(pick(GATE, lambda b: b + GATE), got)
    R.gr[...] = picked(got, pick(experts, router_lane))
    store("gvg", "gog", "gr")
    got = line_total(0, PQ)
    R.gq[...] = got[:, 0:HD]
    R.gk[...] = got[:, HD : 2 * HD]
    store("gq", "gk")

    for i, (buf, dst) in enumerate(((R.wdn_b, R.gdn), (R.wup_b, R.gup))):
        arrived(R.eg_r.at[0:2, i], R.eg_s.at[3 + i])
        rows = rows_of(p)
        for x in range(local):
            got = buf[rows, pl.ds(times(c * local + x, DH), DH)].astype(F32)
            for slot in (0, 2):
                got = got + R.eg_r[slot, i, :, x * DH : (x + 1) * DH].astype(F32)
            dst[x] = got
        store(("gdn", "gup")[i])

    for cp in stores:
        cp.wait()
    gather_end(R.cotb, R.cot_ss)
    gather_end(R.hidb, R.hid_ss)
    for buf, lanes, sem in (
        (R.ra, RA, R.ra_s),
        (R.rb, RV, R.rv_s),
        (R.rb, RQ, R.rq_s),
        (R.rb, RK, R.rk_s),
    ):
        rows_sent(buf, lanes, sem)
    sent(R.maskb.at[0 : nz - 1], R.tiny_s.at[0])
    sent(R.glog_r.at[0 : nz - 1], R.tiny_s.at[1])
    sent(R.gz.at[0 : nz - 1], R.tiny_s.at[3])
    sent(R.gh_r.at[0 : nz - 1], R.gh_sem.at[0])
    sent(R.out_r.at[0 : nz - 1], R.out_sem.at[nz + 1])
    sent(R.pair_r, R.pair_s.at[0])
    sent(R.eg_r, R.eg_s.at[0])
    sent(R.pr.at[0 : nz - 1], R.p_sem.at[0])
    for i in range(2):
        sent(R.pn.at[i, 0 : nz - 1], R.pn_sem.at[i, nz + 1])


def settle_kernel(n, *refs):
    src, dst, held, sems = refs[:n], refs[n : 2 * n], refs[2 * n : 3 * n], refs[-1]
    ins = [pltpu.make_async_copy(src[i], held[i], sems.at[i]) for i in range(n)]
    outs = [pltpu.make_async_copy(held[i], dst[i], sems.at[i]) for i in range(n)]
    for cp in ins:
        cp.start()
    for there, back in zip(ins, outs):
        there.wait()
        back.start()
    for cp in outs:
        cp.wait()


def fused_layer(nd, nz, *args):
    (tokens, cotangent, seq_lengths, routes, head_experts, norm_gain) = args[:6]
    (w_query, w_key, w_value, w_output, w_value_gate, w_output_gate, w_router) = args[6:13]
    w_up, w_down = args[13:]
    C = tokens.shape[0]
    local = w_up.shape[0]
    experts = w_router.shape[1]
    own_e = 2 * local
    pad_e = -(-own_e // 16) * 16
    EF, HF, HD = own_e * DH, local * DH, H * DH
    EV = EA * HD
    S = D // (nd * nz * 2)
    SL = S * nz
    PW = 2 * EV + 2 * HD + LANES
    s = Scratch()
    s.vmem("wqk_b", (D, 2 * HD), BF16)
    s.vmem("wv_b", (D, EV), BF16)
    s.vmem("wo_b", (D, EV), BF16)
    s.vmem("wup_b", (D, EF), BF16)
    s.vmem("wdn_b", (D, EF), BF16)
    s.vmem("wg_b", (D, LANES), BF16)
    s.vmem("wrl_b", (D, LANES), BF16)
    s.vmem("cotb", (nz * C, D), BF16)
    s.vmem("hidb", (nz * C, D), BF16)
    s.vmem("mask_s", (nz, pad_e, C), BF16)
    s.vmem("maskb", (nz, pad_e, C), BF16)
    s.vmem("std_b", (C, D), F32)
    s.vmem("normed_b", (C, D), BF16)
    s.vmem("q_b", (C, HD), BF16)
    s.vmem("k_b", (C, HD), BF16)
    s.vmem("v_b", (C, HD), BF16)
    s.vmem("gate_b", (C, LANES), F32)
    s.vmem("val_b", (C, EV), F32)
    s.vmem("prob_b", (H, C, C), F32)
    s.vmem("att_b", (C, HD), F32)
    s.vmem("mix_b", (C, EV), BF16)
    s.vmem("hid_f", (C, D), F32)
    s.vmem("lt", (D, 4 * LANES), BF16)
    s.vmem("ltr", (2 * nd, SL, 4 * LANES), BF16)
    s.vmem("ra", (2 * nd * C, HD + LANES), BF16)
    s.vmem("rb", (2 * nd * C, 3 * HD + LANES), BF16)
    s.vmem("gact", (nz * C, EF), BF16)
    s.vmem("gra", (nz * C, EF), BF16)
    for name in ("gh_s", "gh_r", "out_s"):
        s.vmem(name, (nz, C, D), BF16)
    s.vmem("out_r", (nz + 1, C, D), BF16)
    s.vmem("gh_x", (2, C, D), BF16)
    for name in ("glog_s", "glog_r"):
        s.vmem(name, (nz, pad_e, C), BF16)
    s.vmem("dg", (D // nd, EF), BF16)
    s.vmem("pair_r", (2, nd, D // nd, HF), BF16)
    s.vmem("eg_r", (nd - 1, 2, D // nd, HF), BF16)
    s.vmem("ghid_f", (C, D), F32)
    s.vmem("ghid_b", (C, D), BF16)
    s.vmem("gatt_b", (C, HD), BF16)
    s.vmem("gval_f", (C, HD), F32)
    s.vmem("small_b", (C, LANES), BF16)
    s.vmem("pb", (SL, PW), BF16)
    s.vmem("pr", (nz, S, PW - 2 * EV), BF16)
    s.vmem("pn", (2, nz + 1, S, EV), BF16)
    s.vmem("gp", (2 * nd, D // LANES, LANES), F32)
    s.vmem("gz_s", (D // LANES, LANES), F32)
    s.vmem("gz", (nz, D // LANES, LANES), F32)
    s.sems("ld", 5)
    for name in ("cot_ss", "hid_ss"):
        s.sems(name, nz + 1)
    for name in ("cot_rs", "hid_rs", "tiny_s", "tiny_r", "lt_s", "gh_sem", "pair_s"):
        s.sems(name, 4)
    for name in ("ra_s", "rv_s", "rq_s", "rk_s"):
        s.sems(name, 6)
    s.sems("w_s", 2)
    s.sems("eg_s", 5)
    s.sems("p_sem", 3)
    s.sems("out_sem", nz + 2)
    s.sems("pn_sem", 2, nz + 2)

    def out(*shape, dtype=F32):
        return jax.ShapeDtypeStruct(shape, dtype)

    hbm = pl.BlockSpec(memory_space=pl.ANY)
    names = in_hbm(SMALL) + WEIGHTS + in_hbm(OUTPUTS)
    results = (
        out(C, D, dtype=BF16),
        out(C, D),
        out(1, S),
        out(S, HD),
        out(S, HD),
        out(S, EV),
        out(S, EV),
        out(EA * H, S),
        out(EA * H, S),
        out(S, experts),
        out(local, D // nd, DH),
        out(local, D // nd, DH),
    )
    for name, x in zip(OUTPUTS, results):
        s.vmem(name, x.shape, x.dtype)
    s.vmem("tokens", (C, D), BF16)
    s.vmem("cot", (C, D), BF16)
    s.add("lens", pltpu.SMEM((1, 2), jnp.int32))
    s.vmem("rt", (TOPK, C), jnp.int32)
    s.vmem("het", (2 * H, C), jnp.int32)
    s.vmem("gain", (1, D), F32)
    s.vmem("wvg", (EA * H, D), BF16)
    s.vmem("wog", (EA * H, D), BF16)
    s.vmem("wr", (experts, D), BF16)
    s.sems("ld_in", len(OUTPUTS))
    outs = pl.pallas_call(
        functools.partial(layer_kernel, names + tuple(s.names), nd, nz, local),
        out_shape=results,
        in_specs=[hbm] * 15,
        out_specs=[hbm] * len(OUTPUTS),
        scratch_shapes=s.shapes,
        compiler_params=pltpu.CompilerParams(
            collective_id=0, has_side_effects=True, vmem_limit_bytes=VMEM_LIMIT
        ),
    )(
        tokens,
        cotangent,
        seq_lengths,
        routes.T,
        head_experts.reshape(C, 2 * H).T,
        norm_gain.reshape(1, D),
        w_value_gate.T,
        w_output_gate.T,
        w_router.T,
        w_query,
        w_key,
        w_value,
        w_output,
        w_up,
        w_down,
    )
    outs = list(
        pl.pallas_call(
            functools.partial(settle_kernel, len(outs)),
            out_shape=results,
            in_specs=[hbm] * len(outs),
            out_specs=[hbm] * len(outs),
            scratch_shapes=[pltpu.VMEM(x.shape, x.dtype) for x in outs]
            + [pltpu.SemaphoreType.DMA((len(outs),))],
            compiler_params=pltpu.CompilerParams(vmem_limit_bytes=VMEM_LIMIT),
        )(*outs)
    )
    outs[2] = outs[2].reshape(S)
    for i in (7, 8):
        outs[i] = outs[i].T
    return tuple(outs)


VMEM_LIMIT = 62 * 1024 * 1024


def fits(nd, nz, count, experts):
    own_e = experts // nz
    pad_e = -(-own_e // 16) * 16
    return (
        count == LANES
        and nz == 4
        and nd == 4
        and own_e % 4 == 0
        and D % (nd * nz * 2 * 16) == 0
        and LANES % (D // (nd * nz * 2)) == 0
        and 2 * EA * H + nz * pad_e <= LANES
    )


def per_device(nd, ne, *args):
    count, experts = args[0].shape[0], args[12].shape[1]
    if ne % 2 == 0 and fits(nd, ne // 2, count, experts):
        return fused_layer(nd, ne // 2, *args)
    return routed_layer(*args)


def solution(mesh):
    return jax.shard_map(
        functools.partial(per_device, mesh.shape["dp"], mesh.shape["expert"]),
        mesh=mesh,
        in_specs=(
            P(("dp", "expert"), None),
            P(("dp", "expert"), None),
            P(("dp", "expert"), None),
            P(("dp", "expert"), None),
            P(("dp", "expert"), None, None),
            P(),
            P(),
            P(),
            P(),
            P(),
            P(),
            P(),
            P(),
            P("expert", None, None),
            P("expert", None, None),
        ),
        out_specs=(
            P(("dp", "expert"), None),
            P(("dp", "expert"), None),
            P(("dp", "expert")),
            P(("dp", "expert"), None),
            P(("dp", "expert"), None),
            P(("dp", "expert"), None),
            P(("dp", "expert"), None),
            P(("dp", "expert"), None),
            P(("dp", "expert"), None),
            P(("dp", "expert"), None),
            P("expert", "dp", None),
            P("expert", "dp", None),
        ),
        check_vma=False,
    )
```

```python
import functools
import math

import jax
import jax.numpy as jnp
from jax import lax
from jax.experimental import pallas as pl
from jax.experimental.pallas import tpu as pltpu
from jax.sharding import PartitionSpec as P

D = 1024
H = 4
DH = 128
EA = 5
TOPK = 16


norm_eps = 1e-05
rope_base = 10000.0
masked_score = -1e30


def sequence_layout(lengths, count):
    bounds = jnp.cumsum(lengths)
    starts = bounds - lengths
    places = jnp.arange(count, dtype=jnp.int32)
    seq_ids = jnp.sum((places[:, None] >= bounds[None, :]).astype(jnp.int32), axis=1)
    live = places < bounds[-1]
    slot_ids = jnp.arange(lengths.shape[0], dtype=jnp.int32)
    first = jnp.sum(jnp.where(seq_ids[:, None] == slot_ids[None, :], starts[None, :], 0), axis=1)
    positions = jnp.where(live, places - first, 0)
    return (seq_ids, live, positions)


def rope_tables(positions, width):
    half = width // 2
    freq = rope_base ** (-(jnp.arange(half, dtype=jnp.float32) * 2.0 / width))
    angles = positions.astype(jnp.float32)[:, None] * freq[None, :]
    return (jnp.cos(angles), jnp.sin(angles))


def rotate(field, cosine, sine):
    half = field.shape[-1] // 2
    first, second = (field[..., :half], field[..., half:])
    cos_h, sin_h = (cosine[:, None, :], sine[:, None, :])
    return jnp.concatenate(
        [first * cos_h - second * sin_h, second * cos_h + first * sin_h], axis=-1
    )


def rotate_back(field, cosine, sine):
    half = field.shape[-1] // 2
    first, second = (field[..., :half], field[..., half:])
    cos_h, sin_h = (cosine[:, None, :], sine[:, None, :])
    return jnp.concatenate(
        [first * cos_h + second * sin_h, second * cos_h - first * sin_h], axis=-1
    )


def slot_tables(routes, experts, most):
    count = routes.shape[0] * routes.shape[1]
    flat = routes.reshape(count)
    order = jnp.argsort(flat, stable=True)
    ordered = flat[order]
    firsts = jnp.searchsorted(ordered, jnp.arange(experts, dtype=jnp.int32))
    ranks = jnp.arange(count, dtype=jnp.int32) - firsts[ordered]
    sorted_slots = ordered * most + ranks
    slot_of_row = jnp.zeros((count,), jnp.int32).at[order].set(sorted_slots)
    row_of_slot = jnp.full((experts * most,), count, jnp.int32).at[sorted_slots].set(order)
    return (slot_of_row, row_of_slot)


def routed_layer(
    tokens,
    cotangent,
    seq_lengths,
    routes,
    head_experts,
    norm_gain,
    w_query,
    w_key,
    w_value,
    w_output,
    w_value_gate,
    w_output_gate,
    w_router,
    w_up,
    w_down,
):
    f32 = jnp.float32
    bf16 = jnp.bfloat16
    count = tokens.shape[0]
    experts = w_router.shape[1]
    local_experts = w_up.shape[0]
    owners = lax.axis_size("expert")
    most = 3 * count * TOPK // (2 * experts)
    routed = count * TOPK
    block = min(512, count)
    block_starts = jnp.arange(count // block, dtype=jnp.int32) * block
    scale = DH ** (-0.5)
    contract_last = (((1,), (1,)), ((), ()))
    contract_first = (((0,), (0,)), ((), ()))
    seq_ids, live, positions = sequence_layout(seq_lengths[0], count)
    cosine, sine = rope_tables(positions, DH)
    inputs = tokens.astype(f32)
    centred = inputs - jnp.mean(inputs, axis=-1, keepdims=True)
    inverse = lax.rsqrt(jnp.mean(centred * centred, axis=-1, keepdims=True) + norm_eps)
    standard = centred * inverse
    normed = (standard * norm_gain).astype(bf16)
    query_proj = jnp.dot(normed, w_query, preferred_element_type=f32).reshape(count, H, DH)
    key_proj = jnp.dot(normed, w_key, preferred_element_type=f32).reshape(count, H, DH)
    query_rot = (rotate(query_proj, cosine, sine) * scale).astype(bf16)
    key_rot = rotate(key_proj, cosine, sine).astype(bf16)
    chosen = jnp.any(
        head_experts[:, None, :, :] == jnp.arange(EA, dtype=jnp.int32)[None, :, None, None], axis=-1
    )
    value_gates = jnp.where(
        chosen,
        jax.nn.sigmoid(
            jnp.dot(tokens, w_value_gate, preferred_element_type=f32).reshape(count, EA, H)
        ),
        0.0,
    )
    output_gates = jnp.where(
        chosen,
        jax.nn.sigmoid(
            jnp.dot(tokens, w_output_gate, preferred_element_type=f32).reshape(count, EA, H)
        ),
        0.0,
    )
    value_all = jnp.dot(tokens, w_value, preferred_element_type=f32).reshape(count, EA, H, DH)
    values = jnp.sum(value_gates[..., None] * value_all, axis=1).astype(bf16)

    def allowed_at(start):
        queries = start + jnp.arange(block, dtype=jnp.int32)
        keys = jnp.arange(count, dtype=jnp.int32)
        same = (
            (seq_ids[:, None] == seq_ids[None, :])
            & (keys[None, :] <= queries[:, None])
            & live[None, :]
        )
        return same | (keys[None, :] == queries[:, None])

    def scores_at(start):
        scores = jnp.einsum("qhd,khd->hqk", query_rot, key_rot, preferred_element_type=f32)
        return (query_rot, jnp.where(allowed_at(start)[None], scores, masked_score))

    def attend(start):
        query_block, scores = scores_at(start)
        highest = jnp.max(scores, axis=-1, keepdims=True)
        shifted = jnp.exp(scores - highest)
        totals = jnp.sum(shifted, axis=-1, keepdims=True)
        shares = (shifted / totals).astype(bf16)
        result = jnp.einsum("hqk,khd->qhd", shares, values, preferred_element_type=f32)
        return (result, (highest + jnp.log(totals))[..., 0])

    attended, log_totals = lax.map(attend, block_starts)
    attended = attended.reshape(count, H, DH)
    log_totals = jnp.transpose(log_totals, (1, 0, 2)).reshape(H, count)
    heads_mixed = (
        (output_gates[..., None] * attended[:, None]).astype(bf16).reshape(count, EA * H * DH)
    )
    hidden = inputs + lax.dot_general(
        heads_mixed, w_output, contract_last, preferred_element_type=f32
    )
    hidden_low = hidden.astype(bf16)
    logits = jnp.dot(hidden_low, w_router, preferred_element_type=f32)
    gates = jax.nn.sigmoid(jnp.take_along_axis(logits, routes, axis=1))
    slot_of_row, row_of_slot = slot_tables(routes, experts, most)
    valid = row_of_slot < routed
    safe_row = jnp.minimum(row_of_slot, routed - 1)
    source = safe_row // TOPK
    outgoing = jnp.where(valid[:, None], hidden_low[source], jnp.zeros((), bf16)).reshape(
        owners, local_experts, most, D
    )

    def expert_apply(items):
        raised = jnp.einsum("nemd,edf->nemf", items, w_up, preferred_element_type=f32)
        active = jax.nn.silu(raised).astype(bf16)
        lowered = jnp.einsum("nemf,edf->nemd", active, w_down, preferred_element_type=f32).astype(
            bf16
        )
        return (lowered, raised)

    lowered, raised = expert_apply(
        lax.all_to_all(outgoing, "expert", split_axis=0, concat_axis=0, tiled=True)
    )
    returned = lax.all_to_all(lowered, "expert", split_axis=0, concat_axis=0, tiled=True).reshape(
        experts * most, D
    )
    expert_rows = returned[slot_of_row].reshape(count, TOPK, D)
    output = hidden + jnp.sum(gates[..., None] * expert_rows, axis=1)
    mixed = output.astype(bf16)
    grad_out = cotangent.astype(f32) * live[:, None].astype(f32)
    grad_gates = jnp.sum(grad_out[:, None, :] * expert_rows, axis=2)
    gate_flat = gates.reshape(routed)
    grad_outgoing = (
        jnp.where(valid[:, None], gate_flat[safe_row][:, None] * grad_out[source], 0.0)
        .astype(bf16)
        .reshape(owners, local_experts, most, D)
    )
    grad_lowered = lax.all_to_all(grad_outgoing, "expert", split_axis=0, concat_axis=0, tiled=True)
    items = lax.all_to_all(outgoing, "expert", split_axis=0, concat_axis=0, tiled=True)
    raised = expert_apply(items)[1]
    grad_active = jnp.einsum("nemd,edf->nemf", grad_lowered, w_down, preferred_element_type=f32)
    sigmoid_raised = jax.nn.sigmoid(raised)
    grad_raised = (grad_active * sigmoid_raised * (1.0 + raised * (1.0 - sigmoid_raised))).astype(
        bf16
    )
    grad_items = jnp.einsum("nemf,edf->nemd", grad_raised, w_up, preferred_element_type=f32).astype(
        bf16
    )
    active = jax.nn.silu(raised).astype(bf16)
    grad_items, grad_raised, active = (grad_items, grad_raised, active)
    grad_items, grad_raised, active, grad_arrived, arrived = (
        grad_items,
        grad_raised,
        active,
        grad_lowered,
        items,
    )
    grad_up_local = jnp.einsum("nemd,nemf->edf", arrived, grad_raised, preferred_element_type=f32)
    grad_down_local = jnp.einsum("nemd,nemf->edf", grad_arrived, active, preferred_element_type=f32)
    grad_up, grad_down = (
        lax.psum_scatter(
            grad_up_local.astype(jnp.bfloat16), "dp", scatter_dimension=1, tiled=True
        ).astype(jnp.float32),
        lax.psum_scatter(
            grad_down_local.astype(jnp.bfloat16), "dp", scatter_dimension=1, tiled=True
        ).astype(jnp.float32),
    )
    grad_back = lax.all_to_all(
        grad_items, "expert", split_axis=0, concat_axis=0, tiled=True
    ).reshape(experts * most, D)
    grad_hidden = grad_out + jnp.sum(
        grad_back[slot_of_row].reshape(count, TOPK, D), axis=1, dtype=f32
    )
    grad_picked = grad_gates * gates * (1.0 - gates)
    expert_ids = jnp.arange(experts, dtype=jnp.int32)
    grad_logits = jnp.sum(
        jnp.where(routes[:, :, None] == expert_ids[None, None, :], grad_picked[..., None], 0.0),
        axis=1,
    ).astype(bf16)
    grad_router = lax.dot_general(
        hidden_low, grad_logits, contract_first, preferred_element_type=f32
    )
    grad_hidden = grad_hidden + lax.dot_general(
        grad_logits, w_router, contract_last, preferred_element_type=f32
    )
    grad_hidden_low = grad_hidden.astype(bf16)
    grad_output = lax.dot_general(
        grad_hidden_low, heads_mixed, contract_first, preferred_element_type=f32
    )
    grad_mixed = jnp.dot(grad_hidden_low, w_output, preferred_element_type=f32).reshape(
        count, EA, H, DH
    )
    grad_attended = jnp.sum(output_gates[..., None] * grad_mixed, axis=1).astype(bf16)
    grad_out_gates = jnp.sum(grad_mixed * attended[:, None], axis=-1)
    grad_out_logits = (
        jnp.where(chosen, grad_out_gates * output_gates * (1.0 - output_gates), 0.0)
        .astype(bf16)
        .reshape(count, EA * H)
    )

    def attend_back(carry, start):
        grad_keys, grad_vals = carry
        query_block, scores = scores_at(start)
        shares = jnp.exp(scores - log_totals[..., None])
        grad_shares = jnp.einsum("qhd,khd->hqk", grad_attended, values, preferred_element_type=f32)
        centre = jnp.sum(shares * grad_shares, axis=-1, keepdims=True)
        grad_scores = (shares * (grad_shares - centre)).astype(bf16)
        grad_query_block = jnp.einsum(
            "hqk,khd->qhd", grad_scores, key_rot, preferred_element_type=f32
        )
        grad_keys = grad_keys + jnp.einsum(
            "hqk,qhd->khd", grad_scores, query_block, preferred_element_type=f32
        )
        grad_vals = grad_vals + jnp.einsum(
            "hqk,qhd->khd", shares.astype(bf16), grad_attended, preferred_element_type=f32
        )
        return ((grad_keys, grad_vals), grad_query_block)

    zero_heads = jnp.zeros((count, H, DH), f32)
    (grad_keys, grad_vals), grad_queries = lax.scan(
        attend_back, (zero_heads, zero_heads), block_starts
    )
    grad_queries = grad_queries.reshape(count, H, DH)
    grad_query_proj = (
        rotate_back(grad_queries * scale, cosine, sine).astype(bf16).reshape(count, H * DH)
    )
    grad_key_proj = rotate_back(grad_keys, cosine, sine).astype(bf16).reshape(count, H * DH)
    grad_value_all = (
        (value_gates[..., None] * grad_vals[:, None]).astype(bf16).reshape(count, EA * H * DH)
    )
    grad_value_gates = jnp.sum(grad_vals[:, None] * value_all, axis=-1)
    grad_value_logits = (
        jnp.where(chosen, grad_value_gates * value_gates * (1.0 - value_gates), 0.0)
        .astype(bf16)
        .reshape(count, EA * H)
    )
    grad_query = lax.dot_general(
        normed, grad_query_proj, contract_first, preferred_element_type=f32
    )
    grad_key = lax.dot_general(normed, grad_key_proj, contract_first, preferred_element_type=f32)
    grad_value = lax.dot_general(tokens, grad_value_all, contract_first, preferred_element_type=f32)
    grad_value_gate = lax.dot_general(
        tokens, grad_value_logits, contract_first, preferred_element_type=f32
    )
    grad_output_gate = lax.dot_general(
        tokens, grad_out_logits, contract_first, preferred_element_type=f32
    )
    grad_normed = lax.dot_general(
        grad_query_proj, w_query, contract_last, preferred_element_type=f32
    ) + lax.dot_general(grad_key_proj, w_key, contract_last, preferred_element_type=f32)
    grad_gain = jnp.sum(grad_normed * standard, axis=0)
    grad_standard = grad_normed * norm_gain
    grad_tokens = grad_hidden + inverse * (
        grad_standard
        - jnp.mean(grad_standard, axis=-1, keepdims=True)
        - standard * jnp.mean(grad_standard * standard, axis=-1, keepdims=True)
    )
    grad_tokens = (
        grad_tokens
        + lax.dot_general(grad_value_all, w_value, contract_last, preferred_element_type=f32)
        + lax.dot_general(
            grad_value_logits, w_value_gate, contract_last, preferred_element_type=f32
        )
        + lax.dot_general(grad_out_logits, w_output_gate, contract_last, preferred_element_type=f32)
    )
    summed = (
        lax.psum_scatter(grad_gain, ("dp", "expert"), scatter_dimension=0, tiled=True),
        lax.psum_scatter(grad_query, ("dp", "expert"), scatter_dimension=0, tiled=True),
        lax.psum_scatter(grad_key, ("dp", "expert"), scatter_dimension=0, tiled=True),
        lax.psum_scatter(grad_value, ("dp", "expert"), scatter_dimension=0, tiled=True),
        lax.psum_scatter(grad_output, ("dp", "expert"), scatter_dimension=0, tiled=True),
        lax.psum_scatter(grad_value_gate, ("dp", "expert"), scatter_dimension=0, tiled=True),
        lax.psum_scatter(grad_output_gate, ("dp", "expert"), scatter_dimension=0, tiled=True),
        lax.psum_scatter(grad_router, ("dp", "expert"), scatter_dimension=0, tiled=True),
    )
    return (
        mixed,
        grad_tokens,
        summed[0],
        summed[1],
        summed[2],
        summed[3],
        summed[4],
        summed[5],
        summed[6],
        summed[7],
        grad_up,
        grad_down,
    )


F32 = jnp.float32
BF16 = jnp.bfloat16
MESH = pl.DeviceIdType.MESH
LANES = 128


def mm(a, b):
    return lax.dot_general(a, b, (((1,), (0,)), ((), ())), preferred_element_type=F32)


def mm_t(a, b):
    return lax.dot_general(a, b, (((1,), (1,)), ((), ())), preferred_element_type=F32)


def tmm(a, b):
    return lax.dot_general(a, b, (((0,), (0,)), ((), ())), preferred_element_type=F32)


def iota(shape, axis):
    return lax.broadcasted_iota(jnp.int32, shape, axis)


def column(x, j, width=LANES):
    return jnp.broadcast_to(x[:, j : j + 1], (x.shape[0], width))


def sigmoid(x):
    return 1.0 / (1.0 + jnp.exp(-x))


class Scratch:
    def __init__(self):
        self.names, self.shapes = [], []

    def add(self, name, shape):
        self.names.append(name)
        self.shapes.append(shape)

    def vmem(self, name, shape, dtype):
        self.add(name, pltpu.VMEM(shape, dtype))

    def sems(self, name, *shape):
        self.add(name, pltpu.SemaphoreType.DMA(shape))


SMALL = ("tokens", "cot", "lens", "rt", "het", "gain", "wvg", "wog", "wr")
WEIGHTS = ("wq", "wk", "wv", "wo", "wu", "wd")
OUTPUTS = ("mixed", "gtok", "ggain", "gq", "gk", "gv", "go", "gvg", "gog", "gr", "gup", "gdn")


def in_hbm(names):
    return tuple(name + "_h" for name in names)


def layer_kernel(names, nd, nz, local, *refs):
    r = dict(zip(names, refs))
    R = type("R", (), r)
    C = R.tokens.shape[0]
    own_e = 2 * local
    pad_e = R.maskb.shape[1]
    EF = own_e * DH
    HF = local * DH
    HD = H * DH
    EV = EA * HD
    S = D // (nd * nz * 2)
    SL = S * nz
    GATE = EA * H
    p = lax.axis_index("dp")
    e = lax.axis_index("expert")
    z = e // 2
    c = e % 2
    sib = 1 - c

    def dev(p_, z_, c_):
        return (p_, z_ * 2 + c_)

    def times(i, n):
        return pl.multiple_of(i * n, n)

    def remote(src, dst, ss, rs, to):
        return pltpu.make_async_remote_copy(
            src_ref=src, dst_ref=dst, send_sem=ss, recv_sem=rs, device_id=to, device_id_type=MESH
        )

    def arrived(dst, rs):
        remote(dst, dst, rs, rs, dev(p, z, sib)).wait_recv()

    def sent(src, ss):
        remote(src, src, ss, ss, dev(p, z, sib)).wait_send()

    beside = p + 1 - 2 * lax.rem(p, 2)
    across = lax.rem(p + 2, nd)
    diagonal = lax.rem(beside + 2, nd)

    def core_cols(cc):
        return pl.ds(times(cc, HF), HF)

    def plane(k):
        return (p, beside, across, diagonal)[k]

    def line(k):
        return lax.rem(z + k, nz)

    barrier = pltpu.get_barrier_semaphore()
    partners = [dev(p, z, sib)]
    partners += [dev(p, line(k), c) for k in range(1, nz)]
    for k in range(1, nd):
        partners += [dev(plane(k), z, c), dev(plane(k), z, sib)]
    for to in partners:
        pl.semaphore_signal(barrier, inc=1, device_id=to, device_id_type=MESH)

    loads = {}

    def load(name, src, dst, sem):
        cp = pltpu.make_async_copy(src, dst, sem)
        cp.start()
        loads[name] = cp

    def loaded(*names):
        for name in names:
            loads.pop(name).wait()

    def landed(dst, sem):
        pltpu.make_async_copy(dst, dst, sem).wait()

    for i, name in enumerate(("cot", "lens", "rt", "tokens", "gain", "het", "wvg", "wog", "wr")):
        load(name, r[name + "_h"], r[name], R.ld_in.at[i])
    loaded("lens")
    l0 = R.lens[0, 0]
    b1 = l0 + R.lens[0, 1]
    row = iota((C, LANES), 0)
    lane = iota((C, LANES), 1)
    seq_r = (row >= l0).astype(jnp.int32) + (row >= b1).astype(jnp.int32)
    seq_c = (lane >= l0).astype(jnp.int32) + (lane >= b1).astype(jnp.int32)
    live = row < b1
    allowed = ((seq_r == seq_c) & (lane <= row) & (lane < b1)) | (row == lane)
    live_f = jnp.where(live, 1.0, 0.0).astype(F32)
    start = jnp.where(seq_r == 0, 0, l0)
    position = jnp.where(live, row - start, 0).astype(F32)

    loaded("cot")
    for b in range(D // LANES):
        cols = slice(b * LANES, (b + 1) * LANES)
        R.cotb[pl.ds(times(z, C), C), cols] = (R.cot[:, cols].astype(F32) * live_f).astype(BF16)
    load("qk", R.wq, R.wqk_b.at[:, 0:HD], R.ld.at[0])
    load("qk", R.wk, R.wqk_b.at[:, HD : 2 * HD], R.ld.at[0])
    load("v", R.wv, R.wv_b, R.ld.at[1])
    for i in range(local):
        col = times(c * local + i, DH)
        load("up", R.wu.at[i], R.wup_b.at[:, pl.ds(col, DH)], R.ld.at[2])
        load("dn", R.wd.at[i], R.wdn_b.at[:, pl.ds(col, DH)], R.ld.at[3])
    load("o", R.wo, R.wo_b, R.ld.at[4])
    loaded("rt")
    ids = iota((pad_e, C), 0)
    for zz in range(nz):
        named = jnp.zeros((pad_e, C), F32)
        for k in range(TOPK):
            hit = jnp.broadcast_to(R.rt[k : k + 1, :], (pad_e, C)) == ids + zz * own_e
            named = jnp.where(hit & (ids < own_e), 1.0, named)
        R.mask_s[zz] = named.astype(BF16)
    R.maskb[z] = R.mask_s[z]

    pl.semaphore_wait(barrier, len(partners))

    def block(buf, o):
        return buf.at[pl.ds(times(o, C), C), :]

    def pass_on(buf, ss, rs, o, right, left):
        @pl.when(right)
        def _():
            remote(block(buf, o), block(buf, o), ss.at[o], rs.at[o], dev(p, z + 1, c)).start()

        @pl.when(left)
        def _():
            way = jnp.where(o == z, nz, o)
            remote(block(buf, o), block(buf, o), ss.at[way], rs.at[o], dev(p, z - 1, c)).start()

    def passed(buf, ss, o, right, left):
        @pl.when(right)
        def _():
            sent(block(buf, o), ss.at[o])

        @pl.when(left)
        def _():
            sent(block(buf, o), ss.at[jnp.where(o == z, nz, o)])

    def gather_own(buf, ss, rs):
        pass_on(buf, ss, rs, z, z < nz - 1, z > 0)

    def gather_on(buf, ss, rs, o):
        arrived(block(buf, o), rs.at[o])
        pass_on(buf, ss, rs, o, (o < z) & (z < nz - 1), (o > z) & (z > 0))

    def gather_step(buf, ss, rs, k):
        @pl.when(z >= k)
        def _():
            gather_on(buf, ss, rs, z - k)

        @pl.when(z + k < nz)
        def _():
            gather_on(buf, ss, rs, z + k)

    def gather_end(buf, ss):
        passed(buf, ss, z, z < nz - 1, z > 0)
        for k in range(1, nz):

            @pl.when(z >= k)
            def _():
                passed(buf, ss, z - k, z < nz - 1, False)

            @pl.when(z + k < nz)
            def _():
                passed(buf, ss, z + k, False, z > 0)

    gather_own(R.cotb, R.cot_ss, R.cot_rs)
    for k in range(1, nz):
        o = line(k)
        remote(R.mask_s.at[o], R.maskb.at[z], R.tiny_s.at[0], R.tiny_r.at[0], dev(p, o, c)).start()

    loaded("tokens", "gain", "het", "wvg", "wog", "wr")

    s_row, s_col = iota((GATE, LANES), 0), iota((GATE, LANES), 1)
    to_v = jnp.where(s_row == s_col, 1.0, 0.0).astype(BF16)
    to_o = jnp.where(s_row + GATE == s_col, 1.0, 0.0).astype(BF16)
    R.wg_b[...] = (tmm(R.wvg[...], to_v) + tmm(R.wog[...], to_o)).astype(BF16)
    experts = R.wr.shape[0]
    r_row, r_col = iota((experts, LANES), 0), iota((experts, LANES), 1)
    to_r = jnp.where((r_row == r_col + z * own_e) & (r_col < own_e), 1.0, 0.0).astype(BF16)
    R.wrl_b[...] = tmm(R.wr[...], to_r).astype(BF16)

    half = lax.rem(lane, DH // 2).astype(F32)
    angle = position * jnp.exp(half * (-2.0 / DH * math.log(rope_base)))
    cosine = jnp.cos(angle)
    sine = jnp.where(lane < DH // 2, -jnp.sin(angle), jnp.sin(angle))

    def rot(v):
        return v * cosine + pltpu.roll(v, DH // 2, 1) * sine

    def rot_back(v):
        return v * cosine - pltpu.roll(v, DH // 2, 1) * sine

    inputs = R.tokens[...].astype(F32)
    centred = inputs - jnp.mean(inputs, axis=-1, keepdims=True)
    inverse = lax.rsqrt(jnp.mean(centred * centred, axis=-1, keepdims=True) + norm_eps)
    standard = centred * inverse
    R.std_b[...] = standard
    R.normed_b[...] = (standard * R.gain[...]).astype(BF16)

    landed(R.wqk_b, R.ld.at[0])
    scale = DH ** (-0.5)
    qk = mm(R.normed_b[...], R.wqk_b[:, 0:HD])
    for h in range(H):
        hs = slice(h * DH, (h + 1) * DH)
        R.q_b[:, hs] = (rot(qk[:, hs]) * scale).astype(BF16)
    qk = mm(R.normed_b[...], R.wqk_b[:, HD : 2 * HD])
    for h in range(H):
        hs = slice(h * DH, (h + 1) * DH)
        R.k_b[:, hs] = rot(qk[:, hs]).astype(BF16)

    hit = []
    for j in range(GATE):
        x, h = divmod(j, H)
        one = (R.het[2 * h : 2 * h + 1, :] == x) | (R.het[2 * h + 1 : 2 * h + 2, :] == x)
        hit.append(jnp.where(one, 1.0, 0.0).astype(F32))
    hit = jnp.concatenate(hit + hit + [jnp.zeros((LANES - 2 * GATE, C), F32)], axis=0)
    R.gate_b[...] = sigmoid(mm(R.tokens[...], R.wg_b[...])) * hit.T

    landed(R.wup_b.at[:, core_cols(c)], R.ld.at[2])
    landed(R.wdn_b.at[:, core_cols(c)], R.ld.at[3])
    for i, buf in enumerate((R.wup_b, R.wdn_b)):
        part = buf.at[:, pl.ds(times(c, HF), HF)]
        cp = remote(part, part, R.w_s.at[0], R.w_s.at[1], dev(p, z, sib))
        cp.start()

    landed(R.wv_b, R.ld.at[1])
    gates = R.gate_b[...]
    total = [None] * H
    for x in range(EA):
        R.val_b[:, x * HD : (x + 1) * HD] = mm(R.tokens[...], R.wv_b[:, x * HD : (x + 1) * HD])
        for h in range(H):
            lo = x * HD + h * DH
            term = column(gates, x * H + h) * R.val_b[:, lo : lo + DH]
            total[h] = term if x == 0 else total[h] + term
    for h in range(H):
        R.v_b[:, h * DH : (h + 1) * DH] = total[h].astype(BF16)

    for h in range(H):
        hs = slice(h * DH, (h + 1) * DH)
        scores = jnp.where(allowed, mm_t(R.q_b[:, hs], R.k_b[:, hs]), masked_score)
        shifted = jnp.exp(scores - jnp.max(scores, axis=-1, keepdims=True))
        shares = shifted / jnp.sum(shifted, axis=-1, keepdims=True)
        R.prob_b[h] = shares
        R.att_b[:, hs] = mm(shares.astype(BF16), R.v_b[:, hs])

    for x in range(EA):
        for h in range(H):
            lo = x * HD + h * DH
            R.mix_b[:, lo : lo + DH] = (
                column(gates, GATE + x * H + h) * R.att_b[:, h * DH : (h + 1) * DH]
            ).astype(BF16)
    landed(R.wo_b, R.ld.at[4])
    half_d = D // 2
    for b in range(2):
        cols = slice(b * half_d, (b + 1) * half_d)
        hidden = R.tokens[:, cols].astype(F32) + mm_t(R.mix_b[...], R.wo_b[cols, :])
        R.hid_f[:, cols] = hidden
        R.hidb[pl.ds(times(z, C), C), cols] = hidden.astype(BF16)
    gather_own(R.hidb, R.hid_ss, R.hid_rs)
    gather_step(R.cotb, R.cot_ss, R.cot_rs, 1)

    def put_turned(x, w):
        for b in range(D // LANES):
            t = x[:, b * LANES : (b + 1) * LANES].astype(F32).T.astype(BF16)
            for q in range(LANES // S):
                i = (b * LANES) // S + q
                pp, zz, cc = i // (2 * nz), (i % (2 * nz)) // 2, i % 2
                at = (pp * 2 + cc) * SL + zz * S
                R.lt[at : at + S, w * LANES : (w + 1) * LANES] = t[q * S : (q + 1) * S, :]

    plane_all = [(k, dc) for k in range(nd) for dc in range(2) if k or dc]

    def side(dc):
        return sib if dc else c

    def send_turned(w0, w1, ss, rs):
        lanes = slice(w0 * LANES, w1 * LANES)
        for k, dc in plane_all:
            to = plane(k)
            slot = 2 * k + dc
            at = times(to * 2 + side(dc), SL)
            cp = remote(
                R.lt.at[pl.ds(at, SL), lanes],
                R.ltr.at[slot, :, lanes],
                ss,
                rs,
                dev(to, z, side(dc)),
            )
            cp.start()
        R.ltr[0, :, lanes] = R.lt[pl.ds(times(p * 2 + c, SL), SL), lanes]

    def turned_here(w0, w1, ss, rs):
        there = R.ltr.at[1 : 2 * nd, :, w0 * LANES : w1 * LANES]
        sent(there, ss)
        arrived(there, rs)

    def rows_at(buf, lanes, slot):
        return buf.at[slot * C : (slot + 1) * C, lanes]

    def send_rows(buf, lanes, sem, ways=(1, 2)):
        for k in ways:
            remote(
                rows_at(buf, lanes, 0),
                rows_at(buf, lanes, 2 * k),
                sem.at[0],
                sem.at[k],
                dev(plane(k), z, c),
            ).start()
        hand_over(buf, lanes, sem, 0)

    def hand_over(buf, lanes, sem, k):
        remote(
            rows_at(buf, lanes, 2 * k),
            rows_at(buf, lanes, 2 * k + 1),
            sem.at[0],
            sem.at[5 if k == 3 else 4],
            dev(p, z, sib),
        ).start()

    def hand_near(buf, lanes, sem, via):
        for k in (via, 3 - via) if via else (1, 2):
            arrived(rows_at(buf, lanes, 2 * k), sem.at[k])
            if k == via:
                remote(
                    rows_at(buf, lanes, 2 * k),
                    rows_at(buf, lanes, 6),
                    sem.at[0],
                    sem.at[3],
                    dev(plane(3 - via), z, c),
                ).start()
            hand_over(buf, lanes, sem, k)

    def hand_far(buf, lanes, sem):
        arrived(rows_at(buf, lanes, 6), sem.at[3])
        hand_over(buf, lanes, sem, 3)

    def near_here(buf, lanes, sem):
        arrived(buf.at[0 : 3 * C, lanes], sem.at[4])

    def far_here(buf, lanes, sem):
        arrived(rows_at(buf, lanes, 7), sem.at[5])

    def rows_sent(buf, lanes, sem):
        sent(buf.at[0 : 7 * C, lanes], sem.at[0])

    put_turned(R.tokens[...], 0)
    put_turned(R.normed_b[...], 1)
    put_turned(R.hid_f[...], 2)
    send_turned(0, 3, R.lt_s.at[0], R.lt_s.at[1])
    R.ra[0:C, 0:HD] = R.att_b[...].astype(BF16)
    R.ra[0:C, HD : HD + LANES] = gates.astype(BF16)
    RA = slice(0, HD + LANES)
    send_rows(R.ra, RA, R.ra_s)

    sent(R.wup_b, R.w_s.at[0])
    arrived(R.wup_b, R.w_s.at[1])

    least = jnp.minimum(z, nz - 1 - z)
    inner = least > 0
    left_half = z < nz // 2
    near = jnp.where(inner, jnp.where(left_half, 0, nz - 1), jnp.where(left_half, 1, nz - 2))
    fellow = jnp.where(left_half, nz // 2, nz // 2 - 1)
    far = jnp.where(left_half, nz - 1, 0)

    def origin(k):
        paired = k <= 2 * least
        dist = jnp.where(paired, (k + 1) // 2, k - least)
        left = jnp.where(paired, lax.rem(k, 2) == 1, z > nz - 1 - z)
        return jnp.where(k == 0, z, jnp.where(left, z - dist, z + dist))

    def expert_block(k, carry):
        o = origin(k)
        rows = pl.ds(times(o, C), C)

        @pl.when((k == 1) & inner)
        def _():
            gather_on(R.hidb, R.hid_ss, R.hid_rs, origin(1))

        @pl.when((k > 0) & (k + inner.astype(jnp.int32) < nz))
        def _():
            gather_on(R.hidb, R.hid_ss, R.hid_rs, origin(k + inner.astype(jnp.int32)))

        @pl.when(k == jnp.where(inner, 1, 2))
        def _():
            for far_step in range(2, nz - 1):
                gather_step(R.cotb, R.cot_ss, R.cot_rs, far_step)

        @pl.when(k > 0)
        def _():
            @pl.when((o == z - nz + 1) | (o == z + nz - 1))
            def _():
                arrived(block(R.cotb, o), R.cot_rs.at[o])

        @pl.when(k == 1)
        def _():
            arrived(R.maskb.at[0 : nz - 1], R.tiny_r.at[0])

        hb = R.hidb[rows, :]
        cb = R.cotb[rows, :]
        named = R.maskb[o].astype(F32)
        named = jnp.concatenate([named, jnp.zeros((LANES - pad_e, C), F32)], axis=0).T
        g = sigmoid(mm(hb, R.wrl_b[...])) * named
        glog = jnp.zeros((C, LANES), F32)
        for q in range(2):
            cols = slice(q * HF, (q + 1) * HF)
            raised = mm(hb, R.wup_b[:, cols])
            back = mm(cb, R.wdn_b[:, cols])
            for i in range(local):
                j = q * local + i
                u = raised[:, i * DH : (i + 1) * DH]
                a = back[:, i * DH : (i + 1) * DH]
                gj = column(g, j)
                s = sigmoid(u)
                act = u * s
                lo = j * DH
                R.gact[rows, lo : lo + DH] = (gj * act).astype(BF16)
                R.gra[rows, lo : lo + DH] = (gj * a * (s * (1.0 + u * (1.0 - s)))).astype(BF16)
                gg = jnp.sum(a * act, axis=1, keepdims=True)
                glog = jnp.where(lane == j, jnp.broadcast_to(gg, (C, LANES)), glog)
        glog = glog * g * (1.0 - g)
        low = glog.astype(BF16)
        R.glog_s[o] = glog.T[0:pad_e, :].astype(BF16)
        for b in range(2):
            cols = slice(b * half_d, (b + 1) * half_d)
            gh = mm_t(R.gra[rows, :], R.wup_b[cols, :]) + mm_t(low, R.wrl_b[cols, :])
            R.gh_s[o, :, cols] = gh.astype(BF16)

        @pl.when(k > 0)
        def _():
            remote(
                R.glog_s.at[o], R.glog_r.at[z], R.tiny_s.at[1], R.tiny_r.at[1], dev(p, o, c)
            ).start()

        @pl.when((k > 0) & (least == 0) & (o != fellow))
        def _():
            send_back(o)

        @pl.when((k > 0) & (least == 0) & (o == fellow))
        def _():
            send_by(o, near, 0)

        @pl.when((k > 0) & inner & (o == far))
        def _():
            send_by(o, fellow, 1)

        @pl.when(k == 2)
        def _():
            hand_near(R.ra, RA, R.ra_s, 2)

        @pl.when((k == 2) & (least == 0))
        def _():
            there = pl.ds(times(near, C), C)
            for b in range(2):
                cols = slice(b * half_d, (b + 1) * half_d)
                R.out_s[near, :, cols] = mm_t(R.gact[there, :], R.wdn_b[cols, :]).astype(BF16)
            slot = jnp.where(z == 0, near, nz)
            remote(
                R.out_s.at[near],
                R.out_r.at[slot],
                R.out_sem.at[nz + 1],
                R.out_sem.at[slot],
                dev(p, near, c),
            ).start()

        return carry

    def send_back(o):
        remote(R.gh_s.at[o], R.gh_r.at[z], R.gh_sem.at[0], R.gh_sem.at[1], dev(p, o, c)).start()

    def send_by(o, by, slot):
        remote(
            R.gh_s.at[o], R.gh_x.at[slot], R.gh_sem.at[0], R.gh_sem.at[2 + slot], dev(p, by, c)
        ).start()

    def relay_back(o, slot):
        arrived(R.gh_x.at[slot], R.gh_sem.at[2 + slot])
        R.gh_s[o] = (R.gh_s[o].astype(F32) + R.gh_x[slot].astype(F32)).astype(BF16)
        send_back(o)

    lax.fori_loop(0, nz, expert_block, 0)

    def rows_of(at):
        return pl.ds(times(at, rows_d), rows_d)


    rows_d = D // nd

    def grad_at(i, k, cc):
        if i == 0 and k == 3:
            return R.dg.at[:, core_cols(cc)]
        return (R.wdn_b, R.wup_b)[i].at[rows_of(plane(k)), core_cols(cc)]

    def expert_grad(i, k):
        left, right = ((R.cotb, R.gact), (R.hidb, R.gra))[i]
        for cc in (sib, c):
            grad_at(i, k, cc)[...] = tmm(left[:, rows_of(plane(k))], right[:, core_cols(cc)]).astype(BF16)
            if cc is sib:
                remote(
                    grad_at(i, k, sib),
                    R.pair_r.at[i, k],
                    R.pair_s.at[0],
                    R.pair_s.at[1 + i if k == 3 else 3],
                    dev(p, z, sib),
                ).start()

    def pair_sum(i, k):
        if k == 3:
            arrived(R.pair_r.at[i, k], R.pair_s.at[1 + i])
        own = grad_at(i, k, c)
        own[...] = (own[...].astype(F32) + R.pair_r[i, k].astype(F32)).astype(BF16)

    def part_on(i, k, to, slot):
        remote(
            grad_at(i, k, c),
            R.eg_r.at[slot, i],
            R.eg_s.at[0],
            R.eg_s.at[1 + i if slot == 1 else 3 + i],
            dev(plane(to), z, c),
        ).start()

    def first_half(i, n):
        first = 1 if i == 0 else 2
        rows = slice(n * rows_d // 2, (n + 1) * rows_d // 2)
        remote(
            grad_at(i, first, c).at[rows],
            R.eg_r.at[0, i, rows],
            R.eg_s.at[0],
            R.eg_s.at[3 + i],
            dev(plane(first), z, c),
        ).start()

    def expert_grad_relay(i):
        second = 2 if i == 0 else 1

        @pl.when(least == 0)
        def _():
            first_half(i, 1)

        arrived(R.eg_r.at[1, i], R.eg_s.at[1 + i])
        own = grad_at(i, second, c)
        own[...] = (own[...].astype(F32) + R.eg_r[1, i].astype(F32)).astype(BF16)
        part_on(i, second, second, 2)

    def to_place(own, got, ss, rs, o):
        remote(own(o), got(z), ss, rs, dev(p, o, c)).start()

    def run(own, got, ss, rs, k, n):
        def hand(d, slot, to):
            if k > 1:
                arrived(got(d), rs.at[d])
                own(d)[...] = (own(d)[...].astype(F32) + got(d)[...].astype(F32)).astype(BF16)
            remote(own(d), got(slot), ss, rs.at[slot], dev(p, to, c)).start()

        @pl.when(z == k - 1)
        def _():
            hand(nz - 1 - n, nz - 1 - n, k)

        @pl.when(z == nz - k)
        def _():
            hand(n, nz if n == nz - k - 1 else n, nz - k - 1)

    def run_end(total, got, rs):
        for there, slot in ((z > 0, z), (z < nz - 1, nz)):

            @pl.when(there)
            def _():
                arrived(got(slot), rs.at[slot])
                total[...] += got(slot)[...].astype(F32)

    out_sum = (lambda d: R.out_s.at[d], lambda d: R.out_r.at[d], R.out_sem.at[nz + 1], R.out_sem)
    out_run = functools.partial(run, *out_sum)

    def grad_sum(i, lanes):
        return (
            lambda d: R.pb.at[d * S : (d + 1) * S, lanes],
            lambda d: R.pn.at[i, d],
            R.pn_sem.at[i, nz + 1],
            R.pn_sem.at[i],
        )

    def part_sum(i, lanes):
        return (
            lambda o: R.pb.at[pl.ds(times(o, S), S), lanes],
            lambda o: R.pr.at[o, :, slice(lanes.start - 2 * EV, lanes.stop - 2 * EV)],
            R.p_sem.at[0],
            R.p_sem.at[1 + i],
        )

    expert_grad(1, 3)
    expert_grad(0, 3)
    for i, to in ((1, 2), (0, 1)):
        pair_sum(i, 3)
        part_on(i, 3, to, 1)

    def out_tile(t, carry):
        rows = pl.ds(times(t, 256), 256)
        got = mm_t(R.gact[...], R.wdn_b[rows, :]).astype(BF16)
        for o in range(nz):

            @pl.when(inner | (o != near))
            def _():
                R.out_s[o, :, rows] = got[o * C : (o + 1) * C, :]

        return carry

    lax.fori_loop(0, D // 256, out_tile, 0)
    out_run(1, 0)

    @pl.when(inner)
    def _():
        relay_back(near, 1)
        relay_back(fellow, 0)

    for k in (1, 2, 0):
        expert_grad(1, k)
        expert_grad(0, k)
    def sum_pairs():
        arrived(R.pair_r.at[:, 0:3], R.pair_s.at[3])
        for k in (1, 2, 0):
            pair_sum(1, k)
            pair_sum(0, k)

    @pl.when(inner)
    def _():
        sum_pairs()
        for i in range(2):
            for n in range(2):
                first_half(i, n)

    hand_far(R.ra, RA, R.ra_s)
    turned_here(0, 3, R.lt_s.at[0], R.lt_s.at[1])

    R.ghid_f[...] = R.cotb[pl.ds(times(z, C), C), :].astype(F32) + R.gh_s[z].astype(F32)

    arrived(R.gh_r.at[0:2], R.gh_sem.at[1])

    def add_back(o):
        R.ghid_f[...] += R.gh_r[o].astype(F32)

    add_back(near)
    add_back(jnp.where(inner, fellow, far))

    arrived(R.glog_r.at[0 : nz - 1], R.tiny_r.at[1])
    out_run(1, 1)
    R.glog_r[z] = R.glog_s[z]
    R.ghid_b[...] = R.ghid_f[...].astype(BF16)
    put_turned(R.ghid_f[...], 3)
    send_turned(3, 4, R.lt_s.at[2], R.lt_s.at[3])
    out_run(2, 0)

    gates = R.gate_b[...]
    small = jnp.zeros((C, LANES), F32)
    gatt = [None] * H
    for x in range(EA):
        gmix = mm(R.ghid_b[...], R.wo_b[:, x * HD : (x + 1) * HD])
        for h in range(H):
            hs = slice(h * DH, (h + 1) * DH)
            j = GATE + x * H + h
            term = column(gates, j) * gmix[:, hs]
            gatt[h] = term if x == 0 else gatt[h] + term
            gg = jnp.sum(gmix[:, hs] * R.att_b[:, hs], axis=1, keepdims=True)
            small = jnp.where(lane == j, jnp.broadcast_to(gg, (C, LANES)), small)
    for h in range(H):
        hs = slice(h * DH, (h + 1) * DH)
        low = gatt[h].astype(BF16)
        R.gatt_b[:, hs] = low
        gval = tmm(R.prob_b[h].astype(BF16), low)
        R.gval_f[:, hs] = gval
        R.rb[0:C, hs] = gval.astype(BF16)
        for x in range(EA):
            lo = x * HD + h * DH
            j = x * H + h
            gg = jnp.sum(gval * R.val_b[:, lo : lo + DH], axis=1, keepdims=True)
            small = jnp.where(lane == j, jnp.broadcast_to(gg, (C, LANES)), small)
    small = small * gates * (1.0 - gates)
    glog = jnp.concatenate(
        [jnp.zeros((2 * GATE, C), F32)]
        + [R.glog_r[o].astype(F32) for o in range(nz)]
        + [jnp.zeros((LANES - 2 * GATE - nz * pad_e, C), F32)],
        axis=0,
    )
    R.small_b[...] = small.astype(BF16)
    R.rb[0:C, HD : HD + LANES] = (small + glog.T).astype(BF16)
    RV = slice(0, HD + LANES)
    send_rows(R.rb, RV, R.rv_s, (1, 2, 3))

    q0 = HD + LANES
    for h in range(H):
        hs = slice(h * DH, (h + 1) * DH)
        low = R.gatt_b[:, hs]
        gsh = mm_t(low, R.v_b[:, hs])
        prob = R.prob_b[h]
        centre = jnp.sum(prob * gsh, axis=-1, keepdims=True)
        gs = (prob * (gsh - centre)).astype(BF16)
        R.rb[0:C, q0 + h * DH : q0 + (h + 1) * DH] = rot_back(
            mm(gs, R.k_b[:, hs]) * scale
        ).astype(BF16)
        R.rb[0:C, q0 + HD + h * DH : q0 + HD + (h + 1) * DH] = rot_back(
            tmm(gs, R.q_b[:, hs])
        ).astype(BF16)
    RQ, RK = slice(q0, q0 + HD), slice(q0 + HD, q0 + 2 * HD)
    send_rows(R.rb, RQ, R.rq_s)
    send_rows(R.rb, RK, R.rk_s)


    def turned_of(w):
        return jnp.concatenate(
            [R.ltr[s, :, w * LANES : (w + 1) * LANES] for s in range(2 * nd)], axis=1
        )

    def send_part(part, lanes):
        for o in (far, fellow, near):
            to_place(*part_sum(part, lanes), o)

    def gate_rows(dst, rows_of, g0, s0, s1):
        rows = slice(s0 * C, s1 * C)
        for x in range(EA):
            for h in range(H):
                lo = x * HD + h * DH
                gx = column(R.ra[rows, HD : HD + LANES], g0 + x * H + h)
                dst[rows, lo : lo + DH] = gx * rows_of[rows, h * DH : (h + 1) * DH]

    def gated_grad(w, gated, at):
        left = turned_of(w)
        for x in range(EA):
            cols = slice(x * HD, (x + 1) * HD)
            R.pb[:, at + x * HD : at + (x + 1) * HD] = mm(left, gated[:, cols]).astype(BF16)

    PO, PV, PQ, PS = (
        slice(0, EV),
        slice(EV, 2 * EV),
        slice(2 * EV, 2 * EV + 2 * HD),
        slice(2 * EV + 2 * HD, 2 * EV + 2 * HD + LANES),
    )
    near_here(R.ra, RA, R.ra_s)
    far_here(R.ra, RA, R.ra_s)
    gate_rows(R.wo_b, R.ra, GATE, 0, 2 * nd)
    turned_here(3, 4, R.lt_s.at[2], R.lt_s.at[3])
    gated_grad(3, R.wo_b, 0)
    o_run = functools.partial(run, *grad_sum(0, PO))
    v_run = functools.partial(run, *grad_sum(1, PV))
    o_run(1, 0)
    o_run(1, 1)
    out_run(2, 1)
    out_run(3, 0)
    gproj = mm_t(R.rb[0:C, q0 : q0 + 2 * HD], R.wqk_b[...])
    standard = R.std_b[...]
    column_sum = jnp.sum(gproj * standard, axis=0, keepdims=True)
    for b in range(D // LANES):
        R.gp[0, b : b + 1, :] = column_sum[:, b * LANES : (b + 1) * LANES]
    for k, dc in plane_all:
        slot = 2 * k + dc
        cp = remote(
            R.gp.at[0], R.gp.at[slot], R.tiny_s.at[2], R.tiny_r.at[2], dev(plane(k), z, side(dc))
        )
        cp.start()

    @pl.when(least == 0)
    def _():
        sum_pairs()
        first_half(0, 0)
        first_half(1, 0)

    hand_near(R.rb, RV, R.rv_s, 0)

    inputs = R.tokens[...].astype(F32)
    centred = inputs - jnp.mean(inputs, axis=-1, keepdims=True)
    inverse = lax.rsqrt(jnp.mean(centred * centred, axis=-1, keepdims=True) + norm_eps)
    gs = gproj * R.gain[...]
    gtok = R.ghid_f[...] + inverse * (
        gs
        - jnp.mean(gs, axis=-1, keepdims=True)
        - standard * jnp.mean(gs * standard, axis=-1, keepdims=True)
    )
    R.gtok[...] = gtok
    for x in range(EA):
        for h in range(H):
            lo = x * HD + h * DH
            R.mix_b[:, lo : lo + DH] = (
                column(gates, x * H + h) * R.gval_f[:, h * DH : (h + 1) * DH]
            ).astype(BF16)
    for b in range(2):
        cols = slice(b * half_d, (b + 1) * half_d)
        R.gtok[:, cols] += mm_t(R.mix_b[...], R.wv_b[cols, :]) + mm_t(
            R.small_b[...], R.wg_b[cols, :]
        )


    o_run(2, 0)
    near_here(R.rb, RV, R.rv_s)
    gate_rows(R.wv_b, R.rb, 0, 0, 6)
    o_run(2, 1)
    hand_far(R.rb, RV, R.rv_s)
    far_here(R.rb, RV, R.rv_s)
    gate_rows(R.wv_b, R.rb, 0, 6, 8)
    gated_grad(0, R.wv_b, EV)
    v_run(1, 0)
    hand_near(R.rb, RK, R.rk_s, 2)
    hand_near(R.rb, RQ, R.rq_s, 1)
    v_run(1, 1)
    expert_grad_relay(0)
    expert_grad_relay(1)
    o_run(3, 0)
    total = R.gp[0]
    sent(R.gp.at[1:], R.tiny_s.at[2])
    arrived(R.gp.at[1:], R.tiny_r.at[2])
    for k, dc in plane_all:
        total = total + R.gp[2 * k + dc]
    R.gz_s[...] = total
    for k in range(1, nz):
        o = line(k)
        remote(R.gz_s, R.gz.at[z], R.tiny_s.at[3], R.tiny_r.at[3], dev(p, o, c)).start()

    lane_s = iota((SL, LANES), 1)
    small_t = mm(turned_of(0), R.rb[:, HD : HD + LANES])
    small_h = mm(turned_of(2), R.rb[:, HD : HD + LANES])
    R.pb[:, PS] = jnp.where(lane_s < 2 * GATE, small_t, small_h).astype(BF16)
    send_part(1, PS)
    o_run(1, 2)
    v_run(2, 0)
    v_run(2, 1)
    v_run(3, 0)

    hand_far(R.rb, RQ, R.rq_s)
    hand_far(R.rb, RK, R.rk_s)
    for lanes, sem in ((RQ, R.rq_s), (RK, R.rk_s)):
        near_here(R.rb, lanes, sem)
        far_here(R.rb, lanes, sem)
    left = turned_of(1)
    for b in range(2):
        lo = q0 + b * HD
        R.pb[:, 2 * EV + b * HD : 2 * EV + (b + 1) * HD] = mm(left, R.rb[:, lo : lo + HD]).astype(
            BF16
        )
    send_part(0, PQ)
    v_run(1, 2)
    R.hid_f[...] += R.out_s[z].astype(F32)
    run_end(R.hid_f, out_sum[1], R.out_sem)
    R.mixed[...] = R.hid_f[...].astype(BF16)

    arrived(R.gz.at[0 : nz - 1], R.tiny_r.at[3])
    for k in range(1, nz):
        total = total + R.gz[line(k)]
    first = (p * 2 * nz + z * 2 + c) * S
    pick_row = iota((D // LANES, LANES), 0) == first // LANES
    line_sum = jnp.sum(jnp.where(pick_row, total, 0.0), axis=0, keepdims=True)
    shift = lax.rem(LANES - lax.rem(first, LANES), LANES)
    line_sum = pltpu.roll(jnp.broadcast_to(line_sum, (8, LANES)), shift, 1)
    R.ggain[...] = line_sum[0:1, 0:S]

    own_rows = pl.ds(times(z, S), S)

    def line_total(part, lanes):
        got = R.pb[own_rows, lanes].astype(F32)
        slots = part_sum(part, lanes)[1]
        arrived(slots(slice(0, nz - 1)), R.p_sem.at[1 + part])
        for k in range(1, nz):
            got = got + slots(line(k))[...].astype(F32)
        return got

    for i, (dst, lanes) in enumerate(((R.go, PO), (R.gv, PV))):
        dst[...] = R.pb[own_rows, lanes].astype(F32)
        run_end(dst, grad_sum(i, lanes)[1], R.pn_sem.at[i])
    got = line_total(1, PS)

    def pick(width, source):
        a, b = iota((width, LANES), 1), iota((width, LANES), 0)
        return jnp.where(a == source(b), 1.0, 0.0).astype(F32)

    def picked(left, right):
        return lax.dot_general(
            left,
            right,
            (((1,), (1,)), ((), ())),
            preferred_element_type=F32,
            precision=lax.Precision.HIGHEST,
        )

    def router_lane(b):
        at = jnp.zeros_like(b)
        for o in range(nz):
            at = jnp.where(b >= o * own_e, 2 * GATE + o * pad_e + b - o * own_e, at)
        return at

    R.gvg[...] = picked(pick(GATE, lambda b: b), got)
    R.gog[...] = picked(pick(GATE, lambda b: b + GATE), got)
    R.gr[...] = picked(got, pick(experts, router_lane))
    got = line_total(0, PQ)
    R.gq[...] = got[:, 0:HD]
    R.gk[...] = got[:, HD : 2 * HD]

    for i, (buf, dst) in enumerate(((R.wdn_b, R.gdn), (R.wup_b, R.gup))):
        arrived(R.eg_r.at[0:2, i], R.eg_s.at[3 + i])
        rows = rows_of(p)
        for x in range(local):
            got = buf[rows, pl.ds(times(c * local + x, DH), DH)].astype(F32)
            for slot in (0, 2):
                got = got + R.eg_r[slot, i, :, x * DH : (x + 1) * DH].astype(F32)
            dst[x] = got

    gather_end(R.cotb, R.cot_ss)
    gather_end(R.hidb, R.hid_ss)
    for buf, lanes, sem in (
        (R.ra, RA, R.ra_s),
        (R.rb, RV, R.rv_s),
        (R.rb, RQ, R.rq_s),
        (R.rb, RK, R.rk_s),
    ):
        rows_sent(buf, lanes, sem)
    sent(R.maskb.at[0 : nz - 1], R.tiny_s.at[0])
    sent(R.glog_r.at[0 : nz - 1], R.tiny_s.at[1])
    sent(R.gz.at[0 : nz - 1], R.tiny_s.at[3])
    sent(R.gh_r.at[0 : nz - 1], R.gh_sem.at[0])
    sent(R.out_r.at[0 : nz - 1], R.out_sem.at[nz + 1])
    sent(R.pair_r, R.pair_s.at[0])
    sent(R.eg_r, R.eg_s.at[0])
    sent(R.pr.at[0 : nz - 1], R.p_sem.at[0])
    for i in range(2):
        sent(R.pn.at[i, 0 : nz - 1], R.pn_sem.at[i, nz + 1])


def settle_kernel(*refs):
    n = len(refs) // 2
    copies = [pltpu.make_async_copy(refs[i], refs[n + i], refs[-1].at[i]) for i in range(n)]
    for cp in copies:
        cp.start()
    for cp in copies:
        cp.wait()


def fused_layer(nd, nz, *args):
    (tokens, cotangent, seq_lengths, routes, head_experts, norm_gain) = args[:6]
    (w_query, w_key, w_value, w_output, w_value_gate, w_output_gate, w_router) = args[6:13]
    w_up, w_down = args[13:]
    C = tokens.shape[0]
    local = w_up.shape[0]
    experts = w_router.shape[1]
    own_e = 2 * local
    pad_e = -(-own_e // 16) * 16
    EF, HF, HD = own_e * DH, local * DH, H * DH
    EV = EA * HD
    S = D // (nd * nz * 2)
    SL = S * nz
    PW = 2 * EV + 2 * HD + LANES
    s = Scratch()
    s.vmem("wqk_b", (D, 2 * HD), BF16)
    s.vmem("wv_b", (D, EV), BF16)
    s.vmem("wo_b", (D, EV), BF16)
    s.vmem("wup_b", (D, EF), BF16)
    s.vmem("wdn_b", (D, EF), BF16)
    s.vmem("wg_b", (D, LANES), BF16)
    s.vmem("wrl_b", (D, LANES), BF16)
    s.vmem("cotb", (nz * C, D), BF16)
    s.vmem("hidb", (nz * C, D), BF16)
    s.vmem("mask_s", (nz, pad_e, C), BF16)
    s.vmem("maskb", (nz, pad_e, C), BF16)
    s.vmem("std_b", (C, D), F32)
    s.vmem("normed_b", (C, D), BF16)
    s.vmem("q_b", (C, HD), BF16)
    s.vmem("k_b", (C, HD), BF16)
    s.vmem("v_b", (C, HD), BF16)
    s.vmem("gate_b", (C, LANES), F32)
    s.vmem("val_b", (C, EV), F32)
    s.vmem("prob_b", (H, C, C), F32)
    s.vmem("att_b", (C, HD), F32)
    s.vmem("mix_b", (C, EV), BF16)
    s.vmem("hid_f", (C, D), F32)
    s.vmem("lt", (D, 4 * LANES), BF16)
    s.vmem("ltr", (2 * nd, SL, 4 * LANES), BF16)
    s.vmem("ra", (2 * nd * C, HD + LANES), BF16)
    s.vmem("rb", (2 * nd * C, 3 * HD + LANES), BF16)
    s.vmem("gact", (nz * C, EF), BF16)
    s.vmem("gra", (nz * C, EF), BF16)
    for name in ("gh_s", "gh_r", "out_s"):
        s.vmem(name, (nz, C, D), BF16)
    s.vmem("out_r", (nz + 1, C, D), BF16)
    s.vmem("gh_x", (2, C, D), BF16)
    for name in ("glog_s", "glog_r"):
        s.vmem(name, (nz, pad_e, C), BF16)
    s.vmem("dg", (D // nd, EF), BF16)
    s.vmem("pair_r", (2, nd, D // nd, HF), BF16)
    s.vmem("eg_r", (nd - 1, 2, D // nd, HF), BF16)
    s.vmem("ghid_f", (C, D), F32)
    s.vmem("ghid_b", (C, D), BF16)
    s.vmem("gatt_b", (C, HD), BF16)
    s.vmem("gval_f", (C, HD), F32)
    s.vmem("small_b", (C, LANES), BF16)
    s.vmem("pb", (SL, PW), BF16)
    s.vmem("pr", (nz, S, PW - 2 * EV), BF16)
    s.vmem("pn", (2, nz + 1, S, EV), BF16)
    s.vmem("gp", (2 * nd, D // LANES, LANES), F32)
    s.vmem("gz_s", (D // LANES, LANES), F32)
    s.vmem("gz", (nz, D // LANES, LANES), F32)
    s.sems("ld", 5)
    for name in ("cot_ss", "hid_ss"):
        s.sems(name, nz + 1)
    for name in ("cot_rs", "hid_rs", "tiny_s", "tiny_r", "lt_s", "gh_sem", "pair_s"):
        s.sems(name, 4)
    for name in ("ra_s", "rv_s", "rq_s", "rk_s"):
        s.sems(name, 6)
    s.sems("w_s", 2)
    s.sems("eg_s", 5)
    s.sems("p_sem", 3)
    s.sems("out_sem", nz + 2)
    s.sems("pn_sem", 2, nz + 2)

    def out(*shape, dtype=F32):
        return jax.ShapeDtypeStruct(shape, dtype)

    hbm = pl.BlockSpec(memory_space=pl.ANY)
    vmem = pl.BlockSpec(memory_space=pltpu.VMEM)
    names = in_hbm(SMALL) + WEIGHTS + OUTPUTS
    results = (
        out(C, D, dtype=BF16),
        out(C, D),
        out(1, S),
        out(S, HD),
        out(S, HD),
        out(S, EV),
        out(S, EV),
        out(EA * H, S),
        out(EA * H, S),
        out(S, experts),
        out(local, D // nd, DH),
        out(local, D // nd, DH),
    )
    s.vmem("tokens", (C, D), BF16)
    s.vmem("cot", (C, D), BF16)
    s.add("lens", pltpu.SMEM((1, 2), jnp.int32))
    s.vmem("rt", (TOPK, C), jnp.int32)
    s.vmem("het", (2 * H, C), jnp.int32)
    s.vmem("gain", (1, D), F32)
    s.vmem("wvg", (EA * H, D), BF16)
    s.vmem("wog", (EA * H, D), BF16)
    s.vmem("wr", (experts, D), BF16)
    s.sems("ld_in", len(SMALL))
    outs = pl.pallas_call(
        functools.partial(layer_kernel, names + tuple(s.names), nd, nz, local),
        out_shape=[pltpu.VMEM(x.shape, x.dtype) for x in results],
        in_specs=[hbm] * 15,
        out_specs=[vmem] * len(OUTPUTS),
        scratch_shapes=s.shapes,
        compiler_params=pltpu.CompilerParams(
            collective_id=0, has_side_effects=True, vmem_limit_bytes=VMEM_LIMIT
        ),
    )(
        tokens,
        cotangent,
        seq_lengths,
        routes.T,
        head_experts.reshape(C, 2 * H).T,
        norm_gain.reshape(1, D),
        w_value_gate.T,
        w_output_gate.T,
        w_router.T,
        w_query,
        w_key,
        w_value,
        w_output,
        w_up,
        w_down,
    )
    outs = list(
        pl.pallas_call(
            settle_kernel,
            out_shape=results,
            in_specs=[vmem] * len(outs),
            out_specs=[hbm] * len(outs),
            scratch_shapes=[pltpu.SemaphoreType.DMA((len(outs),))],
        )(*[pltpu.with_memory_space_constraint(x, pltpu.VMEM) for x in outs])
    )
    outs[2] = outs[2].reshape(S)
    for i in (7, 8):
        outs[i] = outs[i].T
    return tuple(outs)


VMEM_LIMIT = 58 * 1024 * 1024


def fits(nd, nz, count, experts):
    own_e = experts // nz
    pad_e = -(-own_e // 16) * 16
    return (
        count == LANES
        and nz == 4
        and nd == 4
        and own_e % 4 == 0
        and D % (nd * nz * 2 * 16) == 0
        and LANES % (D // (nd * nz * 2)) == 0
        and 2 * EA * H + nz * pad_e <= LANES
    )


def per_device(nd, ne, *args):
    count, experts = args[0].shape[0], args[12].shape[1]
    if ne % 2 == 0 and fits(nd, ne // 2, count, experts):
        return fused_layer(nd, ne // 2, *args)
    return routed_layer(*args)


def solution(mesh):
    return jax.shard_map(
        functools.partial(per_device, mesh.shape["dp"], mesh.shape["expert"]),
        mesh=mesh,
        in_specs=(
            P(("dp", "expert"), None),
            P(("dp", "expert"), None),
            P(("dp", "expert"), None),
            P(("dp", "expert"), None),
            P(("dp", "expert"), None, None),
            P(),
            P(),
            P(),
            P(),
            P(),
            P(),
            P(),
            P(),
            P("expert", None, None),
            P("expert", None, None),
        ),
        out_specs=(
            P(("dp", "expert"), None),
            P(("dp", "expert"), None),
            P(("dp", "expert")),
            P(("dp", "expert"), None),
            P(("dp", "expert"), None),
            P(("dp", "expert"), None),
            P(("dp", "expert"), None),
            P(("dp", "expert"), None),
            P(("dp", "expert"), None),
            P(("dp", "expert"), None),
            P("expert", "dp", None),
            P("expert", "dp", None),
        ),
        check_vma=False,
    )
```

```python
import functools
import math

import jax
import jax.numpy as jnp
from jax import lax
from jax.experimental import pallas as pl
from jax.experimental.pallas import tpu as pltpu
from jax.sharding import PartitionSpec as P

D = 1024
H = 4
DH = 128
EA = 5
TOPK = 16


norm_eps = 1e-05
rope_base = 10000.0
masked_score = -1e30


def sequence_layout(lengths, count):
    bounds = jnp.cumsum(lengths)
    starts = bounds - lengths
    places = jnp.arange(count, dtype=jnp.int32)
    seq_ids = jnp.sum((places[:, None] >= bounds[None, :]).astype(jnp.int32), axis=1)
    live = places < bounds[-1]
    slot_ids = jnp.arange(lengths.shape[0], dtype=jnp.int32)
    first = jnp.sum(jnp.where(seq_ids[:, None] == slot_ids[None, :], starts[None, :], 0), axis=1)
    positions = jnp.where(live, places - first, 0)
    return (seq_ids, live, positions)


def rope_tables(positions, width):
    half = width // 2
    freq = rope_base ** (-(jnp.arange(half, dtype=jnp.float32) * 2.0 / width))
    angles = positions.astype(jnp.float32)[:, None] * freq[None, :]
    return (jnp.cos(angles), jnp.sin(angles))


def rotate(field, cosine, sine):
    half = field.shape[-1] // 2
    first, second = (field[..., :half], field[..., half:])
    cos_h, sin_h = (cosine[:, None, :], sine[:, None, :])
    return jnp.concatenate(
        [first * cos_h - second * sin_h, second * cos_h + first * sin_h], axis=-1
    )


def rotate_back(field, cosine, sine):
    half = field.shape[-1] // 2
    first, second = (field[..., :half], field[..., half:])
    cos_h, sin_h = (cosine[:, None, :], sine[:, None, :])
    return jnp.concatenate(
        [first * cos_h + second * sin_h, second * cos_h - first * sin_h], axis=-1
    )


def slot_tables(routes, experts, most):
    count = routes.shape[0] * routes.shape[1]
    flat = routes.reshape(count)
    order = jnp.argsort(flat, stable=True)
    ordered = flat[order]
    firsts = jnp.searchsorted(ordered, jnp.arange(experts, dtype=jnp.int32))
    ranks = jnp.arange(count, dtype=jnp.int32) - firsts[ordered]
    sorted_slots = ordered * most + ranks
    slot_of_row = jnp.zeros((count,), jnp.int32).at[order].set(sorted_slots)
    row_of_slot = jnp.full((experts * most,), count, jnp.int32).at[sorted_slots].set(order)
    return (slot_of_row, row_of_slot)


def routed_layer(
    tokens,
    cotangent,
    seq_lengths,
    routes,
    head_experts,
    norm_gain,
    w_query,
    w_key,
    w_value,
    w_output,
    w_value_gate,
    w_output_gate,
    w_router,
    w_up,
    w_down,
):
    f32 = jnp.float32
    bf16 = jnp.bfloat16
    count = tokens.shape[0]
    experts = w_router.shape[1]
    local_experts = w_up.shape[0]
    owners = lax.axis_size("expert")
    most = 3 * count * TOPK // (2 * experts)
    routed = count * TOPK
    block = min(512, count)
    block_starts = jnp.arange(count // block, dtype=jnp.int32) * block
    scale = DH ** (-0.5)
    contract_last = (((1,), (1,)), ((), ()))
    contract_first = (((0,), (0,)), ((), ()))
    seq_ids, live, positions = sequence_layout(seq_lengths[0], count)
    cosine, sine = rope_tables(positions, DH)
    inputs = tokens.astype(f32)
    centred = inputs - jnp.mean(inputs, axis=-1, keepdims=True)
    inverse = lax.rsqrt(jnp.mean(centred * centred, axis=-1, keepdims=True) + norm_eps)
    standard = centred * inverse
    normed = (standard * norm_gain).astype(bf16)
    query_proj = jnp.dot(normed, w_query, preferred_element_type=f32).reshape(count, H, DH)
    key_proj = jnp.dot(normed, w_key, preferred_element_type=f32).reshape(count, H, DH)
    query_rot = (rotate(query_proj, cosine, sine) * scale).astype(bf16)
    key_rot = rotate(key_proj, cosine, sine).astype(bf16)
    chosen = jnp.any(
        head_experts[:, None, :, :] == jnp.arange(EA, dtype=jnp.int32)[None, :, None, None], axis=-1
    )
    value_gates = jnp.where(
        chosen,
        jax.nn.sigmoid(
            jnp.dot(tokens, w_value_gate, preferred_element_type=f32).reshape(count, EA, H)
        ),
        0.0,
    )
    output_gates = jnp.where(
        chosen,
        jax.nn.sigmoid(
            jnp.dot(tokens, w_output_gate, preferred_element_type=f32).reshape(count, EA, H)
        ),
        0.0,
    )
    value_all = jnp.dot(tokens, w_value, preferred_element_type=f32).reshape(count, EA, H, DH)
    values = jnp.sum(value_gates[..., None] * value_all, axis=1).astype(bf16)

    def allowed_at(start):
        queries = start + jnp.arange(block, dtype=jnp.int32)
        keys = jnp.arange(count, dtype=jnp.int32)
        same = (
            (seq_ids[:, None] == seq_ids[None, :])
            & (keys[None, :] <= queries[:, None])
            & live[None, :]
        )
        return same | (keys[None, :] == queries[:, None])

    def scores_at(start):
        scores = jnp.einsum("qhd,khd->hqk", query_rot, key_rot, preferred_element_type=f32)
        return (query_rot, jnp.where(allowed_at(start)[None], scores, masked_score))

    def attend(start):
        query_block, scores = scores_at(start)
        highest = jnp.max(scores, axis=-1, keepdims=True)
        shifted = jnp.exp(scores - highest)
        totals = jnp.sum(shifted, axis=-1, keepdims=True)
        shares = (shifted / totals).astype(bf16)
        result = jnp.einsum("hqk,khd->qhd", shares, values, preferred_element_type=f32)
        return (result, (highest + jnp.log(totals))[..., 0])

    attended, log_totals = lax.map(attend, block_starts)
    attended = attended.reshape(count, H, DH)
    log_totals = jnp.transpose(log_totals, (1, 0, 2)).reshape(H, count)
    heads_mixed = (
        (output_gates[..., None] * attended[:, None]).astype(bf16).reshape(count, EA * H * DH)
    )
    hidden = inputs + lax.dot_general(
        heads_mixed, w_output, contract_last, preferred_element_type=f32
    )
    hidden_low = hidden.astype(bf16)
    logits = jnp.dot(hidden_low, w_router, preferred_element_type=f32)
    gates = jax.nn.sigmoid(jnp.take_along_axis(logits, routes, axis=1))
    slot_of_row, row_of_slot = slot_tables(routes, experts, most)
    valid = row_of_slot < routed
    safe_row = jnp.minimum(row_of_slot, routed - 1)
    source = safe_row // TOPK
    outgoing = jnp.where(valid[:, None], hidden_low[source], jnp.zeros((), bf16)).reshape(
        owners, local_experts, most, D
    )

    def expert_apply(items):
        raised = jnp.einsum("nemd,edf->nemf", items, w_up, preferred_element_type=f32)
        active = jax.nn.silu(raised).astype(bf16)
        lowered = jnp.einsum("nemf,edf->nemd", active, w_down, preferred_element_type=f32).astype(
            bf16
        )
        return (lowered, raised)

    lowered, raised = expert_apply(
        lax.all_to_all(outgoing, "expert", split_axis=0, concat_axis=0, tiled=True)
    )
    returned = lax.all_to_all(lowered, "expert", split_axis=0, concat_axis=0, tiled=True).reshape(
        experts * most, D
    )
    expert_rows = returned[slot_of_row].reshape(count, TOPK, D)
    output = hidden + jnp.sum(gates[..., None] * expert_rows, axis=1)
    mixed = output.astype(bf16)
    grad_out = cotangent.astype(f32) * live[:, None].astype(f32)
    grad_gates = jnp.sum(grad_out[:, None, :] * expert_rows, axis=2)
    gate_flat = gates.reshape(routed)
    grad_outgoing = (
        jnp.where(valid[:, None], gate_flat[safe_row][:, None] * grad_out[source], 0.0)
        .astype(bf16)
        .reshape(owners, local_experts, most, D)
    )
    grad_lowered = lax.all_to_all(grad_outgoing, "expert", split_axis=0, concat_axis=0, tiled=True)
    items = lax.all_to_all(outgoing, "expert", split_axis=0, concat_axis=0, tiled=True)
    raised = expert_apply(items)[1]
    grad_active = jnp.einsum("nemd,edf->nemf", grad_lowered, w_down, preferred_element_type=f32)
    sigmoid_raised = jax.nn.sigmoid(raised)
    grad_raised = (grad_active * sigmoid_raised * (1.0 + raised * (1.0 - sigmoid_raised))).astype(
        bf16
    )
    grad_items = jnp.einsum("nemf,edf->nemd", grad_raised, w_up, preferred_element_type=f32).astype(
        bf16
    )
    active = jax.nn.silu(raised).astype(bf16)
    grad_items, grad_raised, active = (grad_items, grad_raised, active)
    grad_items, grad_raised, active, grad_arrived, arrived = (
        grad_items,
        grad_raised,
        active,
        grad_lowered,
        items,
    )
    grad_up_local = jnp.einsum("nemd,nemf->edf", arrived, grad_raised, preferred_element_type=f32)
    grad_down_local = jnp.einsum("nemd,nemf->edf", grad_arrived, active, preferred_element_type=f32)
    grad_up, grad_down = (
        lax.psum_scatter(
            grad_up_local.astype(jnp.bfloat16), "dp", scatter_dimension=1, tiled=True
        ).astype(jnp.float32),
        lax.psum_scatter(
            grad_down_local.astype(jnp.bfloat16), "dp", scatter_dimension=1, tiled=True
        ).astype(jnp.float32),
    )
    grad_back = lax.all_to_all(
        grad_items, "expert", split_axis=0, concat_axis=0, tiled=True
    ).reshape(experts * most, D)
    grad_hidden = grad_out + jnp.sum(
        grad_back[slot_of_row].reshape(count, TOPK, D), axis=1, dtype=f32
    )
    grad_picked = grad_gates * gates * (1.0 - gates)
    expert_ids = jnp.arange(experts, dtype=jnp.int32)
    grad_logits = jnp.sum(
        jnp.where(routes[:, :, None] == expert_ids[None, None, :], grad_picked[..., None], 0.0),
        axis=1,
    ).astype(bf16)
    grad_router = lax.dot_general(
        hidden_low, grad_logits, contract_first, preferred_element_type=f32
    )
    grad_hidden = grad_hidden + lax.dot_general(
        grad_logits, w_router, contract_last, preferred_element_type=f32
    )
    grad_hidden_low = grad_hidden.astype(bf16)
    grad_output = lax.dot_general(
        grad_hidden_low, heads_mixed, contract_first, preferred_element_type=f32
    )
    grad_mixed = jnp.dot(grad_hidden_low, w_output, preferred_element_type=f32).reshape(
        count, EA, H, DH
    )
    grad_attended = jnp.sum(output_gates[..., None] * grad_mixed, axis=1).astype(bf16)
    grad_out_gates = jnp.sum(grad_mixed * attended[:, None], axis=-1)
    grad_out_logits = (
        jnp.where(chosen, grad_out_gates * output_gates * (1.0 - output_gates), 0.0)
        .astype(bf16)
        .reshape(count, EA * H)
    )

    def attend_back(carry, start):
        grad_keys, grad_vals = carry
        query_block, scores = scores_at(start)
        shares = jnp.exp(scores - log_totals[..., None])
        grad_shares = jnp.einsum("qhd,khd->hqk", grad_attended, values, preferred_element_type=f32)
        centre = jnp.sum(shares * grad_shares, axis=-1, keepdims=True)
        grad_scores = (shares * (grad_shares - centre)).astype(bf16)
        grad_query_block = jnp.einsum(
            "hqk,khd->qhd", grad_scores, key_rot, preferred_element_type=f32
        )
        grad_keys = grad_keys + jnp.einsum(
            "hqk,qhd->khd", grad_scores, query_block, preferred_element_type=f32
        )
        grad_vals = grad_vals + jnp.einsum(
            "hqk,qhd->khd", shares.astype(bf16), grad_attended, preferred_element_type=f32
        )
        return ((grad_keys, grad_vals), grad_query_block)

    zero_heads = jnp.zeros((count, H, DH), f32)
    (grad_keys, grad_vals), grad_queries = lax.scan(
        attend_back, (zero_heads, zero_heads), block_starts
    )
    grad_queries = grad_queries.reshape(count, H, DH)
    grad_query_proj = (
        rotate_back(grad_queries * scale, cosine, sine).astype(bf16).reshape(count, H * DH)
    )
    grad_key_proj = rotate_back(grad_keys, cosine, sine).astype(bf16).reshape(count, H * DH)
    grad_value_all = (
        (value_gates[..., None] * grad_vals[:, None]).astype(bf16).reshape(count, EA * H * DH)
    )
    grad_value_gates = jnp.sum(grad_vals[:, None] * value_all, axis=-1)
    grad_value_logits = (
        jnp.where(chosen, grad_value_gates * value_gates * (1.0 - value_gates), 0.0)
        .astype(bf16)
        .reshape(count, EA * H)
    )
    grad_query = lax.dot_general(
        normed, grad_query_proj, contract_first, preferred_element_type=f32
    )
    grad_key = lax.dot_general(normed, grad_key_proj, contract_first, preferred_element_type=f32)
    grad_value = lax.dot_general(tokens, grad_value_all, contract_first, preferred_element_type=f32)
    grad_value_gate = lax.dot_general(
        tokens, grad_value_logits, contract_first, preferred_element_type=f32
    )
    grad_output_gate = lax.dot_general(
        tokens, grad_out_logits, contract_first, preferred_element_type=f32
    )
    grad_normed = lax.dot_general(
        grad_query_proj, w_query, contract_last, preferred_element_type=f32
    ) + lax.dot_general(grad_key_proj, w_key, contract_last, preferred_element_type=f32)
    grad_gain = jnp.sum(grad_normed * standard, axis=0)
    grad_standard = grad_normed * norm_gain
    grad_tokens = grad_hidden + inverse * (
        grad_standard
        - jnp.mean(grad_standard, axis=-1, keepdims=True)
        - standard * jnp.mean(grad_standard * standard, axis=-1, keepdims=True)
    )
    grad_tokens = (
        grad_tokens
        + lax.dot_general(grad_value_all, w_value, contract_last, preferred_element_type=f32)
        + lax.dot_general(
            grad_value_logits, w_value_gate, contract_last, preferred_element_type=f32
        )
        + lax.dot_general(grad_out_logits, w_output_gate, contract_last, preferred_element_type=f32)
    )
    summed = (
        lax.psum_scatter(grad_gain, ("dp", "expert"), scatter_dimension=0, tiled=True),
        lax.psum_scatter(grad_query, ("dp", "expert"), scatter_dimension=0, tiled=True),
        lax.psum_scatter(grad_key, ("dp", "expert"), scatter_dimension=0, tiled=True),
        lax.psum_scatter(grad_value, ("dp", "expert"), scatter_dimension=0, tiled=True),
        lax.psum_scatter(grad_output, ("dp", "expert"), scatter_dimension=0, tiled=True),
        lax.psum_scatter(grad_value_gate, ("dp", "expert"), scatter_dimension=0, tiled=True),
        lax.psum_scatter(grad_output_gate, ("dp", "expert"), scatter_dimension=0, tiled=True),
        lax.psum_scatter(grad_router, ("dp", "expert"), scatter_dimension=0, tiled=True),
    )
    return (
        mixed,
        grad_tokens,
        summed[0],
        summed[1],
        summed[2],
        summed[3],
        summed[4],
        summed[5],
        summed[6],
        summed[7],
        grad_up,
        grad_down,
    )


F32 = jnp.float32
BF16 = jnp.bfloat16
MESH = pl.DeviceIdType.MESH
LANES = 128


def mm(a, b):
    return lax.dot_general(a, b, (((1,), (0,)), ((), ())), preferred_element_type=F32)


def mm_t(a, b):
    return lax.dot_general(a, b, (((1,), (1,)), ((), ())), preferred_element_type=F32)


def tmm(a, b):
    return lax.dot_general(a, b, (((0,), (0,)), ((), ())), preferred_element_type=F32)


def iota(shape, axis):
    return lax.broadcasted_iota(jnp.int32, shape, axis)


def column(x, j, width=LANES):
    return jnp.broadcast_to(x[:, j : j + 1], (x.shape[0], width))


def sigmoid(x):
    return 1.0 / (1.0 + jnp.exp(-x))


class Scratch:
    def __init__(self):
        self.names, self.shapes = [], []

    def add(self, name, shape):
        self.names.append(name)
        self.shapes.append(shape)

    def vmem(self, name, shape, dtype):
        self.add(name, pltpu.VMEM(shape, dtype))

    def sems(self, name, *shape):
        self.add(name, pltpu.SemaphoreType.DMA(shape))


SMALL = ("tokens", "cot", "lens", "rt", "het", "gain", "wvg", "wog", "wr")
WEIGHTS = ("wq", "wk", "wv", "wo", "wu", "wd")
OUTPUTS = ("mixed", "gtok", "ggain", "gq", "gk", "gv", "go", "gvg", "gog", "gr", "gup", "gdn")


def in_hbm(names):
    return tuple(name + "_h" for name in names)


def layer_kernel(names, nd, nz, local, *refs):
    r = dict(zip(names, refs))
    R = type("R", (), r)
    C = R.tokens.shape[0]
    own_e = 2 * local
    pad_e = R.maskb.shape[1]
    EF = own_e * DH
    HF = local * DH
    HD = H * DH
    EV = EA * HD
    S = D // (nd * nz * 2)
    SL = S * nz
    GATE = EA * H
    p = lax.axis_index("dp")
    e = lax.axis_index("expert")
    z = e // 2
    c = e % 2
    sib = 1 - c

    def dev(p_, z_, c_):
        return (p_, z_ * 2 + c_)

    def times(i, n):
        return pl.multiple_of(i * n, n)

    def remote(src, dst, ss, rs, to):
        return pltpu.make_async_remote_copy(
            src_ref=src, dst_ref=dst, send_sem=ss, recv_sem=rs, device_id=to, device_id_type=MESH
        )

    def arrived(dst, rs):
        remote(dst, dst, rs, rs, dev(p, z, sib)).wait_recv()

    def sent(src, ss):
        remote(src, src, ss, ss, dev(p, z, sib)).wait_send()

    beside = p + 1 - 2 * lax.rem(p, 2)
    across = lax.rem(p + 2, nd)
    diagonal = lax.rem(beside + 2, nd)

    def core_cols(cc):
        return pl.ds(times(cc, HF), HF)

    def plane(k):
        return (p, beside, across, diagonal)[k]

    def line(k):
        return lax.rem(z + k, nz)

    barrier = pltpu.get_barrier_semaphore()
    partners = [dev(p, z, sib)]
    partners += [dev(p, line(k), c) for k in range(1, nz)]
    for k in range(1, nd):
        partners += [dev(plane(k), z, c), dev(plane(k), z, sib)]
    for to in partners:
        pl.semaphore_signal(barrier, inc=1, device_id=to, device_id_type=MESH)

    loads = {}

    def load(name, src, dst, sem):
        cp = pltpu.make_async_copy(src, dst, sem)
        cp.start()
        loads[name] = cp

    def loaded(*names):
        for name in names:
            loads.pop(name).wait()

    def landed(dst, sem):
        pltpu.make_async_copy(dst, dst, sem).wait()

    for i, name in enumerate(("cot", "lens", "rt", "tokens", "gain", "het", "wvg", "wog", "wr")):
        load(name, r[name + "_h"], r[name], R.ld_in.at[i])
    loaded("lens")
    l0 = R.lens[0, 0]
    b1 = l0 + R.lens[0, 1]
    row = iota((C, LANES), 0)
    lane = iota((C, LANES), 1)
    seq_r = (row >= l0).astype(jnp.int32) + (row >= b1).astype(jnp.int32)
    seq_c = (lane >= l0).astype(jnp.int32) + (lane >= b1).astype(jnp.int32)
    live = row < b1
    allowed = ((seq_r == seq_c) & (lane <= row) & (lane < b1)) | (row == lane)
    live_f = jnp.where(live, 1.0, 0.0).astype(F32)
    start = jnp.where(seq_r == 0, 0, l0)
    position = jnp.where(live, row - start, 0).astype(F32)

    loaded("cot")
    for b in range(D // LANES):
        cols = slice(b * LANES, (b + 1) * LANES)
        R.cotb[pl.ds(times(z, C), C), cols] = (R.cot[:, cols].astype(F32) * live_f).astype(BF16)
    load("qk", R.wq, R.wqk_b.at[:, 0:HD], R.ld.at[0])
    load("qk", R.wk, R.wqk_b.at[:, HD : 2 * HD], R.ld.at[0])
    load("v", R.wv, R.wv_b, R.ld.at[1])
    for i in range(local):
        col = times(c * local + i, DH)
        load("up", R.wu.at[i], R.wup_b.at[:, pl.ds(col, DH)], R.ld.at[2])
        load("dn", R.wd.at[i], R.wdn_b.at[:, pl.ds(col, DH)], R.ld.at[3])
    load("o", R.wo, R.wo_b, R.ld.at[4])
    loaded("rt")
    ids = iota((pad_e, C), 0)
    for zz in range(nz):
        named = jnp.zeros((pad_e, C), F32)
        for k in range(TOPK):
            hit = jnp.broadcast_to(R.rt[k : k + 1, :], (pad_e, C)) == ids + zz * own_e
            named = jnp.where(hit & (ids < own_e), 1.0, named)
        R.mask_s[zz] = named.astype(BF16)
    R.maskb[z] = R.mask_s[z]

    pl.semaphore_wait(barrier, len(partners))

    def block(buf, o):
        return buf.at[pl.ds(times(o, C), C), :]

    def pass_on(buf, ss, rs, o, right, left):
        @pl.when(right)
        def _():
            remote(block(buf, o), block(buf, o), ss.at[o], rs.at[o], dev(p, z + 1, c)).start()

        @pl.when(left)
        def _():
            way = jnp.where(o == z, nz, o)
            remote(block(buf, o), block(buf, o), ss.at[way], rs.at[o], dev(p, z - 1, c)).start()

    def passed(buf, ss, o, right, left):
        @pl.when(right)
        def _():
            sent(block(buf, o), ss.at[o])

        @pl.when(left)
        def _():
            sent(block(buf, o), ss.at[jnp.where(o == z, nz, o)])

    def gather_own(buf, ss, rs):
        pass_on(buf, ss, rs, z, z < nz - 1, z > 0)

    def gather_on(buf, ss, rs, o):
        arrived(block(buf, o), rs.at[o])
        pass_on(buf, ss, rs, o, (o < z) & (z < nz - 1), (o > z) & (z > 0))

    def gather_step(buf, ss, rs, k):
        @pl.when(z >= k)
        def _():
            gather_on(buf, ss, rs, z - k)

        @pl.when(z + k < nz)
        def _():
            gather_on(buf, ss, rs, z + k)

    def gather_end(buf, ss):
        passed(buf, ss, z, z < nz - 1, z > 0)
        for k in range(1, nz):

            @pl.when(z >= k)
            def _():
                passed(buf, ss, z - k, z < nz - 1, False)

            @pl.when(z + k < nz)
            def _():
                passed(buf, ss, z + k, False, z > 0)

    gather_own(R.cotb, R.cot_ss, R.cot_rs)
    for k in range(1, nz):
        o = line(k)
        remote(R.mask_s.at[o], R.maskb.at[z], R.tiny_s.at[0], R.tiny_r.at[0], dev(p, o, c)).start()

    loaded("tokens", "gain", "het", "wvg", "wog", "wr")

    s_row, s_col = iota((GATE, LANES), 0), iota((GATE, LANES), 1)
    to_v = jnp.where(s_row == s_col, 1.0, 0.0).astype(BF16)
    to_o = jnp.where(s_row + GATE == s_col, 1.0, 0.0).astype(BF16)
    R.wg_b[...] = (tmm(R.wvg[...], to_v) + tmm(R.wog[...], to_o)).astype(BF16)
    experts = R.wr.shape[0]
    r_row, r_col = iota((experts, LANES), 0), iota((experts, LANES), 1)
    to_r = jnp.where((r_row == r_col + z * own_e) & (r_col < own_e), 1.0, 0.0).astype(BF16)
    R.wrl_b[...] = tmm(R.wr[...], to_r).astype(BF16)

    half = lax.rem(lane, DH // 2).astype(F32)
    angle = position * jnp.exp(half * (-2.0 / DH * math.log(rope_base)))
    cosine = jnp.cos(angle)
    sine = jnp.where(lane < DH // 2, -jnp.sin(angle), jnp.sin(angle))

    def rot(v):
        return v * cosine + pltpu.roll(v, DH // 2, 1) * sine

    def rot_back(v):
        return v * cosine - pltpu.roll(v, DH // 2, 1) * sine

    inputs = R.tokens[...].astype(F32)
    centred = inputs - jnp.mean(inputs, axis=-1, keepdims=True)
    inverse = lax.rsqrt(jnp.mean(centred * centred, axis=-1, keepdims=True) + norm_eps)
    standard = centred * inverse
    R.std_b[...] = standard
    R.normed_b[...] = (standard * R.gain[...]).astype(BF16)

    landed(R.wqk_b, R.ld.at[0])
    scale = DH ** (-0.5)
    qk = mm(R.normed_b[...], R.wqk_b[:, 0:HD])
    for h in range(H):
        hs = slice(h * DH, (h + 1) * DH)
        R.q_b[:, hs] = (rot(qk[:, hs]) * scale).astype(BF16)
    qk = mm(R.normed_b[...], R.wqk_b[:, HD : 2 * HD])
    for h in range(H):
        hs = slice(h * DH, (h + 1) * DH)
        R.k_b[:, hs] = rot(qk[:, hs]).astype(BF16)

    hit = []
    for j in range(GATE):
        x, h = divmod(j, H)
        one = (R.het[2 * h : 2 * h + 1, :] == x) | (R.het[2 * h + 1 : 2 * h + 2, :] == x)
        hit.append(jnp.where(one, 1.0, 0.0).astype(F32))
    hit = jnp.concatenate(hit + hit + [jnp.zeros((LANES - 2 * GATE, C), F32)], axis=0)
    R.gate_b[...] = sigmoid(mm(R.tokens[...], R.wg_b[...])) * hit.T

    landed(R.wup_b.at[:, core_cols(c)], R.ld.at[2])
    landed(R.wdn_b.at[:, core_cols(c)], R.ld.at[3])
    for i, buf in enumerate((R.wup_b, R.wdn_b)):
        part = buf.at[:, pl.ds(times(c, HF), HF)]
        cp = remote(part, part, R.w_s.at[0], R.w_s.at[1], dev(p, z, sib))
        cp.start()

    landed(R.wv_b, R.ld.at[1])
    gates = R.gate_b[...]
    total = [None] * H
    for x in range(EA):
        R.val_b[:, x * HD : (x + 1) * HD] = mm(R.tokens[...], R.wv_b[:, x * HD : (x + 1) * HD])
        for h in range(H):
            lo = x * HD + h * DH
            term = column(gates, x * H + h) * R.val_b[:, lo : lo + DH]
            total[h] = term if x == 0 else total[h] + term
    for h in range(H):
        R.v_b[:, h * DH : (h + 1) * DH] = total[h].astype(BF16)

    for h in range(H):
        hs = slice(h * DH, (h + 1) * DH)
        scores = jnp.where(allowed, mm_t(R.q_b[:, hs], R.k_b[:, hs]), masked_score)
        shifted = jnp.exp(scores - jnp.max(scores, axis=-1, keepdims=True))
        shares = shifted / jnp.sum(shifted, axis=-1, keepdims=True)
        R.prob_b[h] = shares
        R.att_b[:, hs] = mm(shares.astype(BF16), R.v_b[:, hs])

    for x in range(EA):
        for h in range(H):
            lo = x * HD + h * DH
            R.mix_b[:, lo : lo + DH] = (
                column(gates, GATE + x * H + h) * R.att_b[:, h * DH : (h + 1) * DH]
            ).astype(BF16)
    landed(R.wo_b, R.ld.at[4])
    half_d = D // 2
    for b in range(2):
        cols = slice(b * half_d, (b + 1) * half_d)
        hidden = R.tokens[:, cols].astype(F32) + mm_t(R.mix_b[...], R.wo_b[cols, :])
        R.hid_f[:, cols] = hidden
        R.hidb[pl.ds(times(z, C), C), cols] = hidden.astype(BF16)
    gather_own(R.hidb, R.hid_ss, R.hid_rs)
    gather_step(R.cotb, R.cot_ss, R.cot_rs, 1)

    def put_turned(x, w):
        for b in range(D // LANES):
            t = x[:, b * LANES : (b + 1) * LANES].astype(F32).T.astype(BF16)
            for q in range(LANES // S):
                i = (b * LANES) // S + q
                pp, zz, cc = i // (2 * nz), (i % (2 * nz)) // 2, i % 2
                at = (pp * 2 + cc) * SL + zz * S
                R.lt[at : at + S, w * LANES : (w + 1) * LANES] = t[q * S : (q + 1) * S, :]

    plane_all = [(k, dc) for k in range(nd) for dc in range(2) if k or dc]

    def side(dc):
        return sib if dc else c

    def send_turned(w0, w1, ss, rs):
        lanes = slice(w0 * LANES, w1 * LANES)
        for k, dc in plane_all:
            to = plane(k)
            slot = 2 * k + dc
            at = times(to * 2 + side(dc), SL)
            cp = remote(
                R.lt.at[pl.ds(at, SL), lanes],
                R.ltr.at[slot, :, lanes],
                ss,
                rs,
                dev(to, z, side(dc)),
            )
            cp.start()
        R.ltr[0, :, lanes] = R.lt[pl.ds(times(p * 2 + c, SL), SL), lanes]

    def turned_here(w0, w1, ss, rs):
        there = R.ltr.at[1 : 2 * nd, :, w0 * LANES : w1 * LANES]
        sent(there, ss)
        arrived(there, rs)

    def rows_at(buf, lanes, slot):
        return buf.at[slot * C : (slot + 1) * C, lanes]

    def send_rows(buf, lanes, sem, ways=(1, 2)):
        for k in ways:
            remote(
                rows_at(buf, lanes, 0),
                rows_at(buf, lanes, 2 * k),
                sem.at[0],
                sem.at[k],
                dev(plane(k), z, c),
            ).start()
        hand_over(buf, lanes, sem, 0)

    def hand_over(buf, lanes, sem, k):
        remote(
            rows_at(buf, lanes, 2 * k),
            rows_at(buf, lanes, 2 * k + 1),
            sem.at[0],
            sem.at[5 if k == 3 else 4],
            dev(p, z, sib),
        ).start()

    def hand_near(buf, lanes, sem, via):
        for k in (via, 3 - via) if via else (1, 2):
            arrived(rows_at(buf, lanes, 2 * k), sem.at[k])
            if k == via:
                remote(
                    rows_at(buf, lanes, 2 * k),
                    rows_at(buf, lanes, 6),
                    sem.at[0],
                    sem.at[3],
                    dev(plane(3 - via), z, c),
                ).start()
            hand_over(buf, lanes, sem, k)

    def hand_far(buf, lanes, sem):
        arrived(rows_at(buf, lanes, 6), sem.at[3])
        hand_over(buf, lanes, sem, 3)

    def near_here(buf, lanes, sem):
        arrived(buf.at[0 : 3 * C, lanes], sem.at[4])

    def far_here(buf, lanes, sem):
        arrived(rows_at(buf, lanes, 7), sem.at[5])

    def rows_sent(buf, lanes, sem):
        sent(buf.at[0 : 7 * C, lanes], sem.at[0])

    put_turned(R.tokens[...], 0)
    put_turned(R.normed_b[...], 1)
    put_turned(R.hid_f[...], 2)
    send_turned(0, 3, R.lt_s.at[0], R.lt_s.at[1])
    R.ra[0:C, 0:HD] = R.att_b[...].astype(BF16)
    R.ra[0:C, HD : HD + LANES] = gates.astype(BF16)
    RA = slice(0, HD + LANES)
    send_rows(R.ra, RA, R.ra_s)

    sent(R.wup_b, R.w_s.at[0])
    arrived(R.wup_b, R.w_s.at[1])

    least = jnp.minimum(z, nz - 1 - z)
    inner = least > 0
    left_half = z < nz // 2
    near = jnp.where(inner, jnp.where(left_half, 0, nz - 1), jnp.where(left_half, 1, nz - 2))
    fellow = jnp.where(left_half, nz // 2, nz // 2 - 1)
    far = jnp.where(left_half, nz - 1, 0)

    def origin(k):
        paired = k <= 2 * least
        dist = jnp.where(paired, (k + 1) // 2, k - least)
        left = jnp.where(paired, lax.rem(k, 2) == 1, z > nz - 1 - z)
        return jnp.where(k == 0, z, jnp.where(left, z - dist, z + dist))

    def expert_block(k, carry):
        o = origin(k)
        rows = pl.ds(times(o, C), C)

        @pl.when((k == 1) & inner)
        def _():
            gather_on(R.hidb, R.hid_ss, R.hid_rs, origin(1))

        @pl.when((k > 0) & (k + inner.astype(jnp.int32) < nz))
        def _():
            gather_on(R.hidb, R.hid_ss, R.hid_rs, origin(k + inner.astype(jnp.int32)))

        @pl.when(k == jnp.where(inner, 1, 2))
        def _():
            for far_step in range(2, nz - 1):
                gather_step(R.cotb, R.cot_ss, R.cot_rs, far_step)

        @pl.when(k > 0)
        def _():
            @pl.when((o == z - nz + 1) | (o == z + nz - 1))
            def _():
                arrived(block(R.cotb, o), R.cot_rs.at[o])

        @pl.when(k == 1)
        def _():
            arrived(R.maskb.at[0 : nz - 1], R.tiny_r.at[0])

        hb = R.hidb[rows, :]
        cb = R.cotb[rows, :]
        named = R.maskb[o].astype(F32)
        named = jnp.concatenate([named, jnp.zeros((LANES - pad_e, C), F32)], axis=0).T
        g = sigmoid(mm(hb, R.wrl_b[...])) * named
        glog = jnp.zeros((C, LANES), F32)
        for q in range(2):
            cols = slice(q * HF, (q + 1) * HF)
            raised = mm(hb, R.wup_b[:, cols])
            back = mm(cb, R.wdn_b[:, cols])
            for i in range(local):
                j = q * local + i
                u = raised[:, i * DH : (i + 1) * DH]
                a = back[:, i * DH : (i + 1) * DH]
                gj = column(g, j)
                s = sigmoid(u)
                act = u * s
                lo = j * DH
                R.gact[rows, lo : lo + DH] = (gj * act).astype(BF16)
                R.gra[rows, lo : lo + DH] = (gj * a * (s * (1.0 + u * (1.0 - s)))).astype(BF16)
                gg = jnp.sum(a * act, axis=1, keepdims=True)
                glog = jnp.where(lane == j, jnp.broadcast_to(gg, (C, LANES)), glog)
        glog = glog * g * (1.0 - g)
        low = glog.astype(BF16)
        R.glog_s[o] = glog.T[0:pad_e, :].astype(BF16)
        for b in range(2):
            cols = slice(b * half_d, (b + 1) * half_d)
            gh = mm_t(R.gra[rows, :], R.wup_b[cols, :]) + mm_t(low, R.wrl_b[cols, :])
            R.gh_s[o, :, cols] = gh.astype(BF16)

        @pl.when(k > 0)
        def _():
            remote(
                R.glog_s.at[o], R.glog_r.at[z], R.tiny_s.at[1], R.tiny_r.at[1], dev(p, o, c)
            ).start()

        @pl.when((k > 0) & (least == 0) & (o != fellow))
        def _():
            send_back(o)

        @pl.when((k > 0) & (least == 0) & (o == fellow))
        def _():
            send_by(o, near, 0)

        @pl.when((k > 0) & inner & (o == far))
        def _():
            send_by(o, fellow, 1)

        @pl.when(k == 2)
        def _():
            hand_near(R.ra, RA, R.ra_s, 2)

        @pl.when((k == 2) & (least == 0))
        def _():
            there = pl.ds(times(near, C), C)
            for b in range(2):
                cols = slice(b * half_d, (b + 1) * half_d)
                R.out_s[near, :, cols] = mm_t(R.gact[there, :], R.wdn_b[cols, :]).astype(BF16)
            slot = jnp.where(z == 0, near, nz)
            remote(
                R.out_s.at[near],
                R.out_r.at[slot],
                R.out_sem.at[nz + 1],
                R.out_sem.at[slot],
                dev(p, near, c),
            ).start()

        return carry

    def send_back(o):
        remote(R.gh_s.at[o], R.gh_r.at[z], R.gh_sem.at[0], R.gh_sem.at[1], dev(p, o, c)).start()

    def send_by(o, by, slot):
        remote(
            R.gh_s.at[o], R.gh_x.at[slot], R.gh_sem.at[0], R.gh_sem.at[2 + slot], dev(p, by, c)
        ).start()

    def relay_back(o, slot):
        arrived(R.gh_x.at[slot], R.gh_sem.at[2 + slot])
        R.gh_s[o] = (R.gh_s[o].astype(F32) + R.gh_x[slot].astype(F32)).astype(BF16)
        send_back(o)

    lax.fori_loop(0, nz, expert_block, 0)

    def rows_of(at):
        return pl.ds(times(at, rows_d), rows_d)


    rows_d = D // nd

    def grad_at(i, k, cc):
        if i == 0 and k == 3:
            return R.dg.at[:, core_cols(cc)]
        return (R.wdn_b, R.wup_b)[i].at[rows_of(plane(k)), core_cols(cc)]

    def expert_grad(i, k):
        left, right = ((R.cotb, R.gact), (R.hidb, R.gra))[i]
        for cc in (sib, c):
            grad_at(i, k, cc)[...] = tmm(left[:, rows_of(plane(k))], right[:, core_cols(cc)]).astype(BF16)
            if cc is sib:
                remote(
                    grad_at(i, k, sib),
                    R.pair_r.at[i, k],
                    R.pair_s.at[0],
                    R.pair_s.at[1 + i if k == 3 else 3],
                    dev(p, z, sib),
                ).start()

    def pair_sum(i, k):
        if k == 3:
            arrived(R.pair_r.at[i, k], R.pair_s.at[1 + i])
        own = grad_at(i, k, c)
        own[...] = (own[...].astype(F32) + R.pair_r[i, k].astype(F32)).astype(BF16)

    def part_on(i, k, to, slot):
        remote(
            grad_at(i, k, c),
            R.eg_r.at[slot, i],
            R.eg_s.at[0],
            R.eg_s.at[1 + i if slot == 1 else 3 + i],
            dev(plane(to), z, c),
        ).start()

    def first_half(i, n):
        first = 1 if i == 0 else 2
        rows = slice(n * rows_d // 2, (n + 1) * rows_d // 2)
        remote(
            grad_at(i, first, c).at[rows],
            R.eg_r.at[0, i, rows],
            R.eg_s.at[0],
            R.eg_s.at[3 + i],
            dev(plane(first), z, c),
        ).start()

    def expert_grad_relay(i):
        second = 2 if i == 0 else 1

        @pl.when(least == 0)
        def _():
            first_half(i, 1)

        arrived(R.eg_r.at[1, i], R.eg_s.at[1 + i])
        own = grad_at(i, second, c)
        own[...] = (own[...].astype(F32) + R.eg_r[1, i].astype(F32)).astype(BF16)
        part_on(i, second, second, 2)

    def to_place(own, got, ss, rs, o):
        remote(own(o), got(z), ss, rs, dev(p, o, c)).start()

    def run(own, got, ss, rs, k, n):
        def hand(d, slot, to):
            if k > 1:
                arrived(got(d), rs.at[d])
                own(d)[...] = (own(d)[...].astype(F32) + got(d)[...].astype(F32)).astype(BF16)
            remote(own(d), got(slot), ss, rs.at[slot], dev(p, to, c)).start()

        @pl.when(z == k - 1)
        def _():
            hand(nz - 1 - n, nz - 1 - n, k)

        @pl.when(z == nz - k)
        def _():
            hand(n, nz if n == nz - k - 1 else n, nz - k - 1)

    def run_end(total, got, rs):
        for there, slot in ((z > 0, z), (z < nz - 1, nz)):

            @pl.when(there)
            def _():
                arrived(got(slot), rs.at[slot])
                total[...] += got(slot)[...].astype(F32)

    out_sum = (lambda d: R.out_s.at[d], lambda d: R.out_r.at[d], R.out_sem.at[nz + 1], R.out_sem)
    out_run = functools.partial(run, *out_sum)

    def grad_sum(i, lanes):
        return (
            lambda d: R.pb.at[d * S : (d + 1) * S, lanes],
            lambda d: R.pn.at[i, d],
            R.pn_sem.at[i, nz + 1],
            R.pn_sem.at[i],
        )

    def part_sum(i, lanes):
        return (
            lambda o: R.pb.at[pl.ds(times(o, S), S), lanes],
            lambda o: R.pr.at[o, :, slice(lanes.start - 2 * EV, lanes.stop - 2 * EV)],
            R.p_sem.at[0],
            R.p_sem.at[1 + i],
        )

    expert_grad(1, 3)
    expert_grad(0, 3)
    for i, to in ((1, 2), (0, 1)):
        pair_sum(i, 3)
        part_on(i, 3, to, 1)

    def out_tile(t, carry):
        rows = pl.ds(times(t, 256), 256)
        got = mm_t(R.gact[...], R.wdn_b[rows, :]).astype(BF16)
        for o in range(nz):

            @pl.when(inner | (o != near))
            def _():
                R.out_s[o, :, rows] = got[o * C : (o + 1) * C, :]

        return carry

    lax.fori_loop(0, D // 256, out_tile, 0)
    out_run(1, 0)

    @pl.when(inner)
    def _():
        relay_back(near, 1)

    for k in (1, 2, 0):
        expert_grad(1, k)
        expert_grad(0, k)
    def sum_pairs():
        arrived(R.pair_r.at[:, 0:3], R.pair_s.at[3])
        for k in (1, 2, 0):
            pair_sum(1, k)
            pair_sum(0, k)

    @pl.when(inner)
    def _():
        relay_back(fellow, 0)
        sum_pairs()
        for i in range(2):
            for n in range(2):
                first_half(i, n)

    out_run(1, 1)
    hand_far(R.ra, RA, R.ra_s)
    turned_here(0, 3, R.lt_s.at[0], R.lt_s.at[1])

    R.ghid_f[...] = R.cotb[pl.ds(times(z, C), C), :].astype(F32) + R.gh_s[z].astype(F32)

    arrived(R.gh_r.at[0:2], R.gh_sem.at[1])

    def add_back(o):
        R.ghid_f[...] += R.gh_r[o].astype(F32)

    add_back(near)
    add_back(jnp.where(inner, fellow, far))

    arrived(R.glog_r.at[0 : nz - 1], R.tiny_r.at[1])
    R.glog_r[z] = R.glog_s[z]
    R.ghid_b[...] = R.ghid_f[...].astype(BF16)
    put_turned(R.ghid_f[...], 3)
    send_turned(3, 4, R.lt_s.at[2], R.lt_s.at[3])
    out_run(2, 0)

    gates = R.gate_b[...]
    small = jnp.zeros((C, LANES), F32)
    gatt = [None] * H
    for x in range(EA):
        gmix = mm(R.ghid_b[...], R.wo_b[:, x * HD : (x + 1) * HD])
        for h in range(H):
            hs = slice(h * DH, (h + 1) * DH)
            j = GATE + x * H + h
            term = column(gates, j) * gmix[:, hs]
            gatt[h] = term if x == 0 else gatt[h] + term
            gg = jnp.sum(gmix[:, hs] * R.att_b[:, hs], axis=1, keepdims=True)
            small = jnp.where(lane == j, jnp.broadcast_to(gg, (C, LANES)), small)
    for h in range(H):
        hs = slice(h * DH, (h + 1) * DH)
        low = gatt[h].astype(BF16)
        R.gatt_b[:, hs] = low
        gval = tmm(R.prob_b[h].astype(BF16), low)
        R.gval_f[:, hs] = gval
        R.rb[0:C, hs] = gval.astype(BF16)
        for x in range(EA):
            lo = x * HD + h * DH
            j = x * H + h
            gg = jnp.sum(gval * R.val_b[:, lo : lo + DH], axis=1, keepdims=True)
            small = jnp.where(lane == j, jnp.broadcast_to(gg, (C, LANES)), small)
    small = small * gates * (1.0 - gates)
    glog = jnp.concatenate(
        [jnp.zeros((2 * GATE, C), F32)]
        + [R.glog_r[o].astype(F32) for o in range(nz)]
        + [jnp.zeros((LANES - 2 * GATE - nz * pad_e, C), F32)],
        axis=0,
    )
    R.small_b[...] = small.astype(BF16)
    R.rb[0:C, HD : HD + LANES] = (small + glog.T).astype(BF16)
    RV = slice(0, HD + LANES)
    send_rows(R.rb, RV, R.rv_s, (1, 2, 3))

    q0 = HD + LANES
    for h in range(H):
        hs = slice(h * DH, (h + 1) * DH)
        low = R.gatt_b[:, hs]
        gsh = mm_t(low, R.v_b[:, hs])
        prob = R.prob_b[h]
        centre = jnp.sum(prob * gsh, axis=-1, keepdims=True)
        gs = (prob * (gsh - centre)).astype(BF16)
        R.rb[0:C, q0 + h * DH : q0 + (h + 1) * DH] = rot_back(
            mm(gs, R.k_b[:, hs]) * scale
        ).astype(BF16)
        R.rb[0:C, q0 + HD + h * DH : q0 + HD + (h + 1) * DH] = rot_back(
            tmm(gs, R.q_b[:, hs])
        ).astype(BF16)
    RQ, RK = slice(q0, q0 + HD), slice(q0 + HD, q0 + 2 * HD)
    send_rows(R.rb, RQ, R.rq_s)
    send_rows(R.rb, RK, R.rk_s)


    def turned_of(w):
        return jnp.concatenate(
            [R.ltr[s, :, w * LANES : (w + 1) * LANES] for s in range(2 * nd)], axis=1
        )

    def send_part(part, lanes):
        for o in (far, fellow, near):
            to_place(*part_sum(part, lanes), o)

    def gate_rows(dst, rows_of, g0, s0, s1):
        rows = slice(s0 * C, s1 * C)
        for x in range(EA):
            for h in range(H):
                lo = x * HD + h * DH
                gx = column(R.ra[rows, HD : HD + LANES], g0 + x * H + h)
                dst[rows, lo : lo + DH] = gx * rows_of[rows, h * DH : (h + 1) * DH]

    def gated_grad(w, gated, at):
        left = turned_of(w)
        for x in range(EA):
            cols = slice(x * HD, (x + 1) * HD)
            R.pb[:, at + x * HD : at + (x + 1) * HD] = mm(left, gated[:, cols]).astype(BF16)

    PO, PV, PQ, PS = (
        slice(0, EV),
        slice(EV, 2 * EV),
        slice(2 * EV, 2 * EV + 2 * HD),
        slice(2 * EV + 2 * HD, 2 * EV + 2 * HD + LANES),
    )
    near_here(R.ra, RA, R.ra_s)
    far_here(R.ra, RA, R.ra_s)
    out_run(2, 1)
    gate_rows(R.wo_b, R.ra, GATE, 0, 2 * nd)
    turned_here(3, 4, R.lt_s.at[2], R.lt_s.at[3])
    gated_grad(3, R.wo_b, 0)
    o_run = functools.partial(run, *grad_sum(0, PO))
    v_run = functools.partial(run, *grad_sum(1, PV))
    o_run(1, 0)
    o_run(1, 1)
    out_run(3, 0)
    gproj = mm_t(R.rb[0:C, q0 : q0 + 2 * HD], R.wqk_b[...])
    standard = R.std_b[...]
    column_sum = jnp.sum(gproj * standard, axis=0, keepdims=True)
    for b in range(D // LANES):
        R.gp[0, b : b + 1, :] = column_sum[:, b * LANES : (b + 1) * LANES]
    for k, dc in plane_all:
        slot = 2 * k + dc
        cp = remote(
            R.gp.at[0], R.gp.at[slot], R.tiny_s.at[2], R.tiny_r.at[2], dev(plane(k), z, side(dc))
        )
        cp.start()

    @pl.when(least == 0)
    def _():
        sum_pairs()
        first_half(0, 0)
        first_half(1, 0)

    hand_near(R.rb, RV, R.rv_s, 0)

    inputs = R.tokens[...].astype(F32)
    centred = inputs - jnp.mean(inputs, axis=-1, keepdims=True)
    inverse = lax.rsqrt(jnp.mean(centred * centred, axis=-1, keepdims=True) + norm_eps)
    gs = gproj * R.gain[...]
    gtok = R.ghid_f[...] + inverse * (
        gs
        - jnp.mean(gs, axis=-1, keepdims=True)
        - standard * jnp.mean(gs * standard, axis=-1, keepdims=True)
    )
    R.gtok[...] = gtok
    for x in range(EA):
        for h in range(H):
            lo = x * HD + h * DH
            R.mix_b[:, lo : lo + DH] = (
                column(gates, x * H + h) * R.gval_f[:, h * DH : (h + 1) * DH]
            ).astype(BF16)
    for b in range(2):
        cols = slice(b * half_d, (b + 1) * half_d)
        R.gtok[:, cols] += mm_t(R.mix_b[...], R.wv_b[cols, :]) + mm_t(
            R.small_b[...], R.wg_b[cols, :]
        )


    o_run(2, 0)
    near_here(R.rb, RV, R.rv_s)
    gate_rows(R.wv_b, R.rb, 0, 0, 6)
    o_run(2, 1)
    hand_far(R.rb, RV, R.rv_s)
    far_here(R.rb, RV, R.rv_s)
    gate_rows(R.wv_b, R.rb, 0, 6, 8)
    gated_grad(0, R.wv_b, EV)
    v_run(1, 0)
    hand_near(R.rb, RK, R.rk_s, 2)
    hand_near(R.rb, RQ, R.rq_s, 1)
    v_run(1, 1)
    o_run(3, 0)
    total = R.gp[0]
    sent(R.gp.at[1:], R.tiny_s.at[2])
    arrived(R.gp.at[1:], R.tiny_r.at[2])
    for k, dc in plane_all:
        total = total + R.gp[2 * k + dc]
    R.gz_s[...] = total
    for k in range(1, nz):
        o = line(k)
        remote(R.gz_s, R.gz.at[z], R.tiny_s.at[3], R.tiny_r.at[3], dev(p, o, c)).start()

    lane_s = iota((SL, LANES), 1)
    small_t = mm(turned_of(0), R.rb[:, HD : HD + LANES])
    small_h = mm(turned_of(2), R.rb[:, HD : HD + LANES])
    R.pb[:, PS] = jnp.where(lane_s < 2 * GATE, small_t, small_h).astype(BF16)
    send_part(1, PS)
    o_run(1, 2)
    expert_grad_relay(0)
    expert_grad_relay(1)
    v_run(2, 0)
    v_run(2, 1)
    v_run(3, 0)

    hand_far(R.rb, RQ, R.rq_s)
    hand_far(R.rb, RK, R.rk_s)
    for lanes, sem in ((RQ, R.rq_s), (RK, R.rk_s)):
        near_here(R.rb, lanes, sem)
        far_here(R.rb, lanes, sem)
    left = turned_of(1)
    for b in range(2):
        lo = q0 + b * HD
        R.pb[:, 2 * EV + b * HD : 2 * EV + (b + 1) * HD] = mm(left, R.rb[:, lo : lo + HD]).astype(
            BF16
        )
    send_part(0, PQ)
    v_run(1, 2)
    R.hid_f[...] += R.out_s[z].astype(F32)
    run_end(R.hid_f, out_sum[1], R.out_sem)
    R.mixed[...] = R.hid_f[...].astype(BF16)

    arrived(R.gz.at[0 : nz - 1], R.tiny_r.at[3])
    for k in range(1, nz):
        total = total + R.gz[line(k)]
    first = (p * 2 * nz + z * 2 + c) * S
    pick_row = iota((D // LANES, LANES), 0) == first // LANES
    line_sum = jnp.sum(jnp.where(pick_row, total, 0.0), axis=0, keepdims=True)
    shift = lax.rem(LANES - lax.rem(first, LANES), LANES)
    line_sum = pltpu.roll(jnp.broadcast_to(line_sum, (8, LANES)), shift, 1)
    R.ggain[...] = line_sum[0:1, 0:S]

    own_rows = pl.ds(times(z, S), S)

    def line_total(part, lanes):
        got = R.pb[own_rows, lanes].astype(F32)
        slots = part_sum(part, lanes)[1]
        arrived(slots(slice(0, nz - 1)), R.p_sem.at[1 + part])
        for k in range(1, nz):
            got = got + slots(line(k))[...].astype(F32)
        return got

    for i, (dst, lanes) in enumerate(((R.go, PO), (R.gv, PV))):
        dst[...] = R.pb[own_rows, lanes].astype(F32)
        run_end(dst, grad_sum(i, lanes)[1], R.pn_sem.at[i])
    got = line_total(1, PS)

    def pick(width, source):
        a, b = iota((width, LANES), 1), iota((width, LANES), 0)
        return jnp.where(a == source(b), 1.0, 0.0).astype(F32)

    def picked(left, right):
        return lax.dot_general(
            left,
            right,
            (((1,), (1,)), ((), ())),
            preferred_element_type=F32,
            precision=lax.Precision.HIGHEST,
        )

    def router_lane(b):
        at = jnp.zeros_like(b)
        for o in range(nz):
            at = jnp.where(b >= o * own_e, 2 * GATE + o * pad_e + b - o * own_e, at)
        return at

    R.gvg[...] = picked(pick(GATE, lambda b: b), got)
    R.gog[...] = picked(pick(GATE, lambda b: b + GATE), got)
    R.gr[...] = picked(got, pick(experts, router_lane))
    got = line_total(0, PQ)
    R.gq[...] = got[:, 0:HD]
    R.gk[...] = got[:, HD : 2 * HD]

    for i, (buf, dst) in enumerate(((R.wdn_b, R.gdn), (R.wup_b, R.gup))):
        arrived(R.eg_r.at[0:2, i], R.eg_s.at[3 + i])
        rows = rows_of(p)
        for x in range(local):
            got = buf[rows, pl.ds(times(c * local + x, DH), DH)].astype(F32)
            for slot in (0, 2):
                got = got + R.eg_r[slot, i, :, x * DH : (x + 1) * DH].astype(F32)
            dst[x] = got

    gather_end(R.cotb, R.cot_ss)
    gather_end(R.hidb, R.hid_ss)
    for buf, lanes, sem in (
        (R.ra, RA, R.ra_s),
        (R.rb, RV, R.rv_s),
        (R.rb, RQ, R.rq_s),
        (R.rb, RK, R.rk_s),
    ):
        rows_sent(buf, lanes, sem)
    sent(R.maskb.at[0 : nz - 1], R.tiny_s.at[0])
    sent(R.glog_r.at[0 : nz - 1], R.tiny_s.at[1])
    sent(R.gz.at[0 : nz - 1], R.tiny_s.at[3])
    sent(R.gh_r.at[0 : nz - 1], R.gh_sem.at[0])
    sent(R.out_r.at[0 : nz - 1], R.out_sem.at[nz + 1])
    sent(R.pair_r, R.pair_s.at[0])
    sent(R.eg_r, R.eg_s.at[0])
    sent(R.pr.at[0 : nz - 1], R.p_sem.at[0])
    for i in range(2):
        sent(R.pn.at[i, 0 : nz - 1], R.pn_sem.at[i, nz + 1])


def settle_kernel(*refs):
    n = len(refs) // 2
    copies = [pltpu.make_async_copy(refs[i], refs[n + i], refs[-1].at[i]) for i in range(n)]
    for cp in copies:
        cp.start()
    for cp in copies:
        cp.wait()


def fused_layer(nd, nz, *args):
    (tokens, cotangent, seq_lengths, routes, head_experts, norm_gain) = args[:6]
    (w_query, w_key, w_value, w_output, w_value_gate, w_output_gate, w_router) = args[6:13]
    w_up, w_down = args[13:]
    C = tokens.shape[0]
    local = w_up.shape[0]
    experts = w_router.shape[1]
    own_e = 2 * local
    pad_e = -(-own_e // 16) * 16
    EF, HF, HD = own_e * DH, local * DH, H * DH
    EV = EA * HD
    S = D // (nd * nz * 2)
    SL = S * nz
    PW = 2 * EV + 2 * HD + LANES
    s = Scratch()
    s.vmem("wqk_b", (D, 2 * HD), BF16)
    s.vmem("wv_b", (D, EV), BF16)
    s.vmem("wo_b", (D, EV), BF16)
    s.vmem("wup_b", (D, EF), BF16)
    s.vmem("wdn_b", (D, EF), BF16)
    s.vmem("wg_b", (D, LANES), BF16)
    s.vmem("wrl_b", (D, LANES), BF16)
    s.vmem("cotb", (nz * C, D), BF16)
    s.vmem("hidb", (nz * C, D), BF16)
    s.vmem("mask_s", (nz, pad_e, C), BF16)
    s.vmem("maskb", (nz, pad_e, C), BF16)
    s.vmem("std_b", (C, D), F32)
    s.vmem("normed_b", (C, D), BF16)
    s.vmem("q_b", (C, HD), BF16)
    s.vmem("k_b", (C, HD), BF16)
    s.vmem("v_b", (C, HD), BF16)
    s.vmem("gate_b", (C, LANES), F32)
    s.vmem("val_b", (C, EV), F32)
    s.vmem("prob_b", (H, C, C), F32)
    s.vmem("att_b", (C, HD), F32)
    s.vmem("mix_b", (C, EV), BF16)
    s.vmem("hid_f", (C, D), F32)
    s.vmem("lt", (D, 4 * LANES), BF16)
    s.vmem("ltr", (2 * nd, SL, 4 * LANES), BF16)
    s.vmem("ra", (2 * nd * C, HD + LANES), BF16)
    s.vmem("rb", (2 * nd * C, 3 * HD + LANES), BF16)
    s.vmem("gact", (nz * C, EF), BF16)
    s.vmem("gra", (nz * C, EF), BF16)
    for name in ("gh_s", "gh_r", "out_s"):
        s.vmem(name, (nz, C, D), BF16)
    s.vmem("out_r", (nz + 1, C, D), BF16)
    s.vmem("gh_x", (2, C, D), BF16)
    for name in ("glog_s", "glog_r"):
        s.vmem(name, (nz, pad_e, C), BF16)
    s.vmem("dg", (D // nd, EF), BF16)
    s.vmem("pair_r", (2, nd, D // nd, HF), BF16)
    s.vmem("eg_r", (nd - 1, 2, D // nd, HF), BF16)
    s.vmem("ghid_f", (C, D), F32)
    s.vmem("ghid_b", (C, D), BF16)
    s.vmem("gatt_b", (C, HD), BF16)
    s.vmem("gval_f", (C, HD), F32)
    s.vmem("small_b", (C, LANES), BF16)
    s.vmem("pb", (SL, PW), BF16)
    s.vmem("pr", (nz, S, PW - 2 * EV), BF16)
    s.vmem("pn", (2, nz + 1, S, EV), BF16)
    s.vmem("gp", (2 * nd, D // LANES, LANES), F32)
    s.vmem("gz_s", (D // LANES, LANES), F32)
    s.vmem("gz", (nz, D // LANES, LANES), F32)
    s.sems("ld", 5)
    for name in ("cot_ss", "hid_ss"):
        s.sems(name, nz + 1)
    for name in ("cot_rs", "hid_rs", "tiny_s", "tiny_r", "lt_s", "gh_sem", "pair_s"):
        s.sems(name, 4)
    for name in ("ra_s", "rv_s", "rq_s", "rk_s"):
        s.sems(name, 6)
    s.sems("w_s", 2)
    s.sems("eg_s", 5)
    s.sems("p_sem", 3)
    s.sems("out_sem", nz + 2)
    s.sems("pn_sem", 2, nz + 2)

    def out(*shape, dtype=F32):
        return jax.ShapeDtypeStruct(shape, dtype)

    hbm = pl.BlockSpec(memory_space=pl.ANY)
    vmem = pl.BlockSpec(memory_space=pltpu.VMEM)
    names = in_hbm(SMALL) + WEIGHTS + OUTPUTS
    results = (
        out(C, D, dtype=BF16),
        out(C, D),
        out(1, S),
        out(S, HD),
        out(S, HD),
        out(S, EV),
        out(S, EV),
        out(EA * H, S),
        out(EA * H, S),
        out(S, experts),
        out(local, D // nd, DH),
        out(local, D // nd, DH),
    )
    s.vmem("tokens", (C, D), BF16)
    s.vmem("cot", (C, D), BF16)
    s.add("lens", pltpu.SMEM((1, 2), jnp.int32))
    s.vmem("rt", (TOPK, C), jnp.int32)
    s.vmem("het", (2 * H, C), jnp.int32)
    s.vmem("gain", (1, D), F32)
    s.vmem("wvg", (EA * H, D), BF16)
    s.vmem("wog", (EA * H, D), BF16)
    s.vmem("wr", (experts, D), BF16)
    s.sems("ld_in", len(SMALL))
    outs = pl.pallas_call(
        functools.partial(layer_kernel, names + tuple(s.names), nd, nz, local),
        out_shape=[pltpu.VMEM(x.shape, x.dtype) for x in results],
        in_specs=[hbm] * 15,
        out_specs=[vmem] * len(OUTPUTS),
        scratch_shapes=s.shapes,
        compiler_params=pltpu.CompilerParams(
            collective_id=0, has_side_effects=True, vmem_limit_bytes=VMEM_LIMIT
        ),
    )(
        tokens,
        cotangent,
        seq_lengths,
        routes.T,
        head_experts.reshape(C, 2 * H).T,
        norm_gain.reshape(1, D),
        w_value_gate.T,
        w_output_gate.T,
        w_router.T,
        w_query,
        w_key,
        w_value,
        w_output,
        w_up,
        w_down,
    )
    outs = list(
        pl.pallas_call(
            settle_kernel,
            out_shape=results,
            in_specs=[vmem] * len(outs),
            out_specs=[hbm] * len(outs),
            scratch_shapes=[pltpu.SemaphoreType.DMA((len(outs),))],
        )(*[pltpu.with_memory_space_constraint(x, pltpu.VMEM) for x in outs])
    )
    outs[2] = outs[2].reshape(S)
    for i in (7, 8):
        outs[i] = outs[i].T
    return tuple(outs)


VMEM_LIMIT = 58 * 1024 * 1024


def fits(nd, nz, count, experts):
    own_e = experts // nz
    pad_e = -(-own_e // 16) * 16
    return (
        count == LANES
        and nz == 4
        and nd == 4
        and own_e % 4 == 0
        and D % (nd * nz * 2 * 16) == 0
        and LANES % (D // (nd * nz * 2)) == 0
        and 2 * EA * H + nz * pad_e <= LANES
    )


def per_device(nd, ne, *args):
    count, experts = args[0].shape[0], args[12].shape[1]
    if ne % 2 == 0 and fits(nd, ne // 2, count, experts):
        return fused_layer(nd, ne // 2, *args)
    return routed_layer(*args)


def solution(mesh):
    return jax.shard_map(
        functools.partial(per_device, mesh.shape["dp"], mesh.shape["expert"]),
        mesh=mesh,
        in_specs=(
            P(("dp", "expert"), None),
            P(("dp", "expert"), None),
            P(("dp", "expert"), None),
            P(("dp", "expert"), None),
            P(("dp", "expert"), None, None),
            P(),
            P(),
            P(),
            P(),
            P(),
            P(),
            P(),
            P(),
            P("expert", None, None),
            P("expert", None, None),
        ),
        out_specs=(
            P(("dp", "expert"), None),
            P(("dp", "expert"), None),
            P(("dp", "expert")),
            P(("dp", "expert"), None),
            P(("dp", "expert"), None),
            P(("dp", "expert"), None),
            P(("dp", "expert"), None),
            P(("dp", "expert"), None),
            P(("dp", "expert"), None),
            P(("dp", "expert"), None),
            P("expert", "dp", None),
            P("expert", "dp", None),
        ),
        check_vma=False,
    )
```

```python
import functools
import math

import jax
import jax.numpy as jnp
from jax import lax
from jax.experimental import pallas as pl
from jax.experimental.pallas import tpu as pltpu
from jax.sharding import PartitionSpec as P

D = 1024
H = 4
DH = 128
EA = 5
TOPK = 16


norm_eps = 1e-05
rope_base = 10000.0
masked_score = -1e30


def sequence_layout(lengths, count):
    bounds = jnp.cumsum(lengths)
    starts = bounds - lengths
    places = jnp.arange(count, dtype=jnp.int32)
    seq_ids = jnp.sum((places[:, None] >= bounds[None, :]).astype(jnp.int32), axis=1)
    live = places < bounds[-1]
    slot_ids = jnp.arange(lengths.shape[0], dtype=jnp.int32)
    first = jnp.sum(jnp.where(seq_ids[:, None] == slot_ids[None, :], starts[None, :], 0), axis=1)
    positions = jnp.where(live, places - first, 0)
    return (seq_ids, live, positions)


def rope_tables(positions, width):
    half = width // 2
    freq = rope_base ** (-(jnp.arange(half, dtype=jnp.float32) * 2.0 / width))
    angles = positions.astype(jnp.float32)[:, None] * freq[None, :]
    return (jnp.cos(angles), jnp.sin(angles))


def rotate(field, cosine, sine):
    half = field.shape[-1] // 2
    first, second = (field[..., :half], field[..., half:])
    cos_h, sin_h = (cosine[:, None, :], sine[:, None, :])
    return jnp.concatenate(
        [first * cos_h - second * sin_h, second * cos_h + first * sin_h], axis=-1
    )


def rotate_back(field, cosine, sine):
    half = field.shape[-1] // 2
    first, second = (field[..., :half], field[..., half:])
    cos_h, sin_h = (cosine[:, None, :], sine[:, None, :])
    return jnp.concatenate(
        [first * cos_h + second * sin_h, second * cos_h - first * sin_h], axis=-1
    )


def slot_tables(routes, experts, most):
    count = routes.shape[0] * routes.shape[1]
    flat = routes.reshape(count)
    order = jnp.argsort(flat, stable=True)
    ordered = flat[order]
    firsts = jnp.searchsorted(ordered, jnp.arange(experts, dtype=jnp.int32))
    ranks = jnp.arange(count, dtype=jnp.int32) - firsts[ordered]
    sorted_slots = ordered * most + ranks
    slot_of_row = jnp.zeros((count,), jnp.int32).at[order].set(sorted_slots)
    row_of_slot = jnp.full((experts * most,), count, jnp.int32).at[sorted_slots].set(order)
    return (slot_of_row, row_of_slot)


def routed_layer(
    tokens,
    cotangent,
    seq_lengths,
    routes,
    head_experts,
    norm_gain,
    w_query,
    w_key,
    w_value,
    w_output,
    w_value_gate,
    w_output_gate,
    w_router,
    w_up,
    w_down,
):
    f32 = jnp.float32
    bf16 = jnp.bfloat16
    count = tokens.shape[0]
    experts = w_router.shape[1]
    local_experts = w_up.shape[0]
    owners = lax.axis_size("expert")
    most = 3 * count * TOPK // (2 * experts)
    routed = count * TOPK
    block = min(512, count)
    block_starts = jnp.arange(count // block, dtype=jnp.int32) * block
    scale = DH ** (-0.5)
    contract_last = (((1,), (1,)), ((), ()))
    contract_first = (((0,), (0,)), ((), ()))
    seq_ids, live, positions = sequence_layout(seq_lengths[0], count)
    cosine, sine = rope_tables(positions, DH)
    inputs = tokens.astype(f32)
    centred = inputs - jnp.mean(inputs, axis=-1, keepdims=True)
    inverse = lax.rsqrt(jnp.mean(centred * centred, axis=-1, keepdims=True) + norm_eps)
    standard = centred * inverse
    normed = (standard * norm_gain).astype(bf16)
    query_proj = jnp.dot(normed, w_query, preferred_element_type=f32).reshape(count, H, DH)
    key_proj = jnp.dot(normed, w_key, preferred_element_type=f32).reshape(count, H, DH)
    query_rot = (rotate(query_proj, cosine, sine) * scale).astype(bf16)
    key_rot = rotate(key_proj, cosine, sine).astype(bf16)
    chosen = jnp.any(
        head_experts[:, None, :, :] == jnp.arange(EA, dtype=jnp.int32)[None, :, None, None], axis=-1
    )
    value_gates = jnp.where(
        chosen,
        jax.nn.sigmoid(
            jnp.dot(tokens, w_value_gate, preferred_element_type=f32).reshape(count, EA, H)
        ),
        0.0,
    )
    output_gates = jnp.where(
        chosen,
        jax.nn.sigmoid(
            jnp.dot(tokens, w_output_gate, preferred_element_type=f32).reshape(count, EA, H)
        ),
        0.0,
    )
    value_all = jnp.dot(tokens, w_value, preferred_element_type=f32).reshape(count, EA, H, DH)
    values = jnp.sum(value_gates[..., None] * value_all, axis=1).astype(bf16)

    def allowed_at(start):
        queries = start + jnp.arange(block, dtype=jnp.int32)
        keys = jnp.arange(count, dtype=jnp.int32)
        same = (
            (seq_ids[:, None] == seq_ids[None, :])
            & (keys[None, :] <= queries[:, None])
            & live[None, :]
        )
        return same | (keys[None, :] == queries[:, None])

    def scores_at(start):
        scores = jnp.einsum("qhd,khd->hqk", query_rot, key_rot, preferred_element_type=f32)
        return (query_rot, jnp.where(allowed_at(start)[None], scores, masked_score))

    def attend(start):
        query_block, scores = scores_at(start)
        highest = jnp.max(scores, axis=-1, keepdims=True)
        shifted = jnp.exp(scores - highest)
        totals = jnp.sum(shifted, axis=-1, keepdims=True)
        shares = (shifted / totals).astype(bf16)
        result = jnp.einsum("hqk,khd->qhd", shares, values, preferred_element_type=f32)
        return (result, (highest + jnp.log(totals))[..., 0])

    attended, log_totals = lax.map(attend, block_starts)
    attended = attended.reshape(count, H, DH)
    log_totals = jnp.transpose(log_totals, (1, 0, 2)).reshape(H, count)
    heads_mixed = (
        (output_gates[..., None] * attended[:, None]).astype(bf16).reshape(count, EA * H * DH)
    )
    hidden = inputs + lax.dot_general(
        heads_mixed, w_output, contract_last, preferred_element_type=f32
    )
    hidden_low = hidden.astype(bf16)
    logits = jnp.dot(hidden_low, w_router, preferred_element_type=f32)
    gates = jax.nn.sigmoid(jnp.take_along_axis(logits, routes, axis=1))
    slot_of_row, row_of_slot = slot_tables(routes, experts, most)
    valid = row_of_slot < routed
    safe_row = jnp.minimum(row_of_slot, routed - 1)
    source = safe_row // TOPK
    outgoing = jnp.where(valid[:, None], hidden_low[source], jnp.zeros((), bf16)).reshape(
        owners, local_experts, most, D
    )

    def expert_apply(items):
        raised = jnp.einsum("nemd,edf->nemf", items, w_up, preferred_element_type=f32)
        active = jax.nn.silu(raised).astype(bf16)
        lowered = jnp.einsum("nemf,edf->nemd", active, w_down, preferred_element_type=f32).astype(
            bf16
        )
        return (lowered, raised)

    lowered, raised = expert_apply(
        lax.all_to_all(outgoing, "expert", split_axis=0, concat_axis=0, tiled=True)
    )
    returned = lax.all_to_all(lowered, "expert", split_axis=0, concat_axis=0, tiled=True).reshape(
        experts * most, D
    )
    expert_rows = returned[slot_of_row].reshape(count, TOPK, D)
    output = hidden + jnp.sum(gates[..., None] * expert_rows, axis=1)
    mixed = output.astype(bf16)
    grad_out = cotangent.astype(f32) * live[:, None].astype(f32)
    grad_gates = jnp.sum(grad_out[:, None, :] * expert_rows, axis=2)
    gate_flat = gates.reshape(routed)
    grad_outgoing = (
        jnp.where(valid[:, None], gate_flat[safe_row][:, None] * grad_out[source], 0.0)
        .astype(bf16)
        .reshape(owners, local_experts, most, D)
    )
    grad_lowered = lax.all_to_all(grad_outgoing, "expert", split_axis=0, concat_axis=0, tiled=True)
    items = lax.all_to_all(outgoing, "expert", split_axis=0, concat_axis=0, tiled=True)
    raised = expert_apply(items)[1]
    grad_active = jnp.einsum("nemd,edf->nemf", grad_lowered, w_down, preferred_element_type=f32)
    sigmoid_raised = jax.nn.sigmoid(raised)
    grad_raised = (grad_active * sigmoid_raised * (1.0 + raised * (1.0 - sigmoid_raised))).astype(
        bf16
    )
    grad_items = jnp.einsum("nemf,edf->nemd", grad_raised, w_up, preferred_element_type=f32).astype(
        bf16
    )
    active = jax.nn.silu(raised).astype(bf16)
    grad_items, grad_raised, active = (grad_items, grad_raised, active)
    grad_items, grad_raised, active, grad_arrived, arrived = (
        grad_items,
        grad_raised,
        active,
        grad_lowered,
        items,
    )
    grad_up_local = jnp.einsum("nemd,nemf->edf", arrived, grad_raised, preferred_element_type=f32)
    grad_down_local = jnp.einsum("nemd,nemf->edf", grad_arrived, active, preferred_element_type=f32)
    grad_up, grad_down = (
        lax.psum_scatter(
            grad_up_local.astype(jnp.bfloat16), "dp", scatter_dimension=1, tiled=True
        ).astype(jnp.float32),
        lax.psum_scatter(
            grad_down_local.astype(jnp.bfloat16), "dp", scatter_dimension=1, tiled=True
        ).astype(jnp.float32),
    )
    grad_back = lax.all_to_all(
        grad_items, "expert", split_axis=0, concat_axis=0, tiled=True
    ).reshape(experts * most, D)
    grad_hidden = grad_out + jnp.sum(
        grad_back[slot_of_row].reshape(count, TOPK, D), axis=1, dtype=f32
    )
    grad_picked = grad_gates * gates * (1.0 - gates)
    expert_ids = jnp.arange(experts, dtype=jnp.int32)
    grad_logits = jnp.sum(
        jnp.where(routes[:, :, None] == expert_ids[None, None, :], grad_picked[..., None], 0.0),
        axis=1,
    ).astype(bf16)
    grad_router = lax.dot_general(
        hidden_low, grad_logits, contract_first, preferred_element_type=f32
    )
    grad_hidden = grad_hidden + lax.dot_general(
        grad_logits, w_router, contract_last, preferred_element_type=f32
    )
    grad_hidden_low = grad_hidden.astype(bf16)
    grad_output = lax.dot_general(
        grad_hidden_low, heads_mixed, contract_first, preferred_element_type=f32
    )
    grad_mixed = jnp.dot(grad_hidden_low, w_output, preferred_element_type=f32).reshape(
        count, EA, H, DH
    )
    grad_attended = jnp.sum(output_gates[..., None] * grad_mixed, axis=1).astype(bf16)
    grad_out_gates = jnp.sum(grad_mixed * attended[:, None], axis=-1)
    grad_out_logits = (
        jnp.where(chosen, grad_out_gates * output_gates * (1.0 - output_gates), 0.0)
        .astype(bf16)
        .reshape(count, EA * H)
    )

    def attend_back(carry, start):
        grad_keys, grad_vals = carry
        query_block, scores = scores_at(start)
        shares = jnp.exp(scores - log_totals[..., None])
        grad_shares = jnp.einsum("qhd,khd->hqk", grad_attended, values, preferred_element_type=f32)
        centre = jnp.sum(shares * grad_shares, axis=-1, keepdims=True)
        grad_scores = (shares * (grad_shares - centre)).astype(bf16)
        grad_query_block = jnp.einsum(
            "hqk,khd->qhd", grad_scores, key_rot, preferred_element_type=f32
        )
        grad_keys = grad_keys + jnp.einsum(
            "hqk,qhd->khd", grad_scores, query_block, preferred_element_type=f32
        )
        grad_vals = grad_vals + jnp.einsum(
            "hqk,qhd->khd", shares.astype(bf16), grad_attended, preferred_element_type=f32
        )
        return ((grad_keys, grad_vals), grad_query_block)

    zero_heads = jnp.zeros((count, H, DH), f32)
    (grad_keys, grad_vals), grad_queries = lax.scan(
        attend_back, (zero_heads, zero_heads), block_starts
    )
    grad_queries = grad_queries.reshape(count, H, DH)
    grad_query_proj = (
        rotate_back(grad_queries * scale, cosine, sine).astype(bf16).reshape(count, H * DH)
    )
    grad_key_proj = rotate_back(grad_keys, cosine, sine).astype(bf16).reshape(count, H * DH)
    grad_value_all = (
        (value_gates[..., None] * grad_vals[:, None]).astype(bf16).reshape(count, EA * H * DH)
    )
    grad_value_gates = jnp.sum(grad_vals[:, None] * value_all, axis=-1)
    grad_value_logits = (
        jnp.where(chosen, grad_value_gates * value_gates * (1.0 - value_gates), 0.0)
        .astype(bf16)
        .reshape(count, EA * H)
    )
    grad_query = lax.dot_general(
        normed, grad_query_proj, contract_first, preferred_element_type=f32
    )
    grad_key = lax.dot_general(normed, grad_key_proj, contract_first, preferred_element_type=f32)
    grad_value = lax.dot_general(tokens, grad_value_all, contract_first, preferred_element_type=f32)
    grad_value_gate = lax.dot_general(
        tokens, grad_value_logits, contract_first, preferred_element_type=f32
    )
    grad_output_gate = lax.dot_general(
        tokens, grad_out_logits, contract_first, preferred_element_type=f32
    )
    grad_normed = lax.dot_general(
        grad_query_proj, w_query, contract_last, preferred_element_type=f32
    ) + lax.dot_general(grad_key_proj, w_key, contract_last, preferred_element_type=f32)
    grad_gain = jnp.sum(grad_normed * standard, axis=0)
    grad_standard = grad_normed * norm_gain
    grad_tokens = grad_hidden + inverse * (
        grad_standard
        - jnp.mean(grad_standard, axis=-1, keepdims=True)
        - standard * jnp.mean(grad_standard * standard, axis=-1, keepdims=True)
    )
    grad_tokens = (
        grad_tokens
        + lax.dot_general(grad_value_all, w_value, contract_last, preferred_element_type=f32)
        + lax.dot_general(
            grad_value_logits, w_value_gate, contract_last, preferred_element_type=f32
        )
        + lax.dot_general(grad_out_logits, w_output_gate, contract_last, preferred_element_type=f32)
    )
    summed = (
        lax.psum_scatter(grad_gain, ("dp", "expert"), scatter_dimension=0, tiled=True),
        lax.psum_scatter(grad_query, ("dp", "expert"), scatter_dimension=0, tiled=True),
        lax.psum_scatter(grad_key, ("dp", "expert"), scatter_dimension=0, tiled=True),
        lax.psum_scatter(grad_value, ("dp", "expert"), scatter_dimension=0, tiled=True),
        lax.psum_scatter(grad_output, ("dp", "expert"), scatter_dimension=0, tiled=True),
        lax.psum_scatter(grad_value_gate, ("dp", "expert"), scatter_dimension=0, tiled=True),
        lax.psum_scatter(grad_output_gate, ("dp", "expert"), scatter_dimension=0, tiled=True),
        lax.psum_scatter(grad_router, ("dp", "expert"), scatter_dimension=0, tiled=True),
    )
    return (
        mixed,
        grad_tokens,
        summed[0],
        summed[1],
        summed[2],
        summed[3],
        summed[4],
        summed[5],
        summed[6],
        summed[7],
        grad_up,
        grad_down,
    )


F32 = jnp.float32
BF16 = jnp.bfloat16
MESH = pl.DeviceIdType.MESH
LANES = 128


def mm(a, b):
    return lax.dot_general(a, b, (((1,), (0,)), ((), ())), preferred_element_type=F32)


def mm_t(a, b):
    return lax.dot_general(a, b, (((1,), (1,)), ((), ())), preferred_element_type=F32)


def tmm(a, b):
    return lax.dot_general(a, b, (((0,), (0,)), ((), ())), preferred_element_type=F32)


def iota(shape, axis):
    return lax.broadcasted_iota(jnp.int32, shape, axis)


def column(x, j, width=LANES):
    return jnp.broadcast_to(x[:, j : j + 1], (x.shape[0], width))


def sigmoid(x):
    return 1.0 / (1.0 + jnp.exp(-x))


class Scratch:
    def __init__(self):
        self.names, self.shapes = [], []

    def add(self, name, shape):
        self.names.append(name)
        self.shapes.append(shape)

    def vmem(self, name, shape, dtype):
        self.add(name, pltpu.VMEM(shape, dtype))

    def sems(self, name, *shape):
        self.add(name, pltpu.SemaphoreType.DMA(shape))


SMALL = ("tokens", "cot", "lens", "rt", "het", "gain", "wvg", "wog", "wr")
WEIGHTS = ("wq", "wk", "wv", "wo", "wu", "wd")
OUTPUTS = ("mixed", "gtok", "ggain", "gq", "gk", "gv", "go", "gvg", "gog", "gr", "gup", "gdn")


def in_hbm(names):
    return tuple(name + "_h" for name in names)


def layer_kernel(names, nd, nz, local, *refs):
    r = dict(zip(names, refs))
    R = type("R", (), r)
    C = R.tokens.shape[0]
    own_e = 2 * local
    pad_e = R.maskb.shape[1]
    EF = own_e * DH
    HF = local * DH
    HD = H * DH
    EV = EA * HD
    S = D // (nd * nz * 2)
    SL = S * nz
    GATE = EA * H
    p = lax.axis_index("dp")
    e = lax.axis_index("expert")
    z = e // 2
    c = e % 2
    sib = 1 - c

    def dev(p_, z_, c_):
        return (p_, z_ * 2 + c_)

    def times(i, n):
        return pl.multiple_of(i * n, n)

    def remote(src, dst, ss, rs, to):
        return pltpu.make_async_remote_copy(
            src_ref=src, dst_ref=dst, send_sem=ss, recv_sem=rs, device_id=to, device_id_type=MESH
        )

    def arrived(dst, rs):
        remote(dst, dst, rs, rs, dev(p, z, sib)).wait_recv()

    def sent(src, ss):
        remote(src, src, ss, ss, dev(p, z, sib)).wait_send()

    beside = p + 1 - 2 * lax.rem(p, 2)
    across = lax.rem(p + 2, nd)
    diagonal = lax.rem(beside + 2, nd)

    def core_cols(cc):
        return pl.ds(times(cc, HF), HF)

    def plane(k):
        return (p, beside, across, diagonal)[k]

    def line(k):
        return lax.rem(z + k, nz)

    barrier = pltpu.get_barrier_semaphore()
    partners = [dev(p, z, sib)]
    partners += [dev(p, line(k), c) for k in range(1, nz)]
    for k in range(1, nd):
        partners += [dev(plane(k), z, c), dev(plane(k), z, sib)]
    for to in partners:
        pl.semaphore_signal(barrier, inc=1, device_id=to, device_id_type=MESH)

    loads = {}

    def load(name, src, dst, sem):
        cp = pltpu.make_async_copy(src, dst, sem)
        cp.start()
        loads[name] = cp

    def loaded(*names):
        for name in names:
            loads.pop(name).wait()

    def landed(dst, sem):
        pltpu.make_async_copy(dst, dst, sem).wait()

    for i, name in enumerate(("cot", "lens", "rt", "tokens", "gain", "het", "wvg", "wog", "wr")):
        load(name, r[name + "_h"], r[name], R.ld_in.at[i])
    loaded("lens")
    l0 = R.lens[0, 0]
    b1 = l0 + R.lens[0, 1]
    row = iota((C, LANES), 0)
    lane = iota((C, LANES), 1)
    seq_r = (row >= l0).astype(jnp.int32) + (row >= b1).astype(jnp.int32)
    seq_c = (lane >= l0).astype(jnp.int32) + (lane >= b1).astype(jnp.int32)
    live = row < b1
    allowed = ((seq_r == seq_c) & (lane <= row) & (lane < b1)) | (row == lane)
    live_f = jnp.where(live, 1.0, 0.0).astype(F32)
    start = jnp.where(seq_r == 0, 0, l0)
    position = jnp.where(live, row - start, 0).astype(F32)

    loaded("cot")
    for b in range(D // LANES):
        cols = slice(b * LANES, (b + 1) * LANES)
        R.cotb[pl.ds(times(z, C), C), cols] = (R.cot[:, cols].astype(F32) * live_f).astype(BF16)
    load("qk", R.wq, R.wqk_b.at[:, 0:HD], R.ld.at[0])
    load("qk", R.wk, R.wqk_b.at[:, HD : 2 * HD], R.ld.at[0])
    load("v", R.wv, R.wv_b, R.ld.at[1])
    for i in range(local):
        col = times(c * local + i, DH)
        load("up", R.wu.at[i], R.wup_b.at[:, pl.ds(col, DH)], R.ld.at[2])
        load("dn", R.wd.at[i], R.wdn_b.at[:, pl.ds(col, DH)], R.ld.at[3])
    load("o", R.wo, R.wo_b, R.ld.at[4])
    loaded("rt")
    ids = iota((pad_e, C), 0)
    for zz in range(nz):
        named = jnp.zeros((pad_e, C), F32)
        for k in range(TOPK):
            hit = jnp.broadcast_to(R.rt[k : k + 1, :], (pad_e, C)) == ids + zz * own_e
            named = jnp.where(hit & (ids < own_e), 1.0, named)
        R.mask_s[zz] = named.astype(BF16)
    R.maskb[z] = R.mask_s[z]

    pl.semaphore_wait(barrier, len(partners))

    def block(buf, o):
        return buf.at[pl.ds(times(o, C), C), :]

    def pass_on(buf, ss, rs, o, right, left):
        @pl.when(right)
        def _():
            remote(block(buf, o), block(buf, o), ss.at[o], rs.at[o], dev(p, z + 1, c)).start()

        @pl.when(left)
        def _():
            way = jnp.where(o == z, nz, o)
            remote(block(buf, o), block(buf, o), ss.at[way], rs.at[o], dev(p, z - 1, c)).start()

    def passed(buf, ss, o, right, left):
        @pl.when(right)
        def _():
            sent(block(buf, o), ss.at[o])

        @pl.when(left)
        def _():
            sent(block(buf, o), ss.at[jnp.where(o == z, nz, o)])

    def gather_own(buf, ss, rs):
        pass_on(buf, ss, rs, z, z < nz - 1, z > 0)

    def gather_on(buf, ss, rs, o):
        arrived(block(buf, o), rs.at[o])
        pass_on(buf, ss, rs, o, (o < z) & (z < nz - 1), (o > z) & (z > 0))

    def gather_step(buf, ss, rs, k):
        @pl.when(z >= k)
        def _():
            gather_on(buf, ss, rs, z - k)

        @pl.when(z + k < nz)
        def _():
            gather_on(buf, ss, rs, z + k)

    def gather_end(buf, ss):
        passed(buf, ss, z, z < nz - 1, z > 0)
        for k in range(1, nz):

            @pl.when(z >= k)
            def _():
                passed(buf, ss, z - k, z < nz - 1, False)

            @pl.when(z + k < nz)
            def _():
                passed(buf, ss, z + k, False, z > 0)

    gather_own(R.cotb, R.cot_ss, R.cot_rs)
    for k in range(1, nz):
        o = line(k)
        remote(R.mask_s.at[o], R.maskb.at[z], R.tiny_s.at[0], R.tiny_r.at[0], dev(p, o, c)).start()

    loaded("tokens", "gain", "het", "wvg", "wog", "wr")

    s_row, s_col = iota((GATE, LANES), 0), iota((GATE, LANES), 1)
    to_v = jnp.where(s_row == s_col, 1.0, 0.0).astype(BF16)
    to_o = jnp.where(s_row + GATE == s_col, 1.0, 0.0).astype(BF16)
    R.wg_b[...] = (tmm(R.wvg[...], to_v) + tmm(R.wog[...], to_o)).astype(BF16)
    experts = R.wr.shape[0]
    r_row, r_col = iota((experts, LANES), 0), iota((experts, LANES), 1)
    to_r = jnp.where((r_row == r_col + z * own_e) & (r_col < own_e), 1.0, 0.0).astype(BF16)
    R.wrl_b[...] = tmm(R.wr[...], to_r).astype(BF16)

    half = lax.rem(lane, DH // 2).astype(F32)
    angle = position * jnp.exp(half * (-2.0 / DH * math.log(rope_base)))
    cosine = jnp.cos(angle)
    sine = jnp.where(lane < DH // 2, -jnp.sin(angle), jnp.sin(angle))

    def rot(v):
        return v * cosine + pltpu.roll(v, DH // 2, 1) * sine

    def rot_back(v):
        return v * cosine - pltpu.roll(v, DH // 2, 1) * sine

    inputs = R.tokens[...].astype(F32)
    centred = inputs - jnp.mean(inputs, axis=-1, keepdims=True)
    inverse = lax.rsqrt(jnp.mean(centred * centred, axis=-1, keepdims=True) + norm_eps)
    standard = centred * inverse
    R.std_b[...] = standard
    R.normed_b[...] = (standard * R.gain[...]).astype(BF16)

    landed(R.wqk_b, R.ld.at[0])
    scale = DH ** (-0.5)
    qk = mm(R.normed_b[...], R.wqk_b[:, 0:HD])
    for h in range(H):
        hs = slice(h * DH, (h + 1) * DH)
        R.q_b[:, hs] = (rot(qk[:, hs]) * scale).astype(BF16)
    qk = mm(R.normed_b[...], R.wqk_b[:, HD : 2 * HD])
    for h in range(H):
        hs = slice(h * DH, (h + 1) * DH)
        R.k_b[:, hs] = rot(qk[:, hs]).astype(BF16)

    hit = []
    for j in range(GATE):
        x, h = divmod(j, H)
        one = (R.het[2 * h : 2 * h + 1, :] == x) | (R.het[2 * h + 1 : 2 * h + 2, :] == x)
        hit.append(jnp.where(one, 1.0, 0.0).astype(F32))
    hit = jnp.concatenate(hit + hit + [jnp.zeros((LANES - 2 * GATE, C), F32)], axis=0)
    R.gate_b[...] = sigmoid(mm(R.tokens[...], R.wg_b[...])) * hit.T

    landed(R.wup_b.at[:, core_cols(c)], R.ld.at[2])
    landed(R.wdn_b.at[:, core_cols(c)], R.ld.at[3])
    for i, buf in enumerate((R.wup_b, R.wdn_b)):
        part = buf.at[:, pl.ds(times(c, HF), HF)]
        cp = remote(part, part, R.w_s.at[0], R.w_s.at[1], dev(p, z, sib))
        cp.start()

    landed(R.wv_b, R.ld.at[1])
    gates = R.gate_b[...]
    total = [None] * H
    for x in range(EA):
        R.val_b[:, x * HD : (x + 1) * HD] = mm(R.tokens[...], R.wv_b[:, x * HD : (x + 1) * HD])
        for h in range(H):
            lo = x * HD + h * DH
            term = column(gates, x * H + h) * R.val_b[:, lo : lo + DH]
            total[h] = term if x == 0 else total[h] + term
    for h in range(H):
        R.v_b[:, h * DH : (h + 1) * DH] = total[h].astype(BF16)

    for h in range(H):
        hs = slice(h * DH, (h + 1) * DH)
        scores = jnp.where(allowed, mm_t(R.q_b[:, hs], R.k_b[:, hs]), masked_score)
        shifted = jnp.exp(scores - jnp.max(scores, axis=-1, keepdims=True))
        shares = shifted / jnp.sum(shifted, axis=-1, keepdims=True)
        R.prob_b[h] = shares
        R.att_b[:, hs] = mm(shares.astype(BF16), R.v_b[:, hs])

    for x in range(EA):
        for h in range(H):
            lo = x * HD + h * DH
            R.mix_b[:, lo : lo + DH] = (
                column(gates, GATE + x * H + h) * R.att_b[:, h * DH : (h + 1) * DH]
            ).astype(BF16)
    landed(R.wo_b, R.ld.at[4])
    half_d = D // 2
    for b in range(2):
        cols = slice(b * half_d, (b + 1) * half_d)
        hidden = R.tokens[:, cols].astype(F32) + mm_t(R.mix_b[...], R.wo_b[cols, :])
        R.hid_f[:, cols] = hidden
        R.hidb[pl.ds(times(z, C), C), cols] = hidden.astype(BF16)
    gather_own(R.hidb, R.hid_ss, R.hid_rs)
    gather_step(R.cotb, R.cot_ss, R.cot_rs, 1)

    def put_turned(x, w):
        for b in range(D // LANES):
            t = x[:, b * LANES : (b + 1) * LANES].astype(F32).T.astype(BF16)
            for q in range(LANES // S):
                i = (b * LANES) // S + q
                pp, zz, cc = i // (2 * nz), (i % (2 * nz)) // 2, i % 2
                at = (pp * 2 + cc) * SL + zz * S
                R.lt[at : at + S, w * LANES : (w + 1) * LANES] = t[q * S : (q + 1) * S, :]

    plane_all = [(k, dc) for k in range(nd) for dc in range(2) if k or dc]

    def side(dc):
        return sib if dc else c

    def send_turned(w0, w1, ss, rs):
        lanes = slice(w0 * LANES, w1 * LANES)
        for k, dc in plane_all:
            to = plane(k)
            slot = 2 * k + dc
            at = times(to * 2 + side(dc), SL)
            cp = remote(
                R.lt.at[pl.ds(at, SL), lanes],
                R.ltr.at[slot, :, lanes],
                ss,
                rs,
                dev(to, z, side(dc)),
            )
            cp.start()
        R.ltr[0, :, lanes] = R.lt[pl.ds(times(p * 2 + c, SL), SL), lanes]

    def turned_here(w0, w1, ss, rs):
        there = R.ltr.at[1 : 2 * nd, :, w0 * LANES : w1 * LANES]
        sent(there, ss)
        arrived(there, rs)

    def rows_at(buf, lanes, slot):
        return buf.at[slot * C : (slot + 1) * C, lanes]

    def send_rows(buf, lanes, sem, ways=(1, 2)):
        for k in ways:
            remote(
                rows_at(buf, lanes, 0),
                rows_at(buf, lanes, 2 * k),
                sem.at[0],
                sem.at[k],
                dev(plane(k), z, c),
            ).start()
        hand_over(buf, lanes, sem, 0)

    def hand_over(buf, lanes, sem, k):
        remote(
            rows_at(buf, lanes, 2 * k),
            rows_at(buf, lanes, 2 * k + 1),
            sem.at[0],
            sem.at[5 if k == 3 else 4],
            dev(p, z, sib),
        ).start()

    def hand_near(buf, lanes, sem, via):
        for k in (via, 3 - via) if via else (1, 2):
            arrived(rows_at(buf, lanes, 2 * k), sem.at[k])
            if k == via:
                remote(
                    rows_at(buf, lanes, 2 * k),
                    rows_at(buf, lanes, 6),
                    sem.at[0],
                    sem.at[3],
                    dev(plane(3 - via), z, c),
                ).start()
            hand_over(buf, lanes, sem, k)

    def hand_far(buf, lanes, sem):
        arrived(rows_at(buf, lanes, 6), sem.at[3])
        hand_over(buf, lanes, sem, 3)

    def near_here(buf, lanes, sem):
        arrived(buf.at[0 : 3 * C, lanes], sem.at[4])

    def far_here(buf, lanes, sem):
        arrived(rows_at(buf, lanes, 7), sem.at[5])

    def rows_sent(buf, lanes, sem):
        sent(buf.at[0 : 7 * C, lanes], sem.at[0])

    put_turned(R.tokens[...], 0)
    put_turned(R.hid_f[...], 1)
    send_turned(0, 2, R.lt_s.at[0], R.lt_s.at[1])
    R.nrm[0:C, :] = R.normed_b[...]
    RN = slice(0, D)
    send_rows(R.nrm, RN, R.nrm_s)
    R.ra[0:C, 0:HD] = R.att_b[...].astype(BF16)
    R.ra[0:C, HD : HD + LANES] = gates.astype(BF16)
    RA = slice(0, HD + LANES)
    send_rows(R.ra, RA, R.ra_s)

    sent(R.wup_b, R.w_s.at[0])
    arrived(R.wup_b, R.w_s.at[1])

    least = jnp.minimum(z, nz - 1 - z)
    inner = least > 0
    left_half = z < nz // 2
    near = jnp.where(inner, jnp.where(left_half, 0, nz - 1), jnp.where(left_half, 1, nz - 2))
    fellow = jnp.where(left_half, nz // 2, nz // 2 - 1)
    far = jnp.where(left_half, nz - 1, 0)

    def origin(k):
        paired = k <= 2 * least
        dist = jnp.where(paired, (k + 1) // 2, k - least)
        left = jnp.where(paired, lax.rem(k, 2) == 1, z > nz - 1 - z)
        return jnp.where(k == 0, z, jnp.where(left, z - dist, z + dist))

    def expert_block(k, carry):
        o = origin(k)
        rows = pl.ds(times(o, C), C)

        @pl.when((k == 1) & inner)
        def _():
            gather_on(R.hidb, R.hid_ss, R.hid_rs, origin(1))

        @pl.when((k > 0) & (k + inner.astype(jnp.int32) < nz))
        def _():
            gather_on(R.hidb, R.hid_ss, R.hid_rs, origin(k + inner.astype(jnp.int32)))

        @pl.when(k == jnp.where(inner, 1, 2))
        def _():
            for far_step in range(2, nz - 1):
                gather_step(R.cotb, R.cot_ss, R.cot_rs, far_step)

        @pl.when(k > 0)
        def _():
            @pl.when((o == z - nz + 1) | (o == z + nz - 1))
            def _():
                arrived(block(R.cotb, o), R.cot_rs.at[o])

        @pl.when(k == 1)
        def _():
            arrived(R.maskb.at[0 : nz - 1], R.tiny_r.at[0])

        hb = R.hidb[rows, :]
        cb = R.cotb[rows, :]
        named = R.maskb[o].astype(F32)
        named = jnp.concatenate([named, jnp.zeros((LANES - pad_e, C), F32)], axis=0).T
        g = sigmoid(mm(hb, R.wrl_b[...])) * named
        glog = jnp.zeros((C, LANES), F32)
        for q in range(2):
            cols = slice(q * HF, (q + 1) * HF)
            raised = mm(hb, R.wup_b[:, cols])
            back = mm(cb, R.wdn_b[:, cols])
            for i in range(local):
                j = q * local + i
                u = raised[:, i * DH : (i + 1) * DH]
                a = back[:, i * DH : (i + 1) * DH]
                gj = column(g, j)
                s = sigmoid(u)
                act = u * s
                lo = j * DH
                R.gact[rows, lo : lo + DH] = (gj * act).astype(BF16)
                R.gra[rows, lo : lo + DH] = (gj * a * (s * (1.0 + u * (1.0 - s)))).astype(BF16)
                gg = jnp.sum(a * act, axis=1, keepdims=True)
                glog = jnp.where(lane == j, jnp.broadcast_to(gg, (C, LANES)), glog)
        glog = glog * g * (1.0 - g)
        low = glog.astype(BF16)
        R.glog_s[o] = glog.T[0:pad_e, :].astype(BF16)
        for b in range(2):
            cols = slice(b * half_d, (b + 1) * half_d)
            gh = mm_t(R.gra[rows, :], R.wup_b[cols, :]) + mm_t(low, R.wrl_b[cols, :])
            R.gh_s[o, :, cols] = gh.astype(BF16)

        @pl.when(k > 0)
        def _():
            remote(
                R.glog_s.at[o], R.glog_r.at[z], R.tiny_s.at[1], R.tiny_r.at[1], dev(p, o, c)
            ).start()

        @pl.when((k > 0) & (least == 0) & (o != fellow))
        def _():
            send_back(o)

        @pl.when((k > 0) & (least == 0) & (o == fellow))
        def _():
            send_by(o, near, 0)

        @pl.when((k > 0) & inner & (o == far))
        def _():
            send_by(o, fellow, 1)

        @pl.when(k == 2)
        def _():
            hand_near(R.ra, RA, R.ra_s, 2)
            hand_near(R.nrm, RN, R.nrm_s, 1)

        @pl.when((k == 1) & (least == 0))
        def _():
            there = pl.ds(times(near, C), C)
            for b in range(2):
                cols = slice(b * half_d, (b + 1) * half_d)
                R.out_s[near, :, cols] = mm_t(R.gact[there, :], R.wdn_b[cols, :]).astype(BF16)
            slot = jnp.where(z == 0, near, nz)
            remote(
                R.out_s.at[near],
                R.out_r.at[slot],
                R.out_sem.at[nz + 1],
                R.out_sem.at[slot],
                dev(p, near, c),
            ).start()

        return carry

    def send_back(o):
        remote(R.gh_s.at[o], R.gh_r.at[z], R.gh_sem.at[0], R.gh_sem.at[1], dev(p, o, c)).start()

    def send_by(o, by, slot):
        remote(
            R.gh_s.at[o], R.gh_x.at[slot], R.gh_sem.at[0], R.gh_sem.at[2 + slot], dev(p, by, c)
        ).start()

    def relay_back(o, slot):
        arrived(R.gh_x.at[slot], R.gh_sem.at[2 + slot])
        R.gh_s[o] = (R.gh_s[o].astype(F32) + R.gh_x[slot].astype(F32)).astype(BF16)
        send_back(o)

    lax.fori_loop(0, nz, expert_block, 0)

    def rows_of(at):
        return pl.ds(times(at, rows_d), rows_d)


    rows_d = D // nd

    def grad_at(i, k, cc):
        if i == 0 and k == 3:
            return R.dg.at[:, core_cols(cc)]
        return (R.wdn_b, R.wup_b)[i].at[rows_of(plane(k)), core_cols(cc)]

    def expert_grad(i, k):
        left, right = ((R.cotb, R.gact), (R.hidb, R.gra))[i]
        for cc in (sib, c):
            grad_at(i, k, cc)[...] = tmm(left[:, rows_of(plane(k))], right[:, core_cols(cc)]).astype(BF16)
            if cc is sib:
                remote(
                    grad_at(i, k, sib),
                    R.pair_r.at[i, k],
                    R.pair_s.at[0],
                    R.pair_s.at[1 + i if k == 3 else 3],
                    dev(p, z, sib),
                ).start()

    def pair_sum(i, k):
        if k == 3:
            arrived(R.pair_r.at[i, k], R.pair_s.at[1 + i])
        own = grad_at(i, k, c)
        own[...] = (own[...].astype(F32) + R.pair_r[i, k].astype(F32)).astype(BF16)

    def part_on(i, k, to, slot):
        remote(
            grad_at(i, k, c),
            R.eg_r.at[slot, i],
            R.eg_s.at[0],
            R.eg_s.at[1 + i if slot == 1 else 3 + i],
            dev(plane(to), z, c),
        ).start()

    def first_half(i, n):
        first = 1 if i == 0 else 2
        rows = slice(n * rows_d // 2, (n + 1) * rows_d // 2)
        remote(
            grad_at(i, first, c).at[rows],
            R.eg_r.at[0, i, rows],
            R.eg_s.at[0],
            R.eg_s.at[3 + i],
            dev(plane(first), z, c),
        ).start()

    def expert_grad_relay(i):
        second = 2 if i == 0 else 1
        arrived(R.eg_r.at[1, i], R.eg_s.at[1 + i])
        own = grad_at(i, second, c)
        own[...] = (own[...].astype(F32) + R.eg_r[1, i].astype(F32)).astype(BF16)
        part_on(i, second, second, 2)

    def to_place(own, got, ss, rs, o):
        remote(own(o), got(z), ss, rs, dev(p, o, c)).start()

    def run(own, got, ss, rs, k, n):
        def hand(d, slot, to):
            if k > 1:
                arrived(got(d), rs.at[d])
                own(d)[...] = (own(d)[...].astype(F32) + got(d)[...].astype(F32)).astype(BF16)
            remote(own(d), got(slot), ss, rs.at[slot], dev(p, to, c)).start()

        @pl.when(z == k - 1)
        def _():
            hand(nz - 1 - n, nz - 1 - n, k)

        @pl.when(z == nz - k)
        def _():
            hand(n, nz if n == nz - k - 1 else n, nz - k - 1)

    def run_end(total, got, rs):
        for there, slot in ((z > 0, z), (z < nz - 1, nz)):

            @pl.when(there)
            def _():
                arrived(got(slot), rs.at[slot])
                total[...] += got(slot)[...].astype(F32)

    out_sum = (lambda d: R.out_s.at[d], lambda d: R.out_r.at[d], R.out_sem.at[nz + 1], R.out_sem)
    out_run = functools.partial(run, *out_sum)

    def grad_sum(i, lanes):
        held = slice(0, EV) if i == 0 else slice((i - 1) * EV // 2, i * EV // 2)
        return (
            lambda d: R.pb.at[d * S : (d + 1) * S, lanes],
            lambda d: R.pn.at[min(i, 1), d, :, held],
            R.pn_sem.at[i, nz + 1],
            R.pn_sem.at[i],
        )

    def part_sum(i, lanes):
        return (
            lambda o: R.pb.at[pl.ds(times(o, S), S), lanes],
            lambda o: R.pr.at[o, :, slice(lanes.start - 2 * EV, lanes.stop - 2 * EV)],
            R.p_sem.at[0],
            R.p_sem.at[1 + i],
        )

    expert_grad(1, 3)
    expert_grad(0, 3)
    for i, to in ((1, 2), (0, 1)):
        pair_sum(i, 3)
        part_on(i, 3, to, 1)

    def out_tile(t, carry):
        rows = pl.ds(times(t, 256), 256)
        got = mm_t(R.gact[...], R.wdn_b[rows, :]).astype(BF16)
        for o in range(nz):

            @pl.when(inner | (o != near))
            def _():
                R.out_s[o, :, rows] = got[o * C : (o + 1) * C, :]

        return carry

    lax.fori_loop(0, D // 256, out_tile, 0)
    out_run(1, 0)

    @pl.when(inner)
    def _():
        relay_back(near, 1)
        relay_back(fellow, 0)

    for k in (1, 2, 0):
        expert_grad(1, k)
        expert_grad(0, k)
    def sum_pairs():
        arrived(R.pair_r.at[:, 0:3], R.pair_s.at[3])
        for k in (1, 2, 0):
            pair_sum(1, k)
            pair_sum(0, k)

    @pl.when(inner)
    def _():
        sum_pairs()
        for i in range(2):
            for n in range(2):
                first_half(i, n)

    hand_far(R.ra, RA, R.ra_s)
    turned_here(0, 2, R.lt_s.at[0], R.lt_s.at[1])
    hand_far(R.nrm, RN, R.nrm_s)

    R.ghid_f[...] = R.cotb[pl.ds(times(z, C), C), :].astype(F32) + R.gh_s[z].astype(F32)

    arrived(R.gh_r.at[0:2], R.gh_sem.at[1])

    def add_back(o):
        R.ghid_f[...] += R.gh_r[o].astype(F32)

    add_back(near)
    add_back(jnp.where(inner, fellow, far))

    arrived(R.glog_r.at[0 : nz - 1], R.tiny_r.at[1])
    out_run(1, 1)
    R.glog_r[z] = R.glog_s[z]
    R.ghid_b[...] = R.ghid_f[...].astype(BF16)
    put_turned(R.ghid_f[...], 2)
    send_turned(2, 3, R.lt_s.at[2], R.lt_s.at[3])
    out_run(2, 0)

    gates = R.gate_b[...]
    small = jnp.zeros((C, LANES), F32)
    gatt = [None] * H
    for x in range(EA):
        gmix = mm(R.ghid_b[...], R.wo_b[:, x * HD : (x + 1) * HD])
        for h in range(H):
            hs = slice(h * DH, (h + 1) * DH)
            j = GATE + x * H + h
            term = column(gates, j) * gmix[:, hs]
            gatt[h] = term if x == 0 else gatt[h] + term
            gg = jnp.sum(gmix[:, hs] * R.att_b[:, hs], axis=1, keepdims=True)
            small = jnp.where(lane == j, jnp.broadcast_to(gg, (C, LANES)), small)
    for h in range(H):
        hs = slice(h * DH, (h + 1) * DH)
        low = gatt[h].astype(BF16)
        R.gatt_b[:, hs] = low
        gval = tmm(R.prob_b[h].astype(BF16), low)
        R.gval_f[:, hs] = gval
        R.rb[0:C, hs] = gval.astype(BF16)
        for x in range(EA):
            lo = x * HD + h * DH
            j = x * H + h
            gg = jnp.sum(gval * R.val_b[:, lo : lo + DH], axis=1, keepdims=True)
            small = jnp.where(lane == j, jnp.broadcast_to(gg, (C, LANES)), small)
    small = small * gates * (1.0 - gates)
    glog = jnp.concatenate(
        [jnp.zeros((2 * GATE, C), F32)]
        + [R.glog_r[o].astype(F32) for o in range(nz)]
        + [jnp.zeros((LANES - 2 * GATE - nz * pad_e, C), F32)],
        axis=0,
    )
    R.small_b[...] = small.astype(BF16)
    R.rb[0:C, HD : HD + LANES] = (small + glog.T).astype(BF16)
    RV = slice(0, HD + LANES)
    send_rows(R.rb, RV, R.rv_s, (1, 2, 3))

    for h in range(H):
        hs = slice(h * DH, (h + 1) * DH)
        low = R.gatt_b[:, hs]
        gsh = mm_t(low, R.v_b[:, hs])
        prob = R.prob_b[h]
        centre = jnp.sum(prob * gsh, axis=-1, keepdims=True)
        gs = (prob * (gsh - centre)).astype(BF16)
        R.qk_b[:, hs] = rot_back(
            mm(gs, R.k_b[:, hs]) * scale
        ).astype(BF16)
        R.qk_b[:, HD + h * DH : HD + (h + 1) * DH] = rot_back(
            tmm(gs, R.q_b[:, hs])
        ).astype(BF16)
    place = p * 2 + c

    def columns_of(j):
        return pl.ds(times(j, LANES), LANES)

    for k, dc in plane_all:
        slot = 2 * k + dc
        remote(
            R.qk_b.at[:, columns_of(plane(k) * 2 + side(dc))],
            R.qc.at[slot * C : (slot + 1) * C],
            R.qk_s.at[0],
            R.qk_s.at[1],
            dev(plane(k), z, side(dc)),
        ).start()
    R.qc[0:C, :] = R.qk_b[:, columns_of(place)]


    def turned_of(w):
        return jnp.concatenate(
            [R.ltr[s, :, w * LANES : (w + 1) * LANES] for s in range(2 * nd)], axis=1
        )

    def send_part(part, lanes):
        for o in (far, fellow, near):
            to_place(*part_sum(part, lanes), o)

    def gate_rows(dst, rows_of, g0, s0, s1):
        rows = slice(s0 * C, s1 * C)
        for x in range(EA):
            for h in range(H):
                lo = x * HD + h * DH
                gx = column(R.ra[rows, HD : HD + LANES], g0 + x * H + h)
                dst[rows, lo : lo + DH] = gx * rows_of[rows, h * DH : (h + 1) * DH]

    def gated_grad(w, gated, at):
        left = turned_of(w)
        for x in range(EA):
            cols = slice(x * HD, (x + 1) * HD)
            R.pb[:, at + x * HD : at + (x + 1) * HD] = mm(left, gated[:, cols]).astype(BF16)

    PO, PV, PS = slice(0, EV), slice(EV, 2 * EV), slice(2 * EV, 2 * EV + LANES)
    near_here(R.ra, RA, R.ra_s)
    far_here(R.ra, RA, R.ra_s)
    gate_rows(R.wo_b, R.ra, GATE, 0, 2 * nd)
    turned_here(2, 3, R.lt_s.at[2], R.lt_s.at[3])
    gated_grad(2, R.wo_b, 0)
    o_run = functools.partial(run, *grad_sum(0, PO))
    halves = (slice(EV, EV + EV // 2), slice(EV + EV // 2, 2 * EV))

    def v_run(k, n):
        for i, lanes in enumerate(halves):
            run(*grad_sum(1 + i, lanes), k, n)

    o_run(1, 0)
    o_run(1, 1)
    out_run(2, 1)
    out_run(3, 0)
    gproj = mm_t(R.qk_b[...], R.wqk_b[...])
    standard = R.std_b[...]
    column_sum = jnp.sum(gproj * standard, axis=0, keepdims=True)
    for b in range(D // LANES):
        R.gp[0, b : b + 1, :] = column_sum[:, b * LANES : (b + 1) * LANES]
    for k, dc in plane_all:
        slot = 2 * k + dc
        cp = remote(
            R.gp.at[0], R.gp.at[slot], R.tiny_s.at[2], R.tiny_r.at[2], dev(plane(k), z, side(dc))
        )
        cp.start()

    @pl.when(least == 0)
    def _():
        sum_pairs()
        for i in range(2):
            for n in range(2):
                first_half(i, n)

    expert_grad_relay(0)
    expert_grad_relay(1)
    hand_near(R.rb, RV, R.rv_s, 0)

    inputs = R.tokens[...].astype(F32)
    centred = inputs - jnp.mean(inputs, axis=-1, keepdims=True)
    inverse = lax.rsqrt(jnp.mean(centred * centred, axis=-1, keepdims=True) + norm_eps)
    gs = gproj * R.gain[...]
    gtok = R.ghid_f[...] + inverse * (
        gs
        - jnp.mean(gs, axis=-1, keepdims=True)
        - standard * jnp.mean(gs * standard, axis=-1, keepdims=True)
    )
    R.gtok[...] = gtok
    for x in range(EA):
        for h in range(H):
            lo = x * HD + h * DH
            R.mix_b[:, lo : lo + DH] = (
                column(gates, x * H + h) * R.gval_f[:, h * DH : (h + 1) * DH]
            ).astype(BF16)
    for b in range(2):
        cols = slice(b * half_d, (b + 1) * half_d)
        R.gtok[:, cols] += mm_t(R.mix_b[...], R.wv_b[cols, :]) + mm_t(
            R.small_b[...], R.wg_b[cols, :]
        )


    o_run(2, 0)
    near_here(R.rb, RV, R.rv_s)
    gate_rows(R.wv_b, R.rb, 0, 0, 6)
    o_run(2, 1)
    hand_far(R.rb, RV, R.rv_s)
    far_here(R.rb, RV, R.rv_s)
    gate_rows(R.wv_b, R.rb, 0, 6, 8)
    gated_grad(0, R.wv_b, EV)
    v_run(1, 0)
    near_here(R.nrm, RN, R.nrm_s)
    far_here(R.nrm, RN, R.nrm_s)
    arrived(R.qc.at[C:], R.qk_s.at[1])
    turned = tmm(R.qc[...], R.nrm[...])
    for b in range(D // LANES):
        t = turned[:, b * LANES : (b + 1) * LANES].T.astype(BF16)
        for q in range(LANES // S):
            i = (b * LANES) // S + q
            pp, zz, cc = i // (2 * nz), (i % (2 * nz)) // 2, i % 2
            at = (pp * 2 + cc) * S
            R.qp[zz, at : at + S, :] = t[q * S : (q + 1) * S, :]
    v_run(1, 1)
    o_run(3, 0)
    total = R.gp[0]
    sent(R.gp.at[1:], R.tiny_s.at[2])
    arrived(R.gp.at[1:], R.tiny_r.at[2])
    for k, dc in plane_all:
        total = total + R.gp[2 * k + dc]
    R.gz_s[...] = total
    for k in range(1, nz):
        o = line(k)
        remote(R.gz_s, R.gz.at[z], R.tiny_s.at[3], R.tiny_r.at[3], dev(p, o, c)).start()

    lane_s = iota((SL, LANES), 1)
    small_t = mm(turned_of(0), R.rb[:, HD : HD + LANES])
    small_h = mm(turned_of(1), R.rb[:, HD : HD + LANES])
    R.pb[:, PS] = jnp.where(lane_s < 2 * GATE, small_t, small_h).astype(BF16)
    send_part(0, PS)
    v_run(2, 0)
    for o in (far, fellow, near):
        to_place(lambda d: R.qp.at[d], lambda d: R.qr.at[d], R.qk_s.at[2], R.qk_s.at[3], o)
    v_run(2, 1)
    o_run(1, 2)
    v_run(3, 0)

    v_run(1, 2)
    arrived(R.qr.at[0 : nz - 1], R.qk_s.at[3])
    got = R.qp[z].astype(F32)
    for k in range(1, nz):
        got = got + R.qr[line(k)].astype(F32)
    R.qs[...] = got
    for k, dc in plane_all:
        remote(
            R.qs.at[pl.ds(times(plane(k) * 2 + side(dc), S), S)],
            R.qf.at[:, columns_of(place)],
            R.qk_s.at[4],
            R.qk_s.at[5],
            dev(plane(k), z, side(dc)),
        ).start()
    R.qf[:, columns_of(place)] = R.qs[pl.ds(times(place, S), S), :]

    R.hid_f[...] += R.out_s[z].astype(F32)
    run_end(R.hid_f, out_sum[1], R.out_sem)
    R.mixed[...] = R.hid_f[...].astype(BF16)

    arrived(R.gz.at[0 : nz - 1], R.tiny_r.at[3])
    for k in range(1, nz):
        total = total + R.gz[line(k)]
    first = (p * 2 * nz + z * 2 + c) * S
    pick_row = iota((D // LANES, LANES), 0) == first // LANES
    line_sum = jnp.sum(jnp.where(pick_row, total, 0.0), axis=0, keepdims=True)
    shift = lax.rem(LANES - lax.rem(first, LANES), LANES)
    line_sum = pltpu.roll(jnp.broadcast_to(line_sum, (8, LANES)), shift, 1)
    R.ggain[...] = line_sum[0:1, 0:S]

    own_rows = pl.ds(times(z, S), S)

    def line_total(part, lanes):
        got = R.pb[own_rows, lanes].astype(F32)
        slots = part_sum(part, lanes)[1]
        arrived(slots(slice(0, nz - 1)), R.p_sem.at[1 + part])
        for k in range(1, nz):
            got = got + slots(line(k))[...].astype(F32)
        return got

    R.go[...] = R.pb[own_rows, PO].astype(F32)
    run_end(R.go, grad_sum(0, PO)[1], R.pn_sem.at[0])
    R.gv[...] = R.pb[own_rows, PV].astype(F32)
    for i, lanes in enumerate(halves):
        half = R.gv.at[:, lanes.start - EV : lanes.stop - EV]
        run_end(half, grad_sum(1 + i, lanes)[1], R.pn_sem.at[1 + i])
    got = line_total(0, PS)

    def pick(width, source):
        a, b = iota((width, LANES), 1), iota((width, LANES), 0)
        return jnp.where(a == source(b), 1.0, 0.0).astype(F32)

    def picked(left, right):
        return lax.dot_general(
            left,
            right,
            (((1,), (1,)), ((), ())),
            preferred_element_type=F32,
            precision=lax.Precision.HIGHEST,
        )

    def router_lane(b):
        at = jnp.zeros_like(b)
        for o in range(nz):
            at = jnp.where(b >= o * own_e, 2 * GATE + o * pad_e + b - o * own_e, at)
        return at

    R.gvg[...] = picked(pick(GATE, lambda b: b), got)
    R.gog[...] = picked(pick(GATE, lambda b: b + GATE), got)
    R.gr[...] = picked(got, pick(experts, router_lane))
    arrived(R.qs.at[0 : (2 * nd - 1) * S], R.qk_s.at[5])
    R.gq[...] = R.qf[:, 0:HD]
    R.gk[...] = R.qf[:, HD : 2 * HD]

    for i, (buf, dst) in enumerate(((R.wdn_b, R.gdn), (R.wup_b, R.gup))):
        arrived(R.eg_r.at[0:2, i], R.eg_s.at[3 + i])
        rows = rows_of(p)
        for x in range(local):
            got = buf[rows, pl.ds(times(c * local + x, DH), DH)].astype(F32)
            for slot in (0, 2):
                got = got + R.eg_r[slot, i, :, x * DH : (x + 1) * DH].astype(F32)
            dst[x] = got

    gather_end(R.cotb, R.cot_ss)
    gather_end(R.hidb, R.hid_ss)
    for buf, lanes, sem in (
        (R.ra, RA, R.ra_s),
        (R.rb, RV, R.rv_s),
        (R.nrm, RN, R.nrm_s),
    ):
        rows_sent(buf, lanes, sem)
    sent(R.maskb.at[0 : nz - 1], R.tiny_s.at[0])
    sent(R.glog_r.at[0 : nz - 1], R.tiny_s.at[1])
    sent(R.gz.at[0 : nz - 1], R.tiny_s.at[3])
    sent(R.gh_r.at[0 : nz - 1], R.gh_sem.at[0])
    sent(R.out_r.at[0 : nz - 1], R.out_sem.at[nz + 1])
    sent(R.qc.at[C:], R.qk_s.at[0])
    sent(R.qr.at[0 : nz - 1], R.qk_s.at[2])
    sent(R.qs.at[0 : (2 * nd - 1) * S], R.qk_s.at[4])
    sent(R.pair_r, R.pair_s.at[0])
    sent(R.eg_r, R.eg_s.at[0])
    sent(R.pr.at[0 : nz - 1], R.p_sem.at[0])
    sent(R.pn.at[0, 0 : nz - 1], R.pn_sem.at[0, nz + 1])
    for i in range(2):
        sent(R.pn.at[1, 0 : nz - 1, :, 0 : EV // 2], R.pn_sem.at[1 + i, nz + 1])


def settle_kernel(*refs):
    n = len(refs) // 2
    copies = [pltpu.make_async_copy(refs[i], refs[n + i], refs[-1].at[i]) for i in range(n)]
    for cp in copies:
        cp.start()
    for cp in copies:
        cp.wait()


def fused_layer(nd, nz, *args):
    (tokens, cotangent, seq_lengths, routes, head_experts, norm_gain) = args[:6]
    (w_query, w_key, w_value, w_output, w_value_gate, w_output_gate, w_router) = args[6:13]
    w_up, w_down = args[13:]
    C = tokens.shape[0]
    local = w_up.shape[0]
    experts = w_router.shape[1]
    own_e = 2 * local
    pad_e = -(-own_e // 16) * 16
    EF, HF, HD = own_e * DH, local * DH, H * DH
    EV = EA * HD
    S = D // (nd * nz * 2)
    SL = S * nz
    PW = 2 * EV + LANES
    s = Scratch()
    s.vmem("wqk_b", (D, 2 * HD), BF16)
    s.vmem("wv_b", (D, EV), BF16)
    s.vmem("wo_b", (D, EV), BF16)
    s.vmem("wup_b", (D, EF), BF16)
    s.vmem("wdn_b", (D, EF), BF16)
    s.vmem("wg_b", (D, LANES), BF16)
    s.vmem("wrl_b", (D, LANES), BF16)
    s.vmem("cotb", (nz * C, D), BF16)
    s.vmem("hidb", (nz * C, D), BF16)
    s.vmem("mask_s", (nz, pad_e, C), BF16)
    s.vmem("maskb", (nz, pad_e, C), BF16)
    s.vmem("std_b", (C, D), F32)
    s.vmem("normed_b", (C, D), BF16)
    s.vmem("q_b", (C, HD), BF16)
    s.vmem("k_b", (C, HD), BF16)
    s.vmem("v_b", (C, HD), BF16)
    s.vmem("gate_b", (C, LANES), F32)
    s.vmem("val_b", (C, EV), F32)
    s.vmem("prob_b", (H, C, C), F32)
    s.vmem("att_b", (C, HD), F32)
    s.vmem("mix_b", (C, EV), BF16)
    s.vmem("hid_f", (C, D), F32)
    s.vmem("lt", (D, 3 * LANES), BF16)
    s.vmem("ltr", (2 * nd, SL, 3 * LANES), BF16)
    s.vmem("nrm", (2 * nd * C, D), BF16)
    s.vmem("qk_b", (C, 2 * HD), BF16)
    s.vmem("qc", (2 * nd * C, LANES), BF16)
    s.vmem("qp", (nz, D // nz, LANES), BF16)
    s.vmem("qr", (nz, D // nz, LANES), BF16)
    s.vmem("qs", (D // nz, LANES), F32)
    s.vmem("qf", (S, 2 * HD), F32)
    s.vmem("ra", (2 * nd * C, HD + LANES), BF16)
    s.vmem("rb", (2 * nd * C, HD + LANES), BF16)
    s.vmem("gact", (nz * C, EF), BF16)
    s.vmem("gra", (nz * C, EF), BF16)
    for name in ("gh_s", "gh_r", "out_s"):
        s.vmem(name, (nz, C, D), BF16)
    s.vmem("out_r", (nz + 1, C, D), BF16)
    s.vmem("gh_x", (2, C, D), BF16)
    for name in ("glog_s", "glog_r"):
        s.vmem(name, (nz, pad_e, C), BF16)
    s.vmem("dg", (D // nd, EF), BF16)
    s.vmem("pair_r", (2, nd, D // nd, HF), BF16)
    s.vmem("eg_r", (nd - 1, 2, D // nd, HF), BF16)
    s.vmem("ghid_f", (C, D), F32)
    s.vmem("ghid_b", (C, D), BF16)
    s.vmem("gatt_b", (C, HD), BF16)
    s.vmem("gval_f", (C, HD), F32)
    s.vmem("small_b", (C, LANES), BF16)
    s.vmem("pb", (SL, PW), BF16)
    s.vmem("pr", (nz, S, PW - 2 * EV), BF16)
    s.vmem("pn", (2, nz + 1, S, EV), BF16)
    s.vmem("gp", (2 * nd, D // LANES, LANES), F32)
    s.vmem("gz_s", (D // LANES, LANES), F32)
    s.vmem("gz", (nz, D // LANES, LANES), F32)
    s.sems("ld", 5)
    for name in ("cot_ss", "hid_ss"):
        s.sems(name, nz + 1)
    for name in ("cot_rs", "hid_rs", "tiny_s", "tiny_r", "lt_s", "gh_sem", "pair_s"):
        s.sems(name, 4)
    for name in ("ra_s", "rv_s", "nrm_s", "qk_s"):
        s.sems(name, 6)
    s.sems("w_s", 2)
    s.sems("eg_s", 5)
    s.sems("p_sem", 3)
    s.sems("out_sem", nz + 2)
    s.sems("pn_sem", 3, nz + 2)

    def out(*shape, dtype=F32):
        return jax.ShapeDtypeStruct(shape, dtype)

    hbm = pl.BlockSpec(memory_space=pl.ANY)
    vmem = pl.BlockSpec(memory_space=pltpu.VMEM)
    names = in_hbm(SMALL) + WEIGHTS + OUTPUTS
    results = (
        out(C, D, dtype=BF16),
        out(C, D),
        out(1, S),
        out(S, HD),
        out(S, HD),
        out(S, EV),
        out(S, EV),
        out(EA * H, S),
        out(EA * H, S),
        out(S, experts),
        out(local, D // nd, DH),
        out(local, D // nd, DH),
    )
    s.vmem("tokens", (C, D), BF16)
    s.vmem("cot", (C, D), BF16)
    s.add("lens", pltpu.SMEM((1, 2), jnp.int32))
    s.vmem("rt", (TOPK, C), jnp.int32)
    s.vmem("het", (2 * H, C), jnp.int32)
    s.vmem("gain", (1, D), F32)
    s.vmem("wvg", (EA * H, D), BF16)
    s.vmem("wog", (EA * H, D), BF16)
    s.vmem("wr", (experts, D), BF16)
    s.sems("ld_in", len(SMALL))
    outs = pl.pallas_call(
        functools.partial(layer_kernel, names + tuple(s.names), nd, nz, local),
        out_shape=[pltpu.VMEM(x.shape, x.dtype) for x in results],
        in_specs=[hbm] * 15,
        out_specs=[vmem] * len(OUTPUTS),
        scratch_shapes=s.shapes,
        compiler_params=pltpu.CompilerParams(
            collective_id=0, has_side_effects=True, vmem_limit_bytes=VMEM_LIMIT
        ),
    )(
        tokens,
        cotangent,
        seq_lengths,
        routes.T,
        head_experts.reshape(C, 2 * H).T,
        norm_gain.reshape(1, D),
        w_value_gate.T,
        w_output_gate.T,
        w_router.T,
        w_query,
        w_key,
        w_value,
        w_output,
        w_up,
        w_down,
    )
    outs = list(
        pl.pallas_call(
            settle_kernel,
            out_shape=results,
            in_specs=[vmem] * len(outs),
            out_specs=[hbm] * len(outs),
            scratch_shapes=[pltpu.SemaphoreType.DMA((len(outs),))],
        )(*[pltpu.with_memory_space_constraint(x, pltpu.VMEM) for x in outs])
    )
    outs[2] = outs[2].reshape(S)
    for i in (7, 8):
        outs[i] = outs[i].T
    return tuple(outs)


VMEM_LIMIT = 58 * 1024 * 1024


def fits(nd, nz, count, experts):
    own_e = experts // nz
    pad_e = -(-own_e // 16) * 16
    return (
        count == LANES
        and nz == 4
        and nd == 4
        and own_e % 4 == 0
        and H * DH == nd * LANES
        and D % (nd * nz * 2 * 16) == 0
        and LANES % (D // (nd * nz * 2)) == 0
        and 2 * EA * H + nz * pad_e <= LANES
    )


def per_device(nd, ne, *args):
    count, experts = args[0].shape[0], args[12].shape[1]
    if ne % 2 == 0 and fits(nd, ne // 2, count, experts):
        return fused_layer(nd, ne // 2, *args)
    return routed_layer(*args)


def solution(mesh):
    return jax.shard_map(
        functools.partial(per_device, mesh.shape["dp"], mesh.shape["expert"]),
        mesh=mesh,
        in_specs=(
            P(("dp", "expert"), None),
            P(("dp", "expert"), None),
            P(("dp", "expert"), None),
            P(("dp", "expert"), None),
            P(("dp", "expert"), None, None),
            P(),
            P(),
            P(),
            P(),
            P(),
            P(),
            P(),
            P(),
            P("expert", None, None),
            P("expert", None, None),
        ),
        out_specs=(
            P(("dp", "expert"), None),
            P(("dp", "expert"), None),
            P(("dp", "expert")),
            P(("dp", "expert"), None),
            P(("dp", "expert"), None),
            P(("dp", "expert"), None),
            P(("dp", "expert"), None),
            P(("dp", "expert"), None),
            P(("dp", "expert"), None),
            P(("dp", "expert"), None),
            P("expert", "dp", None),
            P("expert", "dp", None),
        ),
        check_vma=False,
    )
```

```python
import functools
import math

import jax
import jax.numpy as jnp
from jax import lax
from jax.experimental import pallas as pl
from jax.experimental.pallas import tpu as pltpu
from jax.sharding import PartitionSpec as P

D = 1024
H = 4
DH = 128
EA = 5
TOPK = 16


norm_eps = 1e-05
rope_base = 10000.0
masked_score = -1e30


def sequence_layout(lengths, count):
    bounds = jnp.cumsum(lengths)
    starts = bounds - lengths
    places = jnp.arange(count, dtype=jnp.int32)
    seq_ids = jnp.sum((places[:, None] >= bounds[None, :]).astype(jnp.int32), axis=1)
    live = places < bounds[-1]
    slot_ids = jnp.arange(lengths.shape[0], dtype=jnp.int32)
    first = jnp.sum(jnp.where(seq_ids[:, None] == slot_ids[None, :], starts[None, :], 0), axis=1)
    positions = jnp.where(live, places - first, 0)
    return (seq_ids, live, positions)


def rope_tables(positions, width):
    half = width // 2
    freq = rope_base ** (-(jnp.arange(half, dtype=jnp.float32) * 2.0 / width))
    angles = positions.astype(jnp.float32)[:, None] * freq[None, :]
    return (jnp.cos(angles), jnp.sin(angles))


def rotate(field, cosine, sine):
    half = field.shape[-1] // 2
    first, second = (field[..., :half], field[..., half:])
    cos_h, sin_h = (cosine[:, None, :], sine[:, None, :])
    return jnp.concatenate(
        [first * cos_h - second * sin_h, second * cos_h + first * sin_h], axis=-1
    )


def rotate_back(field, cosine, sine):
    half = field.shape[-1] // 2
    first, second = (field[..., :half], field[..., half:])
    cos_h, sin_h = (cosine[:, None, :], sine[:, None, :])
    return jnp.concatenate(
        [first * cos_h + second * sin_h, second * cos_h - first * sin_h], axis=-1
    )


def slot_tables(routes, experts, most):
    count = routes.shape[0] * routes.shape[1]
    flat = routes.reshape(count)
    order = jnp.argsort(flat, stable=True)
    ordered = flat[order]
    firsts = jnp.searchsorted(ordered, jnp.arange(experts, dtype=jnp.int32))
    ranks = jnp.arange(count, dtype=jnp.int32) - firsts[ordered]
    sorted_slots = ordered * most + ranks
    slot_of_row = jnp.zeros((count,), jnp.int32).at[order].set(sorted_slots)
    row_of_slot = jnp.full((experts * most,), count, jnp.int32).at[sorted_slots].set(order)
    return (slot_of_row, row_of_slot)


def routed_layer(
    tokens,
    cotangent,
    seq_lengths,
    routes,
    head_experts,
    norm_gain,
    w_query,
    w_key,
    w_value,
    w_output,
    w_value_gate,
    w_output_gate,
    w_router,
    w_up,
    w_down,
):
    f32 = jnp.float32
    bf16 = jnp.bfloat16
    count = tokens.shape[0]
    experts = w_router.shape[1]
    local_experts = w_up.shape[0]
    owners = lax.axis_size("expert")
    most = 3 * count * TOPK // (2 * experts)
    routed = count * TOPK
    block = min(512, count)
    block_starts = jnp.arange(count // block, dtype=jnp.int32) * block
    scale = DH ** (-0.5)
    contract_last = (((1,), (1,)), ((), ()))
    contract_first = (((0,), (0,)), ((), ()))
    seq_ids, live, positions = sequence_layout(seq_lengths[0], count)
    cosine, sine = rope_tables(positions, DH)
    inputs = tokens.astype(f32)
    centred = inputs - jnp.mean(inputs, axis=-1, keepdims=True)
    inverse = lax.rsqrt(jnp.mean(centred * centred, axis=-1, keepdims=True) + norm_eps)
    standard = centred * inverse
    normed = (standard * norm_gain).astype(bf16)
    query_proj = jnp.dot(normed, w_query, preferred_element_type=f32).reshape(count, H, DH)
    key_proj = jnp.dot(normed, w_key, preferred_element_type=f32).reshape(count, H, DH)
    query_rot = (rotate(query_proj, cosine, sine) * scale).astype(bf16)
    key_rot = rotate(key_proj, cosine, sine).astype(bf16)
    chosen = jnp.any(
        head_experts[:, None, :, :] == jnp.arange(EA, dtype=jnp.int32)[None, :, None, None], axis=-1
    )
    value_gates = jnp.where(
        chosen,
        jax.nn.sigmoid(
            jnp.dot(tokens, w_value_gate, preferred_element_type=f32).reshape(count, EA, H)
        ),
        0.0,
    )
    output_gates = jnp.where(
        chosen,
        jax.nn.sigmoid(
            jnp.dot(tokens, w_output_gate, preferred_element_type=f32).reshape(count, EA, H)
        ),
        0.0,
    )
    value_all = jnp.dot(tokens, w_value, preferred_element_type=f32).reshape(count, EA, H, DH)
    values = jnp.sum(value_gates[..., None] * value_all, axis=1).astype(bf16)

    def allowed_at(start):
        queries = start + jnp.arange(block, dtype=jnp.int32)
        keys = jnp.arange(count, dtype=jnp.int32)
        same = (
            (seq_ids[:, None] == seq_ids[None, :])
            & (keys[None, :] <= queries[:, None])
            & live[None, :]
        )
        return same | (keys[None, :] == queries[:, None])

    def scores_at(start):
        scores = jnp.einsum("qhd,khd->hqk", query_rot, key_rot, preferred_element_type=f32)
        return (query_rot, jnp.where(allowed_at(start)[None], scores, masked_score))

    def attend(start):
        query_block, scores = scores_at(start)
        highest = jnp.max(scores, axis=-1, keepdims=True)
        shifted = jnp.exp(scores - highest)
        totals = jnp.sum(shifted, axis=-1, keepdims=True)
        shares = (shifted / totals).astype(bf16)
        result = jnp.einsum("hqk,khd->qhd", shares, values, preferred_element_type=f32)
        return (result, (highest + jnp.log(totals))[..., 0])

    attended, log_totals = lax.map(attend, block_starts)
    attended = attended.reshape(count, H, DH)
    log_totals = jnp.transpose(log_totals, (1, 0, 2)).reshape(H, count)
    heads_mixed = (
        (output_gates[..., None] * attended[:, None]).astype(bf16).reshape(count, EA * H * DH)
    )
    hidden = inputs + lax.dot_general(
        heads_mixed, w_output, contract_last, preferred_element_type=f32
    )
    hidden_low = hidden.astype(bf16)
    logits = jnp.dot(hidden_low, w_router, preferred_element_type=f32)
    gates = jax.nn.sigmoid(jnp.take_along_axis(logits, routes, axis=1))
    slot_of_row, row_of_slot = slot_tables(routes, experts, most)
    valid = row_of_slot < routed
    safe_row = jnp.minimum(row_of_slot, routed - 1)
    source = safe_row // TOPK
    outgoing = jnp.where(valid[:, None], hidden_low[source], jnp.zeros((), bf16)).reshape(
        owners, local_experts, most, D
    )

    def expert_apply(items):
        raised = jnp.einsum("nemd,edf->nemf", items, w_up, preferred_element_type=f32)
        active = jax.nn.silu(raised).astype(bf16)
        lowered = jnp.einsum("nemf,edf->nemd", active, w_down, preferred_element_type=f32).astype(
            bf16
        )
        return (lowered, raised)

    lowered, raised = expert_apply(
        lax.all_to_all(outgoing, "expert", split_axis=0, concat_axis=0, tiled=True)
    )
    returned = lax.all_to_all(lowered, "expert", split_axis=0, concat_axis=0, tiled=True).reshape(
        experts * most, D
    )
    expert_rows = returned[slot_of_row].reshape(count, TOPK, D)
    output = hidden + jnp.sum(gates[..., None] * expert_rows, axis=1)
    mixed = output.astype(bf16)
    grad_out = cotangent.astype(f32) * live[:, None].astype(f32)
    grad_gates = jnp.sum(grad_out[:, None, :] * expert_rows, axis=2)
    gate_flat = gates.reshape(routed)
    grad_outgoing = (
        jnp.where(valid[:, None], gate_flat[safe_row][:, None] * grad_out[source], 0.0)
        .astype(bf16)
        .reshape(owners, local_experts, most, D)
    )
    grad_lowered = lax.all_to_all(grad_outgoing, "expert", split_axis=0, concat_axis=0, tiled=True)
    items = lax.all_to_all(outgoing, "expert", split_axis=0, concat_axis=0, tiled=True)
    raised = expert_apply(items)[1]
    grad_active = jnp.einsum("nemd,edf->nemf", grad_lowered, w_down, preferred_element_type=f32)
    sigmoid_raised = jax.nn.sigmoid(raised)
    grad_raised = (grad_active * sigmoid_raised * (1.0 + raised * (1.0 - sigmoid_raised))).astype(
        bf16
    )
    grad_items = jnp.einsum("nemf,edf->nemd", grad_raised, w_up, preferred_element_type=f32).astype(
        bf16
    )
    active = jax.nn.silu(raised).astype(bf16)
    grad_items, grad_raised, active = (grad_items, grad_raised, active)
    grad_items, grad_raised, active, grad_arrived, arrived = (
        grad_items,
        grad_raised,
        active,
        grad_lowered,
        items,
    )
    grad_up_local = jnp.einsum("nemd,nemf->edf", arrived, grad_raised, preferred_element_type=f32)
    grad_down_local = jnp.einsum("nemd,nemf->edf", grad_arrived, active, preferred_element_type=f32)
    grad_up, grad_down = (
        lax.psum_scatter(
            grad_up_local.astype(jnp.bfloat16), "dp", scatter_dimension=1, tiled=True
        ).astype(jnp.float32),
        lax.psum_scatter(
            grad_down_local.astype(jnp.bfloat16), "dp", scatter_dimension=1, tiled=True
        ).astype(jnp.float32),
    )
    grad_back = lax.all_to_all(
        grad_items, "expert", split_axis=0, concat_axis=0, tiled=True
    ).reshape(experts * most, D)
    grad_hidden = grad_out + jnp.sum(
        grad_back[slot_of_row].reshape(count, TOPK, D), axis=1, dtype=f32
    )
    grad_picked = grad_gates * gates * (1.0 - gates)
    expert_ids = jnp.arange(experts, dtype=jnp.int32)
    grad_logits = jnp.sum(
        jnp.where(routes[:, :, None] == expert_ids[None, None, :], grad_picked[..., None], 0.0),
        axis=1,
    ).astype(bf16)
    grad_router = lax.dot_general(
        hidden_low, grad_logits, contract_first, preferred_element_type=f32
    )
    grad_hidden = grad_hidden + lax.dot_general(
        grad_logits, w_router, contract_last, preferred_element_type=f32
    )
    grad_hidden_low = grad_hidden.astype(bf16)
    grad_output = lax.dot_general(
        grad_hidden_low, heads_mixed, contract_first, preferred_element_type=f32
    )
    grad_mixed = jnp.dot(grad_hidden_low, w_output, preferred_element_type=f32).reshape(
        count, EA, H, DH
    )
    grad_attended = jnp.sum(output_gates[..., None] * grad_mixed, axis=1).astype(bf16)
    grad_out_gates = jnp.sum(grad_mixed * attended[:, None], axis=-1)
    grad_out_logits = (
        jnp.where(chosen, grad_out_gates * output_gates * (1.0 - output_gates), 0.0)
        .astype(bf16)
        .reshape(count, EA * H)
    )

    def attend_back(carry, start):
        grad_keys, grad_vals = carry
        query_block, scores = scores_at(start)
        shares = jnp.exp(scores - log_totals[..., None])
        grad_shares = jnp.einsum("qhd,khd->hqk", grad_attended, values, preferred_element_type=f32)
        centre = jnp.sum(shares * grad_shares, axis=-1, keepdims=True)
        grad_scores = (shares * (grad_shares - centre)).astype(bf16)
        grad_query_block = jnp.einsum(
            "hqk,khd->qhd", grad_scores, key_rot, preferred_element_type=f32
        )
        grad_keys = grad_keys + jnp.einsum(
            "hqk,qhd->khd", grad_scores, query_block, preferred_element_type=f32
        )
        grad_vals = grad_vals + jnp.einsum(
            "hqk,qhd->khd", shares.astype(bf16), grad_attended, preferred_element_type=f32
        )
        return ((grad_keys, grad_vals), grad_query_block)

    zero_heads = jnp.zeros((count, H, DH), f32)
    (grad_keys, grad_vals), grad_queries = lax.scan(
        attend_back, (zero_heads, zero_heads), block_starts
    )
    grad_queries = grad_queries.reshape(count, H, DH)
    grad_query_proj = (
        rotate_back(grad_queries * scale, cosine, sine).astype(bf16).reshape(count, H * DH)
    )
    grad_key_proj = rotate_back(grad_keys, cosine, sine).astype(bf16).reshape(count, H * DH)
    grad_value_all = (
        (value_gates[..., None] * grad_vals[:, None]).astype(bf16).reshape(count, EA * H * DH)
    )
    grad_value_gates = jnp.sum(grad_vals[:, None] * value_all, axis=-1)
    grad_value_logits = (
        jnp.where(chosen, grad_value_gates * value_gates * (1.0 - value_gates), 0.0)
        .astype(bf16)
        .reshape(count, EA * H)
    )
    grad_query = lax.dot_general(
        normed, grad_query_proj, contract_first, preferred_element_type=f32
    )
    grad_key = lax.dot_general(normed, grad_key_proj, contract_first, preferred_element_type=f32)
    grad_value = lax.dot_general(tokens, grad_value_all, contract_first, preferred_element_type=f32)
    grad_value_gate = lax.dot_general(
        tokens, grad_value_logits, contract_first, preferred_element_type=f32
    )
    grad_output_gate = lax.dot_general(
        tokens, grad_out_logits, contract_first, preferred_element_type=f32
    )
    grad_normed = lax.dot_general(
        grad_query_proj, w_query, contract_last, preferred_element_type=f32
    ) + lax.dot_general(grad_key_proj, w_key, contract_last, preferred_element_type=f32)
    grad_gain = jnp.sum(grad_normed * standard, axis=0)
    grad_standard = grad_normed * norm_gain
    grad_tokens = grad_hidden + inverse * (
        grad_standard
        - jnp.mean(grad_standard, axis=-1, keepdims=True)
        - standard * jnp.mean(grad_standard * standard, axis=-1, keepdims=True)
    )
    grad_tokens = (
        grad_tokens
        + lax.dot_general(grad_value_all, w_value, contract_last, preferred_element_type=f32)
        + lax.dot_general(
            grad_value_logits, w_value_gate, contract_last, preferred_element_type=f32
        )
        + lax.dot_general(grad_out_logits, w_output_gate, contract_last, preferred_element_type=f32)
    )
    summed = (
        lax.psum_scatter(grad_gain, ("dp", "expert"), scatter_dimension=0, tiled=True),
        lax.psum_scatter(grad_query, ("dp", "expert"), scatter_dimension=0, tiled=True),
        lax.psum_scatter(grad_key, ("dp", "expert"), scatter_dimension=0, tiled=True),
        lax.psum_scatter(grad_value, ("dp", "expert"), scatter_dimension=0, tiled=True),
        lax.psum_scatter(grad_output, ("dp", "expert"), scatter_dimension=0, tiled=True),
        lax.psum_scatter(grad_value_gate, ("dp", "expert"), scatter_dimension=0, tiled=True),
        lax.psum_scatter(grad_output_gate, ("dp", "expert"), scatter_dimension=0, tiled=True),
        lax.psum_scatter(grad_router, ("dp", "expert"), scatter_dimension=0, tiled=True),
    )
    return (
        mixed,
        grad_tokens,
        summed[0],
        summed[1],
        summed[2],
        summed[3],
        summed[4],
        summed[5],
        summed[6],
        summed[7],
        grad_up,
        grad_down,
    )


F32 = jnp.float32
BF16 = jnp.bfloat16
MESH = pl.DeviceIdType.MESH
LANES = 128


def mm(a, b):
    return lax.dot_general(a, b, (((1,), (0,)), ((), ())), preferred_element_type=F32)


def mm_t(a, b):
    return lax.dot_general(a, b, (((1,), (1,)), ((), ())), preferred_element_type=F32)


def tmm(a, b):
    return lax.dot_general(a, b, (((0,), (0,)), ((), ())), preferred_element_type=F32)


def iota(shape, axis):
    return lax.broadcasted_iota(jnp.int32, shape, axis)


def column(x, j, width=LANES):
    return jnp.broadcast_to(x[:, j : j + 1], (x.shape[0], width))


def sigmoid(x):
    return 1.0 / (1.0 + jnp.exp(-x))


class Scratch:
    def __init__(self):
        self.names, self.shapes = [], []

    def add(self, name, shape):
        self.names.append(name)
        self.shapes.append(shape)

    def vmem(self, name, shape, dtype):
        self.add(name, pltpu.VMEM(shape, dtype))

    def sems(self, name, *shape):
        self.add(name, pltpu.SemaphoreType.DMA(shape))


SMALL = ("tokens", "cot", "lens", "rt", "het", "gain", "wvg", "wog", "wr")
WEIGHTS = ("wq", "wk", "wv", "wo", "wu", "wd")
OUTPUTS = ("mixed", "gtok", "ggain", "gq", "gk", "gv", "go", "gvg", "gog", "gr", "gup", "gdn")


def in_hbm(names):
    return tuple(name + "_h" for name in names)


def layer_kernel(names, nd, nz, local, *refs):
    r = dict(zip(names, refs))
    R = type("R", (), r)
    C = R.tokens.shape[0]
    own_e = 2 * local
    pad_e = R.maskb.shape[1]
    EF = own_e * DH
    HF = local * DH
    HD = H * DH
    EV = EA * HD
    S = D // (nd * nz * 2)
    SL = S * nz
    GATE = EA * H
    p = lax.axis_index("dp")
    e = lax.axis_index("expert")
    z = e // 2
    c = e % 2
    sib = 1 - c

    def dev(p_, z_, c_):
        return (p_, z_ * 2 + c_)

    def times(i, n):
        return pl.multiple_of(i * n, n)

    def remote(src, dst, ss, rs, to):
        return pltpu.make_async_remote_copy(
            src_ref=src, dst_ref=dst, send_sem=ss, recv_sem=rs, device_id=to, device_id_type=MESH
        )

    def arrived(dst, rs):
        remote(dst, dst, rs, rs, dev(p, z, sib)).wait_recv()

    def sent(src, ss):
        remote(src, src, ss, ss, dev(p, z, sib)).wait_send()

    beside = p + 1 - 2 * lax.rem(p, 2)
    across = lax.rem(p + 2, nd)
    diagonal = lax.rem(beside + 2, nd)

    def core_cols(cc):
        return pl.ds(times(cc, HF), HF)

    def plane(k):
        return (p, beside, across, diagonal)[k]

    def line(k):
        return lax.rem(z + k, nz)

    barrier = pltpu.get_barrier_semaphore()
    partners = [dev(p, z, sib)]
    partners += [dev(p, line(k), c) for k in range(1, nz)]
    for k in range(1, nd):
        partners += [dev(plane(k), z, c), dev(plane(k), z, sib)]
    for to in partners:
        pl.semaphore_signal(barrier, inc=1, device_id=to, device_id_type=MESH)

    loads = {}

    def load(name, src, dst, sem):
        cp = pltpu.make_async_copy(src, dst, sem)
        cp.start()
        loads[name] = cp

    def loaded(*names):
        for name in names:
            loads.pop(name).wait()

    def landed(dst, sem):
        pltpu.make_async_copy(dst, dst, sem).wait()

    for i, name in enumerate(("cot", "lens", "rt", "tokens", "gain", "het", "wvg", "wog", "wr")):
        load(name, r[name + "_h"], r[name], R.ld_in.at[i])
    load("qk", R.wq, R.wqk_b.at[:, 0:HD], R.ld.at[0])
    load("qk", R.wk, R.wqk_b.at[:, HD : 2 * HD], R.ld.at[0])
    loaded("lens")
    l0 = R.lens[0, 0]
    b1 = l0 + R.lens[0, 1]
    row = iota((C, LANES), 0)
    lane = iota((C, LANES), 1)
    seq_r = (row >= l0).astype(jnp.int32) + (row >= b1).astype(jnp.int32)
    seq_c = (lane >= l0).astype(jnp.int32) + (lane >= b1).astype(jnp.int32)
    live = row < b1
    allowed = ((seq_r == seq_c) & (lane <= row) & (lane < b1)) | (row == lane)
    live_f = jnp.where(live, 1.0, 0.0).astype(F32)
    start = jnp.where(seq_r == 0, 0, l0)
    position = jnp.where(live, row - start, 0).astype(F32)

    loaded("cot")
    for b in range(D // LANES):
        cols = slice(b * LANES, (b + 1) * LANES)
        R.cotb[pl.ds(times(z, C), C), cols] = (R.cot[:, cols].astype(F32) * live_f).astype(BF16)
    load("v", R.wv, R.wv_b, R.ld.at[1])
    for i in range(local):
        col = times(c * local + i, DH)
        load("up", R.wu.at[i], R.wup_b.at[:, pl.ds(col, DH)], R.ld.at[2])
        load("dn", R.wd.at[i], R.wdn_b.at[:, pl.ds(col, DH)], R.ld.at[3])
    load("o", R.wo, R.wo_b, R.ld.at[4])
    loaded("rt")
    ids = iota((pad_e, C), 0)
    for zz in range(nz):
        named = jnp.zeros((pad_e, C), F32)
        for k in range(TOPK):
            hit = jnp.broadcast_to(R.rt[k : k + 1, :], (pad_e, C)) == ids + zz * own_e
            named = jnp.where(hit & (ids < own_e), 1.0, named)
        R.mask_s[zz] = named.astype(BF16)
    R.maskb[z] = R.mask_s[z]

    pl.semaphore_wait(barrier, len(partners))

    def block(buf, o):
        return buf.at[pl.ds(times(o, C), C), :]

    def pass_on(buf, ss, rs, o, right, left):
        @pl.when(right)
        def _():
            remote(block(buf, o), block(buf, o), ss.at[o], rs.at[o], dev(p, z + 1, c)).start()

        @pl.when(left)
        def _():
            way = jnp.where(o == z, nz, o)
            remote(block(buf, o), block(buf, o), ss.at[way], rs.at[o], dev(p, z - 1, c)).start()

    def passed(buf, ss, o, right, left):
        @pl.when(right)
        def _():
            sent(block(buf, o), ss.at[o])

        @pl.when(left)
        def _():
            sent(block(buf, o), ss.at[jnp.where(o == z, nz, o)])

    def gather_own(buf, ss, rs):
        pass_on(buf, ss, rs, z, z < nz - 1, z > 0)

    def gather_on(buf, ss, rs, o):
        arrived(block(buf, o), rs.at[o])
        pass_on(buf, ss, rs, o, (o < z) & (z < nz - 1), (o > z) & (z > 0))

    def gather_step(buf, ss, rs, k):
        @pl.when(z >= k)
        def _():
            gather_on(buf, ss, rs, z - k)

        @pl.when(z + k < nz)
        def _():
            gather_on(buf, ss, rs, z + k)

    def gather_end(buf, ss):
        passed(buf, ss, z, z < nz - 1, z > 0)
        for k in range(1, nz):

            @pl.when(z >= k)
            def _():
                passed(buf, ss, z - k, z < nz - 1, False)

            @pl.when(z + k < nz)
            def _():
                passed(buf, ss, z + k, False, z > 0)

    gather_own(R.cotb, R.cot_ss, R.cot_rs)
    for k in range(1, nz):
        o = line(k)
        remote(R.mask_s.at[o], R.maskb.at[z], R.tiny_s.at[0], R.tiny_r.at[0], dev(p, o, c)).start()

    loaded("tokens", "gain", "het", "wvg", "wog", "wr")

    s_row, s_col = iota((GATE, LANES), 0), iota((GATE, LANES), 1)
    to_v = jnp.where(s_row == s_col, 1.0, 0.0).astype(BF16)
    to_o = jnp.where(s_row + GATE == s_col, 1.0, 0.0).astype(BF16)
    R.wg_b[...] = (tmm(R.wvg[...], to_v) + tmm(R.wog[...], to_o)).astype(BF16)
    half = lax.rem(lane, DH // 2).astype(F32)
    angle = position * jnp.exp(half * (-2.0 / DH * math.log(rope_base)))
    cosine = jnp.cos(angle)
    sine = jnp.where(lane < DH // 2, -jnp.sin(angle), jnp.sin(angle))

    def rot(v):
        return v * cosine + pltpu.roll(v, DH // 2, 1) * sine

    def rot_back(v):
        return v * cosine - pltpu.roll(v, DH // 2, 1) * sine

    inputs = R.tokens[...].astype(F32)
    centred = inputs - jnp.mean(inputs, axis=-1, keepdims=True)
    inverse = lax.rsqrt(jnp.mean(centred * centred, axis=-1, keepdims=True) + norm_eps)
    standard = centred * inverse
    R.std_b[...] = standard
    R.normed_b[...] = (standard * R.gain[...]).astype(BF16)

    landed(R.wqk_b, R.ld.at[0])
    scale = DH ** (-0.5)
    qk = mm(R.normed_b[...], R.wqk_b[:, 0:HD])
    for h in range(H):
        hs = slice(h * DH, (h + 1) * DH)
        R.q_b[:, hs] = (rot(qk[:, hs]) * scale).astype(BF16)
    qk = mm(R.normed_b[...], R.wqk_b[:, HD : 2 * HD])
    for h in range(H):
        hs = slice(h * DH, (h + 1) * DH)
        R.k_b[:, hs] = rot(qk[:, hs]).astype(BF16)

    hit = []
    for j in range(GATE):
        x, h = divmod(j, H)
        one = (R.het[2 * h : 2 * h + 1, :] == x) | (R.het[2 * h + 1 : 2 * h + 2, :] == x)
        hit.append(jnp.where(one, 1.0, 0.0).astype(F32))
    hit = jnp.concatenate(hit + hit + [jnp.zeros((LANES - 2 * GATE, C), F32)], axis=0)
    R.gate_b[...] = sigmoid(mm(R.tokens[...], R.wg_b[...])) * hit.T

    landed(R.wup_b.at[:, core_cols(c)], R.ld.at[2])
    landed(R.wdn_b.at[:, core_cols(c)], R.ld.at[3])
    for i, buf in enumerate((R.wup_b, R.wdn_b)):
        part = buf.at[:, pl.ds(times(c, HF), HF)]
        cp = remote(part, part, R.w_s.at[0], R.w_s.at[1], dev(p, z, sib))
        cp.start()

    landed(R.wv_b, R.ld.at[1])
    gates = R.gate_b[...]
    total = [None] * H
    for b in range(2):
        cols = slice(b * EV // 2, (b + 1) * EV // 2)
        R.val_b[:, cols] = mm(R.tokens[...], R.wv_b[:, cols])
    for x in range(EA):
        for h in range(H):
            lo = x * HD + h * DH
            term = column(gates, x * H + h) * R.val_b[:, lo : lo + DH]
            total[h] = term if x == 0 else total[h] + term
    for h in range(H):
        R.v_b[:, h * DH : (h + 1) * DH] = total[h].astype(BF16)

    for h in range(H):
        hs = slice(h * DH, (h + 1) * DH)
        scores = jnp.where(allowed, mm_t(R.q_b[:, hs], R.k_b[:, hs]), masked_score)
        shifted = jnp.exp(scores - jnp.max(scores, axis=-1, keepdims=True))
        shares = shifted / jnp.sum(shifted, axis=-1, keepdims=True)
        R.prob_b[h] = shares
        R.att_b[:, hs] = mm(shares.astype(BF16), R.v_b[:, hs])

    for x in range(EA):
        for h in range(H):
            lo = x * HD + h * DH
            R.mix_b[:, lo : lo + DH] = (
                column(gates, GATE + x * H + h) * R.att_b[:, h * DH : (h + 1) * DH]
            ).astype(BF16)
    landed(R.wo_b, R.ld.at[4])
    half_d = D // 2
    hidden = R.tokens[...].astype(F32) + mm_t(R.mix_b[...], R.wo_b[...])
    R.hid_f[...] = hidden
    R.hidb[pl.ds(times(z, C), C), :] = hidden.astype(BF16)
    gather_own(R.hidb, R.hid_ss, R.hid_rs)
    gather_step(R.cotb, R.cot_ss, R.cot_rs, 1)
    experts = R.wr.shape[0]
    r_row, r_col = iota((experts, LANES), 0), iota((experts, LANES), 1)
    to_r = jnp.where((r_row == r_col + z * own_e) & (r_col < own_e), 1.0, 0.0).astype(BF16)
    R.wrl_b[...] = tmm(R.wr[...], to_r).astype(BF16)

    def put_turned(x, w):
        for b in range(D // LANES):
            t = x[:, b * LANES : (b + 1) * LANES].astype(F32).T.astype(BF16)
            for q in range(LANES // S):
                i = (b * LANES) // S + q
                pp, zz, cc = i // (2 * nz), (i % (2 * nz)) // 2, i % 2
                at = (pp * 2 + cc) * SL + zz * S
                R.lt[at : at + S, w * LANES : (w + 1) * LANES] = t[q * S : (q + 1) * S, :]

    plane_all = [(k, dc) for k in range(nd) for dc in range(2) if k or dc]

    def side(dc):
        return sib if dc else c

    def send_turned(w0, w1, ss, rs):
        lanes = slice(w0 * LANES, w1 * LANES)
        for k, dc in plane_all:
            to = plane(k)
            slot = 2 * k + dc
            at = times(to * 2 + side(dc), SL)
            cp = remote(
                R.lt.at[pl.ds(at, SL), lanes],
                R.ltr.at[slot, :, lanes],
                ss,
                rs,
                dev(to, z, side(dc)),
            )
            cp.start()
        R.ltr[0, :, lanes] = R.lt[pl.ds(times(p * 2 + c, SL), SL), lanes]

    def turned_here(w0, w1, ss, rs):
        there = R.ltr.at[1 : 2 * nd, :, w0 * LANES : w1 * LANES]
        sent(there, ss)
        arrived(there, rs)

    def rows_at(buf, lanes, slot):
        return buf.at[slot * C : (slot + 1) * C, lanes]

    def send_rows(buf, lanes, sem, ways=(1, 2)):
        for k in ways:
            remote(
                rows_at(buf, lanes, 0),
                rows_at(buf, lanes, 2 * k),
                sem.at[0],
                sem.at[k],
                dev(plane(k), z, c),
            ).start()
        hand_over(buf, lanes, sem, 0)

    def hand_over(buf, lanes, sem, k):
        remote(
            rows_at(buf, lanes, 2 * k),
            rows_at(buf, lanes, 2 * k + 1),
            sem.at[0],
            sem.at[5 if k == 3 else 4],
            dev(p, z, sib),
        ).start()

    def hand_near(buf, lanes, sem, via):
        for k in (via, 3 - via) if via else (1, 2):
            arrived(rows_at(buf, lanes, 2 * k), sem.at[k])
            if k == via:
                remote(
                    rows_at(buf, lanes, 2 * k),
                    rows_at(buf, lanes, 6),
                    sem.at[0],
                    sem.at[3],
                    dev(plane(3 - via), z, c),
                ).start()
            hand_over(buf, lanes, sem, k)

    def hand_far(buf, lanes, sem):
        arrived(rows_at(buf, lanes, 6), sem.at[3])
        hand_over(buf, lanes, sem, 3)

    def near_here(buf, lanes, sem):
        arrived(buf.at[0 : 3 * C, lanes], sem.at[4])

    def far_here(buf, lanes, sem):
        arrived(rows_at(buf, lanes, 7), sem.at[5])

    def rows_sent(buf, lanes, sem):
        sent(buf.at[0 : 7 * C, lanes], sem.at[0])

    put_turned(R.tokens[...], 0)
    put_turned(R.hid_f[...], 1)
    send_turned(0, 2, R.lt_s.at[0], R.lt_s.at[1])
    R.nrm[0:C, :] = R.normed_b[...]
    RN = slice(0, D)
    send_rows(R.nrm, RN, R.nrm_s)
    R.ra[0:C, 0:HD] = R.att_b[...].astype(BF16)
    R.ra[0:C, HD : HD + LANES] = gates.astype(BF16)
    RA = slice(0, HD + LANES)
    send_rows(R.ra, RA, R.ra_s)

    sent(R.wup_b, R.w_s.at[0])
    arrived(R.wup_b, R.w_s.at[1])

    least = jnp.minimum(z, nz - 1 - z)
    inner = least > 0
    left_half = z < nz // 2
    near = jnp.where(inner, jnp.where(left_half, 0, nz - 1), jnp.where(left_half, 1, nz - 2))
    fellow = jnp.where(left_half, nz // 2, nz // 2 - 1)
    far = jnp.where(left_half, nz - 1, 0)

    def origin(k):
        paired = k <= 2 * least
        dist = jnp.where(paired, (k + 1) // 2, k - least)
        left = jnp.where(paired, lax.rem(k, 2) == 1, z > nz - 1 - z)
        return jnp.where(k == 0, z, jnp.where(left, z - dist, z + dist))

    def expert_block(k, carry):
        o = origin(k)
        rows = pl.ds(times(o, C), C)

        @pl.when((k == 1) & inner)
        def _():
            gather_on(R.hidb, R.hid_ss, R.hid_rs, origin(1))

        @pl.when((k > 0) & (k + inner.astype(jnp.int32) < nz))
        def _():
            gather_on(R.hidb, R.hid_ss, R.hid_rs, origin(k + inner.astype(jnp.int32)))

        @pl.when(k == jnp.where(inner, 1, 2))
        def _():
            for far_step in range(2, nz - 1):
                gather_step(R.cotb, R.cot_ss, R.cot_rs, far_step)

        @pl.when(k > 0)
        def _():
            @pl.when((o == z - nz + 1) | (o == z + nz - 1))
            def _():
                arrived(block(R.cotb, o), R.cot_rs.at[o])

        @pl.when(k == 1)
        def _():
            arrived(R.maskb.at[0 : nz - 1], R.tiny_r.at[0])

        hb = R.hidb[rows, :]
        cb = R.cotb[rows, :]
        named = R.maskb[o].astype(F32)
        named = jnp.concatenate([named, jnp.zeros((LANES - pad_e, C), F32)], axis=0).T
        g = sigmoid(mm(hb, R.wrl_b[...])) * named
        glog = jnp.zeros((C, LANES), F32)
        for q in range(2):
            cols = slice(q * HF, (q + 1) * HF)
            raised = mm(hb, R.wup_b[:, cols])
            back = mm(cb, R.wdn_b[:, cols])
            for i in range(local):
                j = q * local + i
                u = raised[:, i * DH : (i + 1) * DH]
                a = back[:, i * DH : (i + 1) * DH]
                gj = column(g, j)
                s = sigmoid(u)
                act = u * s
                lo = j * DH
                R.gact[rows, lo : lo + DH] = (gj * act).astype(BF16)
                R.gra[rows, lo : lo + DH] = (gj * a * (s * (1.0 + u * (1.0 - s)))).astype(BF16)
                gg = jnp.sum(a * act, axis=1, keepdims=True)
                glog = jnp.where(lane == j, jnp.broadcast_to(gg, (C, LANES)), glog)
        glog = glog * g * (1.0 - g)
        low = glog.astype(BF16)
        R.glog_s[o] = glog.T[0:pad_e, :].astype(BF16)
        for b in range(2):
            cols = slice(b * half_d, (b + 1) * half_d)
            gh = mm_t(R.gra[rows, :], R.wup_b[cols, :]) + mm_t(low, R.wrl_b[cols, :])
            R.gh_s[o, :, cols] = gh.astype(BF16)

        @pl.when(k > 0)
        def _():
            remote(
                R.glog_s.at[o], R.glog_r.at[z], R.tiny_s.at[1], R.tiny_r.at[1], dev(p, o, c)
            ).start()

        @pl.when((k > 0) & (least == 0) & (o != fellow))
        def _():
            send_back(o)

        @pl.when((k > 0) & (least == 0) & (o == fellow))
        def _():
            send_by(o, near, 0)

        @pl.when((k > 0) & inner & (o == far))
        def _():
            send_by(o, fellow, 1)

        @pl.when(k == 2)
        def _():
            hand_near(R.ra, RA, R.ra_s, 2)
            hand_near(R.nrm, RN, R.nrm_s, 1)

        @pl.when((k == 1) & (least == 0))
        def _():
            there = pl.ds(times(near, C), C)
            for b in range(2):
                cols = slice(b * half_d, (b + 1) * half_d)
                R.out_s[near, :, cols] = mm_t(R.gact[there, :], R.wdn_b[cols, :]).astype(BF16)
            slot = jnp.where(z == 0, near, nz)
            remote(
                R.out_s.at[near],
                R.out_r.at[slot],
                R.out_sem.at[nz + 1],
                R.out_sem.at[slot],
                dev(p, near, c),
            ).start()

        return carry

    def send_back(o):
        remote(R.gh_s.at[o], R.gh_r.at[z], R.gh_sem.at[0], R.gh_sem.at[1], dev(p, o, c)).start()

    def send_by(o, by, slot):
        remote(
            R.gh_s.at[o], R.gh_x.at[slot], R.gh_sem.at[0], R.gh_sem.at[2 + slot], dev(p, by, c)
        ).start()

    def relay_back(o, slot):
        arrived(R.gh_x.at[slot], R.gh_sem.at[2 + slot])
        R.gh_s[o] = (R.gh_s[o].astype(F32) + R.gh_x[slot].astype(F32)).astype(BF16)
        send_back(o)

    lax.fori_loop(0, nz, expert_block, 0)

    def rows_of(at):
        return pl.ds(times(at, rows_d), rows_d)


    rows_d = D // nd

    def grad_at(i, k, cc):
        if i == 0 and k == 3:
            return R.dg.at[:, core_cols(cc)]
        return (R.wdn_b, R.wup_b)[i].at[rows_of(plane(k)), core_cols(cc)]

    def expert_grad(i, k):
        left, right = ((R.cotb, R.gact), (R.hidb, R.gra))[i]
        for cc in (sib, c):
            grad_at(i, k, cc)[...] = tmm(left[:, rows_of(plane(k))], right[:, core_cols(cc)]).astype(BF16)
            if cc is sib:
                remote(
                    grad_at(i, k, sib),
                    R.pair_r.at[i, k],
                    R.pair_s.at[0],
                    R.pair_s.at[1 + i if k == 3 else 3],
                    dev(p, z, sib),
                ).start()

    def pair_sum(i, k):
        if k == 3:
            arrived(R.pair_r.at[i, k], R.pair_s.at[1 + i])
        own = grad_at(i, k, c)
        own[...] = (own[...].astype(F32) + R.pair_r[i, k].astype(F32)).astype(BF16)

    def part_on(i, k, to, slot):
        remote(
            grad_at(i, k, c),
            R.eg_r.at[slot, i],
            R.eg_s.at[0],
            R.eg_s.at[1 + i if slot == 1 else 3 + i],
            dev(plane(to), z, c),
        ).start()

    def first_half(i, n):
        first = 1 if i == 0 else 2
        rows = slice(n * rows_d // 2, (n + 1) * rows_d // 2)
        remote(
            grad_at(i, first, c).at[rows],
            R.eg_r.at[0, i, rows],
            R.eg_s.at[0],
            R.eg_s.at[3 + i],
            dev(plane(first), z, c),
        ).start()

    def expert_grad_relay(i):
        second = 2 if i == 0 else 1
        arrived(R.eg_r.at[1, i], R.eg_s.at[1 + i])
        own = grad_at(i, second, c)
        own[...] = (own[...].astype(F32) + R.eg_r[1, i].astype(F32)).astype(BF16)
        part_on(i, second, second, 2)

    def to_place(own, got, ss, rs, o):
        remote(own(o), got(z), ss, rs, dev(p, o, c)).start()

    def run(own, got, ss, rs, k, n):
        def hand(d, slot, to):
            if k > 1:
                arrived(got(d), rs.at[d])
                own(d)[...] = (own(d)[...].astype(F32) + got(d)[...].astype(F32)).astype(BF16)
            remote(own(d), got(slot), ss, rs.at[slot], dev(p, to, c)).start()

        @pl.when(z == k - 1)
        def _():
            hand(nz - 1 - n, nz - 1 - n, k)

        @pl.when(z == nz - k)
        def _():
            hand(n, nz if n == nz - k - 1 else n, nz - k - 1)

    def run_end(total, got, rs):
        for there, slot in ((z > 0, z), (z < nz - 1, nz)):

            @pl.when(there)
            def _():
                arrived(got(slot), rs.at[slot])
                total[...] += got(slot)[...].astype(F32)

    out_sum = (lambda d: R.out_s.at[d], lambda d: R.out_r.at[d], R.out_sem.at[nz + 1], R.out_sem)
    out_run = functools.partial(run, *out_sum)

    def grad_sum(i, lanes):
        held = slice(0, EV) if i == 0 else slice((i - 1) * EV // 2, i * EV // 2)
        return (
            lambda d: R.pb.at[d * S : (d + 1) * S, lanes],
            lambda d: R.pn.at[min(i, 1), d, :, held],
            R.pn_sem.at[i, nz + 1],
            R.pn_sem.at[i],
        )

    def part_sum(i, lanes):
        return (
            lambda o: R.pb.at[pl.ds(times(o, S), S), lanes],
            lambda o: R.pr.at[o, :, slice(lanes.start - 2 * EV, lanes.stop - 2 * EV)],
            R.p_sem.at[0],
            R.p_sem.at[1 + i],
        )

    expert_grad(1, 3)
    expert_grad(0, 3)
    for i, to in ((1, 2), (0, 1)):
        pair_sum(i, 3)
        part_on(i, 3, to, 1)

    def out_tile(t, carry):
        rows = pl.ds(times(t, 256), 256)
        got = mm_t(R.gact[...], R.wdn_b[rows, :]).astype(BF16)
        for o in range(nz):

            @pl.when(inner | (o != near))
            def _():
                R.out_s[o, :, rows] = got[o * C : (o + 1) * C, :]

        return carry

    lax.fori_loop(0, D // 256, out_tile, 0)
    out_run(1, 0)

    @pl.when(inner)
    def _():
        relay_back(near, 1)
        relay_back(fellow, 0)

    for k in (1, 2, 0):
        expert_grad(1, k)
        expert_grad(0, k)
    def sum_pairs():
        arrived(R.pair_r.at[:, 0:3], R.pair_s.at[3])
        for k in (1, 2, 0):
            pair_sum(1, k)
            pair_sum(0, k)

    @pl.when(inner)
    def _():
        sum_pairs()
        for i in range(2):
            for n in range(2):
                first_half(i, n)

    hand_far(R.ra, RA, R.ra_s)
    turned_here(0, 2, R.lt_s.at[0], R.lt_s.at[1])
    hand_far(R.nrm, RN, R.nrm_s)

    R.ghid_f[...] = R.cotb[pl.ds(times(z, C), C), :].astype(F32) + R.gh_s[z].astype(F32)

    arrived(R.gh_r.at[0:2], R.gh_sem.at[1])

    def add_back(o):
        R.ghid_f[...] += R.gh_r[o].astype(F32)

    add_back(near)
    add_back(jnp.where(inner, fellow, far))

    arrived(R.glog_r.at[0 : nz - 1], R.tiny_r.at[1])
    out_run(1, 1)
    R.glog_r[z] = R.glog_s[z]
    R.ghid_b[...] = R.ghid_f[...].astype(BF16)
    put_turned(R.ghid_f[...], 2)
    send_turned(2, 3, R.lt_s.at[2], R.lt_s.at[3])
    out_run(2, 0)

    gates = R.gate_b[...]
    small = jnp.zeros((C, LANES), F32)
    gatt = [None] * H
    for x in range(EA):
        gmix = mm(R.ghid_b[...], R.wo_b[:, x * HD : (x + 1) * HD])
        for h in range(H):
            hs = slice(h * DH, (h + 1) * DH)
            j = GATE + x * H + h
            term = column(gates, j) * gmix[:, hs]
            gatt[h] = term if x == 0 else gatt[h] + term
            gg = jnp.sum(gmix[:, hs] * R.att_b[:, hs], axis=1, keepdims=True)
            small = jnp.where(lane == j, jnp.broadcast_to(gg, (C, LANES)), small)
    for h in range(H):
        hs = slice(h * DH, (h + 1) * DH)
        low = gatt[h].astype(BF16)
        R.gatt_b[:, hs] = low
        gval = tmm(R.prob_b[h].astype(BF16), low)
        R.gval_f[:, hs] = gval
        R.rb[0:C, hs] = gval.astype(BF16)
        for x in range(EA):
            lo = x * HD + h * DH
            j = x * H + h
            gg = jnp.sum(gval * R.val_b[:, lo : lo + DH], axis=1, keepdims=True)
            small = jnp.where(lane == j, jnp.broadcast_to(gg, (C, LANES)), small)
    small = small * gates * (1.0 - gates)
    glog = jnp.concatenate(
        [jnp.zeros((2 * GATE, C), F32)]
        + [R.glog_r[o].astype(F32) for o in range(nz)]
        + [jnp.zeros((LANES - 2 * GATE - nz * pad_e, C), F32)],
        axis=0,
    )
    R.small_b[...] = small.astype(BF16)
    R.rb[0:C, HD : HD + LANES] = (small + glog.T).astype(BF16)
    RV = slice(0, HD + LANES)
    send_rows(R.rb, RV, R.rv_s, (1, 2, 3))

    for h in range(H):
        hs = slice(h * DH, (h + 1) * DH)
        low = R.gatt_b[:, hs]
        gsh = mm_t(low, R.v_b[:, hs])
        prob = R.prob_b[h]
        centre = jnp.sum(prob * gsh, axis=-1, keepdims=True)
        gs = (prob * (gsh - centre)).astype(BF16)
        R.qk_b[:, hs] = rot_back(
            mm(gs, R.k_b[:, hs]) * scale
        ).astype(BF16)
        R.qk_b[:, HD + h * DH : HD + (h + 1) * DH] = rot_back(
            tmm(gs, R.q_b[:, hs])
        ).astype(BF16)
    place = p * 2 + c

    def columns_of(j):
        return pl.ds(times(j, LANES), LANES)

    for k, dc in plane_all:
        slot = 2 * k + dc
        remote(
            R.qk_b.at[:, columns_of(plane(k) * 2 + side(dc))],
            R.qc.at[slot * C : (slot + 1) * C],
            R.qk_s.at[0],
            R.qk_s.at[1],
            dev(plane(k), z, side(dc)),
        ).start()
    R.qc[0:C, :] = R.qk_b[:, columns_of(place)]


    def turned_of(w):
        return jnp.concatenate(
            [R.ltr[s, :, w * LANES : (w + 1) * LANES] for s in range(2 * nd)], axis=1
        )

    def send_part(part, lanes):
        for o in (far, fellow, near):
            to_place(*part_sum(part, lanes), o)

    def gate_rows(dst, rows_of, g0, s0, s1):
        rows = slice(s0 * C, s1 * C)
        for x in range(EA):
            for h in range(H):
                lo = x * HD + h * DH
                gx = column(R.ra[rows, HD : HD + LANES], g0 + x * H + h)
                dst[rows, lo : lo + DH] = gx * rows_of[rows, h * DH : (h + 1) * DH]

    def gated_grad(w, gated, at):
        left = turned_of(w)
        for x in range(EA):
            cols = slice(x * HD, (x + 1) * HD)
            R.pb[:, at + x * HD : at + (x + 1) * HD] = mm(left, gated[:, cols]).astype(BF16)

    PO, PV, PS = slice(0, EV), slice(EV, 2 * EV), slice(2 * EV, 2 * EV + LANES)
    near_here(R.ra, RA, R.ra_s)
    far_here(R.ra, RA, R.ra_s)
    gate_rows(R.wo_b, R.ra, GATE, 0, 2 * nd)
    turned_here(2, 3, R.lt_s.at[2], R.lt_s.at[3])
    gated_grad(2, R.wo_b, 0)
    o_run = functools.partial(run, *grad_sum(0, PO))
    halves = (slice(EV, EV + EV // 2), slice(EV + EV // 2, 2 * EV))

    def v_run(k, n):
        for i, lanes in enumerate(halves):
            run(*grad_sum(1 + i, lanes), k, n)

    o_run(1, 0)
    o_run(1, 1)
    out_run(2, 1)
    out_run(3, 0)
    gproj = mm_t(R.qk_b[...], R.wqk_b[...])
    standard = R.std_b[...]
    column_sum = jnp.sum(gproj * standard, axis=0, keepdims=True)
    for b in range(D // LANES):
        R.gp[0, b : b + 1, :] = column_sum[:, b * LANES : (b + 1) * LANES]
    for k, dc in plane_all:
        slot = 2 * k + dc
        cp = remote(
            R.gp.at[0], R.gp.at[slot], R.tiny_s.at[2], R.tiny_r.at[2], dev(plane(k), z, side(dc))
        )
        cp.start()

    @pl.when(least == 0)
    def _():
        sum_pairs()
        for i in range(2):
            for n in range(2):
                first_half(i, n)

    expert_grad_relay(0)
    expert_grad_relay(1)
    hand_near(R.rb, RV, R.rv_s, 0)

    inputs = R.tokens[...].astype(F32)
    centred = inputs - jnp.mean(inputs, axis=-1, keepdims=True)
    inverse = lax.rsqrt(jnp.mean(centred * centred, axis=-1, keepdims=True) + norm_eps)
    gs = gproj * R.gain[...]
    gtok = R.ghid_f[...] + inverse * (
        gs
        - jnp.mean(gs, axis=-1, keepdims=True)
        - standard * jnp.mean(gs * standard, axis=-1, keepdims=True)
    )
    R.gtok[...] = gtok
    for x in range(EA):
        for h in range(H):
            lo = x * HD + h * DH
            R.mix_b[:, lo : lo + DH] = (
                column(gates, x * H + h) * R.gval_f[:, h * DH : (h + 1) * DH]
            ).astype(BF16)
    for b in range(2):
        cols = slice(b * half_d, (b + 1) * half_d)
        R.gtok[:, cols] += mm_t(R.mix_b[...], R.wv_b[cols, :]) + mm_t(
            R.small_b[...], R.wg_b[cols, :]
        )


    o_run(2, 0)
    near_here(R.rb, RV, R.rv_s)
    gate_rows(R.wv_b, R.rb, 0, 0, 6)
    o_run(2, 1)
    hand_far(R.rb, RV, R.rv_s)
    far_here(R.rb, RV, R.rv_s)
    gate_rows(R.wv_b, R.rb, 0, 6, 8)
    gated_grad(0, R.wv_b, EV)
    v_run(1, 0)
    near_here(R.nrm, RN, R.nrm_s)
    far_here(R.nrm, RN, R.nrm_s)
    arrived(R.qc.at[C:], R.qk_s.at[1])
    turned = tmm(R.qc[...], R.nrm[...])
    for b in range(D // LANES):
        t = turned[:, b * LANES : (b + 1) * LANES].T.astype(BF16)
        for q in range(LANES // S):
            i = (b * LANES) // S + q
            pp, zz, cc = i // (2 * nz), (i % (2 * nz)) // 2, i % 2
            at = (pp * 2 + cc) * S
            R.qp[zz, at : at + S, :] = t[q * S : (q + 1) * S, :]
    v_run(1, 1)
    o_run(3, 0)
    total = R.gp[0]
    sent(R.gp.at[1:], R.tiny_s.at[2])
    arrived(R.gp.at[1:], R.tiny_r.at[2])
    for k, dc in plane_all:
        total = total + R.gp[2 * k + dc]
    R.gz_s[...] = total
    for k in range(1, nz):
        o = line(k)
        remote(R.gz_s, R.gz.at[z], R.tiny_s.at[3], R.tiny_r.at[3], dev(p, o, c)).start()

    lane_s = iota((SL, LANES), 1)
    small_t = mm(turned_of(0), R.rb[:, HD : HD + LANES])
    small_h = mm(turned_of(1), R.rb[:, HD : HD + LANES])
    R.pb[:, PS] = jnp.where(lane_s < 2 * GATE, small_t, small_h).astype(BF16)
    send_part(0, PS)
    v_run(2, 0)
    for o in (far, fellow, near):
        to_place(lambda d: R.qp.at[d], lambda d: R.qr.at[d], R.qk_s.at[2], R.qk_s.at[3], o)
    v_run(2, 1)
    o_run(1, 2)
    v_run(3, 0)

    v_run(1, 2)
    arrived(R.qr.at[0 : nz - 1], R.qk_s.at[3])
    got = R.qp[z].astype(F32)
    for k in range(1, nz):
        got = got + R.qr[line(k)].astype(F32)
    R.qs[...] = got
    for k, dc in plane_all:
        remote(
            R.qs.at[pl.ds(times(plane(k) * 2 + side(dc), S), S)],
            R.qf.at[:, columns_of(place)],
            R.qk_s.at[4],
            R.qk_s.at[5],
            dev(plane(k), z, side(dc)),
        ).start()
    R.qf[:, columns_of(place)] = R.qs[pl.ds(times(place, S), S), :]

    R.hid_f[...] += R.out_s[z].astype(F32)
    run_end(R.hid_f, out_sum[1], R.out_sem)
    R.mixed[...] = R.hid_f[...].astype(BF16)

    arrived(R.gz.at[0 : nz - 1], R.tiny_r.at[3])
    for k in range(1, nz):
        total = total + R.gz[line(k)]
    first = (p * 2 * nz + z * 2 + c) * S
    pick_row = iota((D // LANES, LANES), 0) == first // LANES
    line_sum = jnp.sum(jnp.where(pick_row, total, 0.0), axis=0, keepdims=True)
    shift = lax.rem(LANES - lax.rem(first, LANES), LANES)
    line_sum = pltpu.roll(jnp.broadcast_to(line_sum, (8, LANES)), shift, 1)
    R.ggain[...] = line_sum[0:1, 0:S]

    own_rows = pl.ds(times(z, S), S)

    def line_total(part, lanes):
        got = R.pb[own_rows, lanes].astype(F32)
        slots = part_sum(part, lanes)[1]
        arrived(slots(slice(0, nz - 1)), R.p_sem.at[1 + part])
        for k in range(1, nz):
            got = got + slots(line(k))[...].astype(F32)
        return got

    R.go[...] = R.pb[own_rows, PO].astype(F32)
    run_end(R.go, grad_sum(0, PO)[1], R.pn_sem.at[0])
    R.gv[...] = R.pb[own_rows, PV].astype(F32)
    for i, lanes in enumerate(halves):
        half = R.gv.at[:, lanes.start - EV : lanes.stop - EV]
        run_end(half, grad_sum(1 + i, lanes)[1], R.pn_sem.at[1 + i])
    got = line_total(0, PS)

    def pick(width, source):
        a, b = iota((width, LANES), 1), iota((width, LANES), 0)
        return jnp.where(a == source(b), 1.0, 0.0).astype(F32)

    def picked(left, right):
        return lax.dot_general(
            left,
            right,
            (((1,), (1,)), ((), ())),
            preferred_element_type=F32,
            precision=lax.Precision.HIGHEST,
        )

    def router_lane(b):
        at = jnp.zeros_like(b)
        for o in range(nz):
            at = jnp.where(b >= o * own_e, 2 * GATE + o * pad_e + b - o * own_e, at)
        return at

    R.gvg[...] = picked(pick(GATE, lambda b: b), got)
    R.gog[...] = picked(pick(GATE, lambda b: b + GATE), got)
    R.gr[...] = picked(got, pick(experts, router_lane))
    arrived(R.qs.at[0 : (2 * nd - 1) * S], R.qk_s.at[5])
    R.gq[...] = R.qf[:, 0:HD]
    R.gk[...] = R.qf[:, HD : 2 * HD]

    for i, (buf, dst) in enumerate(((R.wdn_b, R.gdn), (R.wup_b, R.gup))):
        arrived(R.eg_r.at[0:2, i], R.eg_s.at[3 + i])
        rows = rows_of(p)
        for x in range(local):
            got = buf[rows, pl.ds(times(c * local + x, DH), DH)].astype(F32)
            for slot in (0, 2):
                got = got + R.eg_r[slot, i, :, x * DH : (x + 1) * DH].astype(F32)
            dst[x] = got

    gather_end(R.cotb, R.cot_ss)
    gather_end(R.hidb, R.hid_ss)
    for buf, lanes, sem in (
        (R.ra, RA, R.ra_s),
        (R.rb, RV, R.rv_s),
        (R.nrm, RN, R.nrm_s),
    ):
        rows_sent(buf, lanes, sem)
    sent(R.maskb.at[0 : nz - 1], R.tiny_s.at[0])
    sent(R.glog_r.at[0 : nz - 1], R.tiny_s.at[1])
    sent(R.gz.at[0 : nz - 1], R.tiny_s.at[3])
    sent(R.gh_r.at[0 : nz - 1], R.gh_sem.at[0])
    sent(R.out_r.at[0 : nz - 1], R.out_sem.at[nz + 1])
    sent(R.qc.at[C:], R.qk_s.at[0])
    sent(R.qr.at[0 : nz - 1], R.qk_s.at[2])
    sent(R.qs.at[0 : (2 * nd - 1) * S], R.qk_s.at[4])
    sent(R.pair_r, R.pair_s.at[0])
    sent(R.eg_r, R.eg_s.at[0])
    sent(R.pr.at[0 : nz - 1], R.p_sem.at[0])
    sent(R.pn.at[0, 0 : nz - 1], R.pn_sem.at[0, nz + 1])
    for i in range(2):
        sent(R.pn.at[1, 0 : nz - 1, :, 0 : EV // 2], R.pn_sem.at[1 + i, nz + 1])


def settle_kernel(*refs):
    n = len(refs) // 2
    copies = [pltpu.make_async_copy(refs[i], refs[n + i], refs[-1].at[i]) for i in range(n)]
    for cp in copies:
        cp.start()
    for cp in copies:
        cp.wait()


def fused_layer(nd, nz, *args):
    (tokens, cotangent, seq_lengths, routes, head_experts, norm_gain) = args[:6]
    (w_query, w_key, w_value, w_output, w_value_gate, w_output_gate, w_router) = args[6:13]
    w_up, w_down = args[13:]
    C = tokens.shape[0]
    local = w_up.shape[0]
    experts = w_router.shape[1]
    own_e = 2 * local
    pad_e = -(-own_e // 16) * 16
    EF, HF, HD = own_e * DH, local * DH, H * DH
    EV = EA * HD
    S = D // (nd * nz * 2)
    SL = S * nz
    PW = 2 * EV + LANES
    s = Scratch()
    s.vmem("wqk_b", (D, 2 * HD), BF16)
    s.vmem("wv_b", (D, EV), BF16)
    s.vmem("wo_b", (D, EV), BF16)
    s.vmem("wup_b", (D, EF), BF16)
    s.vmem("wdn_b", (D, EF), BF16)
    s.vmem("wg_b", (D, LANES), BF16)
    s.vmem("wrl_b", (D, LANES), BF16)
    s.vmem("cotb", (nz * C, D), BF16)
    s.vmem("hidb", (nz * C, D), BF16)
    s.vmem("mask_s", (nz, pad_e, C), BF16)
    s.vmem("maskb", (nz, pad_e, C), BF16)
    s.vmem("std_b", (C, D), F32)
    s.vmem("normed_b", (C, D), BF16)
    s.vmem("q_b", (C, HD), BF16)
    s.vmem("k_b", (C, HD), BF16)
    s.vmem("v_b", (C, HD), BF16)
    s.vmem("gate_b", (C, LANES), F32)
    s.vmem("val_b", (C, EV), F32)
    s.vmem("prob_b", (H, C, C), F32)
    s.vmem("att_b", (C, HD), F32)
    s.vmem("mix_b", (C, EV), BF16)
    s.vmem("hid_f", (C, D), F32)
    s.vmem("lt", (D, 3 * LANES), BF16)
    s.vmem("ltr", (2 * nd, SL, 3 * LANES), BF16)
    s.vmem("nrm", (2 * nd * C, D), BF16)
    s.vmem("qk_b", (C, 2 * HD), BF16)
    s.vmem("qc", (2 * nd * C, LANES), BF16)
    s.vmem("qp", (nz, D // nz, LANES), BF16)
    s.vmem("qr", (nz, D // nz, LANES), BF16)
    s.vmem("qs", (D // nz, LANES), F32)
    s.vmem("qf", (S, 2 * HD), F32)
    s.vmem("ra", (2 * nd * C, HD + LANES), BF16)
    s.vmem("rb", (2 * nd * C, HD + LANES), BF16)
    s.vmem("gact", (nz * C, EF), BF16)
    s.vmem("gra", (nz * C, EF), BF16)
    for name in ("gh_s", "gh_r", "out_s"):
        s.vmem(name, (nz, C, D), BF16)
    s.vmem("out_r", (nz + 1, C, D), BF16)
    s.vmem("gh_x", (2, C, D), BF16)
    for name in ("glog_s", "glog_r"):
        s.vmem(name, (nz, pad_e, C), BF16)
    s.vmem("dg", (D // nd, EF), BF16)
    s.vmem("pair_r", (2, nd, D // nd, HF), BF16)
    s.vmem("eg_r", (nd - 1, 2, D // nd, HF), BF16)
    s.vmem("ghid_f", (C, D), F32)
    s.vmem("ghid_b", (C, D), BF16)
    s.vmem("gatt_b", (C, HD), BF16)
    s.vmem("gval_f", (C, HD), F32)
    s.vmem("small_b", (C, LANES), BF16)
    s.vmem("pb", (SL, PW), BF16)
    s.vmem("pr", (nz, S, PW - 2 * EV), BF16)
    s.vmem("pn", (2, nz + 1, S, EV), BF16)
    s.vmem("gp", (2 * nd, D // LANES, LANES), F32)
    s.vmem("gz_s", (D // LANES, LANES), F32)
    s.vmem("gz", (nz, D // LANES, LANES), F32)
    s.sems("ld", 5)
    for name in ("cot_ss", "hid_ss"):
        s.sems(name, nz + 1)
    for name in ("cot_rs", "hid_rs", "tiny_s", "tiny_r", "lt_s", "gh_sem", "pair_s"):
        s.sems(name, 4)
    for name in ("ra_s", "rv_s", "nrm_s", "qk_s"):
        s.sems(name, 6)
    s.sems("w_s", 2)
    s.sems("eg_s", 5)
    s.sems("p_sem", 3)
    s.sems("out_sem", nz + 2)
    s.sems("pn_sem", 3, nz + 2)

    def out(*shape, dtype=F32):
        return jax.ShapeDtypeStruct(shape, dtype)

    hbm = pl.BlockSpec(memory_space=pl.ANY)
    vmem = pl.BlockSpec(memory_space=pltpu.VMEM)
    names = in_hbm(SMALL) + WEIGHTS + OUTPUTS
    results = (
        out(C, D, dtype=BF16),
        out(C, D),
        out(1, S),
        out(S, HD),
        out(S, HD),
        out(S, EV),
        out(S, EV),
        out(EA * H, S),
        out(EA * H, S),
        out(S, experts),
        out(local, D // nd, DH),
        out(local, D // nd, DH),
    )
    s.vmem("tokens", (C, D), BF16)
    s.vmem("cot", (C, D), BF16)
    s.add("lens", pltpu.SMEM((1, 2), jnp.int32))
    s.vmem("rt", (TOPK, C), jnp.int32)
    s.vmem("het", (2 * H, C), jnp.int32)
    s.vmem("gain", (1, D), F32)
    s.vmem("wvg", (EA * H, D), BF16)
    s.vmem("wog", (EA * H, D), BF16)
    s.vmem("wr", (experts, D), BF16)
    s.sems("ld_in", len(SMALL))
    outs = pl.pallas_call(
        functools.partial(layer_kernel, names + tuple(s.names), nd, nz, local),
        out_shape=[pltpu.VMEM(x.shape, x.dtype) for x in results],
        in_specs=[hbm] * 15,
        out_specs=[vmem] * len(OUTPUTS),
        scratch_shapes=s.shapes,
        compiler_params=pltpu.CompilerParams(
            collective_id=0, has_side_effects=True, vmem_limit_bytes=VMEM_LIMIT
        ),
    )(
        tokens,
        cotangent,
        seq_lengths,
        routes.T,
        head_experts.reshape(C, 2 * H).T,
        norm_gain.reshape(1, D),
        w_value_gate.T,
        w_output_gate.T,
        w_router.T,
        w_query,
        w_key,
        w_value,
        w_output,
        w_up,
        w_down,
    )
    outs = list(
        pl.pallas_call(
            settle_kernel,
            out_shape=results,
            in_specs=[vmem] * len(outs),
            out_specs=[hbm] * len(outs),
            scratch_shapes=[pltpu.SemaphoreType.DMA((len(outs),))],
        )(*[pltpu.with_memory_space_constraint(x, pltpu.VMEM) for x in outs])
    )
    outs[2] = outs[2].reshape(S)
    for i in (7, 8):
        outs[i] = outs[i].T
    return tuple(outs)


VMEM_LIMIT = 58 * 1024 * 1024


def fits(nd, nz, count, experts):
    own_e = experts // nz
    pad_e = -(-own_e // 16) * 16
    return (
        count == LANES
        and nz == 4
        and nd == 4
        and own_e % 4 == 0
        and H * DH == nd * LANES
        and D % (nd * nz * 2 * 16) == 0
        and LANES % (D // (nd * nz * 2)) == 0
        and 2 * EA * H + nz * pad_e <= LANES
    )


def per_device(nd, ne, *args):
    count, experts = args[0].shape[0], args[12].shape[1]
    if ne % 2 == 0 and fits(nd, ne // 2, count, experts):
        return fused_layer(nd, ne // 2, *args)
    return routed_layer(*args)


def solution(mesh):
    return jax.shard_map(
        functools.partial(per_device, mesh.shape["dp"], mesh.shape["expert"]),
        mesh=mesh,
        in_specs=(
            P(("dp", "expert"), None),
            P(("dp", "expert"), None),
            P(("dp", "expert"), None),
            P(("dp", "expert"), None),
            P(("dp", "expert"), None, None),
            P(),
            P(),
            P(),
            P(),
            P(),
            P(),
            P(),
            P(),
            P("expert", None, None),
            P("expert", None, None),
        ),
        out_specs=(
            P(("dp", "expert"), None),
            P(("dp", "expert"), None),
            P(("dp", "expert")),
            P(("dp", "expert"), None),
            P(("dp", "expert"), None),
            P(("dp", "expert"), None),
            P(("dp", "expert"), None),
            P(("dp", "expert"), None),
            P(("dp", "expert"), None),
            P(("dp", "expert"), None),
            P("expert", "dp", None),
            P("expert", "dp", None),
        ),
        check_vma=False,
    )
```
